32 devices in a mesh: tile: 8 (over z, y), grp: 4 (over x, core).
Axes of the slice: x: 2, y: 2, z: 4, core: 2. Of those that a mesh axis runs over, the one named last changes fastest.
Arguments:
- object_field: float32 [2, 2, 2048, 512], P(None, None, 'tile', 'grp'), may hold values from -5 to 5
- probe: float32 [2, 256, 256], replicated, may hold values from -5 to 5
- offsets: int32 [8, 8, 2], P('tile', 'grp'), may hold values from 0 to 256, as said below
- slot_range: int32 [8, 2], P('tile'), may hold values from 0 to 8, as said below
- measured: float32 [8, 8, 256, 256], P('tile', 'grp'), may hold values from 0 to 2
Outputs:
- object_grad: float32 [2, 2, 2048, 512], P(None, None, 'tile', 'grp')
- probe_grad: float32 [2, 256, 256], replicated
The draws below stay inside these ranges and needn't reach their ends.
Inputs may be any that keep to these rules, and one draw needn't show every extreme that they name: `offsets`: the first number is a row offset within the strip, 0 to 255, and 0 for every slot of the last strip; the second is a column offset of 0 to 256. `slot_range`: for each pair of strips 2i and 2i+1 there is one b with strip 2i using slots 0 to b - 1 and strip 2i+1 using slots b to 7; other slots are empty.
All inputs are finite; a program needn't handle non-finite values.
Results may differ from the reference program's by a relative error of at most 0.00017.
Values sent between devices are 32-bit elements; how exact they have to be, the bound alone decides.
No kernel may reach another device: no remote copies, remote signals or barrier semaphores. Data moves between devices by JAX's collectives and lax.ppermute only.
A program may use at most 64 MiB of HBM per device.

```python
import math
import jax
import jax.numpy as jnp
from jax import lax

PW = 256
SLICES = 2
STRIPS = 8
SH = 256
MOST = 8
ROWS = 2048
COLS = 512


def draw_offsets(key, part):
    key = jax.random.fold_in(key, 5)
    key_rows, key_cols = jax.random.split(key)
    rows_drawn = jax.random.randint(key_rows, (STRIPS, MOST), 0, SH)
    not_last = (jnp.arange(STRIPS) < STRIPS - 1).astype(jnp.int32)
    rows_drawn = rows_drawn * not_last[:, None]
    cols_drawn = jax.random.randint(key_cols, (STRIPS, MOST), 0, COLS - PW + 1)
    return jnp.stack([rows_drawn, cols_drawn], -1).astype(jnp.int32)


def draw_slot_range(key, part):
    key = jax.random.fold_in(key, 11)
    split_at = jax.random.randint(key, (STRIPS // 2,), 0, MOST + 1)
    zeros = jnp.zeros_like(split_at)
    full = jnp.full_like(split_at, MOST)
    upper = jnp.stack([zeros, split_at], -1)
    lower = jnp.stack([split_at, full], -1)
    return jnp.stack([upper, lower], 1).reshape(STRIPS, 2).astype(jnp.int32)


def steps_of(stream_key, dims, cuts, low, top_value):
    level = 1.0
    for dim, parts in cuts:
        steps = jax.random.uniform(jax.random.fold_in(jax.random.fold_in(stream_key, 6), dim), (parts,), jnp.float32, low / len(cuts), top_value / len(cuts))
        level = level * jnp.repeat(jnp.exp(steps), dims[dim] // parts).reshape((-1,) + (1,) * (len(dims) - 1 - dim))
    return level


def bell_draw(key, shape, width, limit, cuts=(), kind=jnp.bfloat16):
    entries = jax.random.normal(key, shape, jnp.float32) * width
    if len(cuts) > 0:
        entries = steps_of(key, shape, cuts, -0.22, 0.18) * entries
    return jnp.clip(entries, min=-limit, max=limit).astype(kind)


def setup_inputs(seed: int = 0) -> dict:
    key_list = jax.random.split(jax.random.key(seed), 6)
    return {
        "object_field": bell_draw(key_list[0], (2, SLICES, ROWS, COLS), 0.7, 5.0, ((2, 8), (3, 4)), jnp.float32),
        "probe": bell_draw(key_list[1], (2, PW, PW), 0.7, 5.0, (), jnp.float32),
        "offsets": draw_offsets(jax.random.fold_in(key_list[5], 71), 0),
        "slot_range": draw_slot_range(jax.random.fold_in(key_list[5], 71), 0),
        "measured": jnp.clip(2.0 * jax.random.uniform(key_list[4], (STRIPS, MOST, PW, PW), jnp.float32) ** steps_of(key_list[4], (STRIPS, MOST, PW, PW), ((0, 8), (1, 4)), -0.2, 0.2), 0.0, 2.0),
    }


GRAD_WEIGHT = 0.0625

def fresnel_kernel():
    freq = jnp.arange(PW, dtype=jnp.int32)
    freq = jnp.where(freq < PW // 2, freq, freq - PW)
    total = (freq[:, None] * freq[:, None] + freq[None, :] * freq[None, :]) % (2 * PW)
    phase = -math.pi / PW * total.astype(jnp.float32)
    return (jnp.cos(phase), jnp.sin(phase))

def transform(data_re, data_im, inverse):
    joined = lax.complex(data_re, data_im)
    if inverse:
        result = jnp.fft.ifft2(joined, norm='ortho')
    else:
        result = jnp.fft.fft2(joined, norm='ortho')
    return (jnp.real(result), jnp.imag(result))

def position_grad(patch, probe, target, kernel):
    kern_re, kern_im = kernel
    wave_re, wave_im = (probe[0], probe[1])
    entering = []
    for layer in range(SLICES):
        trans_re, trans_im = (patch[0, layer], patch[1, layer])
        entering.append((wave_re, wave_im))
        exit_re = wave_re * trans_re - wave_im * trans_im
        exit_im = wave_re * trans_im + wave_im * trans_re
        if layer < SLICES - 1:
            spec_re, spec_im = transform(exit_re, exit_im, False)
            spec_re, spec_im = (spec_re * kern_re - spec_im * kern_im, spec_re * kern_im + spec_im * kern_re)
            wave_re, wave_im = transform(spec_re, spec_im, True)
        else:
            far_re, far_im = transform(exit_re, exit_im, False)
    excess = 2.0 * GRAD_WEIGHT * (far_re * far_re + far_im * far_im - target)
    back_re, back_im = transform(excess * far_re, excess * far_im, True)
    grads = []
    for layer in reversed(range(SLICES)):
        trans_re, trans_im = (patch[0, layer], patch[1, layer])
        enter_re, enter_im = entering[layer]
        grads.append((enter_re * back_re + enter_im * back_im, enter_re * back_im - enter_im * back_re))
        up_re = trans_re * back_re + trans_im * back_im
        up_im = trans_re * back_im - trans_im * back_re
        if layer > 0:
            spec_re, spec_im = transform(up_re, up_im, False)
            spec_re, spec_im = (spec_re * kern_re + spec_im * kern_im, spec_im * kern_re - spec_re * kern_im)
            back_re, back_im = transform(spec_re, spec_im, True)
    grads = grads[::-1]
    object_term = jnp.stack([jnp.stack([pair[0] for pair in grads]), jnp.stack([pair[1] for pair in grads])])
    return (object_term, jnp.stack([up_re, up_im]))

def reference(object_field, probe, offsets, slot_range, measured):
    kernel = fresnel_kernel()
    strip_index = jnp.arange(STRIPS, dtype=jnp.int32)
    slot_index = jnp.arange(MOST, dtype=jnp.int32)
    first_rows = (offsets[:, :, 0] + (strip_index * SH)[:, None]).astype(jnp.int32)
    used = (slot_index[None, :] >= slot_range[:, 0:1]) & (slot_index[None, :] < slot_range[:, 1:2])
    live = jnp.where(used, 1.0, 0.0).astype(jnp.float32)
    items = (first_rows.reshape(-1), offsets[:, :, 1].reshape(-1).astype(jnp.int32), live.reshape(-1), measured.reshape(STRIPS * MOST, PW, PW))

    def visit(carry, item):
        row_at, column_at, weight, target = item
        zero = jnp.zeros((), jnp.int32)
        start = (zero, zero, row_at, column_at)
        patch = lax.dynamic_slice(object_field, start, (2, SLICES, PW, PW))
        object_term, probe_term = position_grad(patch, probe, target, kernel)
        current = lax.dynamic_slice(carry[0], start, (2, SLICES, PW, PW))
        total = lax.dynamic_update_slice(carry[0], current + object_term * weight, start)
        return ((total, carry[1] + probe_term * weight), None)
    init = (jnp.zeros_like(object_field), jnp.zeros_like(probe))
    (object_grad, probe_grad), unused = lax.scan(visit, init, items)
    return (object_grad, probe_grad)
```

```python
import functools
import math

import jax
import jax.numpy as jnp
import ml_dtypes
import numpy as np
from jax import lax
from jax.experimental import pallas as pl
from jax.experimental.pallas import tpu as pltpu
from jax.sharding import Mesh, PartitionSpec as P

GRAD_WEIGHT = 0.0625
PLANE = ("half", "col", "core")
VMEM_LIMIT = 48 * 1024 * 1024


def split_bf16(table):
    high = table.astype(ml_dtypes.bfloat16)
    low = (table - high.astype(np.float64)).astype(ml_dtypes.bfloat16)
    return high, low


def tables(width):
    index = np.arange(width, dtype=np.int64)
    scale = 1.0 / math.sqrt(width)
    phase = -2.0 * math.pi / width * (index[:, None] * index[None, :] % width)
    shift = index[:, None] - index[None, :]
    chirp = math.pi / width * (shift * shift % (2 * width)) - math.pi / 4.0
    out = []
    for angle in (phase, chirp):
        real, imag = np.cos(angle) * scale, np.sin(angle) * scale
        for axis in (0, 1):
            out.extend(split_bf16(np.concatenate([real, imag], axis=axis)))
    return out


def split(value):
    high = value.astype(jnp.bfloat16)
    low = (value - high.astype(jnp.float32)).astype(jnp.bfloat16)
    return high, low


def dot(left, right):
    return jnp.dot(left, right, preferred_element_type=jnp.float32)


def times_right(re, im, high, low, conj):
    width = re.shape[0]
    sign = 1.0 if conj else -1.0
    left = jnp.concatenate(
        [jnp.concatenate([re, sign * im], 1), jnp.concatenate([im, -sign * re], 1)], 0
    )
    left_high, left_low = split(left)
    out = dot(left_high, high) + dot(left_low, high) + dot(left_high, low)
    return out[:width], out[width:]


def times_left(re, im, high, low, conj):
    width = re.shape[0]
    sign = 1.0 if conj else -1.0
    right = jnp.concatenate(
        [jnp.concatenate([re, im], 1), jnp.concatenate([sign * im, -sign * re], 1)], 0
    )
    right_high, right_low = split(right)
    out = dot(high, right_high) + dot(high, right_low) + dot(low, right_high)
    return out[:, :width], out[:, width:]


def transform(re, im, tabs, conj):
    right_high, right_low, left_high, left_low = (tab[...] for tab in tabs)
    re, im = times_right(re, im, right_high, right_low, conj)
    return times_left(re, im, left_high, left_low, conj)


def position_kernel(
    place, patch, probe, meas, fr_h, fr_l, fl_h, fl_l, cr_h, cr_l, cl_h, cl_l, grad, probe_grad
):
    far_tabs = (fr_h, fr_l, fl_h, fl_l)
    near_tabs = (cr_h, cr_l, cl_h, cl_l)
    row, col, mine = place[0], place[1], place[2]
    width = probe.shape[-1]

    def load(plane):
        return jnp.concatenate([patch[plane, 0], patch[plane, 1]], axis=1)

    def store(plane, value):
        half = width // 2
        grad[plane, 0] = value[:, :half]
        grad[plane, 1] = value[:, half:]

    def roll(value, rows, cols):
        return pltpu.roll(pltpu.roll(value, rows, 0), cols, 1)

    wave_re, wave_im = roll(probe[0], row, col), roll(probe[1], row, col)
    o0_re, o0_im, o1_re, o1_im = load(0), load(2), load(1), load(3)
    exit_re = wave_re * o0_re - wave_im * o0_im
    exit_im = wave_re * o0_im + wave_im * o0_re
    mid_re, mid_im = transform(exit_re, exit_im, near_tabs, False)
    exit_re = mid_re * o1_re - mid_im * o1_im
    exit_im = mid_re * o1_im + mid_im * o1_re
    far_re, far_im = transform(exit_re, exit_im, far_tabs, False)
    target = jnp.where(mine == 1, meas[0], meas[1])
    excess = 2.0 * GRAD_WEIGHT * (far_re * far_re + far_im * far_im - target)
    back_re, back_im = transform(excess * far_re, excess * far_im, far_tabs, True)
    store(1, mid_re * back_re + mid_im * back_im)
    store(3, mid_re * back_im - mid_im * back_re)
    up_re = o1_re * back_re + o1_im * back_im
    up_im = o1_re * back_im - o1_im * back_re
    back_re, back_im = transform(up_re, up_im, near_tabs, True)
    wave_re, wave_im = roll(probe[0], row, col), roll(probe[1], row, col)
    o0_re, o0_im = load(0), load(2)
    store(0, wave_re * back_re + wave_im * back_im)
    store(2, wave_re * back_im - wave_im * back_re)
    up_re = o0_re * back_re + o0_im * back_im
    up_im = o0_re * back_im - o0_im * back_re
    back_row, back_col = lax.rem(width - row, width), lax.rem(2 * width - col, width)
    probe_grad[0] = roll(up_re, back_row, back_col)
    probe_grad[1] = roll(up_im, back_row, back_col)


def receivers():
    return [2 * (2 * col + core) + half for half in range(2) for col in range(2) for core in range(2)]


def pick_kernel(info, where, own, below, out):
    rows, cols = out.shape[1], out.shape[2]
    row_ids = lax.broadcasted_iota(jnp.int32, (rows, cols), 0)
    col_ids = lax.broadcasted_iota(jnp.int32, (rows, cols), 1) + where[0] * cols
    for place, slot in enumerate(receivers()):
        lower, row, col = info[slot, 0], info[slot, 1], info[slot, 2]
        upper_rows = row_ids >= row
        left_cols = col_ids >= col

        def merged(half, lower=lower, upper_rows=upper_rows):
            second = own[1, half]
            top = jnp.where(lower == 1, second, own[0, half])
            bottom = jnp.where(lower == 1, below[half], second)
            return jnp.where(upper_rows, top, bottom)

        out[place] = jnp.where(left_cols, merged(0), merged(1))


def add_kernel(info, where, parts, own, below):
    rows, cols = parts.shape[1], parts.shape[2]
    row_ids = lax.broadcasted_iota(jnp.int32, (rows, cols), 0)
    col_ids = lax.broadcasted_iota(jnp.int32, (rows, cols), 1) + where[0] * cols
    slots = receivers()
    for strip in range(3):
        sums = [jnp.zeros((rows, cols), jnp.float32)] * 2
        for place, slot in enumerate(slots):
            lower, row, col = info[slot, 0], info[slot, 1], info[slot, 2]
            first = jnp.where(strip == lower, row, jnp.where(strip == lower + 1, 0, rows))
            last = jnp.where(strip == lower, rows, jnp.where(strip == lower + 1, row, 0))
            part = jnp.where((row_ids >= first) & (row_ids < last), parts[place], 0.0)
            left = jnp.where(col_ids >= col, part, 0.0)
            sums = [sums[0] + left, sums[1] + (part - left)]
        for half in range(2):
            if strip < 2:
                own[strip, half] = sums[half]
            else:
                below[half] = sums[half]


SMEM = pl.BlockSpec(memory_space=pltpu.SMEM)
VMEM = pl.BlockSpec(memory_space=pltpu.VMEM)


def call(kernel, out_shape, scalars, arrays, flops, **kwargs):
    outs = out_shape if isinstance(out_shape, (list, tuple)) else [out_shape]
    moved = sum(math.prod(x.shape) * x.dtype.itemsize for x in [*arrays, *outs])
    return pl.pallas_call(
        kernel,
        out_shape=out_shape,
        in_specs=[SMEM] * len(scalars) + [VMEM] * len(arrays),
        out_specs=jax.tree.map(lambda unused: VMEM, out_shape),
        compiler_params=pltpu.CompilerParams(vmem_limit_bytes=VMEM_LIMIT),
        cost_estimate=pl.CostEstimate(flops=flops, bytes_accessed=moved, transcendentals=0),
        **kwargs,
    )(*scalars, *arrays)


def shape(*dims):
    return jax.ShapeDtypeStruct(dims, jnp.float32)


def local(object_field, probe, offsets, slot_range, measured):
    width = probe.shape[-1]
    planes, rows, cols = 4, object_field.shape[2], object_field.shape[3]
    pairs = lax.axis_size("pair")
    half, core = lax.axis_index("half"), lax.axis_index("core")

    places = lax.all_gather(offsets[0], PLANE, axis=0, tiled=False)
    places = places.reshape(2, -1, offsets.shape[2])
    split_at = jnp.where(half == 0, slot_range[0, 1], slot_range[0, 0])
    slots = jnp.arange(places.shape[1], dtype=jnp.int32)
    lower = (slots >= split_at).astype(jnp.int32)
    place = jnp.where(lower[:, None] == 1, places[1], places[0])
    info = jnp.concatenate([lower[:, None], place], axis=1)
    where = core[None]
    my_slot = 2 * (2 * lax.axis_index("col") + core) + half
    my_info = lax.dynamic_slice_in_dim(info, my_slot, 1, 0)[0]
    mine = (my_info[0] == half).astype(jnp.int32)
    my_place = jnp.stack([my_info[1], my_info[2], mine])

    kept = lax.dynamic_index_in_dim(measured[0], half, 0, keepdims=False)
    given = lax.dynamic_index_in_dim(measured[0], 1 - half, 0, keepdims=False)
    taken = lax.ppermute(given, "half", [(0, 1), (1, 0)])
    meas = jnp.stack([kept, taken])

    block = object_field.reshape(planes, rows, cols)
    own = lax.all_to_all(block, ("half", "col"), 0, 0, tiled=True).reshape(2, 2, rows, cols)
    below = lax.ppermute(own[0], "pair", [(k, k - 1) for k in range(1, pairs)])
    parts = call(pick_kernel, shape(8, rows, cols), (info, where), (own, below), 8 * rows * cols)
    patch = lax.all_to_all(parts, PLANE, 0, 0, tiled=True).reshape(planes, 2, rows, cols)

    tabs = [jnp.asarray(tab) for tab in tables(width)]
    far_right, near_right = tabs[0:2], tabs[4:6]
    far_left, near_left = tabs[2:4], tabs[6:8]
    order = [*far_right, *far_left, *near_right, *near_left]
    grad, probe_part = call(
        position_kernel,
        [shape(planes, 2, rows, cols), shape(2, width, width)],
        (my_place,),
        (patch, probe, meas, *order),
        8 * 24 * width**3,
    )

    got = lax.all_to_all(grad.reshape(8, rows, cols), PLANE, 0, 0, tiled=True)
    sums, lower_sums = call(
        add_kernel,
        [shape(2, 2, rows, cols), shape(2, rows, cols)],
        (info, where),
        (got,),
        48 * rows * cols,
    )
    above = lax.ppermute(lower_sums, "pair", [(k, k + 1) for k in range(pairs - 1)])
    total = jnp.stack([sums[0] + above, sums[1]])
    mine_out = lax.all_to_all(total.reshape(4, rows, cols), ("half", "col"), 0, 0, tiled=True)
    object_grad = mine_out.reshape(object_field.shape)

    band = lax.psum_scatter(probe_part, PLANE, scatter_dimension=1, tiled=True)
    band = lax.psum(band, "pair")
    probe_grad = lax.all_gather(band, PLANE, axis=1, tiled=True)
    return (object_grad, probe_grad)


def solution(mesh):
    tile, grp = mesh.shape["tile"], mesh.shape["grp"]
    devices = mesh.devices.reshape(tile // 2, 2, 2, grp // 2)
    inner = Mesh(devices, ("pair", "half", "col", "core"))
    strip, cols = ("pair", "half"), ("col", "core")
    in_specs = (
        P(None, None, strip, cols),
        P(),
        P(strip, cols, None),
        P(strip, None),
        P(strip, cols, None, None),
    )
    out_specs = (P(None, None, strip, cols), P())
    return jax.shard_map(local, mesh=inner, in_specs=in_specs, out_specs=out_specs, check_vma=False)
```

```python
import functools
import math

import jax
import jax.numpy as jnp
import ml_dtypes
import numpy as np
from jax import lax
from jax.experimental import pallas as pl
from jax.experimental.pallas import tpu as pltpu
from jax.sharding import Mesh, PartitionSpec as P

GRAD_WEIGHT = 0.0625
PLANE = ("half", "col", "core")
VMEM_LIMIT = 48 * 1024 * 1024


def tables(width):
    index = np.arange(width, dtype=np.int64)
    scale = 1.0 / math.sqrt(width)
    phase = -2.0 * math.pi / width * (index[:, None] * index[None, :] % width)
    shift = index[:, None] - index[None, :]
    chirp = math.pi / width * (shift * shift % (2 * width)) - math.pi / 4.0
    out = []
    for angle in (phase, chirp):
        table = np.concatenate([np.cos(angle) * scale, np.sin(angle) * scale], axis=0)
        high = table.astype(ml_dtypes.bfloat16)
        low = (table - high.astype(np.float64)).astype(ml_dtypes.bfloat16)
        out.extend([high, low])
    return out


def split(value):
    high = value.astype(jnp.bfloat16)
    low = (value - high.astype(jnp.float32)).astype(jnp.bfloat16)
    return high, low


def dot(left, right):
    return jnp.dot(left, right, preferred_element_type=jnp.float32)


def parts_of(re, im, conj):
    sign = 1.0 if conj else -1.0
    re_high, re_low = split(re)
    im_high, im_low = split(im)
    return (re_high, im_high, sign * im_high, -sign * re_high), (re_low, im_low, sign * im_low, -sign * re_low)


def times_right(re, im, high, low, conj):
    width = re.shape[0]

    def stack(part):
        return jnp.concatenate(
            [jnp.concatenate([part[0], part[2]], 1), jnp.concatenate([part[1], part[3]], 1)], 0
        )

    left_high, left_low = (stack(part) for part in parts_of(re, im, conj))
    out = dot(left_high, high[...]) + dot(left_low, high[...]) + dot(left_high, low[...])
    return out[:width], out[width:]


def times_left(re, im, high, low, conj):
    width = re.shape[0]
    part_high, part_low = parts_of(re, im, conj)

    def product(table, part):
        plain = dot(table[:width], jnp.concatenate(part[:2], 1))
        return plain + dot(table[width:], jnp.concatenate(part[2:], 1))

    out = product(high, part_high) + product(high, part_low) + product(low, part_high)
    return out[:, :width], out[:, width:]


def transform(re, im, tabs, conj):
    re, im = times_right(re, im, *tabs, conj)
    return times_left(re, im, *tabs, conj)


def slot_place(offs, split_at, flat, slot):
    lower = jnp.where(slot >= split_at, 1, 0)
    holder = jnp.bitwise_xor(4 * lower + slot // 2, flat)
    at = 2 * (slot % 2)
    return lower, offs[holder, at], offs[holder, at + 1]


def slot_of(half, col, core):
    return 2 * (2 * col + core) + half


def receivers():
    return [slot_of(half, col, core) for half in range(2) for col in range(2) for core in range(2)]


def position_kernel(
    where, slot_range, offs, patch, probe, measured, taken, far_high, far_low, near_high, near_low, grad
):
    far_tabs, near_tabs = (far_high, far_low), (near_high, near_low)
    half, col, core = where[0], where[1], where[2]
    split_at = slot_range[0, 1 - half]
    lower, row_at, col_at = slot_place(offs, split_at, 4 * half + 2 * col + core, slot_of(half, col, core))
    width = probe.shape[-1]
    lanes = width // 2

    def load(plane):
        return jnp.concatenate([patch[2 * plane], patch[2 * plane + 1]], axis=1)

    def store(plane, value):
        grad[2 * plane, :width] = value[:, :lanes]
        grad[2 * plane + 1, :width] = value[:, lanes:]

    def roll(value, rows, cols):
        return pltpu.roll(pltpu.roll(value, rows, 0), cols, 1)

    wave_re, wave_im = roll(probe[0], row_at, col_at), roll(probe[1], row_at, col_at)
    o0_re, o0_im, o1_re, o1_im = load(0), load(2), load(1), load(3)
    exit_re = wave_re * o0_re - wave_im * o0_im
    exit_im = wave_re * o0_im + wave_im * o0_re
    mid_re, mid_im = transform(exit_re, exit_im, near_tabs, False)
    exit_re = mid_re * o1_re - mid_im * o1_im
    exit_im = mid_re * o1_im + mid_im * o1_re
    far_re, far_im = transform(exit_re, exit_im, far_tabs, False)
    target = jnp.where(lower == half, measured[0, half], taken[...])
    excess = 2.0 * GRAD_WEIGHT * (far_re * far_re + far_im * far_im - target)
    back_re, back_im = transform(excess * far_re, excess * far_im, far_tabs, True)
    store(1, mid_re * back_re + mid_im * back_im)
    store(3, mid_re * back_im - mid_im * back_re)
    up_re = o1_re * back_re + o1_im * back_im
    up_im = o1_re * back_im - o1_im * back_re
    back_re, back_im = transform(up_re, up_im, near_tabs, True)
    wave_re, wave_im = roll(probe[0], row_at, col_at), roll(probe[1], row_at, col_at)
    o0_re, o0_im = load(0), load(2)
    store(0, wave_re * back_re + wave_im * back_im)
    store(2, wave_re * back_im - wave_im * back_re)
    up_re = o0_re * back_re + o0_im * back_im
    up_im = o0_re * back_im - o0_im * back_re
    back_row, back_col = lax.rem(width - row_at, width), lax.rem(2 * width - col_at, width)
    band = 2 * width // 8
    for part, value in enumerate((up_re, up_im)):
        value = roll(value, back_row, back_col)
        for step in range(4):
            rows = value[step * band : (step + 1) * band]
            grad[4 * part + step, width : width + band] = rows[:, :lanes]
            grad[4 * part + step, width + band :] = rows[:, lanes:]


def pick_kernel(where, slot_range, offs, own, below00, below01, below10, below11, out):
    rows, cols = out.shape[1], out.shape[2]
    half, col, core = where[0], where[1], where[2]
    flat = 4 * half + 2 * col + core
    split_at = slot_range[0, 1 - half]
    row_ids = lax.broadcasted_iota(jnp.int32, (rows, cols), 0)
    col_ids = lax.broadcasted_iota(jnp.int32, (rows, cols), 1) + core * cols
    same = jnp.where(half == 0, below00[...], below10[...])
    other = jnp.where(half == 0, below01[...], below11[...])
    below = (jnp.where(col == 0, same, other), jnp.where(col == 0, other, same))
    for place, slot in enumerate(receivers()):
        lower, row_at, col_at = slot_place(offs, split_at, flat, slot)
        upper_rows = row_ids >= row_at
        left_cols = col_ids >= col_at

        def merged(side, lower=lower, upper_rows=upper_rows):
            second = own[2 + side]
            top = jnp.where(lower == 1, second, own[side])
            bottom = jnp.where(lower == 1, below[side], second)
            return jnp.where(upper_rows, top, bottom)

        out[place] = jnp.where(left_cols, merged(0), merged(1))


def add_kernel(where, slot_range, offs, parts, own, below0, below1, probe_band):
    rows, cols = own.shape[1], own.shape[2]
    half, col, core = where[0], where[1], where[2]
    flat = 4 * half + 2 * col + core
    split_at = slot_range[0, 1 - half]
    row_ids = lax.broadcasted_iota(jnp.int32, (rows, cols), 0)
    col_ids = lax.broadcasted_iota(jnp.int32, (rows, cols), 1) + core * cols
    slots = receivers()
    for strip in range(3):
        sums = [jnp.zeros((rows, cols), jnp.float32)] * 2
        for place, slot in enumerate(slots):
            lower, row_at, col_at = slot_place(offs, split_at, flat, slot)
            first = jnp.where(strip == lower, row_at, jnp.where(strip == lower + 1, 0, rows))
            last = jnp.where(strip == lower, rows, jnp.where(strip == lower + 1, row_at, 0))
            part = jnp.where((row_ids >= first) & (row_ids < last), parts[place, :rows], 0.0)
            left = jnp.where(col_ids >= col_at, part, 0.0)
            sums = [sums[0] + left, sums[1] + (part - left)]
        if strip < 2:
            own[2 * strip], own[2 * strip + 1] = sums
        else:
            below0[...] = jnp.where(col == 0, sums[0], sums[1])
            below1[...] = jnp.where(col == 0, sums[1], sums[0])
    band = probe_band.shape[0]
    total = parts[0, rows:]
    for place in range(1, len(slots)):
        total = total + parts[place, rows:]
    probe_band[:, :cols] = total[:band]
    probe_band[:, cols:] = total[band:]


SMEM = pl.BlockSpec(memory_space=pltpu.SMEM)
VMEM = pl.BlockSpec(memory_space=pltpu.VMEM)


def call(kernel, out_shape, scalars, arrays, flops, **kwargs):
    outs = out_shape if isinstance(out_shape, (list, tuple)) else [out_shape]
    moved = sum(math.prod(x.shape) * x.dtype.itemsize for x in [*arrays, *outs])
    return pl.pallas_call(
        kernel,
        out_shape=out_shape,
        in_specs=[SMEM] * len(scalars) + [VMEM] * len(arrays),
        out_specs=jax.tree.map(lambda unused: VMEM, out_shape),
        compiler_params=pltpu.CompilerParams(vmem_limit_bytes=VMEM_LIMIT),
        cost_estimate=pl.CostEstimate(flops=flops, bytes_accessed=moved, transcendentals=0),
        **kwargs,
    )(*scalars, *arrays)


def shape(*dims):
    return jax.ShapeDtypeStruct(dims, jnp.float32)


def shift_pairs(pairs, step, half, turn):
    out = []
    for pair in range(pairs - 1):
        for col in range(2):
            lower, upper = 4 * (pair + 1) + (col ^ turn), 4 * pair + 2 * half + col
            out.append((lower, upper) if step == 1 else (upper, lower))
    return out


def local(object_field, probe, offsets, slot_range, measured):
    width = probe.shape[-1]
    planes, rows, cols = 4, object_field.shape[2], object_field.shape[3]
    pairs = lax.axis_size("pair")
    half, col, core = (lax.axis_index(name) for name in PLANE)
    where = jnp.stack([half, col, core])

    block = object_field.reshape(planes, rows, cols)
    own = lax.all_to_all(block, ("half", "col"), 0, 0, tiled=True)
    mine = offsets.reshape(1, -1)
    offs = [mine] + [lax.ppermute(mine, PLANE, [(k, k ^ turn) for k in range(8)]) for turn in range(1, 8)]
    offs = jnp.concatenate(offs, axis=0)
    below = []
    for to_half in range(2):
        for turn in range(2):
            plane = lax.dynamic_index_in_dim(block, 2 * to_half + (col ^ turn), 0, keepdims=False)
            below.append(lax.ppermute(plane, ("pair", "half", "col"), shift_pairs(pairs, 1, to_half, turn)))
    given = lax.dynamic_index_in_dim(measured[0], 1 - half, 0, keepdims=False)
    taken = lax.ppermute(given, "half", [(0, 1), (1, 0)])

    scalars = (where, slot_range, offs)
    parts = call(pick_kernel, shape(8, rows, cols), scalars, (own, *below), 8 * rows * cols)
    patch = lax.all_to_all(parts, PLANE, 0, 0, tiled=True)
    tabs = [jnp.asarray(tab) for tab in tables(width)]
    band = 2 * width // 8
    grad = call(
        position_kernel,
        shape(8, rows + 2 * band, cols),
        scalars,
        (patch, probe, measured, taken, *tabs),
        8 * 24 * width**3,
    )
    got = lax.all_to_all(grad, PLANE, 0, 0, tiled=True)
    sums, *lower_sums, probe_band = call(
        add_kernel,
        [shape(4, rows, cols), shape(rows, cols), shape(rows, cols), shape(band, width)],
        scalars,
        (got,),
        48 * rows * cols,
    )
    added = []
    for from_half in range(2):
        for turn in range(2):
            perm = shift_pairs(pairs, -1, from_half, turn)
            added.append(lax.ppermute(lower_sums[turn], ("pair", "half", "col"), perm))
    mine_out = lax.all_to_all(sums, ("half", "col"), 0, 0, tiled=True)
    probe_band = jnp.sum(lax.all_gather(probe_band, "pair", axis=0), axis=0)
    probe_grad = lax.all_gather(probe_band, PLANE, axis=0, tiled=True).reshape(probe.shape)
    straight = [jnp.where(col == 0, added[2 * k], added[2 * k + 1]) for k in range(2)]
    crossed = [jnp.where(col == 0, added[2 * k + 1], added[2 * k]) for k in range(2)]
    above = jnp.stack([straight[0], crossed[0], straight[1], crossed[1]])
    object_grad = (mine_out + above).reshape(object_field.shape)
    return (object_grad, probe_grad)


def solution(mesh):
    tile, grp = mesh.shape["tile"], mesh.shape["grp"]
    devices = mesh.devices.reshape(tile // 2, 2, 2, grp // 2)
    inner = Mesh(devices, ("pair", "half", "col", "core"))
    strip, cols = ("pair", "half"), ("col", "core")
    in_specs = (
        P(None, None, strip, cols),
        P(),
        P(strip, cols, None),
        P(strip, None),
        P(strip, cols, None, None),
    )
    out_specs = (P(None, None, strip, cols), P())
    return jax.shard_map(local, mesh=inner, in_specs=in_specs, out_specs=out_specs, check_vma=False)
```

```python
import functools
import math

import jax
import jax.numpy as jnp
import ml_dtypes
import numpy as np
from jax import lax
from jax.experimental import pallas as pl
from jax.experimental.pallas import tpu as pltpu
from jax.sharding import Mesh, PartitionSpec as P

GRAD_WEIGHT = 0.0625
PLANE = ("half", "col", "core")
VMEM_LIMIT = 48 * 1024 * 1024


def tables(width):
    index = np.arange(width, dtype=np.int64)
    scale = 1.0 / math.sqrt(width)
    phase = -2.0 * math.pi / width * (index[:, None] * index[None, :] % width)
    shift = index[:, None] - index[None, :]
    chirp = math.pi / width * (shift * shift % (2 * width)) - math.pi / 4.0
    out = []
    for angle in (phase, chirp):
        table = np.concatenate([np.cos(angle) * scale, np.sin(angle) * scale], axis=0)
        high = table.astype(ml_dtypes.bfloat16)
        low = (table - high.astype(np.float64)).astype(ml_dtypes.bfloat16)
        out.extend([high, low])
    return out


def split(value):
    high = value.astype(jnp.bfloat16)
    low = (value - high.astype(jnp.float32)).astype(jnp.bfloat16)
    return high, low


def dot(left, right):
    return jnp.dot(left, right, preferred_element_type=jnp.float32)


def parts_of(re, im, conj):
    sign = 1.0 if conj else -1.0
    re_high, re_low = split(re)
    im_high, im_low = split(im)
    return (re_high, im_high, sign * im_high, -sign * re_high), (re_low, im_low, sign * im_low, -sign * re_low)


def times_right(re, im, high, low, conj):
    width = re.shape[0]

    def stack(part):
        return jnp.concatenate(
            [jnp.concatenate([part[0], part[2]], 1), jnp.concatenate([part[1], part[3]], 1)], 0
        )

    left_high, left_low = (stack(part) for part in parts_of(re, im, conj))
    out = dot(left_high, high[...]) + dot(left_low, high[...]) + dot(left_high, low[...])
    return out[:width], out[width:]


def times_left(re, im, high, low, conj):
    width = re.shape[0]
    part_high, part_low = parts_of(re, im, conj)

    def product(table, part):
        plain = dot(table[:width], jnp.concatenate(part[:2], 1))
        return plain + dot(table[width:], jnp.concatenate(part[2:], 1))

    out = product(high, part_high) + product(high, part_low) + product(low, part_high)
    return out[:, :width], out[:, width:]


def transform(re, im, tabs, conj):
    re, im = times_right(re, im, *tabs, conj)
    return times_left(re, im, *tabs, conj)


def slot_of(half, col, core):
    return 2 * (2 * col + core) + half


def receivers():
    return [slot_of(half, col, core) for half in range(2) for col in range(2) for core in range(2)]


def slot_place(offs, split_at, slot):
    lower = jnp.where(slot >= split_at, 1, 0)
    at = 2 * (slot % 4)
    return lower, offs[2 * lower + slot // 4, at], offs[2 * lower + slot // 4, at + 1]


def position_kernel(
    where, slot_range, offs, patch, probe, measured, taken, far_high, far_low, near_high, near_low, grad
):
    far_tabs, near_tabs = (far_high, far_low), (near_high, near_low)
    half, col, core = where[0], where[1], where[2]
    split_at = slot_range[0, 1 - half]
    lower, row_at, col_at = slot_place(offs, split_at, slot_of(half, col, core))
    width = probe.shape[-1]
    lanes = width // 2

    def load(plane):
        return jnp.concatenate([patch[2 * plane], patch[2 * plane + 1]], axis=1)

    def store(plane, value):
        grad[2 * plane, :width] = value[:, :lanes]
        grad[2 * plane + 1, :width] = value[:, lanes:]

    def roll(value, rows, cols):
        return pltpu.roll(pltpu.roll(value, rows, 0), cols, 1)

    wave_re, wave_im = roll(probe[0], row_at, col_at), roll(probe[1], row_at, col_at)
    o0_re, o0_im, o1_re, o1_im = load(0), load(2), load(1), load(3)
    exit_re = wave_re * o0_re - wave_im * o0_im
    exit_im = wave_re * o0_im + wave_im * o0_re
    mid_re, mid_im = transform(exit_re, exit_im, near_tabs, False)
    exit_re = mid_re * o1_re - mid_im * o1_im
    exit_im = mid_re * o1_im + mid_im * o1_re
    far_re, far_im = transform(exit_re, exit_im, far_tabs, False)
    target = jnp.where(lower == half, measured[0, half], taken[...])
    excess = 2.0 * GRAD_WEIGHT * (far_re * far_re + far_im * far_im - target)
    back_re, back_im = transform(excess * far_re, excess * far_im, far_tabs, True)
    store(1, mid_re * back_re + mid_im * back_im)
    store(3, mid_re * back_im - mid_im * back_re)
    up_re = o1_re * back_re + o1_im * back_im
    up_im = o1_re * back_im - o1_im * back_re
    back_re, back_im = transform(up_re, up_im, near_tabs, True)
    wave_re, wave_im = roll(probe[0], row_at, col_at), roll(probe[1], row_at, col_at)
    o0_re, o0_im = load(0), load(2)
    store(0, wave_re * back_re + wave_im * back_im)
    store(2, wave_re * back_im - wave_im * back_re)
    up_re = o0_re * back_re + o0_im * back_im
    up_im = o0_re * back_im - o0_im * back_re
    back_row, back_col = lax.rem(width - row_at, width), lax.rem(2 * width - col_at, width)
    band = 2 * width // 8
    for part, value in enumerate((up_re, up_im)):
        value = roll(value, back_row, back_col)
        for step in range(4):
            rows = value[step * band : (step + 1) * band]
            grad[4 * part + step, width : width + band] = rows[:, :lanes]
            grad[4 * part + step, width + band :] = rows[:, lanes:]


def pick_kernel(where, slot_range, own, below00, below01, below10, below11, out):
    rows, cols = out.shape[1], out.shape[2]
    half, col, core = where[0], where[1], where[2]
    split_at = slot_range[0, 1 - half]
    row_ids = lax.broadcasted_iota(jnp.int32, (rows, cols), 0).astype(jnp.float32)
    col_ids = (lax.broadcasted_iota(jnp.int32, (rows, cols), 1) + core * cols).astype(jnp.float32)
    same = jnp.where(half == 0, below00[...], below10[...])
    other = jnp.where(half == 0, below01[...], below11[...])
    below = (jnp.where(col == 0, same, other), jnp.where(col == 0, other, same))
    for place, slot in enumerate(receivers()):
        lower = jnp.where(slot >= split_at, 1, 0)
        at = rows + 2 * (slot % 4)
        offs = jnp.where(lower == 1, own[2 + slot // 4, at : at + 2], own[slot // 4, at : at + 2])
        upper_rows = row_ids >= offs[0:1]
        left_cols = col_ids >= offs[1:2]

        def merged(side, lower=lower, upper_rows=upper_rows):
            second = own[2 + side, :rows]
            top = jnp.where(lower == 1, second, own[side, :rows])
            bottom = jnp.where(lower == 1, below[side], second)
            return jnp.where(upper_rows, top, bottom)

        out[place] = jnp.where(left_cols, merged(0), merged(1))


def add_kernel(where, slot_range, offs, parts, own, below0, below1, probe_band):
    rows, cols = own.shape[1], own.shape[2]
    half, col, core = where[0], where[1], where[2]
    split_at = slot_range[0, 1 - half]
    row_ids = lax.broadcasted_iota(jnp.int32, (rows, cols), 0)
    col_ids = lax.broadcasted_iota(jnp.int32, (rows, cols), 1) + core * cols
    slots = receivers()
    for strip in range(3):
        sums = [jnp.zeros((rows, cols), jnp.float32)] * 2
        for place, slot in enumerate(slots):
            lower, row_at, col_at = slot_place(offs, split_at, slot)
            first = jnp.where(strip == lower, row_at, jnp.where(strip == lower + 1, 0, rows))
            last = jnp.where(strip == lower, rows, jnp.where(strip == lower + 1, row_at, 0))
            part = jnp.where((row_ids >= first) & (row_ids < last), parts[place, :rows], 0.0)
            left = jnp.where(col_ids >= col_at, part, 0.0)
            sums = [sums[0] + left, sums[1] + (part - left)]
        if strip < 2:
            own[2 * strip], own[2 * strip + 1] = sums
        else:
            below0[...] = jnp.where(col == 0, sums[0], sums[1])
            below1[...] = jnp.where(col == 0, sums[1], sums[0])
    band = probe_band.shape[0]
    total = parts[0, rows:]
    for place in range(1, len(slots)):
        total = total + parts[place, rows:]
    probe_band[:, :cols] = total[:band]
    probe_band[:, cols:] = total[band:]


SMEM = pl.BlockSpec(memory_space=pltpu.SMEM)
VMEM = pl.BlockSpec(memory_space=pltpu.VMEM)


def call(kernel, out_shape, scalars, arrays, flops, **kwargs):
    outs = out_shape if isinstance(out_shape, (list, tuple)) else [out_shape]
    moved = sum(math.prod(x.shape) * x.dtype.itemsize for x in [*arrays, *outs])
    return pl.pallas_call(
        kernel,
        out_shape=out_shape,
        in_specs=[SMEM] * len(scalars) + [VMEM] * len(arrays),
        out_specs=jax.tree.map(lambda unused: VMEM, out_shape),
        compiler_params=pltpu.CompilerParams(vmem_limit_bytes=VMEM_LIMIT),
        cost_estimate=pl.CostEstimate(flops=flops, bytes_accessed=moved, transcendentals=0),
        **kwargs,
    )(*scalars, *arrays)


def shape(*dims):
    return jax.ShapeDtypeStruct(dims, jnp.float32)


def shift_pairs(pairs, step, half, turn):
    out = []
    for pair in range(pairs - 1):
        for col in range(2):
            lower, upper = 4 * (pair + 1) + (col ^ turn), 4 * pair + 2 * half + col
            out.append((lower, upper) if step == 1 else (upper, lower))
    return out


def sum_over(value, axis, size):
    if size & (size - 1):
        return lax.psum(value, axis)
    step = 1
    while step < size:
        value = value + lax.ppermute(value, axis, [(k, k ^ step) for k in range(size)])
        step *= 2
    return value


def local(object_field, probe, offsets, slot_range, measured):
    width = probe.shape[-1]
    planes, rows, cols = 4, object_field.shape[2], object_field.shape[3]
    pairs = lax.axis_size("pair")
    half, col, core = (lax.axis_index(name) for name in PLANE)
    where = jnp.stack([half, col, core])

    block = object_field.reshape(planes, rows, cols)
    mine = offsets.reshape(1, -1).astype(jnp.float32)
    sibling = lax.ppermute(mine, "core", [(0, 1), (1, 0)])
    places = jnp.where(core == 0, jnp.concatenate([mine, sibling], 1), jnp.concatenate([sibling, mine], 1))
    places = jnp.broadcast_to(places.reshape(1, -1, 1), (planes, places.size, cols))
    own = lax.all_to_all(jnp.concatenate([block, places], axis=1), ("half", "col"), 0, 0, tiled=True)
    below = []
    for to_half in range(2):
        for turn in range(2):
            plane = lax.dynamic_index_in_dim(block, 2 * to_half + (col ^ turn), 0, keepdims=False)
            below.append(lax.ppermute(plane, ("pair", "half", "col"), shift_pairs(pairs, 1, to_half, turn)))
    given = lax.dynamic_index_in_dim(measured[0], 1 - half, 0, keepdims=False)
    taken = lax.ppermute(given, "half", [(0, 1), (1, 0)])

    own, taken = lax.optimization_barrier((own, taken))
    parts = call(pick_kernel, shape(8, rows, cols), (where, slot_range), (own, *below), 8 * rows * cols)
    scalars = (where, slot_range, own[:, rows:, 0].astype(jnp.int32))
    patch = lax.all_to_all(parts, PLANE, 0, 0, tiled=True)
    tabs = [jnp.asarray(tab) for tab in tables(width)]
    band = 2 * width // 8
    grad = call(
        position_kernel,
        shape(8, rows + 2 * band, cols),
        scalars,
        (patch, probe, measured, taken, *tabs),
        8 * 24 * width**3,
    )
    got = lax.all_to_all(grad, PLANE, 0, 0, tiled=True)
    sums, *lower_sums, probe_band = call(
        add_kernel,
        [shape(4, rows, cols), shape(rows, cols), shape(rows, cols), shape(band, width)],
        scalars,
        (got,),
        48 * rows * cols,
    )
    added = []
    for from_half in range(2):
        for turn in range(2):
            perm = shift_pairs(pairs, -1, from_half, turn)
            added.append(lax.ppermute(lower_sums[turn], ("pair", "half", "col"), perm))
    mine_out = lax.all_to_all(sums, ("half", "col"), 0, 0, tiled=True)
    probe_band = sum_over(probe_band, "pair", pairs)
    probe_grad = lax.all_gather(probe_band, PLANE, axis=0, tiled=True).reshape(probe.shape)
    straight = [jnp.where(col == 0, added[2 * k], added[2 * k + 1]) for k in range(2)]
    crossed = [jnp.where(col == 0, added[2 * k + 1], added[2 * k]) for k in range(2)]
    above = jnp.stack([straight[0], crossed[0], straight[1], crossed[1]])
    object_grad = (mine_out + above).reshape(object_field.shape)
    return (object_grad, probe_grad)


def solution(mesh):
    tile, grp = mesh.shape["tile"], mesh.shape["grp"]
    devices = mesh.devices.reshape(tile // 2, 2, 2, grp // 2)
    inner = Mesh(devices, ("pair", "half", "col", "core"))
    strip, cols = ("pair", "half"), ("col", "core")
    in_specs = (
        P(None, None, strip, cols),
        P(),
        P(strip, cols, None),
        P(strip, None),
        P(strip, cols, None, None),
    )
    out_specs = (P(None, None, strip, cols), P())
    return jax.shard_map(local, mesh=inner, in_specs=in_specs, out_specs=out_specs, check_vma=False)
```

```python
import functools
import math

import jax
import jax.numpy as jnp
import ml_dtypes
import numpy as np
from jax import lax
from jax.experimental import pallas as pl
from jax.experimental.pallas import tpu as pltpu
from jax.sharding import Mesh, PartitionSpec as P

GRAD_WEIGHT = 0.0625
PLANE = ("half", "col", "core")
VMEM_LIMIT = 24 * 1024 * 1024


def tables(width):
    index = np.arange(width, dtype=np.int64)
    scale = 1.0 / math.sqrt(width)
    phase = -2.0 * math.pi / width * (index[:, None] * index[None, :] % width)
    shift = index[:, None] - index[None, :]
    chirp = math.pi / width * (shift * shift % (2 * width)) - math.pi / 4.0
    out = []
    for angle in (phase, chirp):
        real, imag = np.cos(angle) * scale, np.sin(angle) * scale
        table = np.concatenate([-imag, real, imag, real, -imag], axis=0)
        high = table.astype(ml_dtypes.bfloat16)
        low = (table - high.astype(np.float64)).astype(ml_dtypes.bfloat16)
        out.extend([high, low])
    return np.stack(out)


def split(value):
    high = value.astype(jnp.bfloat16)
    low = (value - high.astype(jnp.float32)).astype(jnp.bfloat16)
    return high, low


def dot(left, right):
    return jnp.dot(left, right, preferred_element_type=jnp.float32)


def transform(re, im, tabs, first, conj):
    width = re.shape[0]

    def rows(which, start):
        return tabs[first + which, start * width : (start + 2) * width]

    re_high, re_low = split(re)
    im_high, im_low = split(im)
    high = jnp.concatenate([re_high, im_high], 1)
    both = jnp.concatenate([high, jnp.concatenate([re_low, im_low], 1)], 0)

    def product(start):
        twice = dot(both, rows(0, start))
        return twice[:width] + (twice[width:] + dot(high, rows(1, start)))

    re, im = (product(1), product(0)) if conj else (product(3), product(2))
    by_re, by_im = (3, 2) if conj else (1, 0)
    re_high, re_low = split(re)
    im_high, im_low = split(im)
    out = dot(rows(0, by_re), re_low) + dot(rows(0, by_im), im_low)
    out += dot(rows(1, by_re), re_high) + dot(rows(1, by_im), im_high)
    out += dot(rows(0, by_re), re_high) + dot(rows(0, by_im), im_high)
    return out[:width], out[width:]


def slot_of(half, col, core):
    return 2 * (2 * col + core) + half


def receivers():
    return [slot_of(half, col, core) for half in range(2) for col in range(2) for core in range(2)]


def slot_place(offs, split_at, slot):
    lower = jnp.where(slot >= split_at, 1, 0)
    holder, at = 4 * lower + slot // 2, 2 * (slot % 2)
    return lower, offs[holder, at], offs[holder, at + 1]


def position_kernel(where, slot_range, offs, patch, probe, measured, taken, tabs, grad):
    half, col, core = where[0], where[1], where[2]
    split_at = slot_range[0, 1 - half]
    lower, row_at, col_at = slot_place(offs, split_at, slot_of(half, col, core))
    width = probe.shape[-1]
    rows, band = width // 2, width // 4

    def load(plane):
        return jnp.concatenate([patch[2 * plane], patch[2 * plane + 1]], axis=0)

    def store(plane, value):
        grad[2 * plane, :rows] = value[:rows]
        grad[2 * plane + 1, :rows] = value[rows:]

    def roll(value, rows, cols):
        return pltpu.roll(pltpu.roll(value, rows, 0), cols, 1)

    wave_re, wave_im = roll(probe[0], row_at, col_at), roll(probe[1], row_at, col_at)
    o0_re, o0_im, o1_re, o1_im = load(0), load(2), load(1), load(3)
    exit_re = wave_re * o0_re - wave_im * o0_im
    exit_im = wave_re * o0_im + wave_im * o0_re
    mid_re, mid_im = transform(exit_re, exit_im, tabs, 2, False)
    exit_re = mid_re * o1_re - mid_im * o1_im
    exit_im = mid_re * o1_im + mid_im * o1_re
    far_re, far_im = transform(exit_re, exit_im, tabs, 0, False)
    target = jnp.where(lower == half, measured[0, half], taken[...])
    excess = 2.0 * GRAD_WEIGHT * (far_re * far_re + far_im * far_im - target)
    back_re, back_im = transform(excess * far_re, excess * far_im, tabs, 0, True)
    store(1, mid_re * back_re + mid_im * back_im)
    store(3, mid_re * back_im - mid_im * back_re)
    up_re = o1_re * back_re + o1_im * back_im
    up_im = o1_re * back_im - o1_im * back_re
    back_re, back_im = transform(up_re, up_im, tabs, 2, True)
    wave_re, wave_im = roll(probe[0], row_at, col_at), roll(probe[1], row_at, col_at)
    o0_re, o0_im = load(0), load(2)
    store(0, wave_re * back_re + wave_im * back_im)
    store(2, wave_re * back_im - wave_im * back_re)
    up_re = o0_re * back_re + o0_im * back_im
    up_im = o0_re * back_im - o0_im * back_re
    back_row, back_col = lax.rem(width - row_at, width), lax.rem(2 * width - col_at, width)
    for part, value in enumerate((up_re, up_im)):
        value = roll(value, back_row, back_col)
        for step in range(4):
            grad[4 * part + step, rows:] = value[step * band : (step + 1) * band]


def pick_kernel(where, slot_range, offs, own, below, out):
    rows, lanes = out.shape[1], out.shape[2] // 2
    half, core = where[0], where[2]
    split_at = slot_range[0, 1 - half]
    row_ids = lax.broadcasted_iota(jnp.int32, (rows, lanes), 0) + core * rows
    col_ids = lax.broadcasted_iota(jnp.int32, (rows, lanes), 1)
    for place, slot in enumerate(receivers()):
        lower, row_at, col_at = slot_place(offs, split_at, slot)
        upper_rows = row_ids >= row_at
        for part in range(2):

            def merged(side, lower=lower, upper_rows=upper_rows, part=part):
                at = 2 * side + part
                second = own[4 + at, :rows]
                top = jnp.where(lower == 1, second, own[at, :rows])
                bottom = jnp.where(lower == 1, below[at, :rows], second)
                return jnp.where(upper_rows, top, bottom)

            left_cols = col_ids + part * lanes >= col_at
            out[place, :, part * lanes : (part + 1) * lanes] = jnp.where(left_cols, merged(0), merged(1))


def add_kernel(where, slot_range, offs, parts, own, below, probe_band):
    rows, lanes = own.shape[1], own.shape[2]
    half, core = where[0], where[2]
    split_at = slot_range[0, 1 - half]
    row_ids = lax.broadcasted_iota(jnp.int32, (rows, lanes), 0) + core * rows
    col_ids = lax.broadcasted_iota(jnp.int32, (rows, lanes), 1)
    slots = receivers()
    for strip in range(3):
        for part in range(2):
            sums = [jnp.zeros((rows, lanes), jnp.float32)] * 2
            for place, slot in enumerate(slots):
                lower, row_at, col_at = slot_place(offs, split_at, slot)
                first = jnp.where(strip == lower, row_at, jnp.where(strip == lower + 1, 0, 2 * rows))
                last = jnp.where(strip == lower, 2 * rows, jnp.where(strip == lower + 1, row_at, 0))
                value = parts[place, :rows, part * lanes : (part + 1) * lanes]
                value = jnp.where((row_ids >= first) & (row_ids < last), value, 0.0)
                left = jnp.where(col_ids + part * lanes >= col_at, value, 0.0)
                sums = [sums[0] + left, sums[1] + (value - left)]
            for side in range(2):
                if strip < 2:
                    own[4 * strip + 2 * side + part] = sums[side]
                else:
                    below[2 * side + part] = sums[side]
    total = parts[0, rows:]
    for place in range(1, len(slots)):
        total = total + parts[place, rows:]
    probe_band[...] = total


SMEM = pl.BlockSpec(memory_space=pltpu.SMEM)
VMEM = pl.BlockSpec(memory_space=pltpu.VMEM)


def call(kernel, out_shape, scalars, arrays, flops, **kwargs):
    outs = out_shape if isinstance(out_shape, (list, tuple)) else [out_shape]
    moved = sum(math.prod(x.shape) * x.dtype.itemsize for x in [*arrays, *outs])
    return pl.pallas_call(
        kernel,
        out_shape=out_shape,
        in_specs=[SMEM] * len(scalars) + [VMEM] * len(arrays),
        out_specs=jax.tree.map(lambda unused: VMEM, out_shape),
        compiler_params=pltpu.CompilerParams(vmem_limit_bytes=VMEM_LIMIT),
        cost_estimate=pl.CostEstimate(flops=flops, bytes_accessed=moved, transcendentals=0),
        **kwargs,
    )(*scalars, *arrays)


def shape(*dims):
    return jax.ShapeDtypeStruct(dims, jnp.float32)


def sum_over(value, axis, size):
    if size & (size - 1):
        return lax.psum(value, axis)
    step = 1
    while step < size:
        value = value + lax.ppermute(value, axis, [(k, k ^ step) for k in range(size)])
        step *= 2
    return value


def local(object_field, probe, offsets, slot_range, measured):
    width, cols = probe.shape[-1], object_field.shape[3]
    rows, band = width // 2, width // 4
    pairs = lax.axis_size("pair")
    half, col, core = (lax.axis_index(name) for name in PLANE)
    where = jnp.stack([half, col, core])

    block = object_field.reshape(8, rows, cols)
    places = jnp.pad(offsets.reshape(1, -1, 1).astype(jnp.float32), ((0, 0), (0, 4), (0, 0)))
    places = jnp.broadcast_to(places, (8, places.shape[1], cols))
    own = lax.all_to_all(jnp.concatenate([block, places], axis=1), PLANE, 0, 0, tiled=True)
    given = lax.dynamic_index_in_dim(measured[0], 1 - half, 0, keepdims=False)
    own, given = lax.optimization_barrier((own, given))
    below = lax.ppermute(own[:4], "pair", [(k, k - 1) for k in range(1, pairs)])
    taken = lax.ppermute(given, "half", [(0, 1), (1, 0)])
    below, taken = lax.optimization_barrier((below, taken))

    scalars = (where, slot_range, own[:, rows : rows + 4, 0].astype(jnp.int32))
    parts = call(pick_kernel, shape(8, rows, width), scalars, (own, below), 32 * rows * width)
    patch = lax.all_to_all(parts, PLANE, 0, 0, tiled=True)
    grad = call(
        position_kernel,
        shape(8, rows + band, width),
        scalars,
        (patch, probe, measured, taken, jnp.asarray(tables(width))),
        8 * 24 * width**3,
    )
    got = lax.all_to_all(grad, PLANE, 0, 0, tiled=True)
    sums, lower_sums, probe_band = call(
        add_kernel,
        [shape(8, rows, cols), shape(4, rows, cols), shape(band, width)],
        scalars,
        (got,),
        96 * rows * width,
    )
    above = lax.ppermute(lower_sums, "pair", [(k, k + 1) for k in range(pairs - 1)])
    probe_band = sum_over(probe_band, "pair", pairs)
    total = jnp.concatenate([sums[:4] + above, sums[4:]])
    object_grad = lax.all_to_all(total, PLANE, 0, 0, tiled=True).reshape(object_field.shape)
    probe_grad = lax.all_gather(probe_band, PLANE, axis=0, tiled=True).reshape(probe.shape)
    return (object_grad, probe_grad)


def solution(mesh):
    tile, grp = mesh.shape["tile"], mesh.shape["grp"]
    devices = mesh.devices.reshape(tile // 2, 2, 2, grp // 2)
    inner = Mesh(devices, ("pair", "half", "col", "core"))
    strip, cols = ("pair", "half"), ("col", "core")
    in_specs = (
        P(None, None, strip, cols),
        P(),
        P(strip, cols, None),
        P(strip, None),
        P(strip, cols, None, None),
    )
    out_specs = (P(None, None, strip, cols), P())
    return jax.shard_map(local, mesh=inner, in_specs=in_specs, out_specs=out_specs, check_vma=False)
```

```python
import functools
import math

import jax
import jax.numpy as jnp
import ml_dtypes
import numpy as np
from jax import lax
from jax.experimental import pallas as pl
from jax.experimental.pallas import tpu as pltpu
from jax.sharding import Mesh, PartitionSpec as P

GRAD_WEIGHT = 0.0625
PLANE = ("half", "col", "core")
AROUND = ("pair", "half", "col")
VMEM_LIMIT = 24 * 1024 * 1024


def tables(width):
    index = np.arange(width, dtype=np.int64)
    scale = 1.0 / math.sqrt(width)
    phase = -2.0 * math.pi / width * (index[:, None] * index[None, :] % width)
    shift = index[:, None] - index[None, :]
    chirp = math.pi / width * (shift * shift % (2 * width)) - math.pi / 4.0
    out = []
    for angle in (phase, chirp):
        real, imag = np.cos(angle) * scale, np.sin(angle) * scale
        table = np.concatenate([-imag, real, imag, real, -imag], axis=0)
        high = table.astype(ml_dtypes.bfloat16)
        low = (table - high.astype(np.float64)).astype(ml_dtypes.bfloat16)
        out.extend([high, low])
    return np.stack(out)


def split(value):
    high = value.astype(jnp.bfloat16)
    low = (value - high.astype(jnp.float32)).astype(jnp.bfloat16)
    return high, low


def dot(left, right):
    return jnp.dot(left, right, preferred_element_type=jnp.float32)


def transform(re, im, tabs, first, conj):
    width = re.shape[0]

    def rows(which, start):
        return tabs[first + which, start * width : (start + 2) * width]

    re_high, re_low = split(re)
    im_high, im_low = split(im)
    high = jnp.concatenate([re_high, im_high], 1)
    both = jnp.concatenate([high, jnp.concatenate([re_low, im_low], 1)], 0)

    def product(start):
        twice = dot(both, rows(0, start))
        return twice[:width] + (twice[width:] + dot(high, rows(1, start)))

    re, im = (product(1), product(0)) if conj else (product(3), product(2))
    by_re, by_im = (3, 2) if conj else (1, 0)
    re_high, re_low = split(re)
    im_high, im_low = split(im)
    out = dot(rows(0, by_re), re_low) + dot(rows(0, by_im), im_low)
    out += dot(rows(1, by_re), re_high) + dot(rows(1, by_im), im_high)
    out += dot(rows(0, by_re), re_high) + dot(rows(0, by_im), im_high)
    return out[:width], out[width:]


def slot_of(half, col, core):
    return 2 * (2 * col + core) + half


def receivers():
    return [slot_of(half, col, core) for half in range(2) for col in range(2) for core in range(2)]


def slot_place(offs, mine, split_at, slot):
    lower = jnp.where(slot >= split_at, 1, 0)
    holder, at = jnp.bitwise_xor(2 * lower + slot // 4, mine), 2 * (slot % 4)
    return lower, offs[holder, at], offs[holder, at + 1]


def deal_kernel(where, offsets, sibling, block, *outs):
    mine, core = 2 * where[0] + where[1], where[2]
    rows, cols = block.shape[1:]
    lines = []
    for holder in range(2):
        for slot in range(2):
            for axis in range(2):
                value = jnp.where(core == holder, offsets[0, slot, axis], sibling[0, slot, axis])
                lines.append(jnp.full((1, cols), value, jnp.int32))
    lines = jnp.concatenate(lines, axis=0).astype(jnp.float32)
    for turn, out in enumerate(outs):
        out[:rows] = block[jnp.bitwise_xor(mine, turn)]
        out[rows:] = lines


def pick_kernel(where, slot_range, *refs):
    gotten, lower_planes, outs, (own, below, parts) = refs[:4], refs[4:8], refs[8:16], refs[16:]
    rows, cols = outs[0].shape
    half, col, core = where[0], where[1], where[2]
    mine = 2 * half + col
    for turn in range(4):
        own[jnp.bitwise_xor(mine, turn)] = gotten[turn][...]
    for turn in range(2):
        plane = jnp.where(half == 0, lower_planes[turn][:rows], lower_planes[2 + turn][:rows])
        below[jnp.bitwise_xor(col, turn)] = plane
    split_at = slot_range[0, 1 - half]
    row_ids = lax.broadcasted_iota(jnp.int32, (rows, cols), 0).astype(jnp.float32)
    col_ids = (lax.broadcasted_iota(jnp.int32, (rows, cols), 1) + core * cols).astype(jnp.float32)
    for place, slot in enumerate(receivers()):
        lower = jnp.where(slot >= split_at, 1, 0)
        at = rows + 2 * (slot % 4)
        offs = own[2 * lower + slot // 4, at : at + 2]
        upper_rows = row_ids >= offs[0:1]
        left_cols = col_ids >= offs[1:2]

        def merged(side, lower=lower, upper_rows=upper_rows):
            second = own[2 + side, :rows]
            top = jnp.where(lower == 1, second, own[side, :rows])
            bottom = jnp.where(lower == 1, below[side], second)
            return jnp.where(upper_rows, top, bottom)

        parts[place] = jnp.where(left_cols, merged(0), merged(1))
    for turn, out in enumerate(outs):
        out[...] = parts[jnp.bitwise_xor(2 * mine + core, turn)]


def position_kernel(where, slot_range, offs, *refs):
    gotten, (probe, measured, taken, tabs), outs, (patch, grad) = refs[:8], refs[8:12], refs[12:20], refs[20:]
    half, col, core = where[0], where[1], where[2]
    mine = 2 * half + col
    flat = 2 * mine + core
    lower, row_at, col_at = slot_place(offs, mine, slot_range[0, 1 - half], slot_of(half, col, core))
    width = probe.shape[-1]
    lanes, band = width // 2, width // 4
    for turn in range(8):
        patch[jnp.bitwise_xor(flat, turn)] = gotten[turn][...]

    def load(plane):
        return jnp.concatenate([patch[2 * plane], patch[2 * plane + 1]], axis=1)

    def store(plane, value):
        grad[2 * plane, :width] = value[:, :lanes]
        grad[2 * plane + 1, :width] = value[:, lanes:]

    def roll(value, rows, cols):
        return pltpu.roll(pltpu.roll(value, rows, 0), cols, 1)

    wave_re, wave_im = roll(probe[0], row_at, col_at), roll(probe[1], row_at, col_at)
    o0_re, o0_im, o1_re, o1_im = load(0), load(2), load(1), load(3)
    exit_re = wave_re * o0_re - wave_im * o0_im
    exit_im = wave_re * o0_im + wave_im * o0_re
    mid_re, mid_im = transform(exit_re, exit_im, tabs, 2, False)
    exit_re = mid_re * o1_re - mid_im * o1_im
    exit_im = mid_re * o1_im + mid_im * o1_re
    far_re, far_im = transform(exit_re, exit_im, tabs, 0, False)
    target = jnp.where(lower == half, measured[0, half], taken[...])
    excess = 2.0 * GRAD_WEIGHT * (far_re * far_re + far_im * far_im - target)
    back_re, back_im = transform(excess * far_re, excess * far_im, tabs, 0, True)
    store(1, mid_re * back_re + mid_im * back_im)
    store(3, mid_re * back_im - mid_im * back_re)
    up_re = o1_re * back_re + o1_im * back_im
    up_im = o1_re * back_im - o1_im * back_re
    back_re, back_im = transform(up_re, up_im, tabs, 2, True)
    wave_re, wave_im = roll(probe[0], row_at, col_at), roll(probe[1], row_at, col_at)
    o0_re, o0_im = load(0), load(2)
    store(0, wave_re * back_re + wave_im * back_im)
    store(2, wave_re * back_im - wave_im * back_re)
    up_re = o0_re * back_re + o0_im * back_im
    up_im = o0_re * back_im - o0_im * back_re
    back_row, back_col = lax.rem(width - row_at, width), lax.rem(2 * width - col_at, width)
    for part, value in enumerate((up_re, up_im)):
        value = roll(value, back_row, back_col)
        for step in range(4):
            rows = value[step * band : (step + 1) * band]
            grad[4 * part + step, width : width + band] = rows[:, :lanes]
            grad[4 * part + step, width + band :] = rows[:, lanes:]
    for turn, out in enumerate(outs):
        out[...] = grad[jnp.bitwise_xor(flat, turn)]


def add_kernel(where, slot_range, offs, *refs):
    parts, outs, below, probe_band, own = refs[:8], refs[8:12], refs[12:14], refs[14], refs[15]
    rows, cols = outs[0].shape
    half, col, core = where[0], where[1], where[2]
    mine = 2 * half + col
    split_at = slot_range[0, 1 - half]
    row_ids = lax.broadcasted_iota(jnp.int32, (rows, cols), 0)
    col_ids = lax.broadcasted_iota(jnp.int32, (rows, cols), 1) + core * cols
    places = []
    for turn in range(8):
        flat = jnp.bitwise_xor(2 * mine + core, turn)
        slot = slot_of(flat // 4, (flat // 2) % 2, flat % 2)
        places.append(slot_place(offs, mine, split_at, slot))
    for strip in range(3):
        sums = [jnp.zeros((rows, cols), jnp.float32)] * 2
        for part, (lower, row_at, col_at) in zip(parts, places):
            first = jnp.where(strip == lower, row_at, jnp.where(strip == lower + 1, 0, rows))
            last = jnp.where(strip == lower, rows, jnp.where(strip == lower + 1, row_at, 0))
            value = jnp.where((row_ids >= first) & (row_ids < last), part[:rows], 0.0)
            left = jnp.where(col_ids >= col_at, value, 0.0)
            sums = [sums[0] + left, sums[1] + (value - left)]
        if strip < 2:
            own[2 * strip], own[2 * strip + 1] = sums
        else:
            below[0][...] = jnp.where(col == 0, sums[0], sums[1])
            below[1][...] = jnp.where(col == 0, sums[1], sums[0])
    for turn, out in enumerate(outs):
        out[...] = own[jnp.bitwise_xor(mine, turn)]
    total = parts[0][rows:]
    for part in parts[1:]:
        total = total + part[rows:]
    band = probe_band.shape[0]
    probe_band[:, :cols] = total[:band]
    probe_band[:, cols:] = total[band:]


def join_kernel(where, *refs):
    mine = 2 * where[0] + where[1]
    for turn in range(4):
        refs[8][jnp.bitwise_xor(mine, turn)] = refs[turn][...] + refs[4 + turn][...]


SMEM = pl.BlockSpec(memory_space=pltpu.SMEM)
VMEM = pl.BlockSpec(memory_space=pltpu.VMEM)


def call(kernel, out_shape, scalars, arrays, flops, scratch=()):
    outs = out_shape if isinstance(out_shape, (list, tuple)) else [out_shape]
    moved = sum(math.prod(x.shape) * x.dtype.itemsize for x in [*arrays, *outs])
    return pl.pallas_call(
        kernel,
        out_shape=out_shape,
        in_specs=[SMEM] * len(scalars) + [VMEM] * len(arrays),
        out_specs=jax.tree.map(lambda unused: VMEM, out_shape),
        compiler_params=pltpu.CompilerParams(vmem_limit_bytes=VMEM_LIMIT),
        cost_estimate=pl.CostEstimate(flops=flops, bytes_accessed=moved, transcendentals=0),
        scratch_shapes=[pltpu.VMEM(dims, jnp.float32) for dims in scratch],
    )(*scalars, *arrays)


def shape(*dims):
    return jax.ShapeDtypeStruct(dims, jnp.float32)


def sum_over(value, axis, size):
    if size & (size - 1):
        return lax.psum(value, axis)
    step = 1
    while step < size:
        value = value + lax.ppermute(value, axis, [(k, k ^ step) for k in range(size)])
        step *= 2
    return value


def deal(values, axes):
    count = len(values)
    return [
        value if turn == 0 else lax.ppermute(value, axes, [(k, k ^ turn) for k in range(count)])
        for turn, value in enumerate(values)
    ]


def shift_pairs(pairs, step, half, turn):
    out = []
    for pair in range(pairs - 1):
        for col in range(2):
            lower, upper = 4 * (pair + 1) + (col ^ turn), 4 * pair + 2 * half + col
            out.append((lower, upper) if step == 1 else (upper, lower))
    return out


def local(object_field, probe, offsets, slot_range, measured):
    width = probe.shape[-1]
    planes, rows, cols = 4, object_field.shape[2], object_field.shape[3]
    band = width // 4
    pairs = lax.axis_size("pair")
    half, col, core = (lax.axis_index(name) for name in PLANE)
    where = jnp.stack([half, col, core])

    sibling = lax.ppermute(offsets, "core", [(0, 1), (1, 0)])
    block = object_field.reshape(planes, rows, cols)
    dealt = call(deal_kernel, [shape(rows + 8, cols)] * 4, (where, offsets, sibling), (block,), 0)
    given = lax.dynamic_index_in_dim(measured[0], 1 - half, 0, keepdims=False)
    below = []
    for turn in range(4):
        below.append(lax.ppermute(dealt[turn], AROUND, shift_pairs(pairs, 1, turn // 2, turn % 2)))
    own = deal(dealt, PLANE[:2])
    taken = lax.ppermute(given, "half", [(0, 1), (1, 0)])
    own[0], taken = lax.optimization_barrier((own[0], taken))

    parts = call(
        pick_kernel,
        [shape(rows, cols)] * 8,
        (where, slot_range),
        (*own, *below),
        32 * rows * width,
        [(planes, rows + 8, cols), (2, rows, cols), (8, rows, cols)],
    )
    scalars = (where, slot_range, jnp.stack([value[rows:, 0] for value in own]).astype(jnp.int32))
    grad = call(
        position_kernel,
        [shape(rows + 2 * band, cols)] * 8,
        scalars,
        (*deal(parts, PLANE), probe, measured, taken, jnp.asarray(tables(width))),
        8 * 24 * width**3,
        [(8, rows, cols), (8, rows + 2 * band, cols)],
    )
    *sums, lower0, lower1, probe_band = call(
        add_kernel,
        [shape(rows, cols)] * 6 + [shape(band, width)],
        scalars,
        deal(grad, PLANE),
        96 * rows * width,
        [(planes, rows, cols)],
    )
    above = []
    for turn in range(4):
        lower = (lower0, lower1)[turn % 2]
        above.append(lax.ppermute(lower, AROUND, shift_pairs(pairs, -1, turn // 2, turn % 2)))
    sums = deal(sums, PLANE[:2])
    probe_band = sum_over(probe_band, "pair", pairs)
    probe_grad = lax.all_gather(probe_band, PLANE, axis=0, tiled=True).reshape(probe.shape)
    object_grad = call(join_kernel, shape(planes, rows, cols), (where,), (*sums, *above), planes * rows * cols)
    return (object_grad.reshape(object_field.shape), probe_grad)


def solution(mesh):
    tile, grp = mesh.shape["tile"], mesh.shape["grp"]
    devices = mesh.devices.reshape(tile // 2, 2, 2, grp // 2)
    inner = Mesh(devices, ("pair", "half", "col", "core"))
    strip, cols = ("pair", "half"), ("col", "core")
    in_specs = (
        P(None, None, strip, cols),
        P(),
        P(strip, cols, None),
        P(strip, None),
        P(strip, cols, None, None),
    )
    out_specs = (P(None, None, strip, cols), P())
    return jax.shard_map(local, mesh=inner, in_specs=in_specs, out_specs=out_specs, check_vma=False)
```

```python
import functools
import math

import jax
import jax.numpy as jnp
import ml_dtypes
import numpy as np
from jax import lax
from jax.experimental import pallas as pl
from jax.experimental.pallas import tpu as pltpu
from jax.sharding import Mesh, PartitionSpec as P

GRAD_WEIGHT = 0.0625
PLANE = ("half", "col", "core")
AROUND = ("pair", "half", "col")
VMEM_LIMIT = 24 * 1024 * 1024


def tables(width):
    index = np.arange(width, dtype=np.int64)
    scale = 1.0 / math.sqrt(width)
    phase = -2.0 * math.pi / width * (index[:, None] * index[None, :] % width)
    shift = index[:, None] - index[None, :]
    chirp = math.pi / width * (shift * shift % (2 * width)) - math.pi / 4.0
    out = []
    for angle in (phase, chirp):
        real, imag = np.cos(angle) * scale, np.sin(angle) * scale
        table = np.concatenate([-imag, real, imag, real, -imag], axis=0)
        high = table.astype(ml_dtypes.bfloat16)
        low = (table - high.astype(np.float64)).astype(ml_dtypes.bfloat16)
        out.extend([high, low])
    return np.stack(out)


def split(value):
    high = value.astype(jnp.bfloat16)
    low = (value - high.astype(jnp.float32)).astype(jnp.bfloat16)
    return high, low


def dot(left, right):
    return jnp.dot(left, right, preferred_element_type=jnp.float32)


def transform(re, im, tabs, first, conj):
    width = re.shape[0]

    def rows(which, start):
        return tabs[first + which, start * width : (start + 2) * width]

    re_high, re_low = split(re)
    im_high, im_low = split(im)
    high = jnp.concatenate([re_high, im_high], 1)
    both = jnp.concatenate([high, jnp.concatenate([re_low, im_low], 1)], 0)

    def product(start):
        twice = dot(both, rows(0, start))
        return twice[:width] + (twice[width:] + dot(high, rows(1, start)))

    re, im = (product(1), product(0)) if conj else (product(3), product(2))
    by_re, by_im = (3, 2) if conj else (1, 0)
    re_high, re_low = split(re)
    im_high, im_low = split(im)
    out = dot(rows(0, by_re), re_low) + dot(rows(0, by_im), im_low)
    out += dot(rows(1, by_re), re_high) + dot(rows(1, by_im), im_high)
    out += dot(rows(0, by_re), re_high) + dot(rows(0, by_im), im_high)
    return out[:width], out[width:]


def slot_of(half, col, core):
    return 2 * (2 * col + core) + half


def receivers():
    return [slot_of(half, col, core) for half in range(2) for col in range(2) for core in range(2)]


def slot_place(offs, mine, split_at, slot):
    lower = jnp.where(slot >= split_at, 1, 0)
    holder, at = jnp.bitwise_xor(2 * lower + slot // 4, mine), 2 * (slot % 4)
    return lower, offs[holder, at], offs[holder, at + 1]


def fetch(pairs, sems):
    copies = [pltpu.make_async_copy(source, into, sems.at[k]) for k, (source, into) in enumerate(pairs)]
    for copy in copies:
        copy.start()
    return copies


def deal_kernel(where, offsets, sibling, block, measured, *refs):
    outs, given, sems = refs[:4], refs[4], refs[5]
    mine, core = 2 * where[0] + where[1], where[2]
    rows, cols = block.shape[1:]
    pairs = [(block.at[jnp.bitwise_xor(mine, turn)], out.at[pl.ds(0, rows)]) for turn, out in enumerate(outs)]
    copies = fetch([*pairs, (measured.at[0, 1 - where[0]], given)], sems)
    lines = []
    for holder in range(2):
        for slot in range(2):
            for axis in range(2):
                value = jnp.where(core == holder, offsets[0, slot, axis], sibling[0, slot, axis])
                lines.append(jnp.full((1, cols), value, jnp.int32))
    lines = jnp.concatenate(lines, axis=0).astype(jnp.float32)
    for out in outs:
        out[rows:] = lines
    for copy in copies:
        copy.wait()


def pick_kernel(where, slot_range, *refs):
    gotten, lower_planes, outs, (own, below, parts) = refs[:4], refs[4:8], refs[8:16], refs[16:]
    rows, cols = outs[0].shape
    half, col, core = where[0], where[1], where[2]
    mine = 2 * half + col
    for turn in range(4):
        own[jnp.bitwise_xor(mine, turn)] = gotten[turn][...]
    for turn in range(2):
        plane = jnp.where(half == 0, lower_planes[turn][:rows], lower_planes[2 + turn][:rows])
        below[jnp.bitwise_xor(col, turn)] = plane
    split_at = slot_range[0, 1 - half]
    row_ids = lax.broadcasted_iota(jnp.int32, (rows, cols), 0).astype(jnp.float32)
    col_ids = (lax.broadcasted_iota(jnp.int32, (rows, cols), 1) + core * cols).astype(jnp.float32)
    for place, slot in enumerate(receivers()):
        lower = jnp.where(slot >= split_at, 1, 0)
        at = rows + 2 * (slot % 4)
        offs = own[2 * lower + slot // 4, at : at + 2]
        upper_rows = row_ids >= offs[0:1]
        left_cols = col_ids >= offs[1:2]

        def merged(side, lower=lower, upper_rows=upper_rows):
            second = own[2 + side, :rows]
            top = jnp.where(lower == 1, second, own[side, :rows])
            bottom = jnp.where(lower == 1, below[side], second)
            return jnp.where(upper_rows, top, bottom)

        parts[place] = jnp.where(left_cols, merged(0), merged(1))
    for turn, out in enumerate(outs):
        out[...] = parts[jnp.bitwise_xor(2 * mine + core, turn)]


def position_kernel(where, slot_range, offs, *refs):
    gotten, taken, (probe_from, measured, tabs_from), outs = refs[:8], refs[8], refs[9:12], refs[12:20]
    patch, grad, probe, kept, tabs, sems = refs[20:]
    half, col, core = where[0], where[1], where[2]
    mine = 2 * half + col
    flat = 2 * mine + core
    lower, row_at, col_at = slot_place(offs, mine, slot_range[0, 1 - half], slot_of(half, col, core))
    width = probe.shape[-1]
    lanes, band = width // 2, width // 4
    probe_copy, near_copy, far_copy, kept_copy = fetch(
        [
            (probe_from, probe),
            (tabs_from.at[pl.ds(2, 2)], tabs.at[pl.ds(2, 2)]),
            (tabs_from.at[pl.ds(0, 2)], tabs.at[pl.ds(0, 2)]),
            (measured.at[0, half], kept),
        ],
        sems,
    )
    for turn in range(8):
        patch[jnp.bitwise_xor(flat, turn)] = gotten[turn][...]

    def load(plane):
        return jnp.concatenate([patch[2 * plane], patch[2 * plane + 1]], axis=1)

    def store(plane, value):
        grad[2 * plane, :width] = value[:, :lanes]
        grad[2 * plane + 1, :width] = value[:, lanes:]

    def roll(value, rows, cols):
        return pltpu.roll(pltpu.roll(value, rows, 0), cols, 1)

    probe_copy.wait()
    wave_re, wave_im = roll(probe[0], row_at, col_at), roll(probe[1], row_at, col_at)
    o0_re, o0_im, o1_re, o1_im = load(0), load(2), load(1), load(3)
    exit_re = wave_re * o0_re - wave_im * o0_im
    exit_im = wave_re * o0_im + wave_im * o0_re
    near_copy.wait()
    mid_re, mid_im = transform(exit_re, exit_im, tabs, 2, False)
    exit_re = mid_re * o1_re - mid_im * o1_im
    exit_im = mid_re * o1_im + mid_im * o1_re
    far_copy.wait()
    far_re, far_im = transform(exit_re, exit_im, tabs, 0, False)
    kept_copy.wait()
    target = jnp.where(lower == half, kept[...], taken[...])
    excess = 2.0 * GRAD_WEIGHT * (far_re * far_re + far_im * far_im - target)
    back_re, back_im = transform(excess * far_re, excess * far_im, tabs, 0, True)
    store(1, mid_re * back_re + mid_im * back_im)
    store(3, mid_re * back_im - mid_im * back_re)
    up_re = o1_re * back_re + o1_im * back_im
    up_im = o1_re * back_im - o1_im * back_re
    back_re, back_im = transform(up_re, up_im, tabs, 2, True)
    wave_re, wave_im = roll(probe[0], row_at, col_at), roll(probe[1], row_at, col_at)
    o0_re, o0_im = load(0), load(2)
    store(0, wave_re * back_re + wave_im * back_im)
    store(2, wave_re * back_im - wave_im * back_re)
    up_re = o0_re * back_re + o0_im * back_im
    up_im = o0_re * back_im - o0_im * back_re
    back_row, back_col = lax.rem(width - row_at, width), lax.rem(2 * width - col_at, width)
    for part, value in enumerate((up_re, up_im)):
        value = roll(value, back_row, back_col)
        for step in range(4):
            rows = value[step * band : (step + 1) * band]
            grad[4 * part + step, width : width + band] = rows[:, :lanes]
            grad[4 * part + step, width + band :] = rows[:, lanes:]
    for turn, out in enumerate(outs):
        out[...] = grad[jnp.bitwise_xor(flat, turn)]


def add_kernel(where, slot_range, offs, *refs):
    parts, outs, below, probe_band, own = refs[:8], refs[8:12], refs[12:14], refs[14], refs[15]
    rows, cols = outs[0].shape
    half, col, core = where[0], where[1], where[2]
    mine = 2 * half + col
    split_at = slot_range[0, 1 - half]
    row_ids = lax.broadcasted_iota(jnp.int32, (rows, cols), 0)
    col_ids = lax.broadcasted_iota(jnp.int32, (rows, cols), 1) + core * cols
    places = []
    for turn in range(8):
        flat = jnp.bitwise_xor(2 * mine + core, turn)
        slot = slot_of(flat // 4, (flat // 2) % 2, flat % 2)
        places.append(slot_place(offs, mine, split_at, slot))
    for strip in range(3):
        sums = [jnp.zeros((rows, cols), jnp.float32)] * 2
        for part, (lower, row_at, col_at) in zip(parts, places):
            first = jnp.where(strip == lower, row_at, jnp.where(strip == lower + 1, 0, rows))
            last = jnp.where(strip == lower, rows, jnp.where(strip == lower + 1, row_at, 0))
            value = jnp.where((row_ids >= first) & (row_ids < last), part[:rows], 0.0)
            left = jnp.where(col_ids >= col_at, value, 0.0)
            sums = [sums[0] + left, sums[1] + (value - left)]
        if strip < 2:
            own[2 * strip], own[2 * strip + 1] = sums
        else:
            below[0][...] = jnp.where(col == 0, sums[0], sums[1])
            below[1][...] = jnp.where(col == 0, sums[1], sums[0])
    for turn, out in enumerate(outs):
        out[...] = own[jnp.bitwise_xor(mine, turn)]
    total = parts[0][rows:]
    for part in parts[1:]:
        total = total + part[rows:]
    band = probe_band.shape[0]
    probe_band[:, :cols] = total[:band]
    probe_band[:, cols:] = total[band:]


def join_kernel(where, *refs):
    (probe, out, probe_out, sums, sems) = refs[8:]
    copies = fetch([(probe, probe_out)], sems)
    mine = 2 * where[0] + where[1]
    for turn in range(4):
        sums[turn] = refs[turn][...] + refs[4 + turn][...]
        copies += fetch([(sums.at[turn], out.at[jnp.bitwise_xor(mine, turn)])], sems.at[pl.ds(1 + turn, 1)])
    for copy in copies:
        copy.wait()


SMEM = pl.BlockSpec(memory_space=pltpu.SMEM)
VMEM = pl.BlockSpec(memory_space=pltpu.VMEM)
HBM = pl.BlockSpec(memory_space=pltpu.HBM)
ANY = pl.BlockSpec(memory_space=pl.ANY)


def call(kernel, outs, scalars, arrays, flops, scratch=(), copies=0):
    outs, arrays = ([x if isinstance(x, tuple) else (x, VMEM) for x in xs] for xs in (outs, arrays))
    moved = sum(math.prod(x.shape) * x.dtype.itemsize for x, unused in [*arrays, *outs])
    scratch = [pltpu.VMEM(dims, jnp.float32) if isinstance(dims, tuple) else dims for dims in scratch]
    return pl.pallas_call(
        kernel,
        out_shape=[x for x, unused in outs],
        in_specs=[SMEM] * len(scalars) + [spec for unused, spec in arrays],
        out_specs=[spec for unused, spec in outs],
        scratch_shapes=scratch + [pltpu.SemaphoreType.DMA((copies,))] * (copies > 0),
        compiler_params=pltpu.CompilerParams(vmem_limit_bytes=VMEM_LIMIT),
        cost_estimate=pl.CostEstimate(flops=flops, bytes_accessed=moved, transcendentals=0),
    )(*scalars, *(pltpu.with_memory_space_constraint(x, pltpu.HBM) if spec is HBM else x for x, spec in arrays))


def shape(*dims):
    return jax.ShapeDtypeStruct(dims, jnp.float32)


def sum_over(value, axis, size):
    if size & (size - 1):
        return lax.psum(value, axis)
    step = 1
    while step < size:
        value = value + lax.ppermute(value, axis, [(k, k ^ step) for k in range(size)])
        step *= 2
    return value


def deal(values, axes):
    count = len(values)
    out = list(values)
    for turn in (6, 7, 2, 4, 3, 5, 1) if count == 8 else (3, 1, 2):
        out[turn] = lax.ppermute(values[turn], axes, [(k, k ^ turn) for k in range(count)])
    return out


def shift_pairs(pairs, step, half, turn):
    out = []
    for pair in range(pairs - 1):
        for col in range(2):
            lower, upper = 4 * (pair + 1) + (col ^ turn), 4 * pair + 2 * half + col
            out.append((lower, upper) if step == 1 else (upper, lower))
    return out


def local(object_field, probe, offsets, slot_range, measured):
    width = probe.shape[-1]
    planes, rows, cols = 4, object_field.shape[2], object_field.shape[3]
    band = width // 4
    pairs = lax.axis_size("pair")
    half, col, core = (lax.axis_index(name) for name in PLANE)
    where = jnp.stack([half, col, core])

    sibling = lax.ppermute(offsets, "core", [(0, 1), (1, 0)])
    offsets, slot_range = (pltpu.with_memory_space_constraint(x, pltpu.HBM) for x in (offsets, slot_range))
    block = object_field.reshape(planes, rows, cols)
    *dealt, given = call(
        deal_kernel,
        [shape(rows + 8, cols)] * 4 + [shape(width, width)],
        (where, offsets, sibling),
        ((block, HBM), (measured, HBM)),
        0,
        copies=5,
    )
    below = []
    for turn in range(4):
        below.append(lax.ppermute(dealt[turn], AROUND, shift_pairs(pairs, 1, turn // 2, turn % 2)))
    own = deal(dealt, PLANE[:2])
    taken = lax.ppermute(given, "half", [(0, 1), (1, 0)])
    own[0], taken = lax.optimization_barrier((own[0], taken))

    parts = call(
        pick_kernel,
        [shape(rows, cols)] * 8,
        (where, slot_range),
        (*own, *below),
        32 * rows * width,
        [(planes, rows + 8, cols), (2, rows, cols), (8, rows, cols)],
    )
    scalars = (where, slot_range, jnp.stack([value[rows:, 0] for value in own]).astype(jnp.int32))
    tabs = jnp.asarray(tables(width))
    grad = call(
        position_kernel,
        [shape(rows + 2 * band, cols)] * 8,
        scalars,
        (*deal(parts, PLANE), taken, (probe, HBM), (measured, HBM), (tabs, HBM)),
        8 * 24 * width**3,
        [(8, rows, cols), (8, rows + 2 * band, cols), probe.shape, (width, width), pltpu.VMEM(tabs.shape, tabs.dtype)],
        copies=4,
    )
    *sums, lower0, lower1, probe_band = call(
        add_kernel,
        [shape(rows, cols)] * 6 + [shape(band, width)],
        scalars,
        deal(grad, PLANE),
        96 * rows * width,
        [(planes, rows, cols)],
    )
    above = []
    for turn in range(4):
        lower = (lower0, lower1)[turn % 2]
        above.append(lax.ppermute(lower, AROUND, shift_pairs(pairs, -1, turn // 2, turn % 2)))
    sums = deal(sums, PLANE[:2])
    probe_band = sum_over(probe_band, "pair", pairs)
    probe_grad = lax.all_gather(probe_band, PLANE, axis=0, tiled=True)
    object_grad, probe_grad = call(
        join_kernel,
        [(shape(planes, rows, cols), HBM), (shape(*probe_grad.shape), HBM)],
        (where,),
        (*sums, *above, (probe_grad, ANY)),
        planes * rows * cols,
        [(planes, rows, cols)],
        copies=5,
    )
    return (object_grad.reshape(object_field.shape), probe_grad.reshape(probe.shape))


def solution(mesh):
    tile, grp = mesh.shape["tile"], mesh.shape["grp"]
    devices = mesh.devices.reshape(tile // 2, 2, 2, grp // 2)
    inner = Mesh(devices, ("pair", "half", "col", "core"))
    strip, cols = ("pair", "half"), ("col", "core")
    in_specs = (
        P(None, None, strip, cols),
        P(),
        P(strip, cols, None),
        P(strip, None),
        P(strip, cols, None, None),
    )
    out_specs = (P(None, None, strip, cols), P())
    return jax.shard_map(local, mesh=inner, in_specs=in_specs, out_specs=out_specs, check_vma=False)
```

```python
import functools
import math

import jax
import jax.numpy as jnp
import ml_dtypes
import numpy as np
from jax import lax
from jax.experimental import pallas as pl
from jax.experimental.pallas import tpu as pltpu
from jax.sharding import Mesh, PartitionSpec as P

GRAD_WEIGHT = 0.0625
PLANE = ("half", "col", "core")
EIGHT, FOUR = (1, 2, 6, 7, 4, 3, 5, 0), (3, 1, 2, 0)
VMEM_LIMIT = 24 * 1024 * 1024


def tables(width):
    index = np.arange(width, dtype=np.int64)
    scale = 1.0 / math.sqrt(width)
    phase = -2.0 * math.pi / width * (index[:, None] * index[None, :] % width)
    shift = index[:, None] - index[None, :]
    chirp = math.pi / width * (shift * shift % (2 * width)) - math.pi / 4.0
    out = []
    for angle in (phase, chirp):
        real, imag = np.cos(angle) * scale, np.sin(angle) * scale
        table = np.concatenate([-imag, real, imag, real, -imag], axis=0)
        high = table.astype(ml_dtypes.bfloat16)
        low = (table - high.astype(np.float64)).astype(ml_dtypes.bfloat16)
        out.extend([high, low])
    return np.stack(out)


def split(value):
    high = value.astype(jnp.bfloat16)
    low = (value - high.astype(jnp.float32)).astype(jnp.bfloat16)
    return high, low


def dot(left, right):
    return jnp.dot(left, right, preferred_element_type=jnp.float32)


def transform(re, im, tabs, first, conj):
    width = re.shape[0]

    def rows(which, start):
        return tabs[first + which, start * width : (start + 2) * width]

    re_high, re_low = split(re)
    im_high, im_low = split(im)
    high = jnp.concatenate([re_high, im_high], 1)
    both = jnp.concatenate([high, jnp.concatenate([re_low, im_low], 1)], 0)

    def product(start):
        twice = dot(both, rows(0, start))
        return twice[:width] + (twice[width:] + dot(high, rows(1, start)))

    re, im = (product(1), product(0)) if conj else (product(3), product(2))
    by_re, by_im = (3, 2) if conj else (1, 0)
    re_high, re_low = split(re)
    im_high, im_low = split(im)
    out = dot(rows(0, by_re), re_low) + dot(rows(0, by_im), im_low)
    out += dot(rows(1, by_re), re_high) + dot(rows(1, by_im), im_high)
    out += dot(rows(0, by_re), re_high) + dot(rows(0, by_im), im_high)
    return out[:width], out[width:]


def slot_of(half, col, core):
    return 2 * (2 * col + core) + half


def receivers():
    return [slot_of(half, col, core) for half in range(2) for col in range(2) for core in range(2)]


def slot_place(offs, mine, split_at, slot):
    lower = jnp.where(slot >= split_at, 1, 0)
    holder, at = jnp.bitwise_xor(2 * lower + slot // 4, mine), 2 * (slot % 4)
    return lower, offs[holder, at], offs[holder, at + 1]


def fetch(pairs, sems):
    copies = [pltpu.make_async_copy(source, into, sems.at[k]) for k, (source, into) in enumerate(pairs)]
    for copy in copies:
        copy.start()
    return copies


def deal_kernel(where, offsets, sibling, block, measured, *refs):
    outs, given, sems = refs[:4], refs[4], refs[5]
    mine, core = 2 * where[0] + where[1], where[2]
    rows, cols = block.shape[1:]
    pairs = [(block.at[jnp.bitwise_xor(mine, turn)], out.at[pl.ds(0, rows)]) for turn, out in zip(FOUR, outs)]
    copies = fetch([*pairs, (measured.at[0, 1 - where[0]], given)], sems)
    lines = []
    for holder in range(2):
        for slot in range(2):
            for axis in range(2):
                value = jnp.where(core == holder, offsets[0, slot, axis], sibling[0, slot, axis])
                lines.append(jnp.full((1, cols), value, jnp.int32))
    lines = jnp.concatenate(lines, axis=0).astype(jnp.float32)
    for out in outs:
        out[rows:] = lines
    for copy in copies:
        copy.wait()


def lowest_kernel(where, *refs):
    gotten, out = dict(zip(FOUR, refs)), refs[4]
    rows = out.shape[1]
    for turn in range(2):
        out[turn] = jnp.where(where[0] == 0, gotten[turn][:rows], gotten[2 + turn][:rows])


def pick_kernel(where, slot_range, *refs):
    gotten, below, outs, (own, parts) = dict(zip(FOUR, refs)), refs[4], refs[5:13], refs[13:]
    rows, cols = outs[0].shape
    half, col, core = where[0], where[1], where[2]
    mine = 2 * half + col
    for turn in range(4):
        own[jnp.bitwise_xor(mine, turn)] = gotten[turn][...]
    split_at = slot_range[0, 1 - half]
    row_ids = lax.broadcasted_iota(jnp.int32, (rows, cols), 0).astype(jnp.float32)
    col_ids = (lax.broadcasted_iota(jnp.int32, (rows, cols), 1) + core * cols).astype(jnp.float32)
    for place, slot in enumerate(receivers()):
        lower = jnp.where(slot >= split_at, 1, 0)
        at = rows + 2 * (slot % 4)
        offs = own[2 * lower + slot // 4, at : at + 2]
        upper_rows = row_ids >= offs[0:1]
        left_cols = col_ids >= offs[1:2]

        def merged(side, lower=lower, upper_rows=upper_rows):
            second = own[2 + side, :rows]
            top = jnp.where(lower == 1, second, own[side, :rows])
            bottom = jnp.where(lower == 1, below[jnp.bitwise_xor(col, side)], second)
            return jnp.where(upper_rows, top, bottom)

        parts[place] = jnp.where(left_cols, merged(0), merged(1))
    for turn, out in zip(EIGHT, outs):
        out[...] = parts[jnp.bitwise_xor(2 * mine + core, turn)]


def position_kernel(where, slot_range, offs, *refs):
    gotten, taken, (probe_from, measured, tabs_from), outs = dict(zip(EIGHT, refs)), refs[8], refs[9:12], refs[12:20]
    patch, grad, probe, kept, tabs, sems = refs[20:]
    half, col, core = where[0], where[1], where[2]
    mine = 2 * half + col
    flat = 2 * mine + core
    lower, row_at, col_at = slot_place(offs, mine, slot_range[0, 1 - half], slot_of(half, col, core))
    width = probe.shape[-1]
    lanes, band = width // 2, width // 4
    probe_copy, near_copy, far_copy, kept_copy = fetch(
        [
            (probe_from, probe),
            (tabs_from.at[pl.ds(2, 2)], tabs.at[pl.ds(2, 2)]),
            (tabs_from.at[pl.ds(0, 2)], tabs.at[pl.ds(0, 2)]),
            (measured.at[0, half], kept),
        ],
        sems,
    )
    for turn in range(8):
        patch[jnp.bitwise_xor(flat, turn)] = gotten[turn][...]

    def load(plane):
        return jnp.concatenate([patch[2 * plane], patch[2 * plane + 1]], axis=1)

    def store(plane, value):
        grad[2 * plane, :width] = value[:, :lanes]
        grad[2 * plane + 1, :width] = value[:, lanes:]

    def roll(value, rows, cols):
        return pltpu.roll(pltpu.roll(value, rows, 0), cols, 1)

    probe_copy.wait()
    wave_re, wave_im = roll(probe[0], row_at, col_at), roll(probe[1], row_at, col_at)
    o0_re, o0_im, o1_re, o1_im = load(0), load(2), load(1), load(3)
    exit_re = wave_re * o0_re - wave_im * o0_im
    exit_im = wave_re * o0_im + wave_im * o0_re
    near_copy.wait()
    mid_re, mid_im = transform(exit_re, exit_im, tabs, 2, False)
    exit_re = mid_re * o1_re - mid_im * o1_im
    exit_im = mid_re * o1_im + mid_im * o1_re
    far_copy.wait()
    far_re, far_im = transform(exit_re, exit_im, tabs, 0, False)
    kept_copy.wait()
    target = jnp.where(lower == half, kept[...], taken[...])
    excess = 2.0 * GRAD_WEIGHT * (far_re * far_re + far_im * far_im - target)
    back_re, back_im = transform(excess * far_re, excess * far_im, tabs, 0, True)
    store(1, mid_re * back_re + mid_im * back_im)
    store(3, mid_re * back_im - mid_im * back_re)
    up_re = o1_re * back_re + o1_im * back_im
    up_im = o1_re * back_im - o1_im * back_re
    back_re, back_im = transform(up_re, up_im, tabs, 2, True)
    wave_re, wave_im = roll(probe[0], row_at, col_at), roll(probe[1], row_at, col_at)
    o0_re, o0_im = load(0), load(2)
    store(0, wave_re * back_re + wave_im * back_im)
    store(2, wave_re * back_im - wave_im * back_re)
    up_re = o0_re * back_re + o0_im * back_im
    up_im = o0_re * back_im - o0_im * back_re
    back_row, back_col = lax.rem(width - row_at, width), lax.rem(2 * width - col_at, width)
    for part, value in enumerate((up_re, up_im)):
        value = roll(value, back_row, back_col)
        for step in range(4):
            rows = value[step * band : (step + 1) * band]
            grad[4 * part + step, width : width + band] = rows[:, :lanes]
            grad[4 * part + step, width + band :] = rows[:, lanes:]
    for turn, out in zip(EIGHT, outs):
        out[...] = grad[jnp.bitwise_xor(flat, turn)]


def add_kernel(where, slot_range, offs, *refs):
    parts, (own, below, probe_band) = refs[:8], refs[8:]
    rows, cols = own.shape[1:]
    half, col, core = where[0], where[1], where[2]
    mine = 2 * half + col
    split_at = slot_range[0, 1 - half]
    row_ids = lax.broadcasted_iota(jnp.int32, (rows, cols), 0)
    col_ids = lax.broadcasted_iota(jnp.int32, (rows, cols), 1) + core * cols
    places = []
    for turn in EIGHT:
        flat = jnp.bitwise_xor(2 * mine + core, turn)
        slot = slot_of(flat // 4, (flat // 2) % 2, flat % 2)
        places.append(slot_place(offs, mine, split_at, slot))
    for strip in range(3):
        sums = [jnp.zeros((rows, cols), jnp.float32)] * 2
        for part, (lower, row_at, col_at) in zip(parts, places):
            first = jnp.where(strip == lower, row_at, jnp.where(strip == lower + 1, 0, rows))
            last = jnp.where(strip == lower, rows, jnp.where(strip == lower + 1, row_at, 0))
            value = jnp.where((row_ids >= first) & (row_ids < last), part[:rows], 0.0)
            left = jnp.where(col_ids >= col_at, value, 0.0)
            sums = [sums[0] + left, sums[1] + (value - left)]
        for side in range(2):
            if strip < 2:
                own[2 * strip + side] = sums[side]
            else:
                below[jnp.bitwise_xor(col, side)] = sums[side]
    total = parts[0][rows:]
    for part in parts[1:]:
        total = total + part[rows:]
    band = probe_band.shape[0]
    probe_band[:, :cols] = total[:band]
    probe_band[:, cols:] = total[band:]


def top_kernel(where, own, above, *outs):
    mine = 2 * where[0] + where[1]
    for turn, out in zip(FOUR, outs):
        extra = jnp.where(where[0] == turn // 2, above[turn % 2], 0.0)
        out[...] = own[jnp.bitwise_xor(mine, turn)] + extra


def join_kernel(where, *refs):
    probe, out, probe_out, sems = refs[4:]
    mine = 2 * where[0] + where[1]
    pairs = [(ref, out.at[jnp.bitwise_xor(mine, turn)]) for turn, ref in zip(FOUR, refs)]
    for copy in fetch([(probe, probe_out), *pairs], sems):
        copy.wait()


SMEM = pl.BlockSpec(memory_space=pltpu.SMEM)
VMEM = pl.BlockSpec(memory_space=pltpu.VMEM)
HBM = pl.BlockSpec(memory_space=pltpu.HBM)
ANY = pl.BlockSpec(memory_space=pl.ANY)


def call(kernel, outs, scalars, arrays, flops, scratch=(), copies=0):
    outs, arrays = ([x if isinstance(x, tuple) else (x, VMEM) for x in xs] for xs in (outs, arrays))
    moved = sum(math.prod(x.shape) * x.dtype.itemsize for x, unused in [*arrays, *outs])
    scratch = [pltpu.VMEM(dims, jnp.float32) if isinstance(dims, tuple) else dims for dims in scratch]
    return pl.pallas_call(
        kernel,
        out_shape=[x for x, unused in outs],
        in_specs=[SMEM] * len(scalars) + [spec for unused, spec in arrays],
        out_specs=[spec for unused, spec in outs],
        scratch_shapes=scratch + [pltpu.SemaphoreType.DMA((copies,))] * (copies > 0),
        compiler_params=pltpu.CompilerParams(vmem_limit_bytes=VMEM_LIMIT),
        cost_estimate=pl.CostEstimate(flops=flops, bytes_accessed=moved, transcendentals=0),
    )(*scalars, *(pltpu.with_memory_space_constraint(x, pltpu.HBM) if spec is HBM else x for x, spec in arrays))


def shape(*dims):
    return jax.ShapeDtypeStruct(dims, jnp.float32)


def sum_over(value, axis, size):
    if size & (size - 1):
        return lax.psum(value, axis)
    step = 1
    while step < size:
        value = value + lax.ppermute(value, axis, [(k, k ^ step) for k in range(size)])
        step *= 2
    return value


def deal(values, axes):
    count = len(values)
    order = EIGHT if count == 8 else FOUR
    return [
        lax.ppermute(value, axes, [(k, k ^ turn) for k in range(count)]) if turn else value
        for turn, value in zip(order, values)
    ]


def sum_over(value, axis, size):
    if size & (size - 1):
        return lax.psum(value, axis)
    step = 1
    while step < size:
        value = value + lax.ppermute(value, axis, [(k, k ^ step) for k in range(size)])
        step *= 2
    return value


def local(object_field, probe, offsets, slot_range, measured):
    width = probe.shape[-1]
    planes, rows, cols = 4, object_field.shape[2], object_field.shape[3]
    band = width // 4
    pairs = lax.axis_size("pair")
    half, col, core = (lax.axis_index(name) for name in PLANE)
    where = jnp.stack([half, col, core])

    sibling = lax.ppermute(offsets, "core", [(0, 1), (1, 0)])
    offsets, slot_range = (pltpu.with_memory_space_constraint(x, pltpu.HBM) for x in (offsets, slot_range))
    block = object_field.reshape(planes, rows, cols)
    *dealt, given = call(
        deal_kernel,
        [shape(rows + 8, cols)] * 4 + [shape(width, width)],
        (where, offsets, sibling),
        ((block, HBM), (measured, HBM)),
        0,
        copies=5,
    )
    own = deal(dealt, PLANE[:2])
    (lowest,) = call(lowest_kernel, [shape(2, rows, cols)], (where,), own, 0)
    lowest, given = lax.optimization_barrier((lowest, given))
    below = lax.ppermute(lowest, "pair", [(k, k - 1) for k in range(1, pairs)])
    taken = lax.ppermute(given, "half", [(0, 1), (1, 0)])
    below, taken = lax.optimization_barrier((below, taken))

    parts = call(
        pick_kernel,
        [shape(rows, cols)] * 8,
        (where, slot_range),
        (*own, below),
        32 * rows * width,
        [(planes, rows + 8, cols), (8, rows, cols)],
    )
    offs = [own[FOUR.index(turn)][rows:, 0] for turn in range(4)]
    scalars = (where, slot_range, jnp.stack(offs).astype(jnp.int32))
    tabs = jnp.asarray(tables(width))
    grad = call(
        position_kernel,
        [shape(rows + 2 * band, cols)] * 8,
        scalars,
        (*deal(parts, PLANE), taken, (probe, HBM), (measured, HBM), (tabs, HBM)),
        8 * 24 * width**3,
        [(8, rows, cols), (8, rows + 2 * band, cols), probe.shape, (width, width), pltpu.VMEM(tabs.shape, tabs.dtype)],
        copies=4,
    )
    sums, lower_sums, probe_band = call(
        add_kernel,
        [shape(planes, rows, cols), shape(2, rows, cols), shape(band, width)],
        scalars,
        deal(grad, PLANE),
        96 * rows * width,
    )
    above = lax.ppermute(lower_sums, "pair", [(k, k + 1) for k in range(pairs - 1)])
    sums = call(top_kernel, [shape(rows, cols)] * 4, (where,), (sums, above), planes * rows * cols)
    sums = deal(sums, PLANE[:2])
    probe_band = sum_over(probe_band, "pair", pairs)
    probe_grad = lax.all_gather(probe_band, PLANE, axis=0, tiled=True)
    object_grad, probe_grad = call(
        join_kernel,
        [(shape(planes, rows, cols), HBM), (shape(*probe_grad.shape), HBM)],
        (where,),
        [(x, ANY) for x in (*sums, probe_grad)],
        0,
        copies=5,
    )
    return (object_grad.reshape(object_field.shape), probe_grad.reshape(probe.shape))


def solution(mesh):
    tile, grp = mesh.shape["tile"], mesh.shape["grp"]
    devices = mesh.devices.reshape(tile // 2, 2, 2, grp // 2)
    inner = Mesh(devices, ("pair", "half", "col", "core"))
    strip, cols = ("pair", "half"), ("col", "core")
    in_specs = (
        P(None, None, strip, cols),
        P(),
        P(strip, cols, None),
        P(strip, None),
        P(strip, cols, None, None),
    )
    out_specs = (P(None, None, strip, cols), P())
    return jax.shard_map(local, mesh=inner, in_specs=in_specs, out_specs=out_specs, check_vma=False)
```

```python
import functools
import math

import jax
import jax.numpy as jnp
import ml_dtypes
import numpy as np
from jax import lax
from jax.experimental import pallas as pl
from jax.experimental.pallas import tpu as pltpu
from jax.sharding import Mesh, PartitionSpec as P

GRAD_WEIGHT = 0.0625
PLANE = ("half", "col", "core")
EIGHT, FOUR = (4, 2, 5, 3, 6, 7, 1, 0), (2, 1, 3, 0)
VMEM_LIMIT = 24 * 1024 * 1024


def tables(width):
    index = np.arange(width, dtype=np.int64)
    scale = 1.0 / math.sqrt(width)
    phase = -2.0 * math.pi / width * (index[:, None] * index[None, :] % width)
    shift = index[:, None] - index[None, :]
    chirp = math.pi / width * (shift * shift % (2 * width)) - math.pi / 4.0
    out = []
    for angle in (phase, chirp):
        real, imag = np.cos(angle) * scale, np.sin(angle) * scale
        table = np.concatenate([-imag, real, imag, real, -imag], axis=0)
        high = table.astype(ml_dtypes.bfloat16)
        low = (table - high.astype(np.float64)).astype(ml_dtypes.bfloat16)
        out.extend([high, low])
    return np.stack(out)


def split(value):
    high = value.astype(jnp.bfloat16)
    low = (value - high.astype(jnp.float32)).astype(jnp.bfloat16)
    return high, low


def dot(left, right):
    return jnp.dot(left, right, preferred_element_type=jnp.float32)


def transform(re, im, tabs, first, conj):
    width = re.shape[0]

    def rows(which, start):
        return tabs[first + which, start * width : (start + 2) * width]

    re_high, re_low = split(re)
    im_high, im_low = split(im)
    high = jnp.concatenate([re_high, im_high], 1)
    both = jnp.concatenate([high, jnp.concatenate([re_low, im_low], 1)], 0)

    def product(start):
        twice = dot(both, rows(0, start))
        return twice[:width] + (twice[width:] + dot(high, rows(1, start)))

    re, im = (product(1), product(0)) if conj else (product(3), product(2))
    by_re, by_im = (3, 2) if conj else (1, 0)
    re_high, re_low = split(re)
    im_high, im_low = split(im)
    out = dot(rows(0, by_re), re_low) + dot(rows(0, by_im), im_low)
    out += dot(rows(1, by_re), re_high) + dot(rows(1, by_im), im_high)
    out += dot(rows(0, by_re), re_high) + dot(rows(0, by_im), im_high)
    return out[:width], out[width:]


def slot_of(half, col, core):
    return 2 * (2 * col + core) + half


def receivers():
    return [slot_of(half, col, core) for half in range(2) for col in range(2) for core in range(2)]


def slot_place(offs, mine, split_at, slot):
    lower = jnp.where(slot >= split_at, 1, 0)
    holder, at = jnp.bitwise_xor(2 * lower + slot // 4, mine), 2 * (slot % 4)
    return lower, offs[holder, at], offs[holder, at + 1]


def fetch(pairs, sems):
    copies = [pltpu.make_async_copy(source, into, sems.at[k]) for k, (source, into) in enumerate(pairs)]
    for copy in copies:
        copy.start()
    return copies


def deal_kernel(where, offsets, sibling, block, measured, *refs):
    outs, given, sems = refs[:4], refs[4], refs[5]
    mine, core = 2 * where[0] + where[1], where[2]
    rows, cols = block.shape[1:]
    pairs = [(block.at[jnp.bitwise_xor(mine, turn)], out.at[pl.ds(0, rows)]) for turn, out in zip(FOUR, outs)]
    copies = fetch([*pairs, (measured.at[0, 1 - where[0]], given)], sems)
    lines = []
    for holder in range(2):
        for slot in range(2):
            for axis in range(2):
                value = jnp.where(core == holder, offsets[0, slot, axis], sibling[0, slot, axis])
                lines.append(jnp.full((1, cols), value, jnp.int32))
    lines = jnp.concatenate(lines, axis=0).astype(jnp.float32)
    for out in outs:
        out[rows:] = lines
    for copy in copies:
        copy.wait()


def lowest_kernel(where, *refs):
    gotten, out = dict(zip(FOUR, refs)), refs[4]
    rows = out.shape[1]
    for turn in range(2):
        out[turn] = jnp.where(where[0] == 0, gotten[turn][:rows], gotten[2 + turn][:rows])


def pick_kernel(where, slot_range, *refs):
    gotten, below, outs, (own, parts) = dict(zip(FOUR, refs)), refs[4], refs[5:13], refs[13:]
    rows, cols = outs[0].shape
    half, col, core = where[0], where[1], where[2]
    mine = 2 * half + col
    for turn in range(4):
        own[jnp.bitwise_xor(mine, turn)] = gotten[turn][...]
    split_at = slot_range[0, 1 - half]
    row_ids = lax.broadcasted_iota(jnp.int32, (rows, cols), 0).astype(jnp.float32)
    col_ids = (lax.broadcasted_iota(jnp.int32, (rows, cols), 1) + core * cols).astype(jnp.float32)
    for place, slot in enumerate(receivers()):
        lower = jnp.where(slot >= split_at, 1, 0)
        at = rows + 2 * (slot % 4)
        offs = own[2 * lower + slot // 4, at : at + 2]
        upper_rows = row_ids >= offs[0:1]
        left_cols = col_ids >= offs[1:2]

        def merged(side, lower=lower, upper_rows=upper_rows):
            second = own[2 + side, :rows]
            top = jnp.where(lower == 1, second, own[side, :rows])
            bottom = jnp.where(lower == 1, below[jnp.bitwise_xor(col, side)], second)
            return jnp.where(upper_rows, top, bottom)

        parts[place] = jnp.where(left_cols, merged(0), merged(1))
    for turn, out in zip(EIGHT, outs):
        out[...] = parts[jnp.bitwise_xor(2 * mine + core, turn)]


def roll(value, rows, cols):
    return pltpu.roll(pltpu.roll(value, rows, 0), cols, 1)


def ready_kernel(where, slot_range, offs, probe_from, measured, tabs_from, probe, kept, tabs, sems):
    half, col, core = where[0], where[1], where[2]
    copies = fetch([(probe_from, probe), (tabs_from, tabs), (measured.at[0, half], kept)], sems)
    slot = slot_of(half, col, core)
    unused, row_at, col_at = slot_place(offs, 2 * half + col, slot_range[0, 1 - half], slot)
    copies[0].wait()
    for part in range(2):
        probe[part] = roll(probe[part], row_at, col_at)
    copies[1].wait()
    copies[2].wait()


def position_kernel(where, slot_range, offs, *refs):
    gotten, (probe, kept, taken, tabs) = dict(zip(EIGHT, refs)), refs[8:12]
    outs, patch, grad = refs[12:20], refs[20], refs[21]
    half, col, core = where[0], where[1], where[2]
    mine = 2 * half + col
    flat = 2 * mine + core
    lower, row_at, col_at = slot_place(offs, mine, slot_range[0, 1 - half], slot_of(half, col, core))
    width = probe.shape[-1]
    lanes, band = width // 2, width // 4
    for turn in range(8):
        patch[jnp.bitwise_xor(flat, turn)] = gotten[turn][...]

    def load(plane):
        return jnp.concatenate([patch[2 * plane], patch[2 * plane + 1]], axis=1)

    def store(plane, value):
        grad[2 * plane, :width] = value[:, :lanes]
        grad[2 * plane + 1, :width] = value[:, lanes:]

    wave_re, wave_im = probe[0], probe[1]
    o0_re, o0_im, o1_re, o1_im = load(0), load(2), load(1), load(3)
    exit_re = wave_re * o0_re - wave_im * o0_im
    exit_im = wave_re * o0_im + wave_im * o0_re
    mid_re, mid_im = transform(exit_re, exit_im, tabs, 2, False)
    exit_re = mid_re * o1_re - mid_im * o1_im
    exit_im = mid_re * o1_im + mid_im * o1_re
    far_re, far_im = transform(exit_re, exit_im, tabs, 0, False)
    target = jnp.where(lower == half, kept[...], taken[...])
    excess = 2.0 * GRAD_WEIGHT * (far_re * far_re + far_im * far_im - target)
    back_re, back_im = transform(excess * far_re, excess * far_im, tabs, 0, True)
    store(1, mid_re * back_re + mid_im * back_im)
    store(3, mid_re * back_im - mid_im * back_re)
    up_re = o1_re * back_re + o1_im * back_im
    up_im = o1_re * back_im - o1_im * back_re
    back_re, back_im = transform(up_re, up_im, tabs, 2, True)
    wave_re, wave_im = probe[0], probe[1]
    o0_re, o0_im = load(0), load(2)
    store(0, wave_re * back_re + wave_im * back_im)
    store(2, wave_re * back_im - wave_im * back_re)
    up_re = o0_re * back_re + o0_im * back_im
    up_im = o0_re * back_im - o0_im * back_re
    back_row, back_col = lax.rem(width - row_at, width), lax.rem(2 * width - col_at, width)
    for part, value in enumerate((up_re, up_im)):
        value = roll(value, back_row, back_col)
        for step in range(4):
            rows = value[step * band : (step + 1) * band]
            grad[4 * part + step, width : width + band] = rows[:, :lanes]
            grad[4 * part + step, width + band :] = rows[:, lanes:]
    for turn, out in zip(EIGHT, outs):
        out[...] = grad[jnp.bitwise_xor(flat, turn)]


def add_parts(where, slot_range, offs, parts, strip, rows, cols):
    half, col, core = where[0], where[1], where[2]
    mine = 2 * half + col
    row_ids = lax.broadcasted_iota(jnp.int32, (rows, cols), 0)
    col_ids = lax.broadcasted_iota(jnp.int32, (rows, cols), 1) + core * cols
    sums = [jnp.zeros((rows, cols), jnp.float32)] * 2
    for turn, part in zip(EIGHT, parts):
        flat = jnp.bitwise_xor(2 * mine + core, turn)
        slot = slot_of(flat // 4, (flat // 2) % 2, flat % 2)
        lower, row_at, col_at = slot_place(offs, mine, slot_range[0, 1 - half], slot)
        first = jnp.where(strip == lower, row_at, jnp.where(strip == lower + 1, 0, rows))
        last = jnp.where(strip == lower, rows, jnp.where(strip == lower + 1, row_at, 0))
        value = jnp.where((row_ids >= first) & (row_ids < last), part[:rows], 0.0)
        left = jnp.where(col_ids >= col_at, value, 0.0)
        sums = [sums[0] + left, sums[1] + (value - left)]
    return sums


def add_below_kernel(where, slot_range, offs, *refs):
    parts, (below, probe_band) = refs[:8], refs[8:]
    rows, cols = below.shape[1:]
    sums = add_parts(where, slot_range, offs, parts, 2, rows, cols)
    for side in range(2):
        below[jnp.bitwise_xor(where[1], side)] = sums[side]
    total = parts[0][rows:]
    for part in parts[1:]:
        total = total + part[rows:]
    band = probe_band.shape[0]
    probe_band[:, :cols] = total[:band]
    probe_band[:, cols:] = total[band:]


def add_own_kernel(where, slot_range, offs, *refs):
    parts, own = refs[:8], refs[8]
    rows, cols = own.shape[1:]
    for strip in range(2):
        own[2 * strip], own[2 * strip + 1] = add_parts(where, slot_range, offs, parts, strip, rows, cols)


def top_kernel(where, own, above, *outs):
    mine = 2 * where[0] + where[1]
    for turn, out in zip(FOUR, outs):
        extra = jnp.where(where[0] == turn // 2, above[turn % 2], 0.0)
        out[...] = own[jnp.bitwise_xor(mine, turn)] + extra


def join_kernel(where, *refs):
    probe, out, probe_out, sems = refs[4:]
    mine = 2 * where[0] + where[1]
    pairs = [(ref, out.at[jnp.bitwise_xor(mine, turn)]) for turn, ref in zip(FOUR, refs)]
    for copy in fetch([(probe, probe_out), *pairs], sems):
        copy.wait()


SMEM = pl.BlockSpec(memory_space=pltpu.SMEM)
VMEM = pl.BlockSpec(memory_space=pltpu.VMEM)
HBM = pl.BlockSpec(memory_space=pltpu.HBM)
ANY = pl.BlockSpec(memory_space=pl.ANY)


def call(kernel, outs, scalars, arrays, flops, scratch=(), copies=0):
    outs, arrays = ([x if isinstance(x, tuple) else (x, VMEM) for x in xs] for xs in (outs, arrays))
    moved = sum(math.prod(x.shape) * x.dtype.itemsize for x, unused in [*arrays, *outs])
    scratch = [pltpu.VMEM(dims, jnp.float32) if isinstance(dims, tuple) else dims for dims in scratch]
    return pl.pallas_call(
        kernel,
        out_shape=[x for x, unused in outs],
        in_specs=[SMEM] * len(scalars) + [spec for unused, spec in arrays],
        out_specs=[spec for unused, spec in outs],
        scratch_shapes=scratch + [pltpu.SemaphoreType.DMA((copies,))] * (copies > 0),
        compiler_params=pltpu.CompilerParams(vmem_limit_bytes=VMEM_LIMIT),
        cost_estimate=pl.CostEstimate(flops=flops, bytes_accessed=moved, transcendentals=0),
    )(*scalars, *(pltpu.with_memory_space_constraint(x, pltpu.HBM) if spec is HBM else x for x, spec in arrays))


def shape(*dims):
    return jax.ShapeDtypeStruct(dims, jnp.float32)


def sum_over(value, axis, size):
    if size & (size - 1):
        return lax.psum(value, axis)
    step = 1
    while step < size:
        value = value + lax.ppermute(value, axis, [(k, k ^ step) for k in range(size)])
        step *= 2
    return value


def deal(values, axes):
    count = len(values)
    order = EIGHT if count == 8 else FOUR
    return [
        lax.ppermute(value, axes, [(k, k ^ turn) for k in range(count)]) if turn else value
        for turn, value in zip(order, values)
    ]


def sum_over(value, axis, size):
    if size & (size - 1):
        return lax.psum(value, axis)
    step = 1
    while step < size:
        value = value + lax.ppermute(value, axis, [(k, k ^ step) for k in range(size)])
        step *= 2
    return value


def local(object_field, probe, offsets, slot_range, measured):
    width = probe.shape[-1]
    planes, rows, cols = 4, object_field.shape[2], object_field.shape[3]
    band = width // 4
    pairs = lax.axis_size("pair")
    half, col, core = (lax.axis_index(name) for name in PLANE)
    where = jnp.stack([half, col, core])

    sibling = lax.ppermute(offsets, "core", [(0, 1), (1, 0)])
    offsets, slot_range = (pltpu.with_memory_space_constraint(x, pltpu.HBM) for x in (offsets, slot_range))
    block = object_field.reshape(planes, rows, cols)
    *dealt, given = call(
        deal_kernel,
        [shape(rows + 8, cols)] * 4 + [shape(width, width)],
        (where, offsets, sibling),
        ((block, HBM), (measured, HBM)),
        0,
        copies=5,
    )
    own = deal(dealt, PLANE[:2])
    (lowest,) = call(lowest_kernel, [shape(2, rows, cols)], (where,), own, 0)
    lowest, given = lax.optimization_barrier((lowest, given))
    below = lax.ppermute(lowest, "pair", [(k, k - 1) for k in range(1, pairs)])
    taken = lax.ppermute(given, "half", [(0, 1), (1, 0)])
    below, taken = lax.optimization_barrier((below, taken))

    parts = call(
        pick_kernel,
        [shape(rows, cols)] * 8,
        (where, slot_range),
        (*own, below),
        32 * rows * width,
        [(planes, rows + 8, cols), (8, rows, cols)],
    )
    offs = [own[FOUR.index(turn)][rows:, 0] for turn in range(4)]
    scalars = (where, slot_range, jnp.stack(offs).astype(jnp.int32))
    tabs = jnp.asarray(tables(width))
    probe, kept, tabs = call(
        ready_kernel,
        [shape(*probe.shape), shape(width, width), jax.ShapeDtypeStruct(tabs.shape, tabs.dtype)],
        scalars,
        ((probe, HBM), (measured, HBM), (tabs, HBM)),
        probe.size,
        copies=3,
    )
    grad = call(
        position_kernel,
        [shape(rows + 2 * band, cols)] * 8,
        scalars,
        (*deal(parts, PLANE), probe, kept, taken, tabs),
        8 * 24 * width**3,
        [(8, rows, cols), (8, rows + 2 * band, cols)],
    )
    got = deal(grad, PLANE)
    lower_sums, probe_band = call(
        add_below_kernel,
        [shape(2, rows, cols), shape(band, width)],
        scalars,
        got,
        32 * rows * width,
    )
    probe_band = sum_over(probe_band, "pair", pairs)
    (sums,) = call(add_own_kernel, [shape(planes, rows, cols)], scalars, got, 64 * rows * width)
    above = lax.ppermute(lower_sums, "pair", [(k, k + 1) for k in range(pairs - 1)])
    sums = call(top_kernel, [shape(rows, cols)] * 4, (where,), (sums, above), planes * rows * cols)
    sums = deal(sums, PLANE[:2])
    probe_grad = lax.all_gather(probe_band, PLANE, axis=0, tiled=True)
    object_grad, probe_grad = call(
        join_kernel,
        [(shape(planes, rows, cols), HBM), (shape(*probe_grad.shape), HBM)],
        (where,),
        [(x, ANY) for x in (*sums, probe_grad)],
        0,
        copies=5,
    )
    return (object_grad.reshape(object_field.shape), probe_grad.reshape(probe.shape))


def solution(mesh):
    tile, grp = mesh.shape["tile"], mesh.shape["grp"]
    devices = mesh.devices.reshape(tile // 2, 2, 2, grp // 2)
    inner = Mesh(devices, ("pair", "half", "col", "core"))
    strip, cols = ("pair", "half"), ("col", "core")
    in_specs = (
        P(None, None, strip, cols),
        P(),
        P(strip, cols, None),
        P(strip, None),
        P(strip, cols, None, None),
    )
    out_specs = (P(None, None, strip, cols), P())
    return jax.shard_map(local, mesh=inner, in_specs=in_specs, out_specs=out_specs, check_vma=False)
```

```python
import functools
import math

import jax
import jax.numpy as jnp
import ml_dtypes
import numpy as np
from jax import lax
from jax.experimental import pallas as pl
from jax.experimental.pallas import tpu as pltpu
from jax.sharding import Mesh, PartitionSpec as P

GRAD_WEIGHT = 0.0625
PLANE = ("half", "col", "core")
EIGHT, FOUR = (4, 2, 5, 3, 6, 7, 1, 0), (2, 1, 3, 0)
VMEM_LIMIT = 24 * 1024 * 1024


def tables(width):
    index = np.arange(width, dtype=np.int64)
    scale = 1.0 / math.sqrt(width)
    phase = -2.0 * math.pi / width * (index[:, None] * index[None, :] % width)
    shift = index[:, None] - index[None, :]
    chirp = math.pi / width * (shift * shift % (2 * width)) - math.pi / 4.0
    out = []
    for angle in (phase, chirp):
        real, imag = np.cos(angle) * scale, np.sin(angle) * scale
        table = np.concatenate([-imag, real, imag, real, -imag], axis=0)
        high = table.astype(ml_dtypes.bfloat16)
        low = (table - high.astype(np.float64)).astype(ml_dtypes.bfloat16)
        out.extend([high, low])
    return np.stack(out)


def split(value):
    high = value.astype(jnp.bfloat16)
    low = (value - high.astype(jnp.float32)).astype(jnp.bfloat16)
    return high, low


def dot(left, right):
    return jnp.dot(left, right, preferred_element_type=jnp.float32)


def transform(re, im, tabs, first, conj):
    width = re.shape[0]

    def rows(which, start):
        return tabs[first + which, start * width : (start + 2) * width]

    re_high, re_low = split(re)
    im_high, im_low = split(im)
    high = jnp.concatenate([re_high, im_high], 1)
    both = jnp.concatenate([high, jnp.concatenate([re_low, im_low], 1)], 0)

    def product(start):
        twice = dot(both, rows(0, start))
        return twice[:width] + (twice[width:] + dot(high, rows(1, start)))

    re, im = (product(1), product(0)) if conj else (product(3), product(2))
    by_re, by_im = (3, 2) if conj else (1, 0)
    re_high, re_low = split(re)
    im_high, im_low = split(im)
    out = dot(rows(0, by_re), re_low) + dot(rows(0, by_im), im_low)
    out += dot(rows(1, by_re), re_high) + dot(rows(1, by_im), im_high)
    out += dot(rows(0, by_re), re_high) + dot(rows(0, by_im), im_high)
    return out[:width], out[width:]


def slot_of(half, col, core):
    return 2 * (2 * col + core) + half


def receivers():
    return [slot_of(half, col, core) for half in range(2) for col in range(2) for core in range(2)]


def slot_place(offs, mine, split_at, slot):
    lower = jnp.where(slot >= split_at, 1, 0)
    holder, at = jnp.bitwise_xor(2 * lower + slot // 4, mine), 2 * (slot % 4)
    return lower, offs[holder, at], offs[holder, at + 1]


def fetch(pairs, sems):
    copies = [pltpu.make_async_copy(source, into, sems.at[k]) for k, (source, into) in enumerate(pairs)]
    for copy in copies:
        copy.start()
    return copies


def deal_kernel(where, offsets, sibling, block, measured, *refs):
    outs, given, sems = refs[:4], refs[4], refs[5]
    mine, core = 2 * where[0] + where[1], where[2]
    rows, cols = block.shape[1:]
    pairs = [(block.at[jnp.bitwise_xor(mine, turn)], out.at[pl.ds(0, rows)]) for turn, out in zip(FOUR, outs)]
    copies = fetch([*pairs, (measured.at[0, 1 - where[0]], given)], sems)
    lines = []
    for holder in range(2):
        for slot in range(2):
            for axis in range(2):
                value = jnp.where(core == holder, offsets[0, slot, axis], sibling[0, slot, axis])
                lines.append(jnp.full((1, cols), value, jnp.int32))
    lines = jnp.concatenate(lines, axis=0).astype(jnp.float32)
    for out in outs:
        out[rows:] = lines
    for copy in copies:
        copy.wait()


def lowest_kernel(where, *refs):
    gotten, out = dict(zip(FOUR, refs)), refs[4]
    rows = out.shape[1]
    for turn in range(2):
        out[turn] = jnp.where(where[0] == 0, gotten[turn][:rows], gotten[2 + turn][:rows])


def pick_kernel(where, slot_range, *refs):
    gotten, below, outs, (own, parts) = dict(zip(FOUR, refs)), refs[4], refs[5:13], refs[13:]
    rows, cols = outs[0].shape
    half, col, core = where[0], where[1], where[2]
    mine = 2 * half + col
    for turn in range(4):
        own[jnp.bitwise_xor(mine, turn)] = gotten[turn][...]
    split_at = slot_range[0, 1 - half]
    row_ids = lax.broadcasted_iota(jnp.int32, (rows, cols), 0).astype(jnp.float32)
    col_ids = (lax.broadcasted_iota(jnp.int32, (rows, cols), 1) + core * cols).astype(jnp.float32)
    for place, slot in enumerate(receivers()):
        lower = jnp.where(slot >= split_at, 1, 0)
        at = rows + 2 * (slot % 4)
        offs = own[2 * lower + slot // 4, at : at + 2]
        upper_rows = row_ids >= offs[0:1]
        left_cols = col_ids >= offs[1:2]

        def merged(side, lower=lower, upper_rows=upper_rows):
            second = own[2 + side, :rows]
            top = jnp.where(lower == 1, second, own[side, :rows])
            bottom = jnp.where(lower == 1, below[jnp.bitwise_xor(col, side)], second)
            return jnp.where(upper_rows, top, bottom)

        parts[place] = jnp.where(left_cols, merged(0), merged(1))
    for turn, out in zip(EIGHT, outs):
        out[...] = parts[jnp.bitwise_xor(2 * mine + core, turn)]


def roll(value, rows, cols):
    return pltpu.roll(pltpu.roll(value, rows, 0), cols, 1)


def ready_kernel(where, slot_range, offs, probe_from, measured, tabs_from, probe, kept, tabs, sems):
    half, col, core = where[0], where[1], where[2]
    copies = fetch([(probe_from, probe), (tabs_from, tabs), (measured.at[0, half], kept)], sems)
    slot = slot_of(half, col, core)
    unused, row_at, col_at = slot_place(offs, 2 * half + col, slot_range[0, 1 - half], slot)
    copies[0].wait()
    for part in range(2):
        probe[part] = roll(probe[part], row_at, col_at)
    copies[1].wait()
    copies[2].wait()


def position_kernel(where, slot_range, offs, *refs):
    gotten, (probe, kept, taken, tabs) = dict(zip(EIGHT, refs)), refs[8:12]
    outs, patch, grad = refs[12:20], refs[20], refs[21]
    half, col, core = where[0], where[1], where[2]
    mine = 2 * half + col
    flat = 2 * mine + core
    lower, row_at, col_at = slot_place(offs, mine, slot_range[0, 1 - half], slot_of(half, col, core))
    width = probe.shape[-1]
    lanes, band = width // 2, width // 4
    for turn in range(8):
        patch[jnp.bitwise_xor(flat, turn)] = gotten[turn][...]

    def load(plane):
        return jnp.concatenate([patch[2 * plane], patch[2 * plane + 1]], axis=1)

    def store(plane, value):
        grad[2 * plane, :width] = value[:, :lanes]
        grad[2 * plane + 1, :width] = value[:, lanes:]

    wave_re, wave_im = probe[0], probe[1]
    o0_re, o0_im, o1_re, o1_im = load(0), load(2), load(1), load(3)
    exit_re = wave_re * o0_re - wave_im * o0_im
    exit_im = wave_re * o0_im + wave_im * o0_re
    mid_re, mid_im = transform(exit_re, exit_im, tabs, 2, False)
    exit_re = mid_re * o1_re - mid_im * o1_im
    exit_im = mid_re * o1_im + mid_im * o1_re
    far_re, far_im = transform(exit_re, exit_im, tabs, 0, False)
    target = jnp.where(lower == half, kept[...], taken[...])
    excess = 2.0 * GRAD_WEIGHT * (far_re * far_re + far_im * far_im - target)
    back_re, back_im = transform(excess * far_re, excess * far_im, tabs, 0, True)
    store(1, mid_re * back_re + mid_im * back_im)
    store(3, mid_re * back_im - mid_im * back_re)
    up_re = o1_re * back_re + o1_im * back_im
    up_im = o1_re * back_im - o1_im * back_re
    back_re, back_im = transform(up_re, up_im, tabs, 2, True)
    wave_re, wave_im = probe[0], probe[1]
    o0_re, o0_im = load(0), load(2)
    store(0, wave_re * back_re + wave_im * back_im)
    store(2, wave_re * back_im - wave_im * back_re)
    up_re = o0_re * back_re + o0_im * back_im
    up_im = o0_re * back_im - o0_im * back_re
    back_row, back_col = lax.rem(width - row_at, width), lax.rem(2 * width - col_at, width)
    for part, value in enumerate((up_re, up_im)):
        value = roll(value, back_row, back_col)
        for step in range(4):
            rows = value[step * band : (step + 1) * band]
            grad[4 * part + step, width : width + band] = rows[:, :lanes]
            grad[4 * part + step, width + band :] = rows[:, lanes:]
    for turn, out in zip(EIGHT, outs):
        out[...] = grad[jnp.bitwise_xor(flat, turn)]


def add_parts(where, slot_range, offs, parts, strip, rows, cols):
    half, col, core = where[0], where[1], where[2]
    mine = 2 * half + col
    row_ids = lax.broadcasted_iota(jnp.int32, (rows, cols), 0)
    col_ids = lax.broadcasted_iota(jnp.int32, (rows, cols), 1) + core * cols
    sums = [jnp.zeros((rows, cols), jnp.float32)] * 2
    for turn, part in zip(EIGHT, parts):
        flat = jnp.bitwise_xor(2 * mine + core, turn)
        slot = slot_of(flat // 4, (flat // 2) % 2, flat % 2)
        lower, row_at, col_at = slot_place(offs, mine, slot_range[0, 1 - half], slot)
        first = jnp.where(strip == lower, row_at, jnp.where(strip == lower + 1, 0, rows))
        last = jnp.where(strip == lower, rows, jnp.where(strip == lower + 1, row_at, 0))
        value = jnp.where((row_ids >= first) & (row_ids < last), part[:rows], 0.0)
        left = jnp.where(col_ids >= col_at, value, 0.0)
        sums = [sums[0] + left, sums[1] + (value - left)]
    return sums


def add_below_kernel(where, slot_range, offs, *refs):
    parts, (below, probe_band) = refs[:8], refs[8:]
    rows, cols = below.shape[1:]
    sums = add_parts(where, slot_range, offs, parts, 2, rows, cols)
    for side in range(2):
        below[jnp.bitwise_xor(where[1], side)] = sums[side]
    total = parts[0][rows:]
    for part in parts[1:]:
        total = total + part[rows:]
    band = probe_band.shape[0]
    probe_band[:, :cols] = total[:band]
    probe_band[:, cols:] = total[band:]


def add_own_kernel(where, slot_range, offs, *refs):
    parts, own = refs[:8], refs[8]
    rows, cols = own.shape[1:]
    for strip in range(2):
        own[2 * strip], own[2 * strip + 1] = add_parts(where, slot_range, offs, parts, strip, rows, cols)


def top_kernel(where, own, above, *outs):
    mine = 2 * where[0] + where[1]
    for turn, out in zip(FOUR, outs):
        extra = jnp.where(where[0] == turn // 2, above[turn % 2], 0.0)
        out[...] = own[jnp.bitwise_xor(mine, turn)] + extra


def join_kernel(where, *refs):
    probe, out, probe_out, sems = refs[4:]
    mine = 2 * where[0] + where[1]
    pairs = [(ref, out.at[jnp.bitwise_xor(mine, turn)]) for turn, ref in zip(FOUR, refs)]
    for copy in fetch([(probe, probe_out), *pairs], sems):
        copy.wait()


SMEM = pl.BlockSpec(memory_space=pltpu.SMEM)
VMEM = pl.BlockSpec(memory_space=pltpu.VMEM)
HBM = pl.BlockSpec(memory_space=pltpu.HBM)
ANY = pl.BlockSpec(memory_space=pl.ANY)


def call(kernel, outs, scalars, arrays, flops, scratch=(), copies=0):
    outs, arrays = ([x if isinstance(x, tuple) else (x, VMEM) for x in xs] for xs in (outs, arrays))
    moved = sum(math.prod(x.shape) * x.dtype.itemsize for x, unused in [*arrays, *outs])
    scratch = [pltpu.VMEM(dims, jnp.float32) if isinstance(dims, tuple) else dims for dims in scratch]
    return pl.pallas_call(
        kernel,
        out_shape=[x for x, unused in outs],
        in_specs=[SMEM] * len(scalars) + [spec for unused, spec in arrays],
        out_specs=[spec for unused, spec in outs],
        scratch_shapes=scratch + [pltpu.SemaphoreType.DMA((copies,))] * (copies > 0),
        compiler_params=pltpu.CompilerParams(vmem_limit_bytes=VMEM_LIMIT),
        cost_estimate=pl.CostEstimate(flops=flops, bytes_accessed=moved, transcendentals=0),
    )(*scalars, *(pltpu.with_memory_space_constraint(x, pltpu.HBM) if spec is HBM else x for x, spec in arrays))


def shape(*dims):
    return jax.ShapeDtypeStruct(dims, jnp.float32)


def sum_over(value, axis, size):
    if size & (size - 1):
        return lax.psum(value, axis)
    step = 1
    while step < size:
        value = value + lax.ppermute(value, axis, [(k, k ^ step) for k in range(size)])
        step *= 2
    return value


def deal(values, axes):
    count = len(values)
    order = EIGHT if count == 8 else FOUR
    return [
        lax.ppermute(value, axes, [(k, k ^ turn) for k in range(count)]) if turn else value
        for turn, value in zip(order, values)
    ]


def sum_over(value, axis, size):
    if size & (size - 1):
        return lax.psum(value, axis)
    step = 1
    while step < size:
        value = value + lax.ppermute(value, axis, [(k, k ^ step) for k in range(size)])
        step *= 2
    return value


def local(object_field, probe, offsets, slot_range, measured):
    width = probe.shape[-1]
    planes, rows, cols = 4, object_field.shape[2], object_field.shape[3]
    band = width // 4
    pairs = lax.axis_size("pair")
    half, col, core = (lax.axis_index(name) for name in PLANE)
    where = jnp.stack([half, col, core])

    sibling = lax.ppermute(offsets, "core", [(0, 1), (1, 0)])
    offsets, slot_range = (pltpu.with_memory_space_constraint(x, pltpu.HBM) for x in (offsets, slot_range))
    block = object_field.reshape(planes, rows, cols)
    *dealt, given = call(
        deal_kernel,
        [shape(rows + 8, cols)] * 4 + [shape(width, width)],
        (where, offsets, sibling),
        ((block, HBM), (measured, HBM)),
        0,
        copies=5,
    )
    own = deal(dealt, PLANE[:2])
    (lowest,) = call(lowest_kernel, [shape(2, rows, cols)], (where,), own, 0)
    lowest, given = lax.optimization_barrier((lowest, given))
    below = lax.ppermute(lowest, "pair", [(k, k - 1) for k in range(1, pairs)])
    taken = lax.ppermute(given, "half", [(0, 1), (1, 0)])
    below, taken = lax.optimization_barrier((below, taken))

    parts = call(
        pick_kernel,
        [shape(rows, cols)] * 8,
        (where, slot_range),
        (*own, below),
        32 * rows * width,
        [(planes, rows + 8, cols), (8, rows, cols)],
    )
    offs = [own[FOUR.index(turn)][rows:, 0] for turn in range(4)]
    scalars = (where, slot_range, jnp.stack(offs).astype(jnp.int32))
    tabs = jnp.asarray(tables(width))
    probe, kept, tabs = call(
        ready_kernel,
        [shape(*probe.shape), shape(width, width), jax.ShapeDtypeStruct(tabs.shape, tabs.dtype)],
        scalars,
        ((probe, HBM), (measured, HBM), (tabs, HBM)),
        probe.size,
        copies=3,
    )
    grad = call(
        position_kernel,
        [shape(rows + 2 * band, cols)] * 8,
        scalars,
        (*deal(parts, PLANE), probe, kept, taken, tabs),
        8 * 24 * width**3,
        [(8, rows, cols), (8, rows + 2 * band, cols)],
    )
    got = deal(grad, PLANE)
    lower_sums, probe_band = call(
        add_below_kernel,
        [shape(2, rows, cols), shape(band, width)],
        scalars,
        got,
        32 * rows * width,
    )
    probe_band = sum_over(probe_band, "pair", pairs)
    (sums,) = call(add_own_kernel, [shape(planes, rows, cols)], scalars, got, 64 * rows * width)
    lower_sums, sums = lax.optimization_barrier((lower_sums, sums))
    above = lax.ppermute(lower_sums, "pair", [(k, k + 1) for k in range(pairs - 1)])
    sums = call(top_kernel, [shape(rows, cols)] * 4, (where,), (sums, above), planes * rows * cols)
    sums = deal(sums, PLANE[:2])
    probe_grad = lax.all_gather(probe_band, PLANE, axis=0, tiled=True)
    object_grad, probe_grad = call(
        join_kernel,
        [(shape(planes, rows, cols), HBM), (shape(*probe_grad.shape), HBM)],
        (where,),
        [(x, ANY) for x in (*sums, probe_grad)],
        0,
        copies=5,
    )
    return (object_grad.reshape(object_field.shape), probe_grad.reshape(probe.shape))


def solution(mesh):
    tile, grp = mesh.shape["tile"], mesh.shape["grp"]
    devices = mesh.devices.reshape(tile // 2, 2, 2, grp // 2)
    inner = Mesh(devices, ("pair", "half", "col", "core"))
    strip, cols = ("pair", "half"), ("col", "core")
    in_specs = (
        P(None, None, strip, cols),
        P(),
        P(strip, cols, None),
        P(strip, None),
        P(strip, cols, None, None),
    )
    out_specs = (P(None, None, strip, cols), P())
    return jax.shard_map(local, mesh=inner, in_specs=in_specs, out_specs=out_specs, check_vma=False)
```

```python
import functools
import math

import jax
import jax.numpy as jnp
import ml_dtypes
import numpy as np
from jax import lax
from jax.experimental import pallas as pl
from jax.experimental.pallas import tpu as pltpu
from jax.sharding import Mesh, PartitionSpec as P

GRAD_WEIGHT = 0.0625
PLANE = ("half", "col", "core")
EIGHT, FOUR = (4, 2, 5, 3, 6, 7, 1, 0), (2, 1, 3, 0)
VMEM_LIMIT = 24 * 1024 * 1024


def tables(width):
    half = width // 2
    index = np.arange(half, dtype=np.int64)
    scale = 1.0 / math.sqrt(width)
    far = np.exp(-2j * math.pi / half * (index[:, None] * index[None, :] % half)) * scale
    near = []
    for offset in (0, half):
        shift = index[:, None] - index[None, :] + offset
        near.append(np.exp(1j * (math.pi / width * (shift * shift % (2 * width)) - math.pi / 4.0)) * scale)
    products = []
    for matrix in ((near[0] + near[1]) / 2.0, (near[0] - near[1]) / 2.0, far):
        for imag in (matrix.imag, -matrix.imag):
            table = np.block([[matrix.real, imag], [-imag, matrix.real]])
            high = table.astype(ml_dtypes.bfloat16)
            low = (table - high.astype(np.float64)).astype(ml_dtypes.bfloat16)
            products.append(np.concatenate([high, low], axis=0))
    angle = -2.0 * math.pi / width * index
    twiddles = []
    for part in (np.cos(angle), np.sin(angle)):
        rows = np.broadcast_to(part[:, None], (half, half))
        twiddles.append(np.concatenate([rows, np.broadcast_to(part[None, :], (8, half))], axis=0))
    order = np.zeros((width, width))
    order[np.arange(width), np.concatenate([2 * index, 2 * index + 1])] = 1.0
    order = np.stack([order, order.T]).astype(ml_dtypes.bfloat16)
    return np.stack(products), np.stack(twiddles).astype(np.float32), order


def split(value):
    high = value.astype(jnp.bfloat16)
    low = (value - high.astype(jnp.float32)).astype(jnp.bfloat16)
    return high, low


def dot(left, right):
    return jnp.dot(left, right, preferred_element_type=jnp.float32)


PLUS, MINUS, FAR = 0, 2, 4


def times_right(re, im, table):
    width = table.shape[1]
    high, low = split(jnp.concatenate([re, im], axis=1))
    twice = dot(jnp.concatenate([high, low], axis=0), table[:width])
    count = re.shape[0]
    out = twice[:count] + (twice[count:] + dot(high, table[width:]))
    return out[:, : width // 2], out[:, width // 2 :]


def times_left(re, im, table):
    width = table.shape[1]
    high, low = split(jnp.concatenate([re, im], axis=0))
    twice = dot(table[...], high)
    out = twice[:width] + (twice[width:] + dot(table[:width], low))
    return out[: width // 2], out[width // 2 :]


def butterfly(first, second):
    return first + second, first - second


def halves(value, axis):
    half = value.shape[axis] // 2
    return (value[:half], value[half:]) if axis == 0 else (value[:, :half], value[:, half:])


def turn_by(re, im, cos, sin):
    return re * cos - im * sin, re * sin + im * cos


def propagate(re, im, tabs, conj):
    for axis in (1, 0):
        (plus_re, minus_re), (plus_im, minus_im) = (butterfly(*halves(x, axis)) for x in (re, im))
        times = times_right if axis else times_left
        pick = int(conj) if axis else 1 - int(conj)
        plus_re, plus_im = times(plus_re, plus_im, tabs.at[PLUS + pick])
        minus_re, minus_im = times(minus_re, minus_im, tabs.at[MINUS + pick])
        re = jnp.concatenate(butterfly(plus_re, minus_re), axis=axis)
        im = jnp.concatenate(butterfly(plus_im, minus_im), axis=axis)
    return re, im


def twiddle(factors, axis, width):
    half = factors.shape[2]
    if axis:
        return factors[0, half : half + 1], factors[1, half : half + 1]
    return tuple(jnp.concatenate([factors[k, :half]] * (width // half), axis=1) for k in range(2))


def to_far(re, im, tabs, factors):
    for axis in (1, 0):
        (even_re, odd_re), (even_im, odd_im) = (butterfly(*halves(x, axis)) for x in (re, im))
        odd_re, odd_im = turn_by(odd_re, odd_im, *twiddle(factors, axis, re.shape[1]))
        times, table = (times_right, tabs.at[FAR]) if axis else (times_left, tabs.at[FAR + 1])
        (even_re, even_im), (odd_re, odd_im) = times(even_re, even_im, table), times(odd_re, odd_im, table)
        re, im = jnp.concatenate([even_re, odd_re], axis=axis), jnp.concatenate([even_im, odd_im], axis=axis)
    return re, im


def from_far(re, im, tabs, factors):
    for axis in (0, 1):
        (even_re, odd_re), (even_im, odd_im) = halves(re, axis), halves(im, axis)
        times, table = (times_right, tabs.at[FAR + 1]) if axis else (times_left, tabs.at[FAR])
        (even_re, even_im), (odd_re, odd_im) = times(even_re, even_im, table), times(odd_re, odd_im, table)
        cos, sin = twiddle(factors, axis, re.shape[1])
        odd_re, odd_im = turn_by(odd_re, odd_im, cos, -sin)
        re = jnp.concatenate(butterfly(even_re, odd_re), axis=axis)
        im = jnp.concatenate(butterfly(even_im, odd_im), axis=axis)
    return re, im


def slot_of(half, col, core):
    return 2 * (2 * col + core) + half


def receivers():
    return [slot_of(half, col, core) for half in range(2) for col in range(2) for core in range(2)]


def slot_place(offs, mine, split_at, slot):
    lower = jnp.where(slot >= split_at, 1, 0)
    holder, at = jnp.bitwise_xor(2 * lower + slot // 4, mine), 2 * (slot % 4)
    return lower, offs[holder, at], offs[holder, at + 1]


def fetch(pairs, sems):
    copies = [pltpu.make_async_copy(source, into, sems.at[k]) for k, (source, into) in enumerate(pairs)]
    for copy in copies:
        copy.start()
    return copies


def deal_kernel(where, offsets, sibling, block, measured, *refs):
    outs, given, sems = refs[:4], refs[4], refs[5]
    mine, core = 2 * where[0] + where[1], where[2]
    rows, cols = block.shape[1:]
    pairs = [(block.at[jnp.bitwise_xor(mine, turn)], out.at[pl.ds(0, rows)]) for turn, out in zip(FOUR, outs)]
    copies = fetch([*pairs, (measured.at[0, 1 - where[0]], given)], sems)
    lines = []
    for holder in range(2):
        for slot in range(2):
            for axis in range(2):
                value = jnp.where(core == holder, offsets[0, slot, axis], sibling[0, slot, axis])
                lines.append(jnp.full((1, cols), value, jnp.int32))
    lines = jnp.concatenate(lines, axis=0).astype(jnp.float32)
    for out in outs:
        out[rows:] = lines
    for copy in copies:
        copy.wait()


def lowest_kernel(where, *refs):
    gotten, out = dict(zip(FOUR, refs)), refs[4]
    rows = out.shape[1]
    for turn in range(2):
        out[turn] = jnp.where(where[0] == 0, gotten[turn][:rows], gotten[2 + turn][:rows])


def pick_kernel(where, slot_range, *refs):
    gotten, below, outs, (own, parts) = dict(zip(FOUR, refs)), refs[4], refs[5:13], refs[13:]
    rows, cols = outs[0].shape
    half, col, core = where[0], where[1], where[2]
    mine = 2 * half + col
    for turn in range(4):
        own[jnp.bitwise_xor(mine, turn)] = gotten[turn][...]
    split_at = slot_range[0, 1 - half]
    row_ids = lax.broadcasted_iota(jnp.int32, (rows, cols), 0).astype(jnp.float32)
    col_ids = (lax.broadcasted_iota(jnp.int32, (rows, cols), 1) + core * cols).astype(jnp.float32)
    for place, slot in enumerate(receivers()):
        lower = jnp.where(slot >= split_at, 1, 0)
        at = rows + 2 * (slot % 4)
        offs = own[2 * lower + slot // 4, at : at + 2]
        upper_rows = row_ids >= offs[0:1]
        left_cols = col_ids >= offs[1:2]

        def merged(side, lower=lower, upper_rows=upper_rows):
            second = own[2 + side, :rows]
            top = jnp.where(lower == 1, second, own[side, :rows])
            bottom = jnp.where(lower == 1, below[jnp.bitwise_xor(col, side)], second)
            return jnp.where(upper_rows, top, bottom)

        parts[place] = jnp.where(left_cols, merged(0), merged(1))
    for turn, out in zip(EIGHT, outs):
        out[...] = parts[jnp.bitwise_xor(2 * mine + core, turn)]


def roll(value, rows, cols):
    return pltpu.roll(pltpu.roll(value, rows, 0), cols, 1)


def ready_kernel(where, slot_range, offs, taken, probe_from, measured, tabs_from, order_from, probe, target, tabs, kept, order, sems):
    half, col, core = where[0], where[1], where[2]
    probe_copy, kept_copy, order_copy, tabs_copy = fetch(
        [(probe_from, probe), (measured.at[0, half], kept), (order_from, order), (tabs_from, tabs)], sems
    )
    slot = slot_of(half, col, core)
    lower, row_at, col_at = slot_place(offs, 2 * half + col, slot_range[0, 1 - half], slot)
    probe_copy.wait()
    for part in range(2):
        probe[part] = roll(probe[part], row_at, col_at)
    kept_copy.wait()
    order_copy.wait()
    rest = jnp.where(lower == half, kept[...], taken[...])
    total = jnp.zeros_like(rest)
    for unused in range(3):
        part = rest.astype(jnp.bfloat16)
        rest = rest - part.astype(jnp.float32)
        total += dot(order[0], dot(part, order[1]).astype(jnp.bfloat16))
    target[...] = total
    tabs_copy.wait()


def position_kernel(where, slot_range, offs, *refs):
    gotten, (probe, target, tabs, factors) = dict(zip(EIGHT, refs)), refs[8:12]
    outs, patch, grad = refs[12:20], refs[20], refs[21]
    half, col, core = where[0], where[1], where[2]
    mine = 2 * half + col
    flat = 2 * mine + core
    unused, row_at, col_at = slot_place(offs, mine, slot_range[0, 1 - half], slot_of(half, col, core))
    width = probe.shape[-1]
    lanes, band = width // 2, width // 4
    for turn in range(8):
        patch[jnp.bitwise_xor(flat, turn)] = gotten[turn][...]

    def load(plane):
        return jnp.concatenate([patch[2 * plane], patch[2 * plane + 1]], axis=1)

    def store(plane, value):
        grad[2 * plane, :width] = value[:, :lanes]
        grad[2 * plane + 1, :width] = value[:, lanes:]

    wave_re, wave_im = probe[0], probe[1]
    o0_re, o0_im, o1_re, o1_im = load(0), load(2), load(1), load(3)
    exit_re = wave_re * o0_re - wave_im * o0_im
    exit_im = wave_re * o0_im + wave_im * o0_re
    mid_re, mid_im = propagate(exit_re, exit_im, tabs, False)
    exit_re = mid_re * o1_re - mid_im * o1_im
    exit_im = mid_re * o1_im + mid_im * o1_re
    far_re, far_im = to_far(exit_re, exit_im, tabs, factors)
    excess = 2.0 * GRAD_WEIGHT * (far_re * far_re + far_im * far_im - target[...])
    back_re, back_im = from_far(excess * far_re, excess * far_im, tabs, factors)
    store(1, mid_re * back_re + mid_im * back_im)
    store(3, mid_re * back_im - mid_im * back_re)
    up_re = o1_re * back_re + o1_im * back_im
    up_im = o1_re * back_im - o1_im * back_re
    back_re, back_im = propagate(up_re, up_im, tabs, True)
    wave_re, wave_im = probe[0], probe[1]
    o0_re, o0_im = load(0), load(2)
    store(0, wave_re * back_re + wave_im * back_im)
    store(2, wave_re * back_im - wave_im * back_re)
    up_re = o0_re * back_re + o0_im * back_im
    up_im = o0_re * back_im - o0_im * back_re
    back_row, back_col = lax.rem(width - row_at, width), lax.rem(2 * width - col_at, width)
    for part, value in enumerate((up_re, up_im)):
        value = roll(value, back_row, back_col)
        for step in range(4):
            rows = value[step * band : (step + 1) * band]
            grad[4 * part + step, width : width + band] = rows[:, :lanes]
            grad[4 * part + step, width + band :] = rows[:, lanes:]
    for turn, out in zip(EIGHT, outs):
        out[...] = grad[jnp.bitwise_xor(flat, turn)]


def add_parts(where, slot_range, offs, parts, strip, rows, cols):
    half, col, core = where[0], where[1], where[2]
    mine = 2 * half + col
    row_ids = lax.broadcasted_iota(jnp.int32, (rows, cols), 0)
    col_ids = lax.broadcasted_iota(jnp.int32, (rows, cols), 1) + core * cols
    sums = [jnp.zeros((rows, cols), jnp.float32)] * 2
    for turn, part in zip(EIGHT, parts):
        flat = jnp.bitwise_xor(2 * mine + core, turn)
        slot = slot_of(flat // 4, (flat // 2) % 2, flat % 2)
        lower, row_at, col_at = slot_place(offs, mine, slot_range[0, 1 - half], slot)
        first = jnp.where(strip == lower, row_at, jnp.where(strip == lower + 1, 0, rows))
        last = jnp.where(strip == lower, rows, jnp.where(strip == lower + 1, row_at, 0))
        value = jnp.where((row_ids >= first) & (row_ids < last), part[:rows], 0.0)
        left = jnp.where(col_ids >= col_at, value, 0.0)
        sums = [sums[0] + left, sums[1] + (value - left)]
    return sums


def add_below_kernel(where, slot_range, offs, *refs):
    parts, (below, probe_band) = refs[:8], refs[8:]
    rows, cols = below.shape[1:]
    sums = add_parts(where, slot_range, offs, parts, 2, rows, cols)
    for side in range(2):
        below[jnp.bitwise_xor(where[1], side)] = sums[side]
    total = parts[0][rows:]
    for part in parts[1:]:
        total = total + part[rows:]
    band = probe_band.shape[0]
    probe_band[:, :cols] = total[:band]
    probe_band[:, cols:] = total[band:]


def add_own_kernel(where, slot_range, offs, *refs):
    parts, own = refs[:8], refs[8]
    rows, cols = own.shape[1:]
    for strip in range(2):
        own[2 * strip], own[2 * strip + 1] = add_parts(where, slot_range, offs, parts, strip, rows, cols)


def top_kernel(where, own, above, *outs):
    mine = 2 * where[0] + where[1]
    for turn, out in zip(FOUR, outs):
        extra = jnp.where(where[0] == turn // 2, above[turn % 2], 0.0)
        out[...] = own[jnp.bitwise_xor(mine, turn)] + extra


def join_kernel(where, *refs):
    probe, out, probe_out, sems = refs[4:]
    mine = 2 * where[0] + where[1]
    pairs = [(ref, out.at[jnp.bitwise_xor(mine, turn)]) for turn, ref in zip(FOUR, refs)]
    for copy in fetch([(probe, probe_out), *pairs], sems):
        copy.wait()


SMEM = pl.BlockSpec(memory_space=pltpu.SMEM)
VMEM = pl.BlockSpec(memory_space=pltpu.VMEM)
HBM = pl.BlockSpec(memory_space=pltpu.HBM)
ANY = pl.BlockSpec(memory_space=pl.ANY)


def call(kernel, outs, scalars, arrays, flops, scratch=(), copies=0):
    outs, arrays = ([x if isinstance(x, tuple) else (x, VMEM) for x in xs] for xs in (outs, arrays))
    moved = sum(math.prod(x.shape) * x.dtype.itemsize for x, unused in [*arrays, *outs])
    scratch = [pltpu.VMEM(dims, jnp.float32) if isinstance(dims, tuple) else dims for dims in scratch]
    return pl.pallas_call(
        kernel,
        out_shape=[x for x, unused in outs],
        in_specs=[SMEM] * len(scalars) + [spec for unused, spec in arrays],
        out_specs=[spec for unused, spec in outs],
        scratch_shapes=scratch + [pltpu.SemaphoreType.DMA((copies,))] * (copies > 0),
        compiler_params=pltpu.CompilerParams(vmem_limit_bytes=VMEM_LIMIT),
        cost_estimate=pl.CostEstimate(flops=flops, bytes_accessed=moved, transcendentals=0),
    )(*scalars, *(pltpu.with_memory_space_constraint(x, pltpu.HBM) if spec is HBM else x for x, spec in arrays))


def shape(*dims):
    return jax.ShapeDtypeStruct(dims, jnp.float32)


def deal(values, axes):
    count = len(values)
    order = EIGHT if count == 8 else FOUR
    return [
        lax.ppermute(value, axes, [(k, k ^ turn) for k in range(count)]) if turn else value
        for turn, value in zip(order, values)
    ]


def sum_over(value, axis, size, first):
    if size & (size - 1):
        return value if first else lax.psum(value, axis)
    step = 1 << first
    while step < size:
        value = value + lax.ppermute(value, axis, [(k, k ^ step) for k in range(size)])
        step *= 2
        if first == 0:
            break
    return value


def local(object_field, probe, offsets, slot_range, measured):
    width = probe.shape[-1]
    planes, rows, cols = 4, object_field.shape[2], object_field.shape[3]
    band = width // 4
    pairs = lax.axis_size("pair")
    half, col, core = (lax.axis_index(name) for name in PLANE)
    where = jnp.stack([half, col, core])

    sibling = lax.ppermute(offsets, "core", [(0, 1), (1, 0)])
    offsets, slot_range = (pltpu.with_memory_space_constraint(x, pltpu.HBM) for x in (offsets, slot_range))
    block = object_field.reshape(planes, rows, cols)
    *dealt, given = call(
        deal_kernel,
        [shape(rows + 8, cols)] * 4 + [shape(width, width)],
        (where, offsets, sibling),
        ((block, HBM), (measured, HBM)),
        0,
        copies=5,
    )
    own = deal(dealt, PLANE[:2])
    (lowest,) = call(lowest_kernel, [shape(2, rows, cols)], (where,), own, 0)
    lowest, given = lax.optimization_barrier((lowest, given))
    below = lax.ppermute(lowest, "pair", [(k, k - 1) for k in range(1, pairs)])
    taken = lax.ppermute(given, "half", [(0, 1), (1, 0)])
    below, taken = lax.optimization_barrier((below, taken))

    parts = call(
        pick_kernel,
        [shape(rows, cols)] * 8,
        (where, slot_range),
        (*own, below),
        32 * rows * width,
        [(planes, rows + 8, cols), (8, rows, cols)],
    )
    offs = [own[FOUR.index(turn)][rows:, 0] for turn in range(4)]
    scalars = (where, slot_range, jnp.stack(offs).astype(jnp.int32))
    tabs, factors, order = (jnp.asarray(table) for table in tables(width))
    probe, target, tabs = call(
        ready_kernel,
        [shape(*probe.shape), shape(width, width), jax.ShapeDtypeStruct(tabs.shape, tabs.dtype)],
        scalars,
        (taken, (probe, HBM), (measured, HBM), (tabs, HBM), (order, HBM)),
        12 * width**3,
        [(width, width), pltpu.VMEM(order.shape, order.dtype)],
        copies=4,
    )
    grad = call(
        position_kernel,
        [shape(rows + 2 * band, cols)] * 8,
        scalars,
        (*deal(parts, PLANE), probe, target, tabs, factors),
        8 * 12 * width**3,
        [(8, rows, cols), (8, rows + 2 * band, cols)],
    )
    got = deal(grad, PLANE)
    lower_sums, probe_band = call(
        add_below_kernel,
        [shape(2, rows, cols), shape(band, width)],
        scalars,
        got,
        32 * rows * width,
    )
    probe_band = sum_over(probe_band, "pair", pairs, 0)
    (sums,) = call(add_own_kernel, [shape(planes, rows, cols)], scalars, got, 64 * rows * width)
    lower_sums, sums, probe_band = lax.optimization_barrier((lower_sums, sums, probe_band))
    above = lax.ppermute(lower_sums, "pair", [(k, k + 1) for k in range(pairs - 1)])
    sums = call(top_kernel, [shape(rows, cols)] * 4, (where,), (sums, above), planes * rows * cols)
    sums = deal(sums, PLANE[:2])
    probe_band = sum_over(probe_band, "pair", pairs, 1)
    probe_grad = lax.all_gather(probe_band, PLANE, axis=0, tiled=True)
    object_grad, probe_grad = call(
        join_kernel,
        [(shape(planes, rows, cols), HBM), (shape(*probe_grad.shape), HBM)],
        (where,),
        [(x, ANY) for x in (*sums, probe_grad)],
        0,
        copies=5,
    )
    return (object_grad.reshape(object_field.shape), probe_grad.reshape(probe.shape))


def solution(mesh):
    tile, grp = mesh.shape["tile"], mesh.shape["grp"]
    devices = mesh.devices.reshape(tile // 2, 2, 2, grp // 2)
    inner = Mesh(devices, ("pair", "half", "col", "core"))
    strip, cols = ("pair", "half"), ("col", "core")
    in_specs = (
        P(None, None, strip, cols),
        P(),
        P(strip, cols, None),
        P(strip, None),
        P(strip, cols, None, None),
    )
    out_specs = (P(None, None, strip, cols), P())
    return jax.shard_map(local, mesh=inner, in_specs=in_specs, out_specs=out_specs, check_vma=False)
```

```python
import functools
import math

import jax
import jax.numpy as jnp
import ml_dtypes
import numpy as np
from jax import lax
from jax.experimental import pallas as pl
from jax.experimental.pallas import tpu as pltpu
from jax.sharding import Mesh, PartitionSpec as P

GRAD_WEIGHT = 0.0625
PLANE = ("half", "col", "core")
EIGHT, FOUR = (4, 2, 5, 3, 6, 7, 1, 0), (2, 1, 3, 0)
VMEM_LIMIT = 24 * 1024 * 1024


def tables(width):
    half = width // 2
    index = np.arange(half, dtype=np.int64)
    scale = 1.0 / math.sqrt(width)
    far = np.exp(-2j * math.pi / half * (index[:, None] * index[None, :] % half)) * scale
    near = []
    for offset in (0, half):
        shift = index[:, None] - index[None, :] + offset
        near.append(np.exp(1j * (math.pi / width * (shift * shift % (2 * width)) - math.pi / 4.0)) * scale)
    products = []
    for matrix in ((near[0] + near[1]) / 2.0, (near[0] - near[1]) / 2.0, far):
        for imag in (matrix.imag, -matrix.imag):
            table = np.block([[matrix.real, imag], [-imag, matrix.real]])
            high = table.astype(ml_dtypes.bfloat16)
            low = (table - high.astype(np.float64)).astype(ml_dtypes.bfloat16)
            products.append(np.concatenate([high, low], axis=0))
    angle = -2.0 * math.pi / width * index
    twiddles = []
    for part in (np.cos(angle), np.sin(angle)):
        rows = np.broadcast_to(part[:, None], (half, half))
        twiddles.append(np.concatenate([rows, np.broadcast_to(part[None, :], (8, half))], axis=0))
    order = np.zeros((width, width))
    order[np.arange(width), np.concatenate([2 * index, 2 * index + 1])] = 1.0
    order = np.stack([order, order.T]).astype(ml_dtypes.bfloat16)
    return np.stack(products), np.stack(twiddles).astype(np.float32), order


def split(value):
    high = value.astype(jnp.bfloat16)
    low = (value - high.astype(jnp.float32)).astype(jnp.bfloat16)
    return high, low


def dot(left, right):
    return jnp.dot(left, right, preferred_element_type=jnp.float32)


PLUS, MINUS, FAR = 0, 2, 4


def times_right(re, im, table):
    width = table.shape[1]
    high, low = split(jnp.concatenate([re, im], axis=1))
    twice = dot(jnp.concatenate([high, low], axis=0), table[:width])
    count = re.shape[0]
    out = twice[:count] + (twice[count:] + dot(high, table[width:]))
    return out[:, : width // 2], out[:, width // 2 :]


def times_left(re, im, table):
    width = table.shape[1]
    high, low = split(jnp.concatenate([re, im], axis=0))
    twice = dot(table[...], high)
    out = twice[:width] + (twice[width:] + dot(table[:width], low))
    return out[: width // 2], out[width // 2 :]


def butterfly(first, second):
    return first + second, first - second


def halves(value, axis):
    half = value.shape[axis] // 2
    return (value[:half], value[half:]) if axis == 0 else (value[:, :half], value[:, half:])


def turn_by(re, im, cos, sin):
    return re * cos - im * sin, re * sin + im * cos


def propagate(re, im, tabs, conj):
    for axis in (1, 0):
        (plus_re, minus_re), (plus_im, minus_im) = (butterfly(*halves(x, axis)) for x in (re, im))
        times = times_right if axis else times_left
        pick = int(conj) if axis else 1 - int(conj)
        plus_re, plus_im = times(plus_re, plus_im, tabs.at[PLUS + pick])
        minus_re, minus_im = times(minus_re, minus_im, tabs.at[MINUS + pick])
        re = jnp.concatenate(butterfly(plus_re, minus_re), axis=axis)
        im = jnp.concatenate(butterfly(plus_im, minus_im), axis=axis)
    return re, im


def twiddle(factors, axis, width):
    half = factors.shape[2]
    if axis:
        return factors[0, half : half + 1], factors[1, half : half + 1]
    return tuple(jnp.concatenate([factors[k, :half]] * (width // half), axis=1) for k in range(2))


def to_far(re, im, tabs, factors):
    for axis in (1, 0):
        (even_re, odd_re), (even_im, odd_im) = (butterfly(*halves(x, axis)) for x in (re, im))
        odd_re, odd_im = turn_by(odd_re, odd_im, *twiddle(factors, axis, re.shape[1]))
        times, table = (times_right, tabs.at[FAR]) if axis else (times_left, tabs.at[FAR + 1])
        (even_re, even_im), (odd_re, odd_im) = times(even_re, even_im, table), times(odd_re, odd_im, table)
        re, im = jnp.concatenate([even_re, odd_re], axis=axis), jnp.concatenate([even_im, odd_im], axis=axis)
    return re, im


def from_far(re, im, tabs, factors):
    for axis in (0, 1):
        (even_re, odd_re), (even_im, odd_im) = halves(re, axis), halves(im, axis)
        times, table = (times_right, tabs.at[FAR + 1]) if axis else (times_left, tabs.at[FAR])
        (even_re, even_im), (odd_re, odd_im) = times(even_re, even_im, table), times(odd_re, odd_im, table)
        cos, sin = twiddle(factors, axis, re.shape[1])
        odd_re, odd_im = turn_by(odd_re, odd_im, cos, -sin)
        re = jnp.concatenate(butterfly(even_re, odd_re), axis=axis)
        im = jnp.concatenate(butterfly(even_im, odd_im), axis=axis)
    return re, im


def slot_of(half, col, core):
    return 2 * (2 * col + core) + half


def receivers():
    return [slot_of(half, col, core) for half in range(2) for col in range(2) for core in range(2)]


def slot_place(offs, mine, split_at, slot):
    lower = jnp.where(slot >= split_at, 1, 0)
    holder, at = jnp.bitwise_xor(2 * lower + slot // 4, mine), 2 * (slot % 4)
    return lower, offs[holder, at], offs[holder, at + 1]


def fetch(pairs, sems):
    copies = [pltpu.make_async_copy(source, into, sems.at[k]) for k, (source, into) in enumerate(pairs)]
    for copy in copies:
        copy.start()
    return copies


def deal_kernel(where, offsets, block, measured, *refs):
    outs, given, sems = refs[:4], refs[4], refs[5]
    mine = 2 * where[0] + where[1]
    rows, cols = block.shape[1:]
    pairs = [(block.at[jnp.bitwise_xor(mine, turn)], out.at[pl.ds(0, rows)]) for turn, out in zip(FOUR, outs)]
    copies = fetch([*pairs, (measured.at[0, 1 - where[0]], given)], sems)
    lines = [jnp.full((1, cols), offsets[0, slot, axis], jnp.int32) for slot in range(2) for axis in range(2)]
    lines = jnp.concatenate(lines * 2, axis=0).astype(jnp.float32)
    for out in outs:
        out[rows:] = lines
    for copy in copies:
        copy.wait()


def lowest_kernel(where, first, second, out):
    rows = out.shape[0]
    out[...] = jnp.where(where[0] == 0, first[:rows], second[:rows])


def pick_kernel(where, slot_range, offs, *refs):
    gotten, below, outs, (own, parts) = dict(zip(FOUR, refs)), refs[4:6], refs[6:14], refs[14:]
    rows, cols = outs[0].shape
    half, col, core = where[0], where[1], where[2]
    mine = 2 * half + col
    for turn in range(4):
        own[jnp.bitwise_xor(mine, turn)] = gotten[turn][:rows]
    split_at = slot_range[0, 1 - half]
    row_ids = lax.broadcasted_iota(jnp.int32, (rows, cols), 0)
    col_ids = lax.broadcasted_iota(jnp.int32, (rows, cols), 1) + core * cols
    below = [jnp.where(col == side, below[0][...], below[1][...]) for side in range(2)]
    for place, slot in enumerate(receivers()):
        lower, row_at, col_at = slot_place(offs, mine, split_at, slot)
        upper_rows = row_ids >= row_at
        left_cols = col_ids >= col_at

        def merged(side, lower=lower, upper_rows=upper_rows):
            second = own[2 + side]
            top = jnp.where(lower == 1, second, own[side])
            bottom = jnp.where(lower == 1, below[side], second)
            return jnp.where(upper_rows, top, bottom)

        parts[place] = jnp.where(left_cols, merged(0), merged(1))
    for turn, out in zip(EIGHT, outs):
        out[...] = parts[jnp.bitwise_xor(2 * mine + core, turn)]


def roll(value, rows, cols):
    return pltpu.roll(pltpu.roll(value, rows, 0), cols, 1)


def ready_kernel(where, slot_range, offs, taken, probe_from, measured, tabs_from, order_from, probe, target, tabs, kept, order, sems):
    half, col, core = where[0], where[1], where[2]
    probe_copy, kept_copy, order_copy, tabs_copy = fetch(
        [(probe_from, probe), (measured.at[0, half], kept), (order_from, order), (tabs_from, tabs)], sems
    )
    slot = slot_of(half, col, core)
    lower, row_at, col_at = slot_place(offs, 2 * half + col, slot_range[0, 1 - half], slot)
    probe_copy.wait()
    for part in range(2):
        probe[part] = roll(probe[part], row_at, col_at)
    kept_copy.wait()
    order_copy.wait()
    rest = jnp.where(lower == half, kept[...], taken[...])
    total = jnp.zeros_like(rest)
    for unused in range(3):
        part = rest.astype(jnp.bfloat16)
        rest = rest - part.astype(jnp.float32)
        total += dot(order[0], dot(part, order[1]).astype(jnp.bfloat16))
    target[...] = total
    tabs_copy.wait()


def position_kernel(where, slot_range, offs, *refs):
    gotten, (probe, target, tabs, factors) = dict(zip(EIGHT, refs)), refs[8:12]
    outs, patch, grad = refs[12:20], refs[20], refs[21]
    half, col, core = where[0], where[1], where[2]
    mine = 2 * half + col
    flat = 2 * mine + core
    unused, row_at, col_at = slot_place(offs, mine, slot_range[0, 1 - half], slot_of(half, col, core))
    width = probe.shape[-1]
    lanes, band = width // 2, width // 4
    for turn in range(8):
        patch[jnp.bitwise_xor(flat, turn)] = gotten[turn][...]

    def load(plane):
        return jnp.concatenate([patch[2 * plane], patch[2 * plane + 1]], axis=1)

    def store(plane, value):
        grad[2 * plane, :width] = value[:, :lanes]
        grad[2 * plane + 1, :width] = value[:, lanes:]

    wave_re, wave_im = probe[0], probe[1]
    o0_re, o0_im, o1_re, o1_im = load(0), load(2), load(1), load(3)
    exit_re = wave_re * o0_re - wave_im * o0_im
    exit_im = wave_re * o0_im + wave_im * o0_re
    mid_re, mid_im = propagate(exit_re, exit_im, tabs, False)
    exit_re = mid_re * o1_re - mid_im * o1_im
    exit_im = mid_re * o1_im + mid_im * o1_re
    far_re, far_im = to_far(exit_re, exit_im, tabs, factors)
    excess = 2.0 * GRAD_WEIGHT * (far_re * far_re + far_im * far_im - target[...])
    back_re, back_im = from_far(excess * far_re, excess * far_im, tabs, factors)
    store(1, mid_re * back_re + mid_im * back_im)
    store(3, mid_re * back_im - mid_im * back_re)
    up_re = o1_re * back_re + o1_im * back_im
    up_im = o1_re * back_im - o1_im * back_re
    back_re, back_im = propagate(up_re, up_im, tabs, True)
    wave_re, wave_im = probe[0], probe[1]
    o0_re, o0_im = load(0), load(2)
    store(0, wave_re * back_re + wave_im * back_im)
    store(2, wave_re * back_im - wave_im * back_re)
    up_re = o0_re * back_re + o0_im * back_im
    up_im = o0_re * back_im - o0_im * back_re
    back_row, back_col = lax.rem(width - row_at, width), lax.rem(2 * width - col_at, width)
    for part, value in enumerate((up_re, up_im)):
        value = roll(value, back_row, back_col)
        for step in range(4):
            rows = value[step * band : (step + 1) * band]
            grad[4 * part + step, width : width + band] = rows[:, :lanes]
            grad[4 * part + step, width + band :] = rows[:, lanes:]
    for turn, out in zip(EIGHT, outs):
        out[...] = grad[jnp.bitwise_xor(flat, turn)]


def add_parts(where, slot_range, offs, parts, strip, rows, cols):
    half, col, core = where[0], where[1], where[2]
    mine = 2 * half + col
    row_ids = lax.broadcasted_iota(jnp.int32, (rows, cols), 0)
    col_ids = lax.broadcasted_iota(jnp.int32, (rows, cols), 1) + core * cols
    sums = [jnp.zeros((rows, cols), jnp.float32)] * 2
    for turn, part in zip(EIGHT, parts):
        flat = jnp.bitwise_xor(2 * mine + core, turn)
        slot = slot_of(flat // 4, (flat // 2) % 2, flat % 2)
        lower, row_at, col_at = slot_place(offs, mine, slot_range[0, 1 - half], slot)
        first = jnp.where(strip == lower, row_at, jnp.where(strip == lower + 1, 0, rows))
        last = jnp.where(strip == lower, rows, jnp.where(strip == lower + 1, row_at, 0))
        value = jnp.where((row_ids >= first) & (row_ids < last), part[:rows], 0.0)
        left = jnp.where(col_ids >= col_at, value, 0.0)
        sums = [sums[0] + left, sums[1] + (value - left)]
    return sums


def add_below_kernel(where, slot_range, offs, *refs):
    parts, (below0, below1, probe_band) = refs[:8], refs[8:]
    rows, cols = below0.shape
    sums = add_parts(where, slot_range, offs, parts, 2, rows, cols)
    below0[...] = jnp.where(where[1] == 0, sums[0], sums[1])
    below1[...] = jnp.where(where[1] == 0, sums[1], sums[0])
    total = parts[0][rows:]
    for part in parts[1:]:
        total = total + part[rows:]
    band = probe_band.shape[0]
    probe_band[:, :cols] = total[:band]
    probe_band[:, cols:] = total[band:]


def add_own_kernel(where, slot_range, offs, *refs):
    parts, own = refs[:8], refs[8]
    rows, cols = own.shape[1:]
    for strip in range(2):
        own[2 * strip], own[2 * strip + 1] = add_parts(where, slot_range, offs, parts, strip, rows, cols)


def top_kernel(turns, where, own, above, *outs):
    mine = 2 * where[0] + where[1]
    for turn, out in zip(turns, outs):
        extra = jnp.where(where[0] == turn // 2, above[...], 0.0)
        out[...] = own[jnp.bitwise_xor(mine, turn)] + extra


def join_kernel(where, *refs):
    probe, out, probe_out, sems = refs[4:]
    mine = 2 * where[0] + where[1]
    pairs = [(ref, out.at[jnp.bitwise_xor(mine, turn)]) for turn, ref in zip(FOUR, refs)]
    for copy in fetch([(probe, probe_out), *pairs], sems):
        copy.wait()


SMEM = pl.BlockSpec(memory_space=pltpu.SMEM)
VMEM = pl.BlockSpec(memory_space=pltpu.VMEM)
HBM = pl.BlockSpec(memory_space=pltpu.HBM)
ANY = pl.BlockSpec(memory_space=pl.ANY)


def call(kernel, outs, scalars, arrays, flops, scratch=(), copies=0):
    outs, arrays = ([x if isinstance(x, tuple) else (x, VMEM) for x in xs] for xs in (outs, arrays))
    moved = sum(math.prod(x.shape) * x.dtype.itemsize for x, unused in [*arrays, *outs])
    scratch = [pltpu.VMEM(dims, jnp.float32) if isinstance(dims, tuple) else dims for dims in scratch]
    return pl.pallas_call(
        kernel,
        out_shape=[x for x, unused in outs],
        in_specs=[SMEM] * len(scalars) + [spec for unused, spec in arrays],
        out_specs=[spec for unused, spec in outs],
        scratch_shapes=scratch + [pltpu.SemaphoreType.DMA((copies,))] * (copies > 0),
        compiler_params=pltpu.CompilerParams(vmem_limit_bytes=VMEM_LIMIT),
        cost_estimate=pl.CostEstimate(flops=flops, bytes_accessed=moved, transcendentals=0),
    )(*scalars, *(pltpu.with_memory_space_constraint(x, pltpu.HBM) if spec is HBM else x for x, spec in arrays))


def shape(*dims):
    return jax.ShapeDtypeStruct(dims, jnp.float32)


def deal(values, axes):
    count = len(values)
    order = EIGHT if count == 8 else FOUR
    return [
        lax.ppermute(value, axes, [(k, k ^ turn) for k in range(count)]) if turn else value
        for turn, value in zip(order, values)
    ]


def sum_over(value, axis, size, first):
    if size & (size - 1):
        return value if first else lax.psum(value, axis)
    step = 1 << first
    while step < size:
        value = value + lax.ppermute(value, axis, [(k, k ^ step) for k in range(size)])
        step *= 2
        if first == 0:
            break
    return value


def local(object_field, probe, offsets, slot_range, measured):
    width = probe.shape[-1]
    planes, rows, cols = 4, object_field.shape[2], object_field.shape[3]
    band = width // 4
    pairs = lax.axis_size("pair")
    half, col, core = (lax.axis_index(name) for name in PLANE)
    where = jnp.stack([half, col, core])

    offsets, slot_range = (pltpu.with_memory_space_constraint(x, pltpu.HBM) for x in (offsets, slot_range))
    block = object_field.reshape(planes, rows, cols)
    *dealt, given = call(
        deal_kernel,
        [shape(rows + 8, cols)] * 4 + [shape(width, width)],
        (where, offsets),
        ((block, HBM), (measured, HBM)),
        0,
        copies=5,
    )
    own = deal(dealt, PLANE[:2])
    turned = dict(zip(FOUR, own))
    offs = jnp.stack([turned[turn][rows : rows + 4, 0] for turn in range(4)]).astype(jnp.int32)
    others = lax.ppermute(offs, "core", [(0, 1), (1, 0)])
    offs = jnp.concatenate([jnp.where(core == 0, offs, others), jnp.where(core == 0, others, offs)], axis=1)
    below, lowest = [], given
    for turn in range(2):
        first, lowest = lax.optimization_barrier((turned[turn], lowest))
        (lowest,) = call(lowest_kernel, [shape(rows, cols)], (where,), (first, turned[2 + turn]), 0)
        below.append(lax.ppermute(lowest, "pair", [(k, k - 1) for k in range(1, pairs)]))
    given, offs = lax.optimization_barrier((given, offs))
    taken = lax.ppermute(given, "half", [(0, 1), (1, 0)])
    below[1], taken = lax.optimization_barrier((below[1], taken))
    scalars = (where, slot_range, offs)

    parts = call(
        pick_kernel,
        [shape(rows, cols)] * 8,
        scalars,
        (*own, *below),
        32 * rows * width,
        [(planes, rows, cols), (8, rows, cols)],
    )
    tabs, factors, order = (jnp.asarray(table) for table in tables(width))
    probe, target, tabs = call(
        ready_kernel,
        [shape(*probe.shape), shape(width, width), jax.ShapeDtypeStruct(tabs.shape, tabs.dtype)],
        scalars,
        (taken, (probe, HBM), (measured, HBM), (tabs, HBM), (order, HBM)),
        12 * width**3,
        [(width, width), pltpu.VMEM(order.shape, order.dtype)],
        copies=4,
    )
    grad = call(
        position_kernel,
        [shape(rows + 2 * band, cols)] * 8,
        scalars,
        (*deal(parts, PLANE), probe, target, tabs, factors),
        8 * 12 * width**3,
        [(8, rows, cols), (8, rows + 2 * band, cols)],
    )
    got = deal(grad, PLANE)
    *lower_sums, probe_band = call(
        add_below_kernel,
        [shape(rows, cols)] * 2 + [shape(band, width)],
        scalars,
        got,
        32 * rows * width,
    )
    probe_band = sum_over(probe_band, "pair", pairs, 0)
    (sums,) = call(add_own_kernel, [shape(planes, rows, cols)], scalars, got, 64 * rows * width)
    *lower_sums, sums, probe_band = lax.optimization_barrier((*lower_sums, sums, probe_band))
    turned = {}
    for turn in range(2):
        above = lax.ppermute(lower_sums[turn], "pair", [(k, k + 1) for k in range(pairs - 1)])
        turns = (turn, 2 + turn)
        kernel = functools.partial(top_kernel, turns)
        turned.update(zip(turns, call(kernel, [shape(rows, cols)] * 2, (where,), (sums, above), 4 * rows * cols)))
    sums = deal([turned[turn] for turn in FOUR], PLANE[:2])
    probe_band = sum_over(probe_band, "pair", pairs, 1)
    probe_grad = lax.all_gather(probe_band, PLANE, axis=0, tiled=True)
    object_grad, probe_grad = call(
        join_kernel,
        [(shape(planes, rows, cols), HBM), (shape(*probe_grad.shape), HBM)],
        (where,),
        [(x, ANY) for x in (*sums, probe_grad)],
        0,
        copies=5,
    )
    return (object_grad.reshape(object_field.shape), probe_grad.reshape(probe.shape))


def solution(mesh):
    tile, grp = mesh.shape["tile"], mesh.shape["grp"]
    devices = mesh.devices.reshape(tile // 2, 2, 2, grp // 2)
    inner = Mesh(devices, ("pair", "half", "col", "core"))
    strip, cols = ("pair", "half"), ("col", "core")
    in_specs = (
        P(None, None, strip, cols),
        P(),
        P(strip, cols, None),
        P(strip, None),
        P(strip, cols, None, None),
    )
    out_specs = (P(None, None, strip, cols), P())
    return jax.shard_map(local, mesh=inner, in_specs=in_specs, out_specs=out_specs, check_vma=False)
```

```python
import functools
import math

import jax
import jax.numpy as jnp
import ml_dtypes
import numpy as np
from jax import lax
from jax.experimental import pallas as pl
from jax.experimental.pallas import tpu as pltpu
from jax.sharding import Mesh, PartitionSpec as P

GRAD_WEIGHT = 0.0625
PLANE = ("half", "col", "core")
EIGHT, FOUR = (4, 2, 5, 3, 6, 7, 1, 0), (2, 1, 3, 0)
VMEM_LIMIT = 24 * 1024 * 1024


def tables(width):
    half = width // 2
    index = np.arange(half, dtype=np.int64)
    scale = 1.0 / math.sqrt(width)
    far = np.exp(-2j * math.pi / half * (index[:, None] * index[None, :] % half)) * scale
    near = []
    for offset in (0, half):
        shift = index[:, None] - index[None, :] + offset
        near.append(np.exp(1j * (math.pi / width * (shift * shift % (2 * width)) - math.pi / 4.0)) * scale)
    products = []
    for matrix in ((near[0] + near[1]) / 2.0, (near[0] - near[1]) / 2.0, far):
        for imag in (matrix.imag, -matrix.imag):
            table = np.block([[matrix.real, imag], [-imag, matrix.real]])
            high = table.astype(ml_dtypes.bfloat16)
            low = (table - high.astype(np.float64)).astype(ml_dtypes.bfloat16)
            products.append(np.concatenate([high, low], axis=0))
    angle = -2.0 * math.pi / width * index
    twiddles = []
    for part in (np.cos(angle), np.sin(angle)):
        rows = np.broadcast_to(part[:, None], (half, half))
        twiddles.append(np.concatenate([rows, np.broadcast_to(part[None, :], (8, half))], axis=0))
    order = np.zeros((width, width))
    order[np.arange(width), np.concatenate([2 * index, 2 * index + 1])] = 1.0
    order = np.stack([order, order.T]).astype(ml_dtypes.bfloat16)
    return np.stack(products), np.stack(twiddles).astype(np.float32), order


def split(value):
    high = value.astype(jnp.bfloat16)
    low = (value - high.astype(jnp.float32)).astype(jnp.bfloat16)
    return high, low


def dot(left, right):
    return jnp.dot(left, right, preferred_element_type=jnp.float32)


PLUS, MINUS, FAR = 0, 2, 4


def times_right(re, im, table):
    width = table.shape[1]
    high, low = split(jnp.concatenate([re, im], axis=1))
    twice = dot(jnp.concatenate([high, low], axis=0), table[:width])
    count = re.shape[0]
    out = twice[:count] + (twice[count:] + dot(high, table[width:]))
    return out[:, : width // 2], out[:, width // 2 :]


def times_left(re, im, table):
    width = table.shape[1]
    high, low = split(jnp.concatenate([re, im], axis=0))
    twice = dot(table[...], high)
    out = twice[:width] + (twice[width:] + dot(table[:width], low))
    return out[: width // 2], out[width // 2 :]


def butterfly(first, second):
    return first + second, first - second


def halves(value, axis):
    half = value.shape[axis] // 2
    return (value[:half], value[half:]) if axis == 0 else (value[:, :half], value[:, half:])


def turn_by(re, im, cos, sin):
    return re * cos - im * sin, re * sin + im * cos


def propagate(re, im, tabs, conj):
    for axis in (1, 0):
        (plus_re, minus_re), (plus_im, minus_im) = (butterfly(*halves(x, axis)) for x in (re, im))
        times = times_right if axis else times_left
        pick = int(conj) if axis else 1 - int(conj)
        plus_re, plus_im = times(plus_re, plus_im, tabs.at[PLUS + pick])
        minus_re, minus_im = times(minus_re, minus_im, tabs.at[MINUS + pick])
        re = jnp.concatenate(butterfly(plus_re, minus_re), axis=axis)
        im = jnp.concatenate(butterfly(plus_im, minus_im), axis=axis)
    return re, im


def twiddle(factors, axis, width):
    half = factors.shape[2]
    if axis:
        return factors[0, half : half + 1], factors[1, half : half + 1]
    return tuple(jnp.concatenate([factors[k, :half]] * (width // half), axis=1) for k in range(2))


def to_far(re, im, tabs, factors):
    for axis in (1, 0):
        (even_re, odd_re), (even_im, odd_im) = (butterfly(*halves(x, axis)) for x in (re, im))
        odd_re, odd_im = turn_by(odd_re, odd_im, *twiddle(factors, axis, re.shape[1]))
        times, table = (times_right, tabs.at[FAR]) if axis else (times_left, tabs.at[FAR + 1])
        (even_re, even_im), (odd_re, odd_im) = times(even_re, even_im, table), times(odd_re, odd_im, table)
        re, im = jnp.concatenate([even_re, odd_re], axis=axis), jnp.concatenate([even_im, odd_im], axis=axis)
    return re, im


def from_far(re, im, tabs, factors):
    for axis in (0, 1):
        (even_re, odd_re), (even_im, odd_im) = halves(re, axis), halves(im, axis)
        times, table = (times_right, tabs.at[FAR + 1]) if axis else (times_left, tabs.at[FAR])
        (even_re, even_im), (odd_re, odd_im) = times(even_re, even_im, table), times(odd_re, odd_im, table)
        cos, sin = twiddle(factors, axis, re.shape[1])
        odd_re, odd_im = turn_by(odd_re, odd_im, cos, -sin)
        re = jnp.concatenate(butterfly(even_re, odd_re), axis=axis)
        im = jnp.concatenate(butterfly(even_im, odd_im), axis=axis)
    return re, im


def slot_of(half, col, core):
    return 2 * (2 * col + core) + half


def receivers():
    return [slot_of(half, col, core) for half in range(2) for col in range(2) for core in range(2)]


def slot_place(offs, mine, split_at, slot):
    lower = jnp.where(slot >= split_at, 1, 0)
    holder, at = jnp.bitwise_xor(2 * lower + slot // 4, mine), 2 * (slot % 4)
    return lower, offs[holder, at], offs[holder, at + 1]


def fetch(pairs, sems):
    copies = [pltpu.make_async_copy(source, into, sems.at[k]) for k, (source, into) in enumerate(pairs)]
    for copy in copies:
        copy.start()
    return copies


def deal_kernel(where, offsets, sibling, block, measured, *refs):
    outs, given, sems = refs[:4], refs[4], refs[5]
    mine, core = 2 * where[0] + where[1], where[2]
    rows, cols = block.shape[1:]
    pairs = [(block.at[jnp.bitwise_xor(mine, turn)], out.at[pl.ds(0, rows)]) for turn, out in zip(FOUR, outs)]
    copies = fetch([*pairs, (measured.at[0, 1 - where[0]], given)], sems)
    lines = []
    for holder in range(2):
        for slot in range(2):
            for axis in range(2):
                value = jnp.where(core == holder, offsets[0, slot, axis], sibling[0, slot, axis])
                lines.append(jnp.full((1, cols), value, jnp.int32))
    lines = jnp.concatenate(lines, axis=0).astype(jnp.float32)
    for out in outs:
        out[rows:] = lines
    for copy in copies:
        copy.wait()


def lowest_kernel(where, *refs):
    gotten, out = dict(zip(FOUR, refs)), refs[4]
    rows = out.shape[1]
    for turn in range(2):
        out[turn] = jnp.where(where[0] == 0, gotten[turn][:rows], gotten[2 + turn][:rows])


def pick_kernel(where, slot_range, *refs):
    gotten, below, outs, (own, parts) = dict(zip(FOUR, refs)), refs[4], refs[5:13], refs[13:]
    rows, cols = outs[0].shape
    half, col, core = where[0], where[1], where[2]
    mine = 2 * half + col
    for turn in range(4):
        own[jnp.bitwise_xor(mine, turn)] = gotten[turn][...]
    split_at = slot_range[0, 1 - half]
    row_ids = lax.broadcasted_iota(jnp.int32, (rows, cols), 0).astype(jnp.float32)
    col_ids = (lax.broadcasted_iota(jnp.int32, (rows, cols), 1) + core * cols).astype(jnp.float32)
    for place, slot in enumerate(receivers()):
        lower = jnp.where(slot >= split_at, 1, 0)
        at = rows + 2 * (slot % 4)
        offs = own[2 * lower + slot // 4, at : at + 2]
        upper_rows = row_ids >= offs[0:1]
        left_cols = col_ids >= offs[1:2]

        def merged(side, lower=lower, upper_rows=upper_rows):
            second = own[2 + side, :rows]
            top = jnp.where(lower == 1, second, own[side, :rows])
            bottom = jnp.where(lower == 1, below[jnp.bitwise_xor(col, side)], second)
            return jnp.where(upper_rows, top, bottom)

        parts[place] = jnp.where(left_cols, merged(0), merged(1))
    for turn, out in zip(EIGHT, outs):
        out[...] = parts[jnp.bitwise_xor(2 * mine + core, turn)]


def roll(value, rows, cols):
    return pltpu.roll(pltpu.roll(value, rows, 0), cols, 1)


def ready_kernel(where, slot_range, offs, taken, probe_from, measured, tabs_from, order_from, probe, target, tabs, kept, order, sems):
    half, col, core = where[0], where[1], where[2]
    probe_copy, kept_copy, order_copy, tabs_copy = fetch(
        [(probe_from, probe), (measured.at[0, half], kept), (order_from, order), (tabs_from, tabs)], sems
    )
    slot = slot_of(half, col, core)
    lower, row_at, col_at = slot_place(offs, 2 * half + col, slot_range[0, 1 - half], slot)
    probe_copy.wait()
    for part in range(2):
        probe[part] = roll(probe[part], row_at, col_at)
    kept_copy.wait()
    order_copy.wait()
    rest = jnp.where(lower == half, kept[...], taken[...])
    total = jnp.zeros_like(rest)
    for unused in range(3):
        part = rest.astype(jnp.bfloat16)
        rest = rest - part.astype(jnp.float32)
        total += dot(order[0], dot(part, order[1]).astype(jnp.bfloat16))
    target[...] = total
    tabs_copy.wait()


def position_kernel(where, slot_range, offs, *refs):
    gotten, (probe, target, tabs, factors) = dict(zip(EIGHT, refs)), refs[8:12]
    outs, patch, grad = refs[12:20], refs[20], refs[21]
    half, col, core = where[0], where[1], where[2]
    mine = 2 * half + col
    flat = 2 * mine + core
    unused, row_at, col_at = slot_place(offs, mine, slot_range[0, 1 - half], slot_of(half, col, core))
    width = probe.shape[-1]
    lanes, band = width // 2, width // 4
    for turn in range(8):
        patch[jnp.bitwise_xor(flat, turn)] = gotten[turn][...]

    def load(plane):
        return jnp.concatenate([patch[2 * plane], patch[2 * plane + 1]], axis=1)

    def store(plane, value):
        grad[2 * plane, :width] = value[:, :lanes]
        grad[2 * plane + 1, :width] = value[:, lanes:]

    wave_re, wave_im = probe[0], probe[1]
    o0_re, o0_im, o1_re, o1_im = load(0), load(2), load(1), load(3)
    exit_re = wave_re * o0_re - wave_im * o0_im
    exit_im = wave_re * o0_im + wave_im * o0_re
    mid_re, mid_im = propagate(exit_re, exit_im, tabs, False)
    exit_re = mid_re * o1_re - mid_im * o1_im
    exit_im = mid_re * o1_im + mid_im * o1_re
    far_re, far_im = to_far(exit_re, exit_im, tabs, factors)
    excess = 2.0 * GRAD_WEIGHT * (far_re * far_re + far_im * far_im - target[...])
    back_re, back_im = from_far(excess * far_re, excess * far_im, tabs, factors)
    store(1, mid_re * back_re + mid_im * back_im)
    store(3, mid_re * back_im - mid_im * back_re)
    up_re = o1_re * back_re + o1_im * back_im
    up_im = o1_re * back_im - o1_im * back_re
    back_re, back_im = propagate(up_re, up_im, tabs, True)
    wave_re, wave_im = probe[0], probe[1]
    o0_re, o0_im = load(0), load(2)
    store(0, wave_re * back_re + wave_im * back_im)
    store(2, wave_re * back_im - wave_im * back_re)
    up_re = o0_re * back_re + o0_im * back_im
    up_im = o0_re * back_im - o0_im * back_re
    back_row, back_col = lax.rem(width - row_at, width), lax.rem(2 * width - col_at, width)
    for part, value in enumerate((up_re, up_im)):
        value = roll(value, back_row, back_col)
        for step in range(4):
            rows = value[step * band : (step + 1) * band]
            grad[4 * part + step, width : width + band] = rows[:, :lanes]
            grad[4 * part + step, width + band :] = rows[:, lanes:]
    for turn, out in zip(EIGHT, outs):
        out[...] = grad[jnp.bitwise_xor(flat, turn)]


def add_parts(where, slot_range, offs, parts, strip, rows, cols):
    half, col, core = where[0], where[1], where[2]
    mine = 2 * half + col
    row_ids = lax.broadcasted_iota(jnp.int32, (rows, cols), 0)
    col_ids = lax.broadcasted_iota(jnp.int32, (rows, cols), 1) + core * cols
    sums = [jnp.zeros((rows, cols), jnp.float32)] * 2
    for turn, part in zip(EIGHT, parts):
        flat = jnp.bitwise_xor(2 * mine + core, turn)
        slot = slot_of(flat // 4, (flat // 2) % 2, flat % 2)
        lower, row_at, col_at = slot_place(offs, mine, slot_range[0, 1 - half], slot)
        first = jnp.where(strip == lower, row_at, jnp.where(strip == lower + 1, 0, rows))
        last = jnp.where(strip == lower, rows, jnp.where(strip == lower + 1, row_at, 0))
        value = jnp.where((row_ids >= first) & (row_ids < last), part[:rows], 0.0)
        left = jnp.where(col_ids >= col_at, value, 0.0)
        sums = [sums[0] + left, sums[1] + (value - left)]
    return sums


def add_below_kernel(where, slot_range, offs, *refs):
    parts, (below0, below1, probe_band) = refs[:8], refs[8:]
    rows, cols = below0.shape
    sums = add_parts(where, slot_range, offs, parts, 2, rows, cols)
    below0[...] = jnp.where(where[1] == 0, sums[0], sums[1])
    below1[...] = jnp.where(where[1] == 0, sums[1], sums[0])
    total = parts[0][rows:]
    for part in parts[1:]:
        total = total + part[rows:]
    band = probe_band.shape[0]
    probe_band[:, :cols] = total[:band]
    probe_band[:, cols:] = total[band:]


def add_own_kernel(where, slot_range, offs, *refs):
    parts, outs, own = refs[:8], refs[8:12], refs[12]
    rows, cols = own.shape[1:]
    for strip in range(2):
        own[2 * strip], own[2 * strip + 1] = add_parts(where, slot_range, offs, parts, strip, rows, cols)
    for turn, out in zip(FOUR, outs):
        out[...] = own[jnp.bitwise_xor(2 * where[0] + where[1], turn)]


def join_kernel(where, *refs):
    probe, out, probe_out, sums, sems = refs[8:]
    copies = fetch([(probe, probe_out)], sems)
    mine = 2 * where[0] + where[1]
    for at, turn in enumerate(FOUR):
        sums[turn] = refs[at][...] + refs[4 + at][...]
        copies += fetch([(sums.at[turn], out.at[jnp.bitwise_xor(mine, turn)])], sems.at[pl.ds(1 + turn, 1)])
    for copy in copies:
        copy.wait()


SMEM = pl.BlockSpec(memory_space=pltpu.SMEM)
VMEM = pl.BlockSpec(memory_space=pltpu.VMEM)
HBM = pl.BlockSpec(memory_space=pltpu.HBM)
ANY = pl.BlockSpec(memory_space=pl.ANY)


def call(kernel, outs, scalars, arrays, flops, scratch=(), copies=0):
    outs, arrays = ([x if isinstance(x, tuple) else (x, VMEM) for x in xs] for xs in (outs, arrays))
    moved = sum(math.prod(x.shape) * x.dtype.itemsize for x, unused in [*arrays, *outs])
    scratch = [pltpu.VMEM(dims, jnp.float32) if isinstance(dims, tuple) else dims for dims in scratch]
    return pl.pallas_call(
        kernel,
        out_shape=[x for x, unused in outs],
        in_specs=[SMEM] * len(scalars) + [spec for unused, spec in arrays],
        out_specs=[spec for unused, spec in outs],
        scratch_shapes=scratch + [pltpu.SemaphoreType.DMA((copies,))] * (copies > 0),
        compiler_params=pltpu.CompilerParams(vmem_limit_bytes=VMEM_LIMIT),
        cost_estimate=pl.CostEstimate(flops=flops, bytes_accessed=moved, transcendentals=0),
    )(*scalars, *(pltpu.with_memory_space_constraint(x, pltpu.HBM) if spec is HBM else x for x, spec in arrays))


def shape(*dims):
    return jax.ShapeDtypeStruct(dims, jnp.float32)


def deal(values, axes):
    count = len(values)
    order = EIGHT if count == 8 else FOUR
    return [
        lax.ppermute(value, axes, [(k, k ^ turn) for k in range(count)]) if turn else value
        for turn, value in zip(order, values)
    ]


def sum_over(value, axis, size, first):
    if size & (size - 1):
        return value if first else lax.psum(value, axis)
    step = 1 << first
    while step < size:
        value = value + lax.ppermute(value, axis, [(k, k ^ step) for k in range(size)])
        step *= 2
        if first == 0:
            break
    return value


def down_pairs(pairs, half, turn):
    places = [(pair, col) for pair in range(pairs - 1) for col in range(2)]
    return [(4 * pair + 2 * half + col, 4 * (pair + 1) + (col ^ turn)) for pair, col in places]


def local(object_field, probe, offsets, slot_range, measured):
    width = probe.shape[-1]
    planes, rows, cols = 4, object_field.shape[2], object_field.shape[3]
    band = width // 4
    pairs = lax.axis_size("pair")
    half, col, core = (lax.axis_index(name) for name in PLANE)
    where = jnp.stack([half, col, core])

    sibling = lax.ppermute(offsets, "core", [(0, 1), (1, 0)])
    offsets, slot_range = (pltpu.with_memory_space_constraint(x, pltpu.HBM) for x in (offsets, slot_range))
    block = object_field.reshape(planes, rows, cols)
    *dealt, given = call(
        deal_kernel,
        [shape(rows + 8, cols)] * 4 + [shape(width, width)],
        (where, offsets, sibling),
        ((block, HBM), (measured, HBM)),
        0,
        copies=5,
    )
    own = deal(dealt, PLANE[:2])
    (lowest,) = call(lowest_kernel, [shape(2, rows, cols)], (where,), own, 0)
    lowest, given = lax.optimization_barrier((lowest, given))
    below = lax.ppermute(lowest, "pair", [(k, k - 1) for k in range(1, pairs)])
    taken = lax.ppermute(given, "half", [(0, 1), (1, 0)])
    below, taken = lax.optimization_barrier((below, taken))

    parts = call(
        pick_kernel,
        [shape(rows, cols)] * 8,
        (where, slot_range),
        (*own, below),
        32 * rows * width,
        [(planes, rows + 8, cols), (8, rows, cols)],
    )
    offs = [own[FOUR.index(turn)][rows:, 0] for turn in range(4)]
    scalars = (where, slot_range, jnp.stack(offs).astype(jnp.int32))
    tabs, factors, order = (jnp.asarray(table) for table in tables(width))
    probe, target, tabs = call(
        ready_kernel,
        [shape(*probe.shape), shape(width, width), jax.ShapeDtypeStruct(tabs.shape, tabs.dtype)],
        scalars,
        (taken, (probe, HBM), (measured, HBM), (tabs, HBM), (order, HBM)),
        12 * width**3,
        [(width, width), pltpu.VMEM(order.shape, order.dtype)],
        copies=4,
    )
    grad = call(
        position_kernel,
        [shape(rows + 2 * band, cols)] * 8,
        scalars,
        (*deal(parts, PLANE), probe, target, tabs, factors),
        8 * 12 * width**3,
        [(8, rows, cols), (8, rows + 2 * band, cols)],
    )
    got = deal(grad, PLANE)
    *lower_sums, probe_band = call(
        add_below_kernel,
        [shape(rows, cols)] * 2 + [shape(band, width)],
        scalars,
        got,
        32 * rows * width,
    )
    probe_band = sum_over(probe_band, "pair", pairs, 0)
    sums = call(add_own_kernel, [shape(rows, cols)] * 4, scalars, got, 64 * rows * width, [(planes, rows, cols)])
    sums = deal(sums, PLANE[:2])
    above = []
    for turn in FOUR:
        above.append(lax.ppermute(lower_sums[turn % 2], ("pair", *PLANE[:2]), down_pairs(pairs, turn // 2, turn % 2)))
    probe_band = sum_over(probe_band, "pair", pairs, 1)
    probe_grad = lax.all_gather(probe_band, PLANE, axis=0, tiled=True)
    object_grad, probe_grad = call(
        join_kernel,
        [(shape(planes, rows, cols), HBM), (shape(*probe_grad.shape), HBM)],
        (where,),
        (*sums, *above, (probe_grad, ANY)),
        planes * rows * cols,
        [(planes, rows, cols)],
        copies=5,
    )
    return (object_grad.reshape(object_field.shape), probe_grad.reshape(probe.shape))


def solution(mesh):
    tile, grp = mesh.shape["tile"], mesh.shape["grp"]
    devices = mesh.devices.reshape(tile // 2, 2, 2, grp // 2)
    inner = Mesh(devices, ("pair", "half", "col", "core"))
    strip, cols = ("pair", "half"), ("col", "core")
    in_specs = (
        P(None, None, strip, cols),
        P(),
        P(strip, cols, None),
        P(strip, None),
        P(strip, cols, None, None),
    )
    out_specs = (P(None, None, strip, cols), P())
    return jax.shard_map(local, mesh=inner, in_specs=in_specs, out_specs=out_specs, check_vma=False)
```

```python
import functools
import math

import jax
import jax.numpy as jnp
import ml_dtypes
import numpy as np
from jax import lax
from jax.experimental import pallas as pl
from jax.experimental.pallas import tpu as pltpu
from jax.sharding import Mesh, PartitionSpec as P

GRAD_WEIGHT = 0.0625
PLANE = ("half", "col", "core")
EIGHT, FOUR = (4, 2, 5, 3, 6, 7, 1, 0), (2, 1, 3, 0)
VMEM_LIMIT = 24 * 1024 * 1024


def tables(width):
    half = width // 2
    index = np.arange(half, dtype=np.int64)
    scale = 1.0 / math.sqrt(width)
    far = np.exp(-2j * math.pi / half * (index[:, None] * index[None, :] % half)) * scale
    near = []
    for offset in (0, half):
        shift = index[:, None] - index[None, :] + offset
        near.append(np.exp(1j * (math.pi / width * (shift * shift % (2 * width)) - math.pi / 4.0)) * scale)
    products = []
    for matrix in ((near[0] + near[1]) / 2.0, (near[0] - near[1]) / 2.0, far):
        for imag in (matrix.imag, -matrix.imag):
            table = np.block([[matrix.real, imag], [-imag, matrix.real]])
            high = table.astype(ml_dtypes.bfloat16)
            low = (table - high.astype(np.float64)).astype(ml_dtypes.bfloat16)
            products.append(np.concatenate([high, low], axis=0))
    angle = -2.0 * math.pi / width * index
    twiddles = []
    for part in (np.cos(angle), np.sin(angle)):
        rows = np.broadcast_to(part[:, None], (half, half))
        twiddles.append(np.concatenate([rows, np.broadcast_to(part[None, :], (8, half))], axis=0))
    order = np.zeros((width, width))
    order[np.arange(width), np.concatenate([2 * index, 2 * index + 1])] = 1.0
    order = np.stack([order, order.T]).astype(ml_dtypes.bfloat16)
    return np.stack(products), np.stack(twiddles).astype(np.float32), order


def split(value):
    high = value.astype(jnp.bfloat16)
    low = (value - high.astype(jnp.float32)).astype(jnp.bfloat16)
    return high, low


def dot(left, right):
    return jnp.dot(left, right, preferred_element_type=jnp.float32)


PLUS, MINUS, FAR = 0, 2, 4


def times_right(re, im, table):
    width = table.shape[1]
    high, low = split(jnp.concatenate([re, im], axis=1))
    twice = dot(jnp.concatenate([high, low], axis=0), table[:width])
    count = re.shape[0]
    out = twice[:count] + (twice[count:] + dot(high, table[width:]))
    return out[:, : width // 2], out[:, width // 2 :]


def times_left(re, im, table):
    width = table.shape[1]
    high, low = split(jnp.concatenate([re, im], axis=0))
    twice = dot(table[...], high)
    out = twice[:width] + (twice[width:] + dot(table[:width], low))
    return out[: width // 2], out[width // 2 :]


def butterfly(first, second):
    return first + second, first - second


def halves(value, axis):
    half = value.shape[axis] // 2
    return (value[:half], value[half:]) if axis == 0 else (value[:, :half], value[:, half:])


def turn_by(re, im, cos, sin):
    return re * cos - im * sin, re * sin + im * cos


def propagate(re, im, tabs, conj):
    for axis in (1, 0):
        (plus_re, minus_re), (plus_im, minus_im) = (butterfly(*halves(x, axis)) for x in (re, im))
        times = times_right if axis else times_left
        pick = int(conj) if axis else 1 - int(conj)
        plus_re, plus_im = times(plus_re, plus_im, tabs.at[PLUS + pick])
        minus_re, minus_im = times(minus_re, minus_im, tabs.at[MINUS + pick])
        re = jnp.concatenate(butterfly(plus_re, minus_re), axis=axis)
        im = jnp.concatenate(butterfly(plus_im, minus_im), axis=axis)
    return re, im


def twiddle(factors, axis, width):
    half = factors.shape[2]
    if axis:
        return factors[0, half : half + 1], factors[1, half : half + 1]
    return tuple(jnp.concatenate([factors[k, :half]] * (width // half), axis=1) for k in range(2))


def to_far(re, im, tabs, factors):
    for axis in (1, 0):
        (even_re, odd_re), (even_im, odd_im) = (butterfly(*halves(x, axis)) for x in (re, im))
        odd_re, odd_im = turn_by(odd_re, odd_im, *twiddle(factors, axis, re.shape[1]))
        times, table = (times_right, tabs.at[FAR]) if axis else (times_left, tabs.at[FAR + 1])
        (even_re, even_im), (odd_re, odd_im) = times(even_re, even_im, table), times(odd_re, odd_im, table)
        re, im = jnp.concatenate([even_re, odd_re], axis=axis), jnp.concatenate([even_im, odd_im], axis=axis)
    return re, im


def from_far(re, im, tabs, factors):
    for axis in (0, 1):
        (even_re, odd_re), (even_im, odd_im) = halves(re, axis), halves(im, axis)
        times, table = (times_right, tabs.at[FAR + 1]) if axis else (times_left, tabs.at[FAR])
        (even_re, even_im), (odd_re, odd_im) = times(even_re, even_im, table), times(odd_re, odd_im, table)
        cos, sin = twiddle(factors, axis, re.shape[1])
        odd_re, odd_im = turn_by(odd_re, odd_im, cos, -sin)
        re = jnp.concatenate(butterfly(even_re, odd_re), axis=axis)
        im = jnp.concatenate(butterfly(even_im, odd_im), axis=axis)
    return re, im


def slot_of(half, col, core):
    return 2 * (2 * col + core) + half


def receivers():
    return [slot_of(half, col, core) for half in range(2) for col in range(2) for core in range(2)]


def slot_place(offs, mine, split_at, slot):
    lower = jnp.where(slot >= split_at, 1, 0)
    holder, at = jnp.bitwise_xor(2 * lower + slot // 4, mine), 2 * (slot % 4)
    return lower, offs[holder, at], offs[holder, at + 1]


def fetch(pairs, sems):
    copies = [pltpu.make_async_copy(source, into, sems.at[k]) for k, (source, into) in enumerate(pairs)]
    for copy in copies:
        copy.start()
    return copies


def deal_kernel(where, offsets, sibling, block, measured, *refs):
    outs, given, sems = refs[:4], refs[4], refs[5]
    mine, core = 2 * where[0] + where[1], where[2]
    rows, cols = block.shape[1:]
    pairs = [(block.at[jnp.bitwise_xor(mine, turn)], out.at[pl.ds(0, rows)]) for turn, out in zip(FOUR, outs)]
    copies = fetch([*pairs, (measured.at[0, 1 - where[0]], given)], sems)
    lines = []
    for holder in range(2):
        for slot in range(2):
            for axis in range(2):
                value = jnp.where(core == holder, offsets[0, slot, axis], sibling[0, slot, axis])
                lines.append(jnp.full((1, cols), value, jnp.int32))
    lines = jnp.concatenate(lines, axis=0).astype(jnp.float32)
    for out in outs:
        out[rows:] = lines
    for copy in copies:
        copy.wait()


def lowest_kernel(where, first, second, out):
    rows = out.shape[0]
    out[...] = jnp.where(where[0] == 0, first[:rows], second[:rows])


def pick_kernel(where, slot_range, *refs):
    gotten, below, outs, (own, parts) = dict(zip(FOUR, refs)), refs[4:7], refs[7:15], refs[15:]
    rows, cols = outs[0].shape
    half, col, core = where[0], where[1], where[2]
    mine = 2 * half + col
    for turn in range(4):
        own[jnp.bitwise_xor(mine, turn)] = gotten[turn][...]
    near = jnp.where(half == 0, below[0][:rows], below[1][:rows])
    below = [jnp.where(col == side, near, below[2][...]) for side in range(2)]
    split_at = slot_range[0, 1 - half]
    row_ids = lax.broadcasted_iota(jnp.int32, (rows, cols), 0).astype(jnp.float32)
    col_ids = (lax.broadcasted_iota(jnp.int32, (rows, cols), 1) + core * cols).astype(jnp.float32)
    for place, slot in enumerate(receivers()):
        lower = jnp.where(slot >= split_at, 1, 0)
        at = rows + 2 * (slot % 4)
        offs = own[2 * lower + slot // 4, at : at + 2]
        upper_rows = row_ids >= offs[0:1]
        left_cols = col_ids >= offs[1:2]

        def merged(side, lower=lower, upper_rows=upper_rows):
            second = own[2 + side, :rows]
            top = jnp.where(lower == 1, second, own[side, :rows])
            bottom = jnp.where(lower == 1, below[side], second)
            return jnp.where(upper_rows, top, bottom)

        parts[place] = jnp.where(left_cols, merged(0), merged(1))
    for turn, out in zip(EIGHT, outs):
        out[...] = parts[jnp.bitwise_xor(2 * mine + core, turn)]


def roll(value, rows, cols):
    return pltpu.roll(pltpu.roll(value, rows, 0), cols, 1)


def ready_kernel(where, slot_range, offs, taken, probe_from, measured, tabs_from, order_from, probe, target, tabs, kept, order, sems):
    half, col, core = where[0], where[1], where[2]
    probe_copy, kept_copy, order_copy, tabs_copy = fetch(
        [(probe_from, probe), (measured.at[0, half], kept), (order_from, order), (tabs_from, tabs)], sems
    )
    slot = slot_of(half, col, core)
    lower, row_at, col_at = slot_place(offs, 2 * half + col, slot_range[0, 1 - half], slot)
    probe_copy.wait()
    for part in range(2):
        probe[part] = roll(probe[part], row_at, col_at)
    kept_copy.wait()
    order_copy.wait()
    rest = jnp.where(lower == half, kept[...], taken[...])
    total = jnp.zeros_like(rest)
    for unused in range(3):
        part = rest.astype(jnp.bfloat16)
        rest = rest - part.astype(jnp.float32)
        total += dot(order[0], dot(part, order[1]).astype(jnp.bfloat16))
    target[...] = total
    tabs_copy.wait()


def position_kernel(where, slot_range, offs, *refs):
    gotten, (probe, target, tabs, factors) = dict(zip(EIGHT, refs)), refs[8:12]
    outs, patch, grad = refs[12:20], refs[20], refs[21]
    half, col, core = where[0], where[1], where[2]
    mine = 2 * half + col
    flat = 2 * mine + core
    unused, row_at, col_at = slot_place(offs, mine, slot_range[0, 1 - half], slot_of(half, col, core))
    width = probe.shape[-1]
    lanes, band = width // 2, width // 4
    for turn in range(8):
        patch[jnp.bitwise_xor(flat, turn)] = gotten[turn][...]

    def load(plane):
        return jnp.concatenate([patch[2 * plane], patch[2 * plane + 1]], axis=1)

    def store(plane, value):
        grad[2 * plane, :width] = value[:, :lanes]
        grad[2 * plane + 1, :width] = value[:, lanes:]

    wave_re, wave_im = probe[0], probe[1]
    o0_re, o0_im, o1_re, o1_im = load(0), load(2), load(1), load(3)
    exit_re = wave_re * o0_re - wave_im * o0_im
    exit_im = wave_re * o0_im + wave_im * o0_re
    mid_re, mid_im = propagate(exit_re, exit_im, tabs, False)
    exit_re = mid_re * o1_re - mid_im * o1_im
    exit_im = mid_re * o1_im + mid_im * o1_re
    far_re, far_im = to_far(exit_re, exit_im, tabs, factors)
    excess = 2.0 * GRAD_WEIGHT * (far_re * far_re + far_im * far_im - target[...])
    back_re, back_im = from_far(excess * far_re, excess * far_im, tabs, factors)
    store(1, mid_re * back_re + mid_im * back_im)
    store(3, mid_re * back_im - mid_im * back_re)
    up_re = o1_re * back_re + o1_im * back_im
    up_im = o1_re * back_im - o1_im * back_re
    back_re, back_im = propagate(up_re, up_im, tabs, True)
    wave_re, wave_im = probe[0], probe[1]
    o0_re, o0_im = load(0), load(2)
    store(0, wave_re * back_re + wave_im * back_im)
    store(2, wave_re * back_im - wave_im * back_re)
    up_re = o0_re * back_re + o0_im * back_im
    up_im = o0_re * back_im - o0_im * back_re
    back_row, back_col = lax.rem(width - row_at, width), lax.rem(2 * width - col_at, width)
    for part, value in enumerate((up_re, up_im)):
        value = roll(value, back_row, back_col)
        for step in range(4):
            rows = value[step * band : (step + 1) * band]
            grad[4 * part + step, width : width + band] = rows[:, :lanes]
            grad[4 * part + step, width + band :] = rows[:, lanes:]
    for turn, out in zip(EIGHT, outs):
        out[...] = grad[jnp.bitwise_xor(flat, turn)]


def add_parts(where, slot_range, offs, parts, strip, rows, cols):
    half, col, core = where[0], where[1], where[2]
    mine = 2 * half + col
    row_ids = lax.broadcasted_iota(jnp.int32, (rows, cols), 0)
    col_ids = lax.broadcasted_iota(jnp.int32, (rows, cols), 1) + core * cols
    sums = [jnp.zeros((rows, cols), jnp.float32)] * 2
    for turn, part in zip(EIGHT, parts):
        flat = jnp.bitwise_xor(2 * mine + core, turn)
        slot = slot_of(flat // 4, (flat // 2) % 2, flat % 2)
        lower, row_at, col_at = slot_place(offs, mine, slot_range[0, 1 - half], slot)
        first = jnp.where(strip == lower, row_at, jnp.where(strip == lower + 1, 0, rows))
        last = jnp.where(strip == lower, rows, jnp.where(strip == lower + 1, row_at, 0))
        value = jnp.where((row_ids >= first) & (row_ids < last), part[:rows], 0.0)
        left = jnp.where(col_ids >= col_at, value, 0.0)
        sums = [sums[0] + left, sums[1] + (value - left)]
    return sums


def add_below_kernel(where, slot_range, offs, *refs):
    parts, out = refs[:8], refs[8]
    cols = out.shape[1]
    rows = 2 * cols
    sums = add_parts(where, slot_range, offs, parts, 2, rows, cols)
    out[:rows] = jnp.where(where[1] == 0, sums[0], sums[1])
    out[rows : 2 * rows] = jnp.where(where[1] == 0, sums[1], sums[0])
    total = parts[0][rows:]
    for part in parts[1:]:
        total = total + part[rows:]
    out[2 * rows :] = total


def add_own_kernel(where, slot_range, offs, *refs):
    parts, own = refs[:8], refs[8]
    rows, cols = own.shape[1:]
    for strip in range(2):
        own[2 * strip], own[2 * strip + 1] = add_parts(where, slot_range, offs, parts, strip, rows, cols)


def top_kernel(where, own, below, above, *refs):
    outs, both = refs[:4], refs[4]
    mine = 2 * where[0] + where[1]
    rows = outs[0].shape[0]
    for turn, out in zip(FOUR, outs):
        start = rows * (turn % 2)
        extra = jnp.where((where[0] == turn // 2) & (where[3] > 0), above[start : start + rows], 0.0)
        out[...] = own[jnp.bitwise_xor(mine, turn)] + extra
    both[0] = below[2 * rows :]
    both[1] = above[2 * rows :]


def band_kernel(where, *refs):
    parts, out, inside = refs[:-2], refs[-2], refs[-1]
    count = inside.shape[0]
    for number in range(count):
        part = parts[number // parts[0].shape[0]][number % parts[0].shape[0]]
        inside[lax.rem(where[3] + count - number, count)] = part
    total = inside[0]
    for number in range(1, count):
        total = total + inside[number]
    band, cols = out.shape[0], total.shape[1]
    out[:, :cols] = total[:band]
    out[:, cols:] = total[band:]


def join_kernel(where, *refs):
    probe, out, probe_out, sems = refs[4:]
    mine = 2 * where[0] + where[1]
    pairs = [(ref, out.at[jnp.bitwise_xor(mine, turn)]) for turn, ref in zip(FOUR, refs)]
    for copy in fetch([(probe, probe_out), *pairs], sems):
        copy.wait()


SMEM = pl.BlockSpec(memory_space=pltpu.SMEM)
VMEM = pl.BlockSpec(memory_space=pltpu.VMEM)
HBM = pl.BlockSpec(memory_space=pltpu.HBM)
ANY = pl.BlockSpec(memory_space=pl.ANY)


def call(kernel, outs, scalars, arrays, flops, scratch=(), copies=0):
    outs, arrays = ([x if isinstance(x, tuple) else (x, VMEM) for x in xs] for xs in (outs, arrays))
    moved = sum(math.prod(x.shape) * x.dtype.itemsize for x, unused in [*arrays, *outs])
    scratch = [pltpu.VMEM(dims, jnp.float32) if isinstance(dims, tuple) else dims for dims in scratch]
    return pl.pallas_call(
        kernel,
        out_shape=[x for x, unused in outs],
        in_specs=[SMEM] * len(scalars) + [spec for unused, spec in arrays],
        out_specs=[spec for unused, spec in outs],
        scratch_shapes=scratch + [pltpu.SemaphoreType.DMA((copies,))] * (copies > 0),
        compiler_params=pltpu.CompilerParams(vmem_limit_bytes=VMEM_LIMIT),
        cost_estimate=pl.CostEstimate(flops=flops, bytes_accessed=moved, transcendentals=0),
    )(*scalars, *(pltpu.with_memory_space_constraint(x, pltpu.HBM) if spec is HBM else x for x, spec in arrays))


def shape(*dims):
    return jax.ShapeDtypeStruct(dims, jnp.float32)


def deal(values, axes):
    count = len(values)
    order = EIGHT if count == 8 else FOUR
    return [
        lax.ppermute(value, axes, [(k, k ^ turn) for k in range(count)]) if turn else value
        for turn, value in zip(order, values)
    ]


def local(object_field, probe, offsets, slot_range, measured):
    width = probe.shape[-1]
    planes, rows, cols = 4, object_field.shape[2], object_field.shape[3]
    band = width // 4
    pairs = lax.axis_size("pair")
    half, col, core = (lax.axis_index(name) for name in PLANE)
    where = jnp.stack([half, col, core, lax.axis_index("pair")])

    sibling = lax.ppermute(offsets, "core", [(0, 1), (1, 0)])
    offsets, slot_range = (pltpu.with_memory_space_constraint(x, pltpu.HBM) for x in (offsets, slot_range))
    block = object_field.reshape(planes, rows, cols)
    *dealt, given = call(
        deal_kernel,
        [shape(rows + 8, cols)] * 4 + [shape(width, width)],
        (where, offsets, sibling),
        ((block, HBM), (measured, HBM)),
        0,
        copies=5,
    )
    dealt = dict(zip(FOUR, dealt))
    below = []
    for to_half in range(2):
        moves = [(2 * (pair + 1), 2 * pair + to_half) for pair in range(pairs - 1)]
        below.append(lax.ppermute(dealt[2 * to_half], ("pair", "half"), moves))
    own = deal([dealt[turn] for turn in FOUR], PLANE[:2])
    below[0], below[1], *own = lax.optimization_barrier((*below, *own))
    turned = dict(zip(FOUR, own))
    (lowest,) = call(lowest_kernel, [shape(rows, cols)], (where,), (turned[1], turned[3]), 0)
    lowest, given = lax.optimization_barrier((lowest, given))
    below.append(lax.ppermute(lowest, "pair", [(k, k - 1) for k in range(1, pairs)]))
    taken = lax.ppermute(given, "half", [(0, 1), (1, 0)])
    below[2], taken = lax.optimization_barrier((below[2], taken))

    parts = call(
        pick_kernel,
        [shape(rows, cols)] * 8,
        (where, slot_range),
        (*own, *below),
        32 * rows * width,
        [(planes, rows + 8, cols), (8, rows, cols)],
    )
    offs = [own[FOUR.index(turn)][rows:, 0] for turn in range(4)]
    scalars = (where, slot_range, jnp.stack(offs).astype(jnp.int32))
    tabs, factors, order = (jnp.asarray(table) for table in tables(width))
    probe, target, tabs = call(
        ready_kernel,
        [shape(*probe.shape), shape(width, width), jax.ShapeDtypeStruct(tabs.shape, tabs.dtype)],
        scalars,
        (taken, (probe, HBM), (measured, HBM), (tabs, HBM), (order, HBM)),
        12 * width**3,
        [(width, width), pltpu.VMEM(order.shape, order.dtype)],
        copies=4,
    )
    grad = call(
        position_kernel,
        [shape(rows + 2 * band, cols)] * 8,
        scalars,
        (*deal(parts, PLANE), probe, target, tabs, factors),
        8 * 12 * width**3,
        [(8, rows, cols), (8, rows + 2 * band, cols)],
    )
    got = deal(grad, PLANE)
    (lower_sums,) = call(add_below_kernel, [shape(2 * rows + 2 * band, cols)], scalars, got, 32 * rows * width)
    above = lax.ppermute(lower_sums, "pair", [(k, (k + 1) % pairs) for k in range(pairs)])
    (sums,) = call(add_own_kernel, [shape(planes, rows, cols)], scalars, got, 64 * rows * width)
    *sums, both = call(
        top_kernel,
        [shape(rows, cols)] * 4 + [shape(2, 2 * band, cols)],
        (where,),
        (sums, lower_sums, above),
        planes * rows * cols,
    )
    sums = deal(sums, PLANE[:2])
    if pairs & (pairs - 1) or pairs == 1:
        bands = [lax.all_gather(both[0], "pair")]
        bands = [bands[0][(lax.axis_index("pair") - jnp.arange(pairs)) % pairs]]
    else:
        bands, step = [both], 2
        while step < pairs:
            near = jnp.concatenate(bands) if len(bands) > 1 else bands[0]
            bands = [near, lax.ppermute(near, "pair", [(k, (k + step) % pairs) for k in range(pairs)])]
            step *= 2
    (probe_band,) = call(
        band_kernel, [shape(band, width)], (where,), bands, pairs * band * width, [(pairs, 2 * band, cols)]
    )
    probe_grad = lax.all_gather(probe_band, PLANE, axis=0, tiled=True)
    object_grad, probe_grad = call(
        join_kernel,
        [(shape(planes, rows, cols), HBM), (shape(*probe_grad.shape), HBM)],
        (where,),
        [(x, ANY) for x in (*sums, probe_grad)],
        0,
        copies=5,
    )
    return (object_grad.reshape(object_field.shape), probe_grad.reshape(probe.shape))


def solution(mesh):
    tile, grp = mesh.shape["tile"], mesh.shape["grp"]
    devices = mesh.devices.reshape(tile // 2, 2, 2, grp // 2)
    inner = Mesh(devices, ("pair", "half", "col", "core"))
    strip, cols = ("pair", "half"), ("col", "core")
    in_specs = (
        P(None, None, strip, cols),
        P(),
        P(strip, cols, None),
        P(strip, None),
        P(strip, cols, None, None),
    )
    out_specs = (P(None, None, strip, cols), P())
    return jax.shard_map(local, mesh=inner, in_specs=in_specs, out_specs=out_specs, check_vma=False)
```

```python
import functools
import math

import jax
import jax.numpy as jnp
import ml_dtypes
import numpy as np
from jax import lax
from jax.experimental import pallas as pl
from jax.experimental.pallas import tpu as pltpu
from jax.sharding import Mesh, PartitionSpec as P

GRAD_WEIGHT = 0.0625
PLANE = ("half", "col", "core")
EIGHT, BACK, FOUR = (4, 2, 5, 3, 6, 7, 1, 0), (1, 4, 2, 5, 3, 6, 7, 0), (2, 1, 3, 0)
VMEM_LIMIT = 24 * 1024 * 1024


def tables(width):
    half = width // 2
    index = np.arange(half, dtype=np.int64)
    scale = 1.0 / math.sqrt(width)
    far = np.exp(-2j * math.pi / half * (index[:, None] * index[None, :] % half)) * scale
    near = []
    for offset in (0, half):
        shift = index[:, None] - index[None, :] + offset
        near.append(np.exp(1j * (math.pi / width * (shift * shift % (2 * width)) - math.pi / 4.0)) * scale)
    products = []
    for matrix in ((near[0] + near[1]) / 2.0, (near[0] - near[1]) / 2.0, far):
        for imag in (matrix.imag, -matrix.imag):
            table = np.block([[matrix.real, imag], [-imag, matrix.real]])
            high = table.astype(ml_dtypes.bfloat16)
            low = (table - high.astype(np.float64)).astype(ml_dtypes.bfloat16)
            products.append(np.concatenate([high, low], axis=0))
    angle = -2.0 * math.pi / width * index
    twiddles = []
    for part in (np.cos(angle), np.sin(angle)):
        rows = np.broadcast_to(part[:, None], (half, half))
        twiddles.append(np.concatenate([rows, np.broadcast_to(part[None, :], (8, half))], axis=0))
    order = np.zeros((width, width))
    order[np.arange(width), np.concatenate([2 * index, 2 * index + 1])] = 1.0
    order = np.stack([order, order.T]).astype(ml_dtypes.bfloat16)
    return np.stack(products), np.stack(twiddles).astype(np.float32), order


def split(value):
    high = value.astype(jnp.bfloat16)
    low = (value - high.astype(jnp.float32)).astype(jnp.bfloat16)
    return high, low


def dot(left, right):
    return jnp.dot(left, right, preferred_element_type=jnp.float32)


PLUS, MINUS, FAR = 0, 2, 4


def times_right(re, im, table):
    width = table.shape[1]
    high, low = split(jnp.concatenate([re, im], axis=1))
    twice = dot(jnp.concatenate([high, low], axis=0), table[:width])
    count = re.shape[0]
    out = twice[:count] + (twice[count:] + dot(high, table[width:]))
    return out[:, : width // 2], out[:, width // 2 :]


def times_left(re, im, table):
    width = table.shape[1]
    high, low = split(jnp.concatenate([re, im], axis=0))
    twice = dot(table[...], high)
    out = twice[:width] + (twice[width:] + dot(table[:width], low))
    return out[: width // 2], out[width // 2 :]


def butterfly(first, second):
    return first + second, first - second


def halves(value, axis):
    half = value.shape[axis] // 2
    return (value[:half], value[half:]) if axis == 0 else (value[:, :half], value[:, half:])


def turn_by(re, im, cos, sin):
    return re * cos - im * sin, re * sin + im * cos


def propagate(re, im, tabs, conj):
    for axis in (1, 0):
        (plus_re, minus_re), (plus_im, minus_im) = (butterfly(*halves(x, axis)) for x in (re, im))
        times = times_right if axis else times_left
        pick = int(conj) if axis else 1 - int(conj)
        plus_re, plus_im = times(plus_re, plus_im, tabs.at[PLUS + pick])
        minus_re, minus_im = times(minus_re, minus_im, tabs.at[MINUS + pick])
        re = jnp.concatenate(butterfly(plus_re, minus_re), axis=axis)
        im = jnp.concatenate(butterfly(plus_im, minus_im), axis=axis)
    return re, im


def twiddle(factors, axis, width):
    half = factors.shape[2]
    if axis:
        return factors[0, half : half + 1], factors[1, half : half + 1]
    return tuple(jnp.concatenate([factors[k, :half]] * (width // half), axis=1) for k in range(2))


def to_far(re, im, tabs, factors):
    for axis in (1, 0):
        (even_re, odd_re), (even_im, odd_im) = (butterfly(*halves(x, axis)) for x in (re, im))
        odd_re, odd_im = turn_by(odd_re, odd_im, *twiddle(factors, axis, re.shape[1]))
        times, table = (times_right, tabs.at[FAR]) if axis else (times_left, tabs.at[FAR + 1])
        (even_re, even_im), (odd_re, odd_im) = times(even_re, even_im, table), times(odd_re, odd_im, table)
        re, im = jnp.concatenate([even_re, odd_re], axis=axis), jnp.concatenate([even_im, odd_im], axis=axis)
    return re, im


def from_far(re, im, tabs, factors):
    for axis in (0, 1):
        (even_re, odd_re), (even_im, odd_im) = halves(re, axis), halves(im, axis)
        times, table = (times_right, tabs.at[FAR + 1]) if axis else (times_left, tabs.at[FAR])
        (even_re, even_im), (odd_re, odd_im) = times(even_re, even_im, table), times(odd_re, odd_im, table)
        cos, sin = twiddle(factors, axis, re.shape[1])
        odd_re, odd_im = turn_by(odd_re, odd_im, cos, -sin)
        re = jnp.concatenate(butterfly(even_re, odd_re), axis=axis)
        im = jnp.concatenate(butterfly(even_im, odd_im), axis=axis)
    return re, im


def slot_of(half, col, core):
    return 2 * (2 * col + core) + half


def receivers():
    return [slot_of(half, col, core) for half in range(2) for col in range(2) for core in range(2)]


def slot_place(offs, mine, split_at, slot):
    lower = jnp.where(slot >= split_at, 1, 0)
    holder, at = jnp.bitwise_xor(2 * lower + slot // 4, mine), 2 * (slot % 4)
    return lower, offs[holder, at], offs[holder, at + 1]


def fetch(pairs, sems):
    copies = [pltpu.make_async_copy(source, into, sems.at[k]) for k, (source, into) in enumerate(pairs)]
    for copy in copies:
        copy.start()
    return copies


def deal_kernel(where, offsets, block, measured, *refs):
    outs, given, sems = refs[:4], refs[4], refs[5]
    mine = 2 * where[0] + where[1]
    rows, cols = block.shape[1:]
    pairs = [(block.at[jnp.bitwise_xor(mine, turn)], out.at[pl.ds(0, rows)]) for turn, out in zip(FOUR, outs)]
    copies = fetch([*pairs, (measured.at[0, 1 - where[0]], given)], sems)
    lines = [jnp.full((1, cols), offsets[0, slot, axis], jnp.int32) for slot in range(2) for axis in range(2)]
    lines = jnp.concatenate(lines * 2, axis=0).astype(jnp.float32)
    for out in outs:
        out[rows:] = lines
    for copy in copies:
        copy.wait()


def lowest_kernel(where, *refs):
    gotten, out = dict(zip(FOUR, refs)), refs[4]
    rows = out.shape[1]
    for turn in range(2):
        out[turn] = jnp.where(where[0] == 0, gotten[turn][:rows], gotten[2 + turn][:rows])


def pick_kernel(where, slot_range, offs, *refs):
    gotten, below, outs, (own, parts) = dict(zip(FOUR, refs)), refs[4], refs[5:13], refs[13:]
    rows, cols = outs[0].shape
    half, col, core = where[0], where[1], where[2]
    mine = 2 * half + col
    for turn in range(4):
        own[jnp.bitwise_xor(mine, turn)] = gotten[turn][:rows]
    split_at = slot_range[0, 1 - half]
    row_ids = lax.broadcasted_iota(jnp.int32, (rows, cols), 0)
    col_ids = lax.broadcasted_iota(jnp.int32, (rows, cols), 1) + core * cols
    for place, slot in enumerate(receivers()):
        lower, row_at, col_at = slot_place(offs, mine, split_at, slot)
        upper_rows = row_ids >= row_at
        left_cols = col_ids >= col_at

        def merged(side, lower=lower, upper_rows=upper_rows):
            second = own[2 + side]
            top = jnp.where(lower == 1, second, own[side])
            bottom = jnp.where(lower == 1, below[jnp.bitwise_xor(col, side)], second)
            return jnp.where(upper_rows, top, bottom)

        parts[place] = jnp.where(left_cols, merged(0), merged(1))
    for turn, out in zip(EIGHT, outs):
        out[...] = parts[jnp.bitwise_xor(2 * mine + core, turn)]


def roll(value, rows, cols):
    return pltpu.roll(pltpu.roll(value, rows, 0), cols, 1)


def ready_kernel(where, slot_range, offs, taken, probe_from, measured, tabs_from, order_from, probe, target, tabs, kept, order, sems):
    half, col, core = where[0], where[1], where[2]
    probe_copy, kept_copy, order_copy, tabs_copy = fetch(
        [(probe_from, probe), (measured.at[0, half], kept), (order_from, order), (tabs_from, tabs)], sems
    )
    slot = slot_of(half, col, core)
    lower, row_at, col_at = slot_place(offs, 2 * half + col, slot_range[0, 1 - half], slot)
    probe_copy.wait()
    for part in range(2):
        probe[part] = roll(probe[part], row_at, col_at)
    kept_copy.wait()
    order_copy.wait()
    rest = jnp.where(lower == half, kept[...], taken[...])
    total = jnp.zeros_like(rest)
    for unused in range(3):
        part = rest.astype(jnp.bfloat16)
        rest = rest - part.astype(jnp.float32)
        total += dot(order[0], dot(part, order[1]).astype(jnp.bfloat16))
    target[...] = total
    tabs_copy.wait()


def position_kernel(where, slot_range, offs, *refs):
    gotten, (probe, target, tabs, factors) = dict(zip(EIGHT, refs)), refs[8:12]
    outs, keep, (patch, grad, bands) = refs[12:20], refs[20], refs[21:]
    half, col, core = where[0], where[1], where[2]
    mine = 2 * half + col
    flat = 2 * mine + core
    unused, row_at, col_at = slot_place(offs, mine, slot_range[0, 1 - half], slot_of(half, col, core))
    width = probe.shape[-1]
    lanes, band = width // 2, width // 4
    for turn in range(8):
        patch[jnp.bitwise_xor(flat, turn)] = gotten[turn][...]

    def load(plane):
        return jnp.concatenate([patch[2 * plane], patch[2 * plane + 1]], axis=1)

    def store(plane, value):
        grad[2 * plane] = value[:, :lanes]
        grad[2 * plane + 1] = value[:, lanes:]

    wave_re, wave_im = probe[0], probe[1]
    o0_re, o0_im, o1_re, o1_im = load(0), load(2), load(1), load(3)
    exit_re = wave_re * o0_re - wave_im * o0_im
    exit_im = wave_re * o0_im + wave_im * o0_re
    mid_re, mid_im = propagate(exit_re, exit_im, tabs, False)
    exit_re = mid_re * o1_re - mid_im * o1_im
    exit_im = mid_re * o1_im + mid_im * o1_re
    far_re, far_im = to_far(exit_re, exit_im, tabs, factors)
    excess = 2.0 * GRAD_WEIGHT * (far_re * far_re + far_im * far_im - target[...])
    back_re, back_im = from_far(excess * far_re, excess * far_im, tabs, factors)
    store(1, mid_re * back_re + mid_im * back_im)
    store(3, mid_re * back_im - mid_im * back_re)
    up_re = o1_re * back_re + o1_im * back_im
    up_im = o1_re * back_im - o1_im * back_re
    back_re, back_im = propagate(up_re, up_im, tabs, True)
    wave_re, wave_im = probe[0], probe[1]
    o0_re, o0_im = load(0), load(2)
    store(0, wave_re * back_re + wave_im * back_im)
    store(2, wave_re * back_im - wave_im * back_re)
    up_re = o0_re * back_re + o0_im * back_im
    up_im = o0_re * back_im - o0_im * back_re
    back_row, back_col = lax.rem(width - row_at, width), lax.rem(2 * width - col_at, width)
    for part, value in enumerate((up_re, up_im)):
        value = roll(value, back_row, back_col)
        for step in range(4):
            rows = value[step * band : (step + 1) * band]
            bands[4 * part + step, :band] = rows[:, :lanes]
            bands[4 * part + step, band:] = rows[:, lanes:]
    for turn, out in zip(BACK, outs):
        out[:width] = grad[jnp.bitwise_xor(flat, turn)]
    for part in range(4):
        keep[part] = bands[2 * part + core]
        start = width + 2 * band * part
        outs[0][start : start + 2 * band] = bands[2 * part + 1 - core]


def pair_kernel(where, keep, got, *outs):
    band = keep.shape[1]
    first = got.shape[0] - 4 * band
    for turn, out in zip(FOUR, outs):
        part = jnp.bitwise_xor(2 * where[0] + where[1], turn)
        out[...] = keep[part] + got[pl.ds(pl.multiple_of(first + band * part, band), band)]


def add_parts(where, slot_range, offs, parts, strip, rows, cols):
    half, col, core = where[0], where[1], where[2]
    mine = 2 * half + col
    row_ids = lax.broadcasted_iota(jnp.int32, (rows, cols), 0)
    col_ids = lax.broadcasted_iota(jnp.int32, (rows, cols), 1) + core * cols
    sums = [jnp.zeros((rows, cols), jnp.float32)] * 2
    for turn, part in zip(BACK, parts):
        flat = jnp.bitwise_xor(2 * mine + core, turn)
        slot = slot_of(flat // 4, (flat // 2) % 2, flat % 2)
        lower, row_at, col_at = slot_place(offs, mine, slot_range[0, 1 - half], slot)
        first = jnp.where(strip == lower, row_at, jnp.where(strip == lower + 1, 0, rows))
        last = jnp.where(strip == lower, rows, jnp.where(strip == lower + 1, row_at, 0))
        value = jnp.where((row_ids >= first) & (row_ids < last), part[:rows], 0.0)
        left = jnp.where(col_ids >= col_at, value, 0.0)
        sums = [sums[0] + left, sums[1] + (value - left)]
    return sums


def add_below_kernel(where, slot_range, offs, *refs):
    parts, quarters, (below, probe_band) = refs[:8], refs[8:12], refs[12:]
    rows, cols = below.shape[1:]
    sums = add_parts(where, slot_range, offs, parts, 2, rows, cols)
    for side in range(2):
        below[jnp.bitwise_xor(where[1], side)] = sums[side]
    total = (quarters[0][...] + quarters[1][...]) + (quarters[2][...] + quarters[3][...])
    band = probe_band.shape[0]
    probe_band[:, :cols] = total[:band]
    probe_band[:, cols:] = total[band:]


def add_own_kernel(where, slot_range, offs, *refs):
    parts, own = refs[:8], refs[8]
    rows, cols = own.shape[1:]
    for strip in range(2):
        own[2 * strip], own[2 * strip + 1] = add_parts(where, slot_range, offs, parts, strip, rows, cols)


def top_kernel(where, own, above, *outs):
    mine = 2 * where[0] + where[1]
    for turn, out in zip(FOUR, outs):
        extra = jnp.where(where[0] == turn // 2, above[turn % 2], 0.0)
        out[...] = own[jnp.bitwise_xor(mine, turn)] + extra


def join_kernel(where, *refs):
    probe, out, probe_out, sems = refs[4:]
    mine = 2 * where[0] + where[1]
    pairs = [(ref, out.at[jnp.bitwise_xor(mine, turn)]) for turn, ref in zip(FOUR, refs)]
    for copy in fetch([(probe, probe_out), *pairs], sems):
        copy.wait()


SMEM = pl.BlockSpec(memory_space=pltpu.SMEM)
VMEM = pl.BlockSpec(memory_space=pltpu.VMEM)
HBM = pl.BlockSpec(memory_space=pltpu.HBM)
ANY = pl.BlockSpec(memory_space=pl.ANY)


def call(kernel, outs, scalars, arrays, flops, scratch=(), copies=0):
    outs, arrays = ([x if isinstance(x, tuple) else (x, VMEM) for x in xs] for xs in (outs, arrays))
    moved = sum(math.prod(x.shape) * x.dtype.itemsize for x, unused in [*arrays, *outs])
    scratch = [pltpu.VMEM(dims, jnp.float32) if isinstance(dims, tuple) else dims for dims in scratch]
    return pl.pallas_call(
        kernel,
        out_shape=[x for x, unused in outs],
        in_specs=[SMEM] * len(scalars) + [spec for unused, spec in arrays],
        out_specs=[spec for unused, spec in outs],
        scratch_shapes=scratch + [pltpu.SemaphoreType.DMA((copies,))] * (copies > 0),
        compiler_params=pltpu.CompilerParams(vmem_limit_bytes=VMEM_LIMIT),
        cost_estimate=pl.CostEstimate(flops=flops, bytes_accessed=moved, transcendentals=0),
    )(*scalars, *(pltpu.with_memory_space_constraint(x, pltpu.HBM) if spec is HBM else x for x, spec in arrays))


def shape(*dims):
    return jax.ShapeDtypeStruct(dims, jnp.float32)


def deal(values, axes, order):
    return [
        lax.ppermute(value, axes, [(k, k ^ turn) for k in range(len(order))]) if turn else value
        for turn, value in zip(order, values)
    ]


def sum_over(value, axis, size, first):
    if size & (size - 1):
        return value if first else lax.psum(value, axis)
    step = 1 << first
    while step < size:
        value = value + lax.ppermute(value, axis, [(k, k ^ step) for k in range(size)])
        step *= 2
        if first == 0:
            break
    return value


def local(object_field, probe, offsets, slot_range, measured):
    width = probe.shape[-1]
    planes, rows, cols = 4, object_field.shape[2], object_field.shape[3]
    band = width // 4
    pairs = lax.axis_size("pair")
    half, col, core = (lax.axis_index(name) for name in PLANE)
    where = jnp.stack([half, col, core])

    offsets, slot_range = (pltpu.with_memory_space_constraint(x, pltpu.HBM) for x in (offsets, slot_range))
    block = object_field.reshape(planes, rows, cols)
    *dealt, given = call(
        deal_kernel,
        [shape(rows + 8, cols)] * 4 + [shape(width, width)],
        (where, offsets),
        ((block, HBM), (measured, HBM)),
        0,
        copies=5,
    )
    own = deal(dealt, PLANE[:2], FOUR)
    (lowest,) = call(lowest_kernel, [shape(2, rows, cols)], (where,), own, 0)
    lowest, given = lax.optimization_barrier((lowest, given))
    below = lax.ppermute(lowest, "pair", [(k, k - 1) for k in range(1, pairs)])
    taken = lax.ppermute(given, "half", [(0, 1), (1, 0)])
    below, taken = lax.optimization_barrier((below, taken))

    turned = dict(zip(FOUR, own))
    offs = jnp.stack([turned[turn][rows : rows + 4, 0] for turn in range(4)]).astype(jnp.int32)
    others = lax.ppermute(offs, "core", [(0, 1), (1, 0)])
    offs = jnp.concatenate([jnp.where(core == 0, offs, others), jnp.where(core == 0, others, offs)], axis=1)
    scalars = (where, slot_range, offs)
    parts = call(
        pick_kernel,
        [shape(rows, cols)] * 8,
        scalars,
        (*own, below),
        32 * rows * width,
        [(planes, rows, cols), (8, rows, cols)],
    )
    tabs, factors, order = (jnp.asarray(table) for table in tables(width))
    probe, target, tabs = call(
        ready_kernel,
        [shape(*probe.shape), shape(width, width), jax.ShapeDtypeStruct(tabs.shape, tabs.dtype)],
        scalars,
        (taken, (probe, HBM), (measured, HBM), (tabs, HBM), (order, HBM)),
        12 * width**3,
        [(width, width), pltpu.VMEM(order.shape, order.dtype)],
        copies=4,
    )
    *grad, keep = call(
        position_kernel,
        [shape(rows + 8 * band, cols)] + [shape(rows, cols)] * 7 + [shape(4, 2 * band, cols)],
        scalars,
        (*deal(parts, PLANE, EIGHT), probe, target, tabs, factors),
        8 * 12 * width**3,
        [(8, rows, cols)] * 2 + [(8, 2 * band, cols)],
    )
    got = deal(grad, PLANE, BACK)
    quarters = call(pair_kernel, [shape(2 * band, cols)] * 4, (where,), (keep, got[0]), 4 * band * width)
    lower_sums, probe_band = call(
        add_below_kernel,
        [shape(2, rows, cols), shape(band, width)],
        scalars,
        (*got, *deal(quarters, PLANE[:2], FOUR)),
        32 * rows * width,
    )
    probe_band = sum_over(probe_band, "pair", pairs, 0)
    (sums,) = call(add_own_kernel, [shape(planes, rows, cols)], scalars, got, 64 * rows * width)
    lower_sums, sums, probe_band = lax.optimization_barrier((lower_sums, sums, probe_band))
    above = lax.ppermute(lower_sums, "pair", [(k, k + 1) for k in range(pairs - 1)])
    sums = call(top_kernel, [shape(rows, cols)] * 4, (where,), (sums, above), planes * rows * cols)
    sums = deal(sums, PLANE[:2], FOUR)
    probe_band = sum_over(probe_band, "pair", pairs, 1)
    probe_grad = lax.all_gather(probe_band, PLANE, axis=0, tiled=True)
    object_grad, probe_grad = call(
        join_kernel,
        [(shape(planes, rows, cols), HBM), (shape(*probe_grad.shape), HBM)],
        (where,),
        [(x, ANY) for x in (*sums, probe_grad)],
        0,
        copies=5,
    )
    return (object_grad.reshape(object_field.shape), probe_grad.reshape(probe.shape))


def solution(mesh):
    tile, grp = mesh.shape["tile"], mesh.shape["grp"]
    devices = mesh.devices.reshape(tile // 2, 2, 2, grp // 2)
    inner = Mesh(devices, ("pair", "half", "col", "core"))
    strip, cols = ("pair", "half"), ("col", "core")
    in_specs = (
        P(None, None, strip, cols),
        P(),
        P(strip, cols, None),
        P(strip, None),
        P(strip, cols, None, None),
    )
    out_specs = (P(None, None, strip, cols), P())
    return jax.shard_map(local, mesh=inner, in_specs=in_specs, out_specs=out_specs, check_vma=False)
```

```python
import functools
import math

import jax
import jax.numpy as jnp
import ml_dtypes
import numpy as np
from jax import lax
from jax.experimental import pallas as pl
from jax.experimental.pallas import tpu as pltpu
from jax.sharding import Mesh, PartitionSpec as P

GRAD_WEIGHT = 0.0625
PLANE = ("half", "col", "core")
EIGHT, BACK, FOUR = (4, 2, 5, 3, 6, 7, 1, 0), (1, 4, 2, 5, 3, 6, 7, 0), (2, 1, 3, 0)
VMEM_LIMIT = 24 * 1024 * 1024


def tables(width):
    half = width // 2
    index = np.arange(half, dtype=np.int64)
    scale = 1.0 / math.sqrt(width)
    far = np.exp(-2j * math.pi / half * (index[:, None] * index[None, :] % half)) * scale
    near = []
    for offset in (0, half):
        shift = index[:, None] - index[None, :] + offset
        near.append(np.exp(1j * (math.pi / width * (shift * shift % (2 * width)) - math.pi / 4.0)) * scale)
    products = []
    for matrix in ((near[0] + near[1]) / 2.0, (near[0] - near[1]) / 2.0, far):
        for imag in (matrix.imag, -matrix.imag):
            table = np.block([[matrix.real, imag], [-imag, matrix.real]])
            high = table.astype(ml_dtypes.bfloat16)
            low = (table - high.astype(np.float64)).astype(ml_dtypes.bfloat16)
            products.append(np.concatenate([high, low], axis=0))
    angle = -2.0 * math.pi / width * index
    twiddles = []
    for part in (np.cos(angle), np.sin(angle)):
        rows = np.broadcast_to(part[:, None], (half, half))
        twiddles.append(np.concatenate([rows, np.broadcast_to(part[None, :], (8, half))], axis=0))
    order = np.zeros((width, width))
    order[np.arange(width), np.concatenate([2 * index, 2 * index + 1])] = 1.0
    order = np.stack([order, order.T]).astype(ml_dtypes.bfloat16)
    return np.stack(products), np.stack(twiddles).astype(np.float32), order


def split(value):
    high = value.astype(jnp.bfloat16)
    low = (value - high.astype(jnp.float32)).astype(jnp.bfloat16)
    return high, low


def dot(left, right):
    return jnp.dot(left, right, preferred_element_type=jnp.float32)


PLUS, MINUS, FAR = 0, 2, 4


def times_right(re, im, table):
    width = table.shape[1]
    high, low = split(jnp.concatenate([re, im], axis=1))
    twice = dot(jnp.concatenate([high, low], axis=0), table[:width])
    count = re.shape[0]
    out = twice[:count] + (twice[count:] + dot(high, table[width:]))
    return out[:, : width // 2], out[:, width // 2 :]


def times_left(re, im, table):
    width = table.shape[1]
    high, low = split(jnp.concatenate([re, im], axis=0))
    twice = dot(table[...], high)
    out = twice[:width] + (twice[width:] + dot(table[:width], low))
    return out[: width // 2], out[width // 2 :]


def butterfly(first, second):
    return first + second, first - second


def halves(value, axis):
    half = value.shape[axis] // 2
    return (value[:half], value[half:]) if axis == 0 else (value[:, :half], value[:, half:])


def turn_by(re, im, cos, sin):
    return re * cos - im * sin, re * sin + im * cos


def propagate(re, im, tabs, conj):
    for axis in (1, 0):
        (plus_re, minus_re), (plus_im, minus_im) = (butterfly(*halves(x, axis)) for x in (re, im))
        times = times_right if axis else times_left
        pick = int(conj) if axis else 1 - int(conj)
        plus_re, plus_im = times(plus_re, plus_im, tabs.at[PLUS + pick])
        minus_re, minus_im = times(minus_re, minus_im, tabs.at[MINUS + pick])
        re = jnp.concatenate(butterfly(plus_re, minus_re), axis=axis)
        im = jnp.concatenate(butterfly(plus_im, minus_im), axis=axis)
    return re, im


def twiddle(factors, axis, width):
    half = factors.shape[2]
    if axis:
        return factors[0, half : half + 1], factors[1, half : half + 1]
    return tuple(jnp.concatenate([factors[k, :half]] * (width // half), axis=1) for k in range(2))


def to_far(re, im, tabs, factors):
    for axis in (1, 0):
        (even_re, odd_re), (even_im, odd_im) = (butterfly(*halves(x, axis)) for x in (re, im))
        odd_re, odd_im = turn_by(odd_re, odd_im, *twiddle(factors, axis, re.shape[1]))
        times, table = (times_right, tabs.at[FAR]) if axis else (times_left, tabs.at[FAR + 1])
        (even_re, even_im), (odd_re, odd_im) = times(even_re, even_im, table), times(odd_re, odd_im, table)
        re, im = jnp.concatenate([even_re, odd_re], axis=axis), jnp.concatenate([even_im, odd_im], axis=axis)
    return re, im


def from_far(re, im, tabs, factors):
    for axis in (0, 1):
        (even_re, odd_re), (even_im, odd_im) = halves(re, axis), halves(im, axis)
        times, table = (times_right, tabs.at[FAR + 1]) if axis else (times_left, tabs.at[FAR])
        (even_re, even_im), (odd_re, odd_im) = times(even_re, even_im, table), times(odd_re, odd_im, table)
        cos, sin = twiddle(factors, axis, re.shape[1])
        odd_re, odd_im = turn_by(odd_re, odd_im, cos, -sin)
        re = jnp.concatenate(butterfly(even_re, odd_re), axis=axis)
        im = jnp.concatenate(butterfly(even_im, odd_im), axis=axis)
    return re, im


def slot_of(half, col, core):
    return 2 * (2 * col + core) + half


def receivers():
    return [slot_of(half, col, core) for half in range(2) for col in range(2) for core in range(2)]


def slot_place(offs, mine, split_at, slot):
    lower = jnp.where(slot >= split_at, 1, 0)
    holder, at = jnp.bitwise_xor(2 * lower + slot // 4, mine), 2 * (slot % 4)
    return lower, offs[holder, at], offs[holder, at + 1]


def fetch(pairs, sems):
    copies = [pltpu.make_async_copy(source, into, sems.at[k]) for k, (source, into) in enumerate(pairs)]
    for copy in copies:
        copy.start()
    return copies


def deal_kernel(where, offsets, block, measured, *refs):
    outs, given, sems = refs[:4], refs[4], refs[5]
    mine = 2 * where[0] + where[1]
    rows, cols = block.shape[1:]
    pairs = [(block.at[jnp.bitwise_xor(mine, turn)], out.at[pl.ds(0, rows)]) for turn, out in zip(FOUR, outs)]
    copies = fetch([*pairs, (measured.at[0, 1 - where[0]], given)], sems)
    lines = [jnp.full((1, cols), offsets[0, slot, axis], jnp.int32) for slot in range(2) for axis in range(2)]
    lines = jnp.concatenate(lines * 2, axis=0).astype(jnp.float32)
    for out in outs:
        out[rows:] = lines
    for copy in copies:
        copy.wait()


def lowest_kernel(where, *refs):
    gotten, out = dict(zip(FOUR, refs)), refs[4]
    rows = out.shape[1]
    for turn in range(2):
        out[turn] = jnp.where(where[0] == 0, gotten[turn][:rows], gotten[2 + turn][:rows])


def pick_kernel(where, slot_range, offs, *refs):
    gotten, below, outs, (own, parts) = dict(zip(FOUR, refs)), refs[4], refs[5:13], refs[13:]
    rows, cols = outs[0].shape
    half, col, core = where[0], where[1], where[2]
    mine = 2 * half + col
    for turn in range(4):
        own[jnp.bitwise_xor(mine, turn)] = gotten[turn][:rows]
    split_at = slot_range[0, 1 - half]
    row_ids = lax.broadcasted_iota(jnp.int32, (rows, cols), 0)
    col_ids = lax.broadcasted_iota(jnp.int32, (rows, cols), 1) + core * cols
    for place, slot in enumerate(receivers()):
        lower, row_at, col_at = slot_place(offs, mine, split_at, slot)
        upper_rows = row_ids >= row_at
        left_cols = col_ids >= col_at

        def merged(side, lower=lower, upper_rows=upper_rows):
            second = own[2 + side]
            top = jnp.where(lower == 1, second, own[side])
            bottom = jnp.where(lower == 1, below[jnp.bitwise_xor(col, side)], second)
            return jnp.where(upper_rows, top, bottom)

        parts[place] = jnp.where(left_cols, merged(0), merged(1))
    for turn, out in zip(EIGHT, outs):
        out[...] = parts[jnp.bitwise_xor(2 * mine + core, turn)]


def roll(value, rows, cols):
    return pltpu.roll(pltpu.roll(value, rows, 0), cols, 1)


def ready_kernel(where, slot_range, offs, taken, probe_from, measured, tabs_from, order_from, probe, target, tabs, kept, order, sems):
    half, col, core = where[0], where[1], where[2]
    probe_copy, kept_copy, order_copy, tabs_copy = fetch(
        [(probe_from, probe), (measured.at[0, half], kept), (order_from, order), (tabs_from, tabs)], sems
    )
    slot = slot_of(half, col, core)
    lower, row_at, col_at = slot_place(offs, 2 * half + col, slot_range[0, 1 - half], slot)
    probe_copy.wait()
    for part in range(2):
        probe[part] = roll(probe[part], row_at, col_at)
    kept_copy.wait()
    order_copy.wait()
    rest = jnp.where(lower == half, kept[...], taken[...])
    total = jnp.zeros_like(rest)
    for unused in range(3):
        part = rest.astype(jnp.bfloat16)
        rest = rest - part.astype(jnp.float32)
        total += dot(order[0], dot(part, order[1]).astype(jnp.bfloat16))
    target[...] = total
    tabs_copy.wait()


def position_kernel(where, slot_range, offs, *refs):
    gotten, (probe, target, tabs, factors) = dict(zip(EIGHT, refs)), refs[8:12]
    outs, keep, (patch, grad, bands) = refs[12:20], refs[20], refs[21:]
    half, col, core = where[0], where[1], where[2]
    mine = 2 * half + col
    flat = 2 * mine + core
    unused, row_at, col_at = slot_place(offs, mine, slot_range[0, 1 - half], slot_of(half, col, core))
    width = probe.shape[-1]
    lanes, band = width // 2, width // 4
    for turn in range(8):
        patch[jnp.bitwise_xor(flat, turn)] = gotten[turn][...]

    def load(plane):
        return jnp.concatenate([patch[2 * plane], patch[2 * plane + 1]], axis=1)

    def store(plane, value):
        grad[2 * plane] = value[:, :lanes]
        grad[2 * plane + 1] = value[:, lanes:]

    wave_re, wave_im = probe[0], probe[1]
    o0_re, o0_im, o1_re, o1_im = load(0), load(2), load(1), load(3)
    exit_re = wave_re * o0_re - wave_im * o0_im
    exit_im = wave_re * o0_im + wave_im * o0_re
    mid_re, mid_im = propagate(exit_re, exit_im, tabs, False)
    exit_re = mid_re * o1_re - mid_im * o1_im
    exit_im = mid_re * o1_im + mid_im * o1_re
    far_re, far_im = to_far(exit_re, exit_im, tabs, factors)
    excess = 2.0 * GRAD_WEIGHT * (far_re * far_re + far_im * far_im - target[...])
    back_re, back_im = from_far(excess * far_re, excess * far_im, tabs, factors)
    store(1, mid_re * back_re + mid_im * back_im)
    store(3, mid_re * back_im - mid_im * back_re)
    up_re = o1_re * back_re + o1_im * back_im
    up_im = o1_re * back_im - o1_im * back_re
    back_re, back_im = propagate(up_re, up_im, tabs, True)
    wave_re, wave_im = probe[0], probe[1]
    o0_re, o0_im = load(0), load(2)
    store(0, wave_re * back_re + wave_im * back_im)
    store(2, wave_re * back_im - wave_im * back_re)
    up_re = o0_re * back_re + o0_im * back_im
    up_im = o0_re * back_im - o0_im * back_re
    back_row, back_col = lax.rem(width - row_at, width), lax.rem(2 * width - col_at, width)
    for part, value in enumerate((up_re, up_im)):
        value = roll(value, back_row, back_col)
        for step in range(4):
            rows = value[step * band : (step + 1) * band]
            bands[4 * part + step, :band] = rows[:, :lanes]
            bands[4 * part + step, band:] = rows[:, lanes:]
    for turn, out in zip(BACK, outs):
        out[:width] = grad[jnp.bitwise_xor(flat, turn)]
    for part in range(4):
        keep[part] = bands[2 * part + core]
        start = width + 2 * band * part
        outs[0][start : start + 2 * band] = bands[2 * part + 1 - core]


def pair_kernel(where, keep, got, *outs):
    band = keep.shape[1]
    first = got.shape[0] - 4 * band
    for turn, out in zip(FOUR, outs):
        part = jnp.bitwise_xor(2 * where[0] + where[1], turn)
        out[...] = keep[part] + got[pl.ds(pl.multiple_of(first + band * part, band), band)]


def add_parts(where, slot_range, offs, parts, strip, rows, cols):
    half, col, core = where[0], where[1], where[2]
    mine = 2 * half + col
    row_ids = lax.broadcasted_iota(jnp.int32, (rows, cols), 0)
    col_ids = lax.broadcasted_iota(jnp.int32, (rows, cols), 1) + core * cols
    sums = [jnp.zeros((rows, cols), jnp.float32)] * 2
    for turn, part in zip(BACK, parts):
        flat = jnp.bitwise_xor(2 * mine + core, turn)
        slot = slot_of(flat // 4, (flat // 2) % 2, flat % 2)
        lower, row_at, col_at = slot_place(offs, mine, slot_range[0, 1 - half], slot)
        first = jnp.where(strip == lower, row_at, jnp.where(strip == lower + 1, 0, rows))
        last = jnp.where(strip == lower, rows, jnp.where(strip == lower + 1, row_at, 0))
        value = jnp.where((row_ids >= first) & (row_ids < last), part[:rows], 0.0)
        left = jnp.where(col_ids >= col_at, value, 0.0)
        sums = [sums[0] + left, sums[1] + (value - left)]
    return sums


def add_below_kernel(where, slot_range, offs, *refs):
    parts, quarters, (below, probe_band) = refs[:8], refs[8:12], refs[12:]
    rows, cols = below.shape[1:]
    sums = add_parts(where, slot_range, offs, parts, 2, rows, cols)
    for side in range(2):
        below[jnp.bitwise_xor(where[1], side)] = sums[side]
    total = (quarters[0][...] + quarters[1][...]) + (quarters[2][...] + quarters[3][...])
    band = probe_band.shape[0]
    probe_band[:, :cols] = total[:band]
    probe_band[:, cols:] = total[band:]


def add_own_kernel(where, slot_range, offs, *refs):
    parts, own = refs[:8], refs[8]
    rows, cols = own.shape[1:]
    for strip in range(2):
        own[2 * strip], own[2 * strip + 1] = add_parts(where, slot_range, offs, parts, strip, rows, cols)


def top_kernel(where, own, above, *outs):
    mine = 2 * where[0] + where[1]
    for turn, out in zip(FOUR, outs):
        extra = jnp.where(where[0] == turn // 2, above[turn % 2], 0.0)
        out[...] = own[jnp.bitwise_xor(mine, turn)] + extra


def join_kernel(where, *refs):
    probe, out, probe_out, sems = refs[4:]
    mine = 2 * where[0] + where[1]
    pairs = [(ref, out.at[jnp.bitwise_xor(mine, turn)]) for turn, ref in zip(FOUR, refs)]
    for copy in fetch([(probe, probe_out), *pairs], sems):
        copy.wait()


SMEM = pl.BlockSpec(memory_space=pltpu.SMEM)
VMEM = pl.BlockSpec(memory_space=pltpu.VMEM)
HBM = pl.BlockSpec(memory_space=pltpu.HBM)
ANY = pl.BlockSpec(memory_space=pl.ANY)


def call(kernel, outs, scalars, arrays, flops, scratch=(), copies=0):
    outs, arrays = ([x if isinstance(x, tuple) else (x, VMEM) for x in xs] for xs in (outs, arrays))
    moved = sum(math.prod(x.shape) * x.dtype.itemsize for x, unused in [*arrays, *outs])
    scratch = [pltpu.VMEM(dims, jnp.float32) if isinstance(dims, tuple) else dims for dims in scratch]
    return pl.pallas_call(
        kernel,
        out_shape=[x for x, unused in outs],
        in_specs=[SMEM] * len(scalars) + [spec for unused, spec in arrays],
        out_specs=[spec for unused, spec in outs],
        scratch_shapes=scratch + [pltpu.SemaphoreType.DMA((copies,))] * (copies > 0),
        compiler_params=pltpu.CompilerParams(vmem_limit_bytes=VMEM_LIMIT),
        cost_estimate=pl.CostEstimate(flops=flops, bytes_accessed=moved, transcendentals=0),
    )(*scalars, *(pltpu.with_memory_space_constraint(x, pltpu.HBM) if spec is HBM else x for x, spec in arrays))


def shape(*dims):
    return jax.ShapeDtypeStruct(dims, jnp.float32)


def deal(values, axes, order):
    return [
        lax.ppermute(value, axes, [(k, k ^ turn) for k in range(len(order))]) if turn else value
        for turn, value in zip(order, values)
    ]


def sum_over(value, axis, size):
    step = 2
    while step < size:
        value = value + lax.ppermute(value, axis, [(k, k ^ step) for k in range(size)])
        step *= 2
    return value


def local(object_field, probe, offsets, slot_range, measured):
    width = probe.shape[-1]
    planes, rows, cols = 4, object_field.shape[2], object_field.shape[3]
    band = width // 4
    pairs = lax.axis_size("pair")
    half, col, core = (lax.axis_index(name) for name in PLANE)
    where = jnp.stack([half, col, core])

    offsets, slot_range = (pltpu.with_memory_space_constraint(x, pltpu.HBM) for x in (offsets, slot_range))
    block = object_field.reshape(planes, rows, cols)
    *dealt, given = call(
        deal_kernel,
        [shape(rows + 8, cols)] * 4 + [shape(width, width)],
        (where, offsets),
        ((block, HBM), (measured, HBM)),
        0,
        copies=5,
    )
    own = deal(dealt, PLANE[:2], FOUR)
    (lowest,) = call(lowest_kernel, [shape(2, rows, cols)], (where,), own, 0)
    lowest, given = lax.optimization_barrier((lowest, given))
    below = lax.ppermute(lowest, "pair", [(k, k - 1) for k in range(1, pairs)])
    taken = lax.ppermute(given, "half", [(0, 1), (1, 0)])
    below, taken = lax.optimization_barrier((below, taken))

    turned = dict(zip(FOUR, own))
    offs = jnp.stack([turned[turn][rows : rows + 4, 0] for turn in range(4)]).astype(jnp.int32)
    others = lax.ppermute(offs, "core", [(0, 1), (1, 0)])
    offs = jnp.concatenate([jnp.where(core == 0, offs, others), jnp.where(core == 0, others, offs)], axis=1)
    scalars = (where, slot_range, offs)
    parts = call(
        pick_kernel,
        [shape(rows, cols)] * 8,
        scalars,
        (*own, below),
        32 * rows * width,
        [(planes, rows, cols), (8, rows, cols)],
    )
    tabs, factors, order = (jnp.asarray(table) for table in tables(width))
    probe, target, tabs = call(
        ready_kernel,
        [shape(*probe.shape), shape(width, width), jax.ShapeDtypeStruct(tabs.shape, tabs.dtype)],
        scalars,
        (taken, (probe, HBM), (measured, HBM), (tabs, HBM), (order, HBM)),
        12 * width**3,
        [(width, width), pltpu.VMEM(order.shape, order.dtype)],
        copies=4,
    )
    *grad, keep = call(
        position_kernel,
        [shape(rows + 8 * band, cols)] + [shape(rows, cols)] * 7 + [shape(4, 2 * band, cols)],
        scalars,
        (*deal(parts, PLANE, EIGHT), probe, target, tabs, factors),
        8 * 12 * width**3,
        [(8, rows, cols)] * 2 + [(8, 2 * band, cols)],
    )
    got = deal(grad, PLANE, BACK)
    quarters = call(pair_kernel, [shape(2 * band, cols)] * 4, (where,), (keep, got[0]), 4 * band * width)
    lower_sums, probe_band = call(
        add_below_kernel,
        [shape(2, rows, cols), shape(band, width)],
        scalars,
        (*got, *deal(quarters, PLANE[:2], FOUR)),
        32 * rows * width,
    )
    above = lax.ppermute(lower_sums, "pair", [(k, k + 1) for k in range(pairs - 1)])
    doubling = pairs > 1 and pairs & (pairs - 1) == 0
    if doubling:
        near = lax.ppermute(probe_band, "pair", [(k, k ^ 1) for k in range(pairs)])
    (sums,) = call(add_own_kernel, [shape(planes, rows, cols)], scalars, got, 64 * rows * width)
    sums = call(top_kernel, [shape(rows, cols)] * 4, (where,), (sums, above), planes * rows * cols)
    if doubling:
        *sums, near = lax.optimization_barrier((*sums, near))
        probe_band = sum_over(probe_band + near, "pair", pairs)
    else:
        probe_band = lax.psum(probe_band, "pair")
    sums = deal(sums, PLANE[:2], FOUR)
    probe_grad = lax.all_gather(probe_band, PLANE, axis=0, tiled=True)
    object_grad, probe_grad = call(
        join_kernel,
        [(shape(planes, rows, cols), HBM), (shape(*probe_grad.shape), HBM)],
        (where,),
        [(x, ANY) for x in (*sums, probe_grad)],
        0,
        copies=5,
    )
    return (object_grad.reshape(object_field.shape), probe_grad.reshape(probe.shape))


def solution(mesh):
    tile, grp = mesh.shape["tile"], mesh.shape["grp"]
    devices = mesh.devices.reshape(tile // 2, 2, 2, grp // 2)
    inner = Mesh(devices, ("pair", "half", "col", "core"))
    strip, cols = ("pair", "half"), ("col", "core")
    in_specs = (
        P(None, None, strip, cols),
        P(),
        P(strip, cols, None),
        P(strip, None),
        P(strip, cols, None, None),
    )
    out_specs = (P(None, None, strip, cols), P())
    return jax.shard_map(local, mesh=inner, in_specs=in_specs, out_specs=out_specs, check_vma=False)
```

```python
import functools
import math

import jax
import jax.numpy as jnp
import ml_dtypes
import numpy as np
from jax import lax
from jax.experimental import pallas as pl
from jax.experimental.pallas import tpu as pltpu
from jax.sharding import Mesh, PartitionSpec as P

GRAD_WEIGHT = 0.0625
PLANE = ("half", "col", "core")
EIGHT, BACK, FOUR = (4, 2, 5, 3, 6, 7, 1, 0), (1, 4, 2, 5, 3, 6, 7, 0), (2, 1, 3, 0)
VMEM_LIMIT = 24 * 1024 * 1024


def tables(width):
    half = width // 2
    index = np.arange(half, dtype=np.int64)
    scale = 1.0 / math.sqrt(width)
    far = np.exp(-2j * math.pi / half * (index[:, None] * index[None, :] % half)) * scale
    near = []
    for offset in (0, half):
        shift = index[:, None] - index[None, :] + offset
        near.append(np.exp(1j * (math.pi / width * (shift * shift % (2 * width)) - math.pi / 4.0)) * scale)
    products = []
    for matrix in ((near[0] + near[1]) / 2.0, (near[0] - near[1]) / 2.0, far):
        for imag in (matrix.imag, -matrix.imag):
            table = np.block([[matrix.real, imag], [-imag, matrix.real]])
            high = table.astype(ml_dtypes.bfloat16)
            low = (table - high.astype(np.float64)).astype(ml_dtypes.bfloat16)
            products.append(np.concatenate([high, low], axis=0))
    angle = -2.0 * math.pi / width * index
    twiddles = []
    for part in (np.cos(angle), np.sin(angle)):
        rows = np.broadcast_to(part[:, None], (half, half))
        twiddles.append(np.concatenate([rows, np.broadcast_to(part[None, :], (8, half))], axis=0))
    order = np.zeros((width, width))
    order[np.arange(width), np.concatenate([2 * index, 2 * index + 1])] = 1.0
    order = np.stack([order, order.T]).astype(ml_dtypes.bfloat16)
    return np.stack(products), np.stack(twiddles).astype(np.float32), order


def split(value):
    high = value.astype(jnp.bfloat16)
    low = (value - high.astype(jnp.float32)).astype(jnp.bfloat16)
    return high, low


def dot(left, right):
    return jnp.dot(left, right, preferred_element_type=jnp.float32)


PLUS, MINUS, FAR = 0, 2, 4


def times_right(re, im, table):
    width = table.shape[1]
    high, low = split(jnp.concatenate([re, im], axis=1))
    twice = dot(jnp.concatenate([high, low], axis=0), table[:width])
    count = re.shape[0]
    out = twice[:count] + (twice[count:] + dot(high, table[width:]))
    return out[:, : width // 2], out[:, width // 2 :]


def times_left(re, im, table):
    width = table.shape[1]
    high, low = split(jnp.concatenate([re, im], axis=0))
    twice = dot(table[...], high)
    out = twice[:width] + (twice[width:] + dot(table[:width], low))
    return out[: width // 2], out[width // 2 :]


def butterfly(first, second):
    return first + second, first - second


def halves(value, axis):
    half = value.shape[axis] // 2
    return (value[:half], value[half:]) if axis == 0 else (value[:, :half], value[:, half:])


def turn_by(re, im, cos, sin):
    return re * cos - im * sin, re * sin + im * cos


def propagate(re, im, tabs, conj):
    for axis in (1, 0):
        (plus_re, minus_re), (plus_im, minus_im) = (butterfly(*halves(x, axis)) for x in (re, im))
        times = times_right if axis else times_left
        pick = int(conj) if axis else 1 - int(conj)
        plus_re, plus_im = times(plus_re, plus_im, tabs.at[PLUS + pick])
        minus_re, minus_im = times(minus_re, minus_im, tabs.at[MINUS + pick])
        re = jnp.concatenate(butterfly(plus_re, minus_re), axis=axis)
        im = jnp.concatenate(butterfly(plus_im, minus_im), axis=axis)
    return re, im


def twiddle(factors, axis, width):
    half = factors.shape[2]
    if axis:
        return factors[0, half : half + 1], factors[1, half : half + 1]
    return tuple(jnp.concatenate([factors[k, :half]] * (width // half), axis=1) for k in range(2))


def to_far(re, im, tabs, factors):
    for axis in (1, 0):
        (even_re, odd_re), (even_im, odd_im) = (butterfly(*halves(x, axis)) for x in (re, im))
        odd_re, odd_im = turn_by(odd_re, odd_im, *twiddle(factors, axis, re.shape[1]))
        times, table = (times_right, tabs.at[FAR]) if axis else (times_left, tabs.at[FAR + 1])
        (even_re, even_im), (odd_re, odd_im) = times(even_re, even_im, table), times(odd_re, odd_im, table)
        re, im = jnp.concatenate([even_re, odd_re], axis=axis), jnp.concatenate([even_im, odd_im], axis=axis)
    return re, im


def from_far(re, im, tabs, factors):
    for axis in (0, 1):
        (even_re, odd_re), (even_im, odd_im) = halves(re, axis), halves(im, axis)
        times, table = (times_right, tabs.at[FAR + 1]) if axis else (times_left, tabs.at[FAR])
        (even_re, even_im), (odd_re, odd_im) = times(even_re, even_im, table), times(odd_re, odd_im, table)
        cos, sin = twiddle(factors, axis, re.shape[1])
        odd_re, odd_im = turn_by(odd_re, odd_im, cos, -sin)
        re = jnp.concatenate(butterfly(even_re, odd_re), axis=axis)
        im = jnp.concatenate(butterfly(even_im, odd_im), axis=axis)
    return re, im


def slot_of(half, col, core):
    return 2 * (2 * col + core) + half


def receivers():
    return [slot_of(half, col, core) for half in range(2) for col in range(2) for core in range(2)]


def slot_place(offs, mine, split_at, slot):
    lower = jnp.where(slot >= split_at, 1, 0)
    holder, at = jnp.bitwise_xor(2 * lower + slot // 4, mine), 2 * (slot % 4)
    return lower, offs[holder, at], offs[holder, at + 1]


def fetch(pairs, sems):
    copies = [pltpu.make_async_copy(source, into, sems.at[k]) for k, (source, into) in enumerate(pairs)]
    for copy in copies:
        copy.start()
    return copies


def deal_kernel(where, offsets, block, measured, *refs):
    outs, given, sems = refs[:4], refs[4], refs[5]
    mine = 2 * where[0] + where[1]
    rows, cols = block.shape[1:]
    pairs = [(block.at[jnp.bitwise_xor(mine, turn)], out.at[pl.ds(0, rows)]) for turn, out in zip(FOUR, outs)]
    copies = fetch([*pairs, (measured.at[0, 1 - where[0]], given)], sems)
    lines = [jnp.full((1, cols), offsets[0, slot, axis], jnp.int32) for slot in range(2) for axis in range(2)]
    lines = jnp.concatenate(lines * 2, axis=0).astype(jnp.float32)
    for out in outs:
        out[rows:] = lines
    for copy in copies:
        copy.wait()


def lowest_kernel(where, *refs):
    gotten, out = dict(zip(FOUR, refs)), refs[4]
    rows = out.shape[1]
    for turn in range(2):
        out[turn] = jnp.where(where[0] == 0, gotten[turn][:rows], gotten[2 + turn][:rows])


def pick_kernel(where, slot_range, offs, *refs):
    gotten, below, outs, (own, parts) = dict(zip(FOUR, refs)), refs[4], refs[5:13], refs[13:]
    rows, cols = outs[0].shape
    half, col, core = where[0], where[1], where[2]
    mine = 2 * half + col
    for turn in range(4):
        own[jnp.bitwise_xor(mine, turn)] = gotten[turn][:rows]
    split_at = slot_range[0, 1 - half]
    row_ids = lax.broadcasted_iota(jnp.int32, (rows, cols), 0)
    col_ids = lax.broadcasted_iota(jnp.int32, (rows, cols), 1) + core * cols
    for place, slot in enumerate(receivers()):
        lower, row_at, col_at = slot_place(offs, mine, split_at, slot)
        upper_rows = row_ids >= row_at
        left_cols = col_ids >= col_at

        def merged(side, lower=lower, upper_rows=upper_rows):
            second = own[2 + side]
            top = jnp.where(lower == 1, second, own[side])
            bottom = jnp.where(lower == 1, below[jnp.bitwise_xor(col, side)], second)
            return jnp.where(upper_rows, top, bottom)

        parts[place] = jnp.where(left_cols, merged(0), merged(1))
    for turn, out in zip(EIGHT, outs):
        out[...] = parts[jnp.bitwise_xor(2 * mine + core, turn)]


def roll(value, rows, cols):
    return pltpu.roll(pltpu.roll(value, rows, 0), cols, 1)


def ready_kernel(where, slot_range, offs, taken, probe_from, measured, tabs_from, order_from, probe, target, tabs, kept, order, sems):
    half, col, core = where[0], where[1], where[2]
    probe_copy, kept_copy, order_copy, tabs_copy = fetch(
        [(probe_from, probe), (measured.at[0, half], kept), (order_from, order), (tabs_from, tabs)], sems
    )
    slot = slot_of(half, col, core)
    lower, row_at, col_at = slot_place(offs, 2 * half + col, slot_range[0, 1 - half], slot)
    probe_copy.wait()
    for part in range(2):
        probe[part] = roll(probe[part], row_at, col_at)
    kept_copy.wait()
    order_copy.wait()
    rest = jnp.where(lower == half, kept[...], taken[...])
    total = jnp.zeros_like(rest)
    for unused in range(3):
        part = rest.astype(jnp.bfloat16)
        rest = rest - part.astype(jnp.float32)
        total += dot(order[0], dot(part, order[1]).astype(jnp.bfloat16))
    target[...] = total
    tabs_copy.wait()


def position_kernel(where, slot_range, offs, *refs):
    gotten, (probe, target, tabs, factors) = dict(zip(EIGHT, refs)), refs[8:12]
    outs, keep, (patch, grad, bands) = refs[12:20], refs[20], refs[21:]
    half, col, core = where[0], where[1], where[2]
    mine = 2 * half + col
    flat = 2 * mine + core
    unused, row_at, col_at = slot_place(offs, mine, slot_range[0, 1 - half], slot_of(half, col, core))
    width = probe.shape[-1]
    lanes, band = width // 2, width // 4
    for turn in range(8):
        patch[jnp.bitwise_xor(flat, turn)] = gotten[turn][...]

    def load(plane):
        return jnp.concatenate([patch[2 * plane], patch[2 * plane + 1]], axis=1)

    def store(plane, value):
        grad[2 * plane] = value[:, :lanes]
        grad[2 * plane + 1] = value[:, lanes:]

    wave_re, wave_im = probe[0], probe[1]
    o0_re, o0_im, o1_re, o1_im = load(0), load(2), load(1), load(3)
    exit_re = wave_re * o0_re - wave_im * o0_im
    exit_im = wave_re * o0_im + wave_im * o0_re
    mid_re, mid_im = propagate(exit_re, exit_im, tabs, False)
    exit_re = mid_re * o1_re - mid_im * o1_im
    exit_im = mid_re * o1_im + mid_im * o1_re
    far_re, far_im = to_far(exit_re, exit_im, tabs, factors)
    excess = 2.0 * GRAD_WEIGHT * (far_re * far_re + far_im * far_im - target[...])
    back_re, back_im = from_far(excess * far_re, excess * far_im, tabs, factors)
    store(1, mid_re * back_re + mid_im * back_im)
    store(3, mid_re * back_im - mid_im * back_re)
    up_re = o1_re * back_re + o1_im * back_im
    up_im = o1_re * back_im - o1_im * back_re
    back_re, back_im = propagate(up_re, up_im, tabs, True)
    wave_re, wave_im = probe[0], probe[1]
    o0_re, o0_im = load(0), load(2)
    store(0, wave_re * back_re + wave_im * back_im)
    store(2, wave_re * back_im - wave_im * back_re)
    up_re = o0_re * back_re + o0_im * back_im
    up_im = o0_re * back_im - o0_im * back_re
    back_row, back_col = lax.rem(width - row_at, width), lax.rem(2 * width - col_at, width)
    for part, value in enumerate((up_re, up_im)):
        value = roll(value, back_row, back_col)
        for step in range(4):
            rows = value[step * band : (step + 1) * band]
            bands[4 * part + step, :band] = rows[:, :lanes]
            bands[4 * part + step, band:] = rows[:, lanes:]
    for turn, out in zip(BACK, outs):
        out[:width] = grad[jnp.bitwise_xor(flat, turn)]
    for part in range(4):
        keep[part] = bands[2 * part + core]
        start = width + 2 * band * part
        outs[0][start : start + 2 * band] = bands[2 * part + 1 - core]


def pair_kernel(where, keep, got, *outs):
    band = keep.shape[1]
    first = got.shape[0] - 4 * band
    for turn, out in zip(FOUR, outs):
        part = jnp.bitwise_xor(2 * where[0] + where[1], turn)
        out[...] = keep[part] + got[pl.ds(pl.multiple_of(first + band * part, band), band)]


def add_parts(where, slot_range, offs, parts, strip, rows, cols):
    half, col, core = where[0], where[1], where[2]
    mine = 2 * half + col
    row_ids = lax.broadcasted_iota(jnp.int32, (rows, cols), 0)
    col_ids = lax.broadcasted_iota(jnp.int32, (rows, cols), 1) + core * cols
    sums = [jnp.zeros((rows, cols), jnp.float32)] * 2
    for turn, part in zip(BACK, parts):
        flat = jnp.bitwise_xor(2 * mine + core, turn)
        slot = slot_of(flat // 4, (flat // 2) % 2, flat % 2)
        lower, row_at, col_at = slot_place(offs, mine, slot_range[0, 1 - half], slot)
        first = jnp.where(strip == lower, row_at, jnp.where(strip == lower + 1, 0, rows))
        last = jnp.where(strip == lower, rows, jnp.where(strip == lower + 1, row_at, 0))
        value = jnp.where((row_ids >= first) & (row_ids < last), part[:rows], 0.0)
        left = jnp.where(col_ids >= col_at, value, 0.0)
        sums = [sums[0] + left, sums[1] + (value - left)]
    return sums


def add_below_kernel(where, slot_range, offs, *refs):
    parts, below = refs[:8], refs[8]
    rows, cols = below.shape[1:]
    sums = add_parts(where, slot_range, offs, parts, 2, rows, cols)
    for side in range(2):
        below[jnp.bitwise_xor(where[1], side)] = sums[side]


def band_kernel(*refs):
    quarters, out = refs[:4], refs[4]
    total = (quarters[0][...] + quarters[1][...]) + (quarters[2][...] + quarters[3][...])
    band, cols = out.shape[0], total.shape[1]
    out[:, :cols] = total[:band]
    out[:, cols:] = total[band:]


def add_own_kernel(where, slot_range, offs, *refs):
    parts, own = refs[:8], refs[8]
    rows, cols = own.shape[1:]
    for strip in range(2):
        own[2 * strip], own[2 * strip + 1] = add_parts(where, slot_range, offs, parts, strip, rows, cols)


def top_kernel(where, own, above, *outs):
    mine = 2 * where[0] + where[1]
    for turn, out in zip(FOUR, outs):
        extra = jnp.where(where[0] == turn // 2, above[turn % 2], 0.0)
        out[...] = own[jnp.bitwise_xor(mine, turn)] + extra


def join_kernel(where, *refs):
    probe, out, probe_out, sems = refs[4:]
    mine = 2 * where[0] + where[1]
    pairs = [(ref, out.at[jnp.bitwise_xor(mine, turn)]) for turn, ref in zip(FOUR, refs)]
    for copy in fetch([(probe, probe_out), *pairs], sems):
        copy.wait()


SMEM = pl.BlockSpec(memory_space=pltpu.SMEM)
VMEM = pl.BlockSpec(memory_space=pltpu.VMEM)
HBM = pl.BlockSpec(memory_space=pltpu.HBM)
ANY = pl.BlockSpec(memory_space=pl.ANY)


def call(kernel, outs, scalars, arrays, flops, scratch=(), copies=0):
    outs, arrays = ([x if isinstance(x, tuple) else (x, VMEM) for x in xs] for xs in (outs, arrays))
    moved = sum(math.prod(x.shape) * x.dtype.itemsize for x, unused in [*arrays, *outs])
    scratch = [pltpu.VMEM(dims, jnp.float32) if isinstance(dims, tuple) else dims for dims in scratch]
    return pl.pallas_call(
        kernel,
        out_shape=[x for x, unused in outs],
        in_specs=[SMEM] * len(scalars) + [spec for unused, spec in arrays],
        out_specs=[spec for unused, spec in outs],
        scratch_shapes=scratch + [pltpu.SemaphoreType.DMA((copies,))] * (copies > 0),
        compiler_params=pltpu.CompilerParams(vmem_limit_bytes=VMEM_LIMIT),
        cost_estimate=pl.CostEstimate(flops=flops, bytes_accessed=moved, transcendentals=0),
    )(*scalars, *(pltpu.with_memory_space_constraint(x, pltpu.HBM) if spec is HBM else x for x, spec in arrays))


def shape(*dims):
    return jax.ShapeDtypeStruct(dims, jnp.float32)


def deal(values, axes, order):
    return [
        lax.ppermute(value, axes, [(k, k ^ turn) for k in range(len(order))]) if turn else value
        for turn, value in zip(order, values)
    ]


def sum_over(value, axis, size):
    step = 2
    while step < size:
        value = value + lax.ppermute(value, axis, [(k, k ^ step) for k in range(size)])
        step *= 2
    return value


def local(object_field, probe, offsets, slot_range, measured):
    width = probe.shape[-1]
    planes, rows, cols = 4, object_field.shape[2], object_field.shape[3]
    band = width // 4
    pairs = lax.axis_size("pair")
    half, col, core = (lax.axis_index(name) for name in PLANE)
    where = jnp.stack([half, col, core])

    offsets, slot_range = (pltpu.with_memory_space_constraint(x, pltpu.HBM) for x in (offsets, slot_range))
    block = object_field.reshape(planes, rows, cols)
    *dealt, given = call(
        deal_kernel,
        [shape(rows + 8, cols)] * 4 + [shape(width, width)],
        (where, offsets),
        ((block, HBM), (measured, HBM)),
        0,
        copies=5,
    )
    own = deal(dealt, PLANE[:2], FOUR)
    (lowest,) = call(lowest_kernel, [shape(2, rows, cols)], (where,), own, 0)
    lowest, given = lax.optimization_barrier((lowest, given))
    below = lax.ppermute(lowest, "pair", [(k, k - 1) for k in range(1, pairs)])
    taken = lax.ppermute(given, "half", [(0, 1), (1, 0)])
    below, taken = lax.optimization_barrier((below, taken))

    turned = dict(zip(FOUR, own))
    offs = jnp.stack([turned[turn][rows : rows + 4, 0] for turn in range(4)]).astype(jnp.int32)
    others = lax.ppermute(offs, "core", [(0, 1), (1, 0)])
    offs = jnp.concatenate([jnp.where(core == 0, offs, others), jnp.where(core == 0, others, offs)], axis=1)
    scalars = (where, slot_range, offs)
    parts = call(
        pick_kernel,
        [shape(rows, cols)] * 8,
        scalars,
        (*own, below),
        32 * rows * width,
        [(planes, rows, cols), (8, rows, cols)],
    )
    tabs, factors, order = (jnp.asarray(table) for table in tables(width))
    probe, target, tabs = call(
        ready_kernel,
        [shape(*probe.shape), shape(width, width), jax.ShapeDtypeStruct(tabs.shape, tabs.dtype)],
        scalars,
        (taken, (probe, HBM), (measured, HBM), (tabs, HBM), (order, HBM)),
        12 * width**3,
        [(width, width), pltpu.VMEM(order.shape, order.dtype)],
        copies=4,
    )
    *grad, keep = call(
        position_kernel,
        [shape(rows + 8 * band, cols)] + [shape(rows, cols)] * 7 + [shape(4, 2 * band, cols)],
        scalars,
        (*deal(parts, PLANE, EIGHT), probe, target, tabs, factors),
        8 * 12 * width**3,
        [(8, rows, cols)] * 2 + [(8, 2 * band, cols)],
    )
    got = deal(grad, PLANE, BACK)
    quarters = call(pair_kernel, [shape(2 * band, cols)] * 4, (where,), (keep, got[0]), 4 * band * width)
    *got, last = lax.optimization_barrier((*got, quarters[-1]))
    quarters = [*quarters[:-1], last]
    (lower_sums,) = call(add_below_kernel, [shape(2, rows, cols)], scalars, got, 32 * rows * width)
    above = lax.ppermute(lower_sums, "pair", [(k, k + 1) for k in range(pairs - 1)])
    (sums,) = call(add_own_kernel, [shape(planes, rows, cols)], scalars, got, 64 * rows * width)
    (probe_band,) = call(band_kernel, [shape(band, width)], (), deal(quarters, PLANE[:2], FOUR), 4 * band * width)
    doubling = pairs > 1 and pairs & (pairs - 1) == 0
    if doubling:
        near = lax.ppermute(probe_band, "pair", [(k, k ^ 1) for k in range(pairs)])
    sums = call(top_kernel, [shape(rows, cols)] * 4, (where,), (sums, above), planes * rows * cols)
    if doubling:
        *sums, near = lax.optimization_barrier((*sums, near))
        probe_band = sum_over(probe_band + near, "pair", pairs)
    else:
        probe_band = lax.psum(probe_band, "pair")
    sums = deal(sums, PLANE[:2], FOUR)
    probe_grad = lax.all_gather(probe_band, PLANE, axis=0, tiled=True)
    object_grad, probe_grad = call(
        join_kernel,
        [(shape(planes, rows, cols), HBM), (shape(*probe_grad.shape), HBM)],
        (where,),
        [(x, ANY) for x in (*sums, probe_grad)],
        0,
        copies=5,
    )
    return (object_grad.reshape(object_field.shape), probe_grad.reshape(probe.shape))


def solution(mesh):
    tile, grp = mesh.shape["tile"], mesh.shape["grp"]
    devices = mesh.devices.reshape(tile // 2, 2, 2, grp // 2)
    inner = Mesh(devices, ("pair", "half", "col", "core"))
    strip, cols = ("pair", "half"), ("col", "core")
    in_specs = (
        P(None, None, strip, cols),
        P(),
        P(strip, cols, None),
        P(strip, None),
        P(strip, cols, None, None),
    )
    out_specs = (P(None, None, strip, cols), P())
    return jax.shard_map(local, mesh=inner, in_specs=in_specs, out_specs=out_specs, check_vma=False)
```

```python
import functools
import math

import jax
import jax.numpy as jnp
import ml_dtypes
import numpy as np
from jax import lax
from jax.experimental import pallas as pl
from jax.experimental.pallas import tpu as pltpu
from jax.sharding import Mesh, PartitionSpec as P

GRAD_WEIGHT = 0.0625
PLANE = ("half", "col", "core")
EIGHT, BACK, FOUR = (4, 2, 5, 3, 6, 7, 1, 0), (1, 4, 2, 5, 3, 6, 7, 0), (2, 1, 3, 0)
VMEM_LIMIT = 24 * 1024 * 1024


def tables(width):
    half = width // 2
    index = np.arange(half, dtype=np.int64)
    scale = 1.0 / math.sqrt(width)
    far = np.exp(-2j * math.pi / half * (index[:, None] * index[None, :] % half)) * scale
    near = []
    for offset in (0, half):
        shift = index[:, None] - index[None, :] + offset
        near.append(np.exp(1j * (math.pi / width * (shift * shift % (2 * width)) - math.pi / 4.0)) * scale)
    products = []
    for matrix in ((near[0] + near[1]) / 2.0, (near[0] - near[1]) / 2.0, far):
        for imag in (matrix.imag, -matrix.imag):
            table = np.block([[matrix.real, imag], [-imag, matrix.real]])
            high = table.astype(ml_dtypes.bfloat16)
            low = (table - high.astype(np.float64)).astype(ml_dtypes.bfloat16)
            products.append(np.concatenate([high, low], axis=0))
    angle = -2.0 * math.pi / width * index
    twiddles = []
    for part in (np.cos(angle), np.sin(angle)):
        rows = np.broadcast_to(part[:, None], (half, half))
        twiddles.append(np.concatenate([rows, np.broadcast_to(part[None, :], (8, half))], axis=0))
    order = np.zeros((width, width))
    order[np.arange(width), np.concatenate([2 * index, 2 * index + 1])] = 1.0
    order = np.stack([order, order.T]).astype(ml_dtypes.bfloat16)
    return np.stack(products), np.stack(twiddles).astype(np.float32), order


def split(value):
    high = value.astype(jnp.bfloat16)
    low = (value - high.astype(jnp.float32)).astype(jnp.bfloat16)
    return high, low


def dot(left, right):
    return jnp.dot(left, right, preferred_element_type=jnp.float32)


PLUS, MINUS, FAR = 0, 2, 4


def times_right(re, im, table):
    width = table.shape[1]
    high, low = split(jnp.concatenate([re, im], axis=1))
    twice = dot(jnp.concatenate([high, low], axis=0), table[:width])
    count = re.shape[0]
    out = twice[:count] + (twice[count:] + dot(high, table[width:]))
    return out[:, : width // 2], out[:, width // 2 :]


def times_left(re, im, table):
    width = table.shape[1]
    high, low = split(jnp.concatenate([re, im], axis=0))
    twice = dot(table[...], high)
    out = twice[:width] + (twice[width:] + dot(table[:width], low))
    return out[: width // 2], out[width // 2 :]


def butterfly(first, second):
    return first + second, first - second


def halves(value, axis):
    half = value.shape[axis] // 2
    return (value[:half], value[half:]) if axis == 0 else (value[:, :half], value[:, half:])


def turn_by(re, im, cos, sin):
    return re * cos - im * sin, re * sin + im * cos


def propagate(re, im, tabs, conj):
    for axis in (1, 0):
        (plus_re, minus_re), (plus_im, minus_im) = (butterfly(*halves(x, axis)) for x in (re, im))
        times = times_right if axis else times_left
        pick = int(conj) if axis else 1 - int(conj)
        plus_re, plus_im = times(plus_re, plus_im, tabs.at[PLUS + pick])
        minus_re, minus_im = times(minus_re, minus_im, tabs.at[MINUS + pick])
        re = jnp.concatenate(butterfly(plus_re, minus_re), axis=axis)
        im = jnp.concatenate(butterfly(plus_im, minus_im), axis=axis)
    return re, im


def twiddle(factors, axis, width):
    half = factors.shape[2]
    if axis:
        return factors[0, half : half + 1], factors[1, half : half + 1]
    return tuple(jnp.concatenate([factors[k, :half]] * (width // half), axis=1) for k in range(2))


def to_far(re, im, tabs, factors):
    for axis in (1, 0):
        (even_re, odd_re), (even_im, odd_im) = (butterfly(*halves(x, axis)) for x in (re, im))
        odd_re, odd_im = turn_by(odd_re, odd_im, *twiddle(factors, axis, re.shape[1]))
        times, table = (times_right, tabs.at[FAR]) if axis else (times_left, tabs.at[FAR + 1])
        (even_re, even_im), (odd_re, odd_im) = times(even_re, even_im, table), times(odd_re, odd_im, table)
        re, im = jnp.concatenate([even_re, odd_re], axis=axis), jnp.concatenate([even_im, odd_im], axis=axis)
    return re, im


def from_far(re, im, tabs, factors):
    for axis in (0, 1):
        (even_re, odd_re), (even_im, odd_im) = halves(re, axis), halves(im, axis)
        times, table = (times_right, tabs.at[FAR + 1]) if axis else (times_left, tabs.at[FAR])
        (even_re, even_im), (odd_re, odd_im) = times(even_re, even_im, table), times(odd_re, odd_im, table)
        cos, sin = twiddle(factors, axis, re.shape[1])
        odd_re, odd_im = turn_by(odd_re, odd_im, cos, -sin)
        re = jnp.concatenate(butterfly(even_re, odd_re), axis=axis)
        im = jnp.concatenate(butterfly(even_im, odd_im), axis=axis)
    return re, im


def slot_of(half, col, core):
    return 2 * (2 * col + core) + half


def receivers():
    return [slot_of(half, col, core) for half in range(2) for col in range(2) for core in range(2)]


def slot_place(offs, mine, split_at, slot):
    lower = jnp.where(slot >= split_at, 1, 0)
    holder, at = jnp.bitwise_xor(2 * lower + slot // 4, mine), 2 * (slot % 4)
    return lower, offs[holder, at], offs[holder, at + 1]


def here():
    return tuple(lax.axis_index(name) for name in PLANE)


def fetch(pairs, sems):
    copies = [pltpu.make_async_copy(source, into, sems.at[k]) for k, (source, into) in enumerate(pairs)]
    for copy in copies:
        copy.start()
    return copies


def deal_kernel(block, measured, offsets_from, *refs):
    outs, given, offsets, sems = refs[:4], refs[4], refs[5], refs[6]
    half, col, unused = here()
    mine = 2 * half + col
    rows, cols = block.shape[1:]
    pairs = [(block.at[jnp.bitwise_xor(mine, turn)], out.at[pl.ds(0, rows)]) for turn, out in zip(FOUR, outs)]
    copies = fetch([(offsets_from, offsets), *pairs, (measured.at[0, 1 - half], given)], sems)
    copies[0].wait()
    lines = [jnp.full((1, cols), offsets[0, slot, axis], jnp.int32) for slot in range(2) for axis in range(2)]
    lines = jnp.concatenate(lines * 2, axis=0).astype(jnp.float32)
    for out in outs:
        out[rows:] = lines
    for copy in copies[1:]:
        copy.wait()


def lowest_kernel(*refs):
    gotten, out = dict(zip(FOUR, refs)), refs[4]
    rows = out.shape[1]
    half = here()[0]
    for turn in range(2):
        out[turn] = jnp.where(half == 0, gotten[turn][:rows], gotten[2 + turn][:rows])


def pick_kernel(slot_range, offs, *refs):
    gotten, below, outs, (own, parts) = dict(zip(FOUR, refs)), refs[4], refs[5:13], refs[13:]
    rows, cols = outs[0].shape
    half, col, core = here()
    mine = 2 * half + col
    for turn in range(4):
        own[jnp.bitwise_xor(mine, turn)] = gotten[turn][:rows]
    split_at = slot_range[0, 1 - half]
    row_ids = lax.broadcasted_iota(jnp.int32, (rows, cols), 0)
    col_ids = lax.broadcasted_iota(jnp.int32, (rows, cols), 1) + core * cols
    for place, slot in enumerate(receivers()):
        lower, row_at, col_at = slot_place(offs, mine, split_at, slot)
        upper_rows = row_ids >= row_at
        left_cols = col_ids >= col_at

        def merged(side, lower=lower, upper_rows=upper_rows):
            second = own[2 + side]
            top = jnp.where(lower == 1, second, own[side])
            bottom = jnp.where(lower == 1, below[jnp.bitwise_xor(col, side)], second)
            return jnp.where(upper_rows, top, bottom)

        parts[place] = jnp.where(left_cols, merged(0), merged(1))
    for turn, out in zip(EIGHT, outs):
        out[...] = parts[jnp.bitwise_xor(2 * mine + core, turn)]


def roll(value, rows, cols):
    return pltpu.roll(pltpu.roll(value, rows, 0), cols, 1)


def ready_kernel(slot_range, offs, taken, probe_from, measured, tabs_from, order_from, probe, target, tabs, kept, order, sems):
    half, col, core = here()
    probe_copy, kept_copy, order_copy, tabs_copy = fetch(
        [(probe_from, probe), (measured.at[0, half], kept), (order_from, order), (tabs_from, tabs)], sems
    )
    slot = slot_of(half, col, core)
    lower, row_at, col_at = slot_place(offs, 2 * half + col, slot_range[0, 1 - half], slot)
    probe_copy.wait()
    for part in range(2):
        probe[part] = roll(probe[part], row_at, col_at)
    kept_copy.wait()
    order_copy.wait()
    rest = jnp.where(lower == half, kept[...], taken[...])
    total = jnp.zeros_like(rest)
    for unused in range(3):
        part = rest.astype(jnp.bfloat16)
        rest = rest - part.astype(jnp.float32)
        total += dot(order[0], dot(part, order[1]).astype(jnp.bfloat16))
    target[...] = total
    tabs_copy.wait()


def position_kernel(slot_range, offs, *refs):
    gotten, (probe, target, tabs, factors) = dict(zip(EIGHT, refs)), refs[8:12]
    outs, keep, (patch, grad, bands) = refs[12:20], refs[20], refs[21:]
    half, col, core = here()
    mine = 2 * half + col
    flat = 2 * mine + core
    unused, row_at, col_at = slot_place(offs, mine, slot_range[0, 1 - half], slot_of(half, col, core))
    width = probe.shape[-1]
    lanes, band = width // 2, width // 4
    for turn in range(8):
        patch[jnp.bitwise_xor(flat, turn)] = gotten[turn][...]

    def load(plane):
        return jnp.concatenate([patch[2 * plane], patch[2 * plane + 1]], axis=1)

    def store(plane, value):
        grad[2 * plane] = value[:, :lanes]
        grad[2 * plane + 1] = value[:, lanes:]

    wave_re, wave_im = probe[0], probe[1]
    o0_re, o0_im, o1_re, o1_im = load(0), load(2), load(1), load(3)
    exit_re = wave_re * o0_re - wave_im * o0_im
    exit_im = wave_re * o0_im + wave_im * o0_re
    mid_re, mid_im = propagate(exit_re, exit_im, tabs, False)
    exit_re = mid_re * o1_re - mid_im * o1_im
    exit_im = mid_re * o1_im + mid_im * o1_re
    far_re, far_im = to_far(exit_re, exit_im, tabs, factors)
    excess = 2.0 * GRAD_WEIGHT * (far_re * far_re + far_im * far_im - target[...])
    back_re, back_im = from_far(excess * far_re, excess * far_im, tabs, factors)
    store(1, mid_re * back_re + mid_im * back_im)
    store(3, mid_re * back_im - mid_im * back_re)
    up_re = o1_re * back_re + o1_im * back_im
    up_im = o1_re * back_im - o1_im * back_re
    back_re, back_im = propagate(up_re, up_im, tabs, True)
    wave_re, wave_im = probe[0], probe[1]
    o0_re, o0_im = load(0), load(2)
    store(0, wave_re * back_re + wave_im * back_im)
    store(2, wave_re * back_im - wave_im * back_re)
    up_re = o0_re * back_re + o0_im * back_im
    up_im = o0_re * back_im - o0_im * back_re
    back_row, back_col = lax.rem(width - row_at, width), lax.rem(2 * width - col_at, width)
    for part, value in enumerate((up_re, up_im)):
        value = roll(value, back_row, back_col)
        for step in range(4):
            rows = value[step * band : (step + 1) * band]
            bands[4 * part + step, :band] = rows[:, :lanes]
            bands[4 * part + step, band:] = rows[:, lanes:]
    for turn, out in zip(BACK, outs):
        out[:width] = grad[jnp.bitwise_xor(flat, turn)]
    for part in range(4):
        keep[part] = bands[2 * part + core]
        start = width + 2 * band * part
        outs[0][start : start + 2 * band] = bands[2 * part + 1 - core]


def pair_kernel(keep, got, *outs):
    band = keep.shape[1]
    half, col, unused = here()
    first = got.shape[0] - 4 * band
    for turn, out in zip(FOUR, outs):
        part = jnp.bitwise_xor(2 * half + col, turn)
        out[...] = keep[part] + got[pl.ds(pl.multiple_of(first + band * part, band), band)]


def add_parts(slot_range, offs, parts, strip, rows, cols):
    half, col, core = here()
    mine = 2 * half + col
    row_ids = lax.broadcasted_iota(jnp.int32, (rows, cols), 0)
    col_ids = lax.broadcasted_iota(jnp.int32, (rows, cols), 1) + core * cols
    sums = [jnp.zeros((rows, cols), jnp.float32)] * 2
    for turn, part in zip(BACK, parts):
        flat = jnp.bitwise_xor(2 * mine + core, turn)
        slot = slot_of(flat // 4, (flat // 2) % 2, flat % 2)
        lower, row_at, col_at = slot_place(offs, mine, slot_range[0, 1 - half], slot)
        first = jnp.where(strip == lower, row_at, jnp.where(strip == lower + 1, 0, rows))
        last = jnp.where(strip == lower, rows, jnp.where(strip == lower + 1, row_at, 0))
        value = jnp.where((row_ids >= first) & (row_ids < last), part[:rows], 0.0)
        left = jnp.where(col_ids >= col_at, value, 0.0)
        sums = [sums[0] + left, sums[1] + (value - left)]
    return sums


def add_below_kernel(slot_range, offs, *refs):
    parts, quarters, (below, probe_band) = refs[:8], refs[8:12], refs[12:]
    rows, cols = below.shape[1:]
    sums = add_parts(slot_range, offs, parts, 2, rows, cols)
    col = here()[1]
    for side in range(2):
        below[jnp.bitwise_xor(col, side)] = sums[side]
    total = (quarters[0][...] + quarters[1][...]) + (quarters[2][...] + quarters[3][...])
    band = probe_band.shape[0]
    probe_band[:, :cols] = total[:band]
    probe_band[:, cols:] = total[band:]


def add_own_kernel(slot_range, offs, *refs):
    parts, own = refs[:8], refs[8]
    rows, cols = own.shape[1:]
    for strip in range(2):
        own[2 * strip], own[2 * strip + 1] = add_parts(slot_range, offs, parts, strip, rows, cols)


def top_kernel(own, above, *outs):
    half, col, unused = here()
    mine = 2 * half + col
    for turn, out in zip(FOUR, outs):
        extra = jnp.where(half == turn // 2, above[turn % 2], 0.0)
        out[...] = own[jnp.bitwise_xor(mine, turn)] + extra


def join_kernel(*refs):
    probe, out, probe_out, sems = refs[4:]
    half, col, unused = here()
    mine = 2 * half + col
    pairs = [(ref, out.at[jnp.bitwise_xor(mine, turn)]) for turn, ref in zip(FOUR, refs)]
    for copy in fetch([(probe, probe_out), *pairs], sems):
        copy.wait()


SMEM = pl.BlockSpec(memory_space=pltpu.SMEM)
VMEM = pl.BlockSpec(memory_space=pltpu.VMEM)
HBM = pl.BlockSpec(memory_space=pltpu.HBM)
ANY = pl.BlockSpec(memory_space=pl.ANY)


def call(kernel, outs, scalars, arrays, flops, scratch=(), copies=0):
    outs, arrays = ([x if isinstance(x, tuple) else (x, VMEM) for x in xs] for xs in (outs, arrays))
    moved = sum(math.prod(x.shape) * x.dtype.itemsize for x, unused in [*arrays, *outs])
    scratch = [pltpu.VMEM(dims, jnp.float32) if isinstance(dims, tuple) else dims for dims in scratch]
    return pl.pallas_call(
        kernel,
        out_shape=[x for x, unused in outs],
        in_specs=[SMEM] * len(scalars) + [spec for unused, spec in arrays],
        out_specs=[spec for unused, spec in outs],
        scratch_shapes=scratch + [pltpu.SemaphoreType.DMA((copies,))] * (copies > 0),
        compiler_params=pltpu.CompilerParams(vmem_limit_bytes=VMEM_LIMIT),
        cost_estimate=pl.CostEstimate(flops=flops, bytes_accessed=moved, transcendentals=0),
    )(*scalars, *(pltpu.with_memory_space_constraint(x, pltpu.HBM) if spec is HBM else x for x, spec in arrays))


def shape(*dims):
    return jax.ShapeDtypeStruct(dims, jnp.float32)


def deal(values, axes, order):
    return [
        lax.ppermute(value, axes, [(k, k ^ turn) for k in range(len(order))]) if turn else value
        for turn, value in zip(order, values)
    ]


def sum_over(value, axis, size):
    step = 2
    while step < size:
        value = value + lax.ppermute(value, axis, [(k, k ^ step) for k in range(size)])
        step *= 2
    return value


def local(object_field, probe, offsets, slot_range, measured):
    width = probe.shape[-1]
    planes, rows, cols = 4, object_field.shape[2], object_field.shape[3]
    band = width // 4
    pairs = lax.axis_size("pair")
    half, col, core = (lax.axis_index(name) for name in PLANE)

    offsets, slot_range = (pltpu.with_memory_space_constraint(x, pltpu.HBM) for x in (offsets, slot_range))
    block = object_field.reshape(planes, rows, cols)
    *dealt, given = call(
        deal_kernel,
        [shape(rows + 8, cols)] * 4 + [shape(width, width)],
        (),
        ((block, HBM), (measured, HBM), (offsets, HBM)),
        0,
        [pltpu.SMEM(offsets.shape, offsets.dtype)],
        copies=6,
    )
    own = deal(dealt, PLANE[:2], FOUR)
    (lowest,) = call(lowest_kernel, [shape(2, rows, cols)], (), own, 0)
    lowest, given = lax.optimization_barrier((lowest, given))
    below = lax.ppermute(lowest, "pair", [(k, k - 1) for k in range(1, pairs)])
    taken = lax.ppermute(given, "half", [(0, 1), (1, 0)])
    below, taken = lax.optimization_barrier((below, taken))

    turned = dict(zip(FOUR, own))
    offs = jnp.stack([turned[turn][rows : rows + 4, 0] for turn in range(4)]).astype(jnp.int32)
    others = lax.ppermute(offs, "core", [(0, 1), (1, 0)])
    offs = jnp.concatenate([jnp.where(core == 0, offs, others), jnp.where(core == 0, others, offs)], axis=1)
    scalars = (slot_range, offs)
    parts = call(
        pick_kernel,
        [shape(rows, cols)] * 8,
        scalars,
        (*own, below),
        32 * rows * width,
        [(planes, rows, cols), (8, rows, cols)],
    )
    tabs, factors, order = (jnp.asarray(table) for table in tables(width))
    probe, target, tabs = call(
        ready_kernel,
        [shape(*probe.shape), shape(width, width), jax.ShapeDtypeStruct(tabs.shape, tabs.dtype)],
        scalars,
        (taken, (probe, HBM), (measured, HBM), (tabs, HBM), (order, HBM)),
        12 * width**3,
        [(width, width), pltpu.VMEM(order.shape, order.dtype)],
        copies=4,
    )
    *grad, keep = call(
        position_kernel,
        [shape(rows + 8 * band, cols)] + [shape(rows, cols)] * 7 + [shape(4, 2 * band, cols)],
        scalars,
        (*deal(parts, PLANE, EIGHT), probe, target, tabs, factors),
        8 * 12 * width**3,
        [(8, rows, cols)] * 2 + [(8, 2 * band, cols)],
    )
    got = deal(grad, PLANE, BACK)
    quarters = call(pair_kernel, [shape(2 * band, cols)] * 4, (), (keep, got[0]), 4 * band * width)
    lower_sums, probe_band = call(
        add_below_kernel,
        [shape(2, rows, cols), shape(band, width)],
        scalars,
        (*got, *deal(quarters, PLANE[:2], FOUR)),
        32 * rows * width,
    )
    above = lax.ppermute(lower_sums, "pair", [(k, k + 1) for k in range(pairs - 1)])
    doubling = pairs > 1 and pairs & (pairs - 1) == 0
    if doubling:
        near = lax.ppermute(probe_band, "pair", [(k, k ^ 1) for k in range(pairs)])
    (sums,) = call(add_own_kernel, [shape(planes, rows, cols)], scalars, got, 64 * rows * width)
    sums = call(top_kernel, [shape(rows, cols)] * 4, (), (sums, above), planes * rows * cols)
    if doubling:
        *sums, near = lax.optimization_barrier((*sums, near))
        probe_band = sum_over(probe_band + near, "pair", pairs)
    else:
        probe_band = lax.psum(probe_band, "pair")
    sums = deal(sums, PLANE[:2], FOUR)
    probe_grad = lax.all_gather(probe_band, PLANE, axis=0, tiled=True)
    object_grad, probe_grad = call(
        join_kernel,
        [(shape(planes, rows, cols), HBM), (shape(*probe_grad.shape), HBM)],
        (),
        [(x, ANY) for x in (*sums, probe_grad)],
        0,
        copies=5,
    )
    return (object_grad.reshape(object_field.shape), probe_grad.reshape(probe.shape))


def solution(mesh):
    tile, grp = mesh.shape["tile"], mesh.shape["grp"]
    devices = mesh.devices.reshape(tile // 2, 2, 2, grp // 2)
    inner = Mesh(devices, ("pair", "half", "col", "core"))
    strip, cols = ("pair", "half"), ("col", "core")
    in_specs = (
        P(None, None, strip, cols),
        P(),
        P(strip, cols, None),
        P(strip, None),
        P(strip, cols, None, None),
    )
    out_specs = (P(None, None, strip, cols), P())
    return jax.shard_map(local, mesh=inner, in_specs=in_specs, out_specs=out_specs, check_vma=False)
```

```python
import functools
import math

import jax
import jax.numpy as jnp
import ml_dtypes
import numpy as np
from jax import lax
from jax.experimental import pallas as pl
from jax.experimental.pallas import tpu as pltpu
from jax.sharding import Mesh, PartitionSpec as P

GRAD_WEIGHT = 0.0625
PLANE = ("half", "col", "core")
EIGHT, BACK, FOUR = (4, 2, 5, 3, 6, 7, 1, 0), (1, 4, 2, 5, 3, 6, 7, 0), (2, 1, 3, 0)
VMEM_LIMIT = 24 * 1024 * 1024


def tables(width):
    half = width // 2
    index = np.arange(half, dtype=np.int64)
    scale = 1.0 / math.sqrt(width)
    far = np.exp(-2j * math.pi / half * (index[:, None] * index[None, :] % half)) * scale
    near = []
    for offset in (0, half):
        shift = index[:, None] - index[None, :] + offset
        near.append(np.exp(1j * (math.pi / width * (shift * shift % (2 * width)) - math.pi / 4.0)) * scale)
    products = []
    for matrix in ((near[0] + near[1]) / 2.0, (near[0] - near[1]) / 2.0, far):
        for imag in (matrix.imag, -matrix.imag):
            table = np.block([[matrix.real, imag], [-imag, matrix.real]])
            high = table.astype(ml_dtypes.bfloat16)
            low = (table - high.astype(np.float64)).astype(ml_dtypes.bfloat16)
            products.append(np.concatenate([high, low], axis=0))
    angle = -2.0 * math.pi / width * index
    twiddles = []
    for part in (np.cos(angle), np.sin(angle)):
        rows = np.broadcast_to(part[:, None], (half, half))
        twiddles.append(np.concatenate([rows, np.broadcast_to(part[None, :], (8, half))], axis=0))
    order = np.zeros((width, width))
    order[np.arange(width), np.concatenate([2 * index, 2 * index + 1])] = 1.0
    order = np.stack([order, order.T]).astype(ml_dtypes.bfloat16)
    return np.stack(products), np.stack(twiddles).astype(np.float32), order


def split(value):
    high = value.astype(jnp.bfloat16)
    low = (value - high.astype(jnp.float32)).astype(jnp.bfloat16)
    return high, low


def dot(left, right):
    return jnp.dot(left, right, preferred_element_type=jnp.float32)


PLUS, MINUS, FAR = 0, 2, 4


def times_right(re, im, table):
    width = table.shape[1]
    high, low = split(jnp.concatenate([re, im], axis=1))
    twice = dot(jnp.concatenate([high, low], axis=0), table[:width])
    count = re.shape[0]
    out = twice[:count] + (twice[count:] + dot(high, table[width:]))
    return out[:, : width // 2], out[:, width // 2 :]


def times_left(re, im, table):
    width = table.shape[1]
    high, low = split(jnp.concatenate([re, im], axis=0))
    twice = dot(table[...], high)
    out = twice[:width] + (twice[width:] + dot(table[:width], low))
    return out[: width // 2], out[width // 2 :]


def butterfly(first, second):
    return first + second, first - second


def halves(value, axis):
    half = value.shape[axis] // 2
    return (value[:half], value[half:]) if axis == 0 else (value[:, :half], value[:, half:])


def turn_by(re, im, cos, sin):
    return re * cos - im * sin, re * sin + im * cos


def propagate(re, im, tabs, conj):
    for axis in (1, 0):
        (plus_re, minus_re), (plus_im, minus_im) = (butterfly(*halves(x, axis)) for x in (re, im))
        times = times_right if axis else times_left
        pick = int(conj) if axis else 1 - int(conj)
        plus_re, plus_im = times(plus_re, plus_im, tabs.at[PLUS + pick])
        minus_re, minus_im = times(minus_re, minus_im, tabs.at[MINUS + pick])
        re = jnp.concatenate(butterfly(plus_re, minus_re), axis=axis)
        im = jnp.concatenate(butterfly(plus_im, minus_im), axis=axis)
    return re, im


def twiddle(factors, axis, width):
    half = factors.shape[2]
    if axis:
        return factors[0, half : half + 1], factors[1, half : half + 1]
    return tuple(jnp.concatenate([factors[k, :half]] * (width // half), axis=1) for k in range(2))


def to_far(re, im, tabs, factors):
    for axis in (1, 0):
        (even_re, odd_re), (even_im, odd_im) = (butterfly(*halves(x, axis)) for x in (re, im))
        odd_re, odd_im = turn_by(odd_re, odd_im, *twiddle(factors, axis, re.shape[1]))
        times, table = (times_right, tabs.at[FAR]) if axis else (times_left, tabs.at[FAR + 1])
        (even_re, even_im), (odd_re, odd_im) = times(even_re, even_im, table), times(odd_re, odd_im, table)
        re, im = jnp.concatenate([even_re, odd_re], axis=axis), jnp.concatenate([even_im, odd_im], axis=axis)
    return re, im


def from_far(re, im, tabs, factors):
    for axis in (0, 1):
        (even_re, odd_re), (even_im, odd_im) = halves(re, axis), halves(im, axis)
        times, table = (times_right, tabs.at[FAR + 1]) if axis else (times_left, tabs.at[FAR])
        (even_re, even_im), (odd_re, odd_im) = times(even_re, even_im, table), times(odd_re, odd_im, table)
        cos, sin = twiddle(factors, axis, re.shape[1])
        odd_re, odd_im = turn_by(odd_re, odd_im, cos, -sin)
        re = jnp.concatenate(butterfly(even_re, odd_re), axis=axis)
        im = jnp.concatenate(butterfly(even_im, odd_im), axis=axis)
    return re, im


def slot_of(half, col, core):
    return 2 * (2 * col + core) + half


def receivers():
    return [slot_of(half, col, core) for half in range(2) for col in range(2) for core in range(2)]


def slot_place(offs, mine, slot):
    lower = jnp.where(slot >= offs[4, 0], 1, 0)
    holder, at = jnp.bitwise_xor(2 * lower + slot // 4, mine), 2 * (slot % 4)
    return lower, offs[holder, at], offs[holder, at + 1]


def here():
    return tuple(lax.axis_index(name) for name in PLANE)


def fetch(pairs, sems):
    copies = [pltpu.make_async_copy(source, into, sems.at[k]) for k, (source, into) in enumerate(pairs)]
    for copy in copies:
        copy.start()
    return copies


def deal_kernel(block, measured, offsets_from, *refs):
    outs, given, offsets, sems = refs[:4], refs[4], refs[5], refs[6]
    half, col, unused = here()
    mine = 2 * half + col
    rows, cols = block.shape[1:]
    pairs = [(block.at[jnp.bitwise_xor(mine, turn)], out.at[pl.ds(0, rows)]) for turn, out in zip(FOUR, outs)]
    copies = fetch([(offsets_from, offsets), *pairs, (measured.at[0, 1 - half], given)], sems)
    copies[0].wait()
    lines = [jnp.full((1, cols), offsets[0, slot, axis], jnp.int32) for slot in range(2) for axis in range(2)]
    lines = jnp.concatenate(lines * 2, axis=0).astype(jnp.float32)
    for out in outs:
        out[rows:] = lines
    for copy in copies[1:]:
        copy.wait()


def lowest_kernel(*refs):
    gotten, out = dict(zip(FOUR, refs)), refs[4]
    rows = out.shape[1]
    half = here()[0]
    for turn in range(2):
        out[turn] = jnp.where(half == 0, gotten[turn][:rows], gotten[2 + turn][:rows])


def pick_kernel(offs, *refs):
    gotten, below, outs, (own, parts) = dict(zip(FOUR, refs)), refs[4], refs[5:13], refs[13:]
    rows, cols = outs[0].shape
    half, col, core = here()
    mine = 2 * half + col
    for turn in range(4):
        own[jnp.bitwise_xor(mine, turn)] = gotten[turn][:rows]
    row_ids = lax.broadcasted_iota(jnp.int32, (rows, cols), 0)
    col_ids = lax.broadcasted_iota(jnp.int32, (rows, cols), 1) + core * cols
    for place, slot in enumerate(receivers()):
        lower, row_at, col_at = slot_place(offs, mine, slot)
        upper_rows = row_ids >= row_at
        left_cols = col_ids >= col_at

        def merged(side, lower=lower, upper_rows=upper_rows):
            second = own[2 + side]
            top = jnp.where(lower == 1, second, own[side])
            bottom = jnp.where(lower == 1, below[jnp.bitwise_xor(col, side)], second)
            return jnp.where(upper_rows, top, bottom)

        parts[place] = jnp.where(left_cols, merged(0), merged(1))
    for turn, out in zip(EIGHT, outs):
        out[...] = parts[jnp.bitwise_xor(2 * mine + core, turn)]


def roll(value, rows, cols):
    return pltpu.roll(pltpu.roll(value, rows, 0), cols, 1)


def ready_kernel(offs, taken, probe_from, measured, tabs_from, order_from, probe, target, tabs, kept, order, sems):
    half, col, core = here()
    probe_copy, kept_copy, order_copy, tabs_copy = fetch(
        [(probe_from, probe), (measured.at[0, half], kept), (order_from, order), (tabs_from, tabs)], sems
    )
    slot = slot_of(half, col, core)
    lower, row_at, col_at = slot_place(offs, 2 * half + col, slot)
    probe_copy.wait()
    for part in range(2):
        probe[part] = roll(probe[part], row_at, col_at)
    kept_copy.wait()
    order_copy.wait()
    rest = jnp.where(lower == half, kept[...], taken[...])
    total = jnp.zeros_like(rest)
    for unused in range(3):
        part = rest.astype(jnp.bfloat16)
        rest = rest - part.astype(jnp.float32)
        total += dot(order[0], dot(part, order[1]).astype(jnp.bfloat16))
    target[...] = total
    tabs_copy.wait()


def position_kernel(offs, *refs):
    gotten, (probe, target, tabs, factors) = dict(zip(EIGHT, refs)), refs[8:12]
    outs, keep, (patch, grad, bands) = refs[12:20], refs[20], refs[21:]
    half, col, core = here()
    mine = 2 * half + col
    flat = 2 * mine + core
    unused, row_at, col_at = slot_place(offs, mine, slot_of(half, col, core))
    width = probe.shape[-1]
    lanes, band = width // 2, width // 4
    for turn in range(8):
        patch[jnp.bitwise_xor(flat, turn)] = gotten[turn][...]

    def load(plane):
        return jnp.concatenate([patch[2 * plane], patch[2 * plane + 1]], axis=1)

    def store(plane, value):
        grad[2 * plane] = value[:, :lanes]
        grad[2 * plane + 1] = value[:, lanes:]

    wave_re, wave_im = probe[0], probe[1]
    o0_re, o0_im, o1_re, o1_im = load(0), load(2), load(1), load(3)
    exit_re = wave_re * o0_re - wave_im * o0_im
    exit_im = wave_re * o0_im + wave_im * o0_re
    mid_re, mid_im = propagate(exit_re, exit_im, tabs, False)
    exit_re = mid_re * o1_re - mid_im * o1_im
    exit_im = mid_re * o1_im + mid_im * o1_re
    far_re, far_im = to_far(exit_re, exit_im, tabs, factors)
    excess = 2.0 * GRAD_WEIGHT * (far_re * far_re + far_im * far_im - target[...])
    back_re, back_im = from_far(excess * far_re, excess * far_im, tabs, factors)
    store(1, mid_re * back_re + mid_im * back_im)
    store(3, mid_re * back_im - mid_im * back_re)
    up_re = o1_re * back_re + o1_im * back_im
    up_im = o1_re * back_im - o1_im * back_re
    back_re, back_im = propagate(up_re, up_im, tabs, True)
    wave_re, wave_im = probe[0], probe[1]
    o0_re, o0_im = load(0), load(2)
    store(0, wave_re * back_re + wave_im * back_im)
    store(2, wave_re * back_im - wave_im * back_re)
    up_re = o0_re * back_re + o0_im * back_im
    up_im = o0_re * back_im - o0_im * back_re
    back_row, back_col = lax.rem(width - row_at, width), lax.rem(2 * width - col_at, width)
    for part, value in enumerate((up_re, up_im)):
        value = roll(value, back_row, back_col)
        for step in range(4):
            rows = value[step * band : (step + 1) * band]
            bands[4 * part + step, :band] = rows[:, :lanes]
            bands[4 * part + step, band:] = rows[:, lanes:]
    for turn, out in zip(BACK, outs):
        out[:width] = grad[jnp.bitwise_xor(flat, turn)]
    for part in range(4):
        keep[part] = bands[2 * part + core]
        start = width + 2 * band * part
        outs[0][start : start + 2 * band] = bands[2 * part + 1 - core]


def pair_kernel(keep, got, *outs):
    band = keep.shape[1]
    half, col, unused = here()
    first = got.shape[0] - 4 * band
    for turn, out in zip(FOUR, outs):
        part = jnp.bitwise_xor(2 * half + col, turn)
        out[...] = keep[part] + got[pl.ds(pl.multiple_of(first + band * part, band), band)]


def add_parts(offs, parts, strip, rows, cols):
    half, col, core = here()
    mine = 2 * half + col
    row_ids = lax.broadcasted_iota(jnp.int32, (rows, cols), 0)
    col_ids = lax.broadcasted_iota(jnp.int32, (rows, cols), 1) + core * cols
    sums = [jnp.zeros((rows, cols), jnp.float32)] * 2
    for turn, part in zip(BACK, parts):
        flat = jnp.bitwise_xor(2 * mine + core, turn)
        slot = slot_of(flat // 4, (flat // 2) % 2, flat % 2)
        lower, row_at, col_at = slot_place(offs, mine, slot)
        first = jnp.where(strip == lower, row_at, jnp.where(strip == lower + 1, 0, rows))
        last = jnp.where(strip == lower, rows, jnp.where(strip == lower + 1, row_at, 0))
        value = jnp.where((row_ids >= first) & (row_ids < last), part[:rows], 0.0)
        left = jnp.where(col_ids >= col_at, value, 0.0)
        sums = [sums[0] + left, sums[1] + (value - left)]
    return sums


def add_below_kernel(offs, *refs):
    parts, quarters, (below, probe_band) = refs[:8], refs[8:12], refs[12:]
    rows, cols = below.shape[1:]
    sums = add_parts(offs, parts, 2, rows, cols)
    col = here()[1]
    for side in range(2):
        below[jnp.bitwise_xor(col, side)] = sums[side]
    total = (quarters[0][...] + quarters[1][...]) + (quarters[2][...] + quarters[3][...])
    band = probe_band.shape[0]
    probe_band[:, :cols] = total[:band]
    probe_band[:, cols:] = total[band:]


def add_own_kernel(offs, *refs):
    parts, own = refs[:8], refs[8]
    rows, cols = own.shape[1:]
    for strip in range(2):
        own[2 * strip], own[2 * strip + 1] = add_parts(offs, parts, strip, rows, cols)


def top_kernel(own, above, *outs):
    half, col, unused = here()
    mine = 2 * half + col
    for turn, out in zip(FOUR, outs):
        extra = jnp.where(half == turn // 2, above[turn % 2], 0.0)
        out[...] = own[jnp.bitwise_xor(mine, turn)] + extra


def join_kernel(*refs):
    probe, out, probe_out, sems = refs[4:]
    half, col, unused = here()
    mine = 2 * half + col
    pairs = [(ref, out.at[jnp.bitwise_xor(mine, turn)]) for turn, ref in zip(FOUR, refs)]
    for copy in fetch([(probe, probe_out), *pairs], sems):
        copy.wait()


SMEM = pl.BlockSpec(memory_space=pltpu.SMEM)
VMEM = pl.BlockSpec(memory_space=pltpu.VMEM)
HBM = pl.BlockSpec(memory_space=pltpu.HBM)
ANY = pl.BlockSpec(memory_space=pl.ANY)


def call(kernel, outs, scalars, arrays, flops, scratch=(), copies=0):
    outs, arrays = ([x if isinstance(x, tuple) else (x, VMEM) for x in xs] for xs in (outs, arrays))
    moved = sum(math.prod(x.shape) * x.dtype.itemsize for x, unused in [*arrays, *outs])
    scratch = [pltpu.VMEM(dims, jnp.float32) if isinstance(dims, tuple) else dims for dims in scratch]
    return pl.pallas_call(
        kernel,
        out_shape=[x for x, unused in outs],
        in_specs=[SMEM] * len(scalars) + [spec for unused, spec in arrays],
        out_specs=[spec for unused, spec in outs],
        scratch_shapes=scratch + [pltpu.SemaphoreType.DMA((copies,))] * (copies > 0),
        compiler_params=pltpu.CompilerParams(vmem_limit_bytes=VMEM_LIMIT),
        cost_estimate=pl.CostEstimate(flops=flops, bytes_accessed=moved, transcendentals=0),
    )(*scalars, *(pltpu.with_memory_space_constraint(x, pltpu.HBM) if spec is HBM else x for x, spec in arrays))


def shape(*dims):
    return jax.ShapeDtypeStruct(dims, jnp.float32)


def deal(values, axes, order):
    return [
        lax.ppermute(value, axes, [(k, k ^ turn) for k in range(len(order))]) if turn else value
        for turn, value in zip(order, values)
    ]


def sum_over(value, axis, size):
    step = 2
    while step < size:
        value = value + lax.ppermute(value, axis, [(k, k ^ step) for k in range(size)])
        step *= 2
    return value


def local(object_field, probe, offsets, slot_range, measured):
    width = probe.shape[-1]
    planes, rows, cols = 4, object_field.shape[2], object_field.shape[3]
    band = width // 4
    pairs = lax.axis_size("pair")
    half, col, core = (lax.axis_index(name) for name in PLANE)

    block = object_field.reshape(planes, rows, cols)
    *dealt, given = call(
        deal_kernel,
        [shape(rows + 8, cols)] * 4 + [shape(width, width)],
        (),
        ((block, HBM), (measured, HBM), (offsets, HBM)),
        0,
        [pltpu.SMEM(offsets.shape, offsets.dtype)],
        copies=6,
    )
    own = deal(dealt, PLANE[:2], FOUR)
    (lowest,) = call(lowest_kernel, [shape(2, rows, cols)], (), own, 0)
    lowest, given = lax.optimization_barrier((lowest, given))
    below = lax.ppermute(lowest, "pair", [(k, k - 1) for k in range(1, pairs)])
    taken = lax.ppermute(given, "half", [(0, 1), (1, 0)])
    below, taken = lax.optimization_barrier((below, taken))

    turned = dict(zip(FOUR, own))
    offs = jnp.stack([turned[turn][rows : rows + 4, 0] for turn in range(4)]).astype(jnp.int32)
    others = lax.ppermute(offs, "core", [(0, 1), (1, 0)])
    offs = jnp.concatenate([jnp.where(core == 0, offs, others), jnp.where(core == 0, others, offs)], axis=1)
    split_at = jnp.where(half == 0, slot_range[0, 1], slot_range[0, 0])
    offs = jnp.concatenate([offs, jnp.full((1, offs.shape[1]), split_at, jnp.int32)], axis=0)
    scalars = (offs,)
    parts = call(
        pick_kernel,
        [shape(rows, cols)] * 8,
        scalars,
        (*own, below),
        32 * rows * width,
        [(planes, rows, cols), (8, rows, cols)],
    )
    tabs, factors, order = (jnp.asarray(table) for table in tables(width))
    probe, target, tabs = call(
        ready_kernel,
        [shape(*probe.shape), shape(width, width), jax.ShapeDtypeStruct(tabs.shape, tabs.dtype)],
        scalars,
        (taken, (probe, HBM), (measured, HBM), (tabs, HBM), (order, HBM)),
        12 * width**3,
        [(width, width), pltpu.VMEM(order.shape, order.dtype)],
        copies=4,
    )
    *grad, keep = call(
        position_kernel,
        [shape(rows + 8 * band, cols)] + [shape(rows, cols)] * 7 + [shape(4, 2 * band, cols)],
        scalars,
        (*deal(parts, PLANE, EIGHT), probe, target, tabs, factors),
        8 * 12 * width**3,
        [(8, rows, cols)] * 2 + [(8, 2 * band, cols)],
    )
    got = deal(grad, PLANE, BACK)
    quarters = call(pair_kernel, [shape(2 * band, cols)] * 4, (), (keep, got[0]), 4 * band * width)
    lower_sums, probe_band = call(
        add_below_kernel,
        [shape(2, rows, cols), shape(band, width)],
        scalars,
        (*got, *deal(quarters, PLANE[:2], FOUR)),
        32 * rows * width,
    )
    above = lax.ppermute(lower_sums, "pair", [(k, k + 1) for k in range(pairs - 1)])
    doubling = pairs > 1 and pairs & (pairs - 1) == 0
    if doubling:
        near = lax.ppermute(probe_band, "pair", [(k, k ^ 1) for k in range(pairs)])
    (sums,) = call(add_own_kernel, [shape(planes, rows, cols)], scalars, got, 64 * rows * width)
    sums = call(top_kernel, [shape(rows, cols)] * 4, (), (sums, above), planes * rows * cols)
    if doubling:
        *sums, near = lax.optimization_barrier((*sums, near))
        probe_band = sum_over(probe_band + near, "pair", pairs)
    else:
        probe_band = lax.psum(probe_band, "pair")
    sums = deal(sums, PLANE[:2], FOUR)
    probe_grad = lax.all_gather(probe_band, PLANE, axis=0, tiled=True)
    object_grad, probe_grad = call(
        join_kernel,
        [(shape(planes, rows, cols), HBM), (shape(*probe_grad.shape), HBM)],
        (),
        [(x, ANY) for x in (*sums, probe_grad)],
        0,
        copies=5,
    )
    return (object_grad.reshape(object_field.shape), probe_grad.reshape(probe.shape))


def solution(mesh):
    tile, grp = mesh.shape["tile"], mesh.shape["grp"]
    devices = mesh.devices.reshape(tile // 2, 2, 2, grp // 2)
    inner = Mesh(devices, ("pair", "half", "col", "core"))
    strip, cols = ("pair", "half"), ("col", "core")
    in_specs = (
        P(None, None, strip, cols),
        P(),
        P(strip, cols, None),
        P(strip, None),
        P(strip, cols, None, None),
    )
    out_specs = (P(None, None, strip, cols), P())
    return jax.shard_map(local, mesh=inner, in_specs=in_specs, out_specs=out_specs, check_vma=False)
```

```python
import functools
import math

import jax
import jax.numpy as jnp
import ml_dtypes
import numpy as np
from jax import lax
from jax.experimental import pallas as pl
from jax.experimental.pallas import tpu as pltpu
from jax.sharding import Mesh, PartitionSpec as P

GRAD_WEIGHT = 0.0625
PLANE = ("half", "col", "core")
EIGHT, BACK, FOUR = (2, 4, 3, 5, 6, 7, 1, 0), (1, 4, 2, 5, 3, 6, 7, 0), (2, 1, 3, 0)
VMEM_LIMIT = 24 * 1024 * 1024


def tables(width):
    half = width // 2
    index = np.arange(half, dtype=np.int64)
    scale = 1.0 / math.sqrt(width)
    far = np.exp(-2j * math.pi / half * (index[:, None] * index[None, :] % half)) * scale
    near = []
    for offset in (0, half):
        shift = index[:, None] - index[None, :] + offset
        near.append(np.exp(1j * (math.pi / width * (shift * shift % (2 * width)) - math.pi / 4.0)) * scale)
    products = []
    for matrix in ((near[0] + near[1]) / 2.0, (near[0] - near[1]) / 2.0, far):
        for imag in (matrix.imag, -matrix.imag):
            table = np.block([[matrix.real, imag], [-imag, matrix.real]])
            high = table.astype(ml_dtypes.bfloat16)
            low = (table - high.astype(np.float64)).astype(ml_dtypes.bfloat16)
            products.append(np.concatenate([high, low], axis=0))
    angle = -2.0 * math.pi / width * index
    twiddles = []
    for part in (np.cos(angle), np.sin(angle)):
        rows = np.broadcast_to(part[:, None], (half, half))
        twiddles.append(np.concatenate([rows, np.broadcast_to(part[None, :], (8, half))], axis=0))
    order = np.zeros((width, width))
    order[np.arange(width), np.concatenate([2 * index, 2 * index + 1])] = 1.0
    order = np.stack([order, order.T]).astype(ml_dtypes.bfloat16)
    return np.stack(products), np.stack(twiddles).astype(np.float32), order


def split(value):
    high = value.astype(jnp.bfloat16)
    low = (value - high.astype(jnp.float32)).astype(jnp.bfloat16)
    return high, low


def dot(left, right):
    return jnp.dot(left, right, preferred_element_type=jnp.float32)


PLUS, MINUS, FAR = 0, 2, 4


def times_right(re, im, table):
    width = table.shape[1]
    high, low = split(jnp.concatenate([re, im], axis=1))
    twice = dot(jnp.concatenate([high, low], axis=0), table[:width])
    count = re.shape[0]
    out = twice[:count] + (twice[count:] + dot(high, table[width:]))
    return out[:, : width // 2], out[:, width // 2 :]


def times_left(re, im, table):
    width = table.shape[1]
    high, low = split(jnp.concatenate([re, im], axis=0))
    twice = dot(table[...], high)
    out = twice[:width] + (twice[width:] + dot(table[:width], low))
    return out[: width // 2], out[width // 2 :]


def butterfly(first, second):
    return first + second, first - second


def halves(value, axis):
    half = value.shape[axis] // 2
    return (value[:half], value[half:]) if axis == 0 else (value[:, :half], value[:, half:])


def turn_by(re, im, cos, sin):
    return re * cos - im * sin, re * sin + im * cos


def propagate(re, im, tabs, conj):
    for axis in (1, 0):
        (plus_re, minus_re), (plus_im, minus_im) = (butterfly(*halves(x, axis)) for x in (re, im))
        times = times_right if axis else times_left
        pick = int(conj) if axis else 1 - int(conj)
        plus_re, plus_im = times(plus_re, plus_im, tabs.at[PLUS + pick])
        minus_re, minus_im = times(minus_re, minus_im, tabs.at[MINUS + pick])
        re = jnp.concatenate(butterfly(plus_re, minus_re), axis=axis)
        im = jnp.concatenate(butterfly(plus_im, minus_im), axis=axis)
    return re, im


def twiddle(factors, axis, width):
    half = factors.shape[2]
    if axis:
        return factors[0, half : half + 1], factors[1, half : half + 1]
    return tuple(jnp.concatenate([factors[k, :half]] * (width // half), axis=1) for k in range(2))


def to_far(re, im, tabs, factors):
    for axis in (1, 0):
        (even_re, odd_re), (even_im, odd_im) = (butterfly(*halves(x, axis)) for x in (re, im))
        odd_re, odd_im = turn_by(odd_re, odd_im, *twiddle(factors, axis, re.shape[1]))
        times, table = (times_right, tabs.at[FAR]) if axis else (times_left, tabs.at[FAR + 1])
        (even_re, even_im), (odd_re, odd_im) = times(even_re, even_im, table), times(odd_re, odd_im, table)
        re, im = jnp.concatenate([even_re, odd_re], axis=axis), jnp.concatenate([even_im, odd_im], axis=axis)
    return re, im


def from_far(re, im, tabs, factors):
    for axis in (0, 1):
        (even_re, odd_re), (even_im, odd_im) = halves(re, axis), halves(im, axis)
        times, table = (times_right, tabs.at[FAR + 1]) if axis else (times_left, tabs.at[FAR])
        (even_re, even_im), (odd_re, odd_im) = times(even_re, even_im, table), times(odd_re, odd_im, table)
        cos, sin = twiddle(factors, axis, re.shape[1])
        odd_re, odd_im = turn_by(odd_re, odd_im, cos, -sin)
        re = jnp.concatenate(butterfly(even_re, odd_re), axis=axis)
        im = jnp.concatenate(butterfly(even_im, odd_im), axis=axis)
    return re, im


def slot_of(half, col, core):
    return 2 * (2 * col + core) + half


def receivers():
    return [slot_of(half, col, core) for half in range(2) for col in range(2) for core in range(2)]


def slot_place(offs, mine, slot):
    lower = jnp.where(slot >= offs[4, 0], 1, 0)
    holder, at = jnp.bitwise_xor(2 * lower + slot // 4, mine), 2 * (slot % 4)
    return lower, offs[holder, at], offs[holder, at + 1]


def here():
    return tuple(lax.axis_index(name) for name in PLANE)


def fetch(pairs, sems):
    copies = [pltpu.make_async_copy(source, into, sems.at[k]) for k, (source, into) in enumerate(pairs)]
    for copy in copies:
        copy.start()
    return copies


def deal_kernel(block, measured, offsets_from, *refs):
    outs, given, offsets, sems = refs[:4], refs[4], refs[5], refs[6]
    half, col, unused = here()
    mine = 2 * half + col
    rows, cols = block.shape[1:]
    pairs = [(block.at[jnp.bitwise_xor(mine, turn)], out.at[pl.ds(0, rows)]) for turn, out in zip(FOUR, outs)]
    copies = fetch([(offsets_from, offsets), *pairs, (measured.at[0, 1 - half], given)], sems)
    copies[0].wait()
    lines = [jnp.full((1, cols), offsets[0, slot, axis], jnp.int32) for slot in range(2) for axis in range(2)]
    lines = jnp.concatenate(lines * 2, axis=0).astype(jnp.float32)
    for out in outs:
        out[rows:] = lines
    for copy in copies[1:]:
        copy.wait()


def lowest_kernel(*refs):
    gotten, out = dict(zip(FOUR, refs)), refs[4]
    rows = out.shape[1]
    half = here()[0]
    for turn in range(2):
        out[turn] = jnp.where(half == 0, gotten[turn][:rows], gotten[2 + turn][:rows])


def pick_kernel(offs, *refs):
    gotten, below, outs, (own, parts) = dict(zip(FOUR, refs)), refs[4], refs[5:13], refs[13:]
    rows, cols = outs[0].shape
    half, col, core = here()
    mine = 2 * half + col
    for turn in range(4):
        own[jnp.bitwise_xor(mine, turn)] = gotten[turn][:rows]
    row_ids = lax.broadcasted_iota(jnp.int32, (rows, cols), 0)
    col_ids = lax.broadcasted_iota(jnp.int32, (rows, cols), 1) + core * cols
    for place, slot in enumerate(receivers()):
        lower, row_at, col_at = slot_place(offs, mine, slot)
        upper_rows = row_ids >= row_at
        left_cols = col_ids >= col_at

        def merged(side, lower=lower, upper_rows=upper_rows):
            second = own[2 + side]
            top = jnp.where(lower == 1, second, own[side])
            bottom = jnp.where(lower == 1, below[jnp.bitwise_xor(col, side)], second)
            return jnp.where(upper_rows, top, bottom)

        parts[place] = jnp.where(left_cols, merged(0), merged(1))
    for turn, out in zip(EIGHT, outs):
        out[...] = parts[jnp.bitwise_xor(2 * mine + core, turn)]


def roll(value, rows, cols):
    return pltpu.roll(pltpu.roll(value, rows, 0), cols, 1)


def ready_kernel(offs, taken, probe_from, measured, tabs_from, order_from, probe, target, tabs, kept, order, sems):
    half, col, core = here()
    probe_copy, kept_copy, order_copy, tabs_copy = fetch(
        [(probe_from, probe), (measured.at[0, half], kept), (order_from, order), (tabs_from, tabs)], sems
    )
    slot = slot_of(half, col, core)
    lower, row_at, col_at = slot_place(offs, 2 * half + col, slot)
    probe_copy.wait()
    for part in range(2):
        probe[part] = roll(probe[part], row_at, col_at)
    kept_copy.wait()
    order_copy.wait()
    rest = jnp.where(lower == half, kept[...], taken[...])
    total = jnp.zeros_like(rest)
    for unused in range(3):
        part = rest.astype(jnp.bfloat16)
        rest = rest - part.astype(jnp.float32)
        total += dot(order[0], dot(part, order[1]).astype(jnp.bfloat16))
    target[...] = total
    tabs_copy.wait()


def position_kernel(offs, *refs):
    gotten, (probe, target, tabs, factors) = dict(zip(EIGHT, refs)), refs[8:12]
    outs, keep, (patch, grad, bands) = refs[12:20], refs[20], refs[21:]
    half, col, core = here()
    mine = 2 * half + col
    flat = 2 * mine + core
    unused, row_at, col_at = slot_place(offs, mine, slot_of(half, col, core))
    width = probe.shape[-1]
    lanes, band = width // 2, width // 4
    for turn in range(8):
        patch[jnp.bitwise_xor(flat, turn)] = gotten[turn][...]

    def load(plane):
        return jnp.concatenate([patch[2 * plane], patch[2 * plane + 1]], axis=1)

    def store(plane, value):
        grad[2 * plane] = value[:, :lanes]
        grad[2 * plane + 1] = value[:, lanes:]

    wave_re, wave_im = probe[0], probe[1]
    o0_re, o0_im, o1_re, o1_im = load(0), load(2), load(1), load(3)
    exit_re = wave_re * o0_re - wave_im * o0_im
    exit_im = wave_re * o0_im + wave_im * o0_re
    mid_re, mid_im = propagate(exit_re, exit_im, tabs, False)
    exit_re = mid_re * o1_re - mid_im * o1_im
    exit_im = mid_re * o1_im + mid_im * o1_re
    far_re, far_im = to_far(exit_re, exit_im, tabs, factors)
    excess = 2.0 * GRAD_WEIGHT * (far_re * far_re + far_im * far_im - target[...])
    back_re, back_im = from_far(excess * far_re, excess * far_im, tabs, factors)
    store(1, mid_re * back_re + mid_im * back_im)
    store(3, mid_re * back_im - mid_im * back_re)
    up_re = o1_re * back_re + o1_im * back_im
    up_im = o1_re * back_im - o1_im * back_re
    back_re, back_im = propagate(up_re, up_im, tabs, True)
    wave_re, wave_im = probe[0], probe[1]
    o0_re, o0_im = load(0), load(2)
    store(0, wave_re * back_re + wave_im * back_im)
    store(2, wave_re * back_im - wave_im * back_re)
    up_re = o0_re * back_re + o0_im * back_im
    up_im = o0_re * back_im - o0_im * back_re
    back_row, back_col = lax.rem(width - row_at, width), lax.rem(2 * width - col_at, width)
    for part, value in enumerate((up_re, up_im)):
        value = roll(value, back_row, back_col)
        for step in range(4):
            rows = value[step * band : (step + 1) * band]
            bands[4 * part + step, :band] = rows[:, :lanes]
            bands[4 * part + step, band:] = rows[:, lanes:]
    for turn, out in zip(BACK, outs):
        out[:width] = grad[jnp.bitwise_xor(flat, turn)]
    for part in range(4):
        keep[part] = bands[2 * part + core]
        start = width + 2 * band * part
        outs[0][start : start + 2 * band] = bands[2 * part + 1 - core]


def pair_kernel(keep, got, *outs):
    band = keep.shape[1]
    half, col, unused = here()
    first = got.shape[0] - 4 * band
    for turn, out in zip(FOUR, outs):
        part = jnp.bitwise_xor(2 * half + col, turn)
        out[...] = keep[part] + got[pl.ds(pl.multiple_of(first + band * part, band), band)]


def add_parts(offs, parts, strip, rows, cols):
    half, col, core = here()
    mine = 2 * half + col
    row_ids = lax.broadcasted_iota(jnp.int32, (rows, cols), 0)
    col_ids = lax.broadcasted_iota(jnp.int32, (rows, cols), 1) + core * cols
    sums = [jnp.zeros((rows, cols), jnp.float32)] * 2
    for turn, part in zip(BACK, parts):
        flat = jnp.bitwise_xor(2 * mine + core, turn)
        slot = slot_of(flat // 4, (flat // 2) % 2, flat % 2)
        lower, row_at, col_at = slot_place(offs, mine, slot)
        first = jnp.where(strip == lower, row_at, jnp.where(strip == lower + 1, 0, rows))
        last = jnp.where(strip == lower, rows, jnp.where(strip == lower + 1, row_at, 0))
        value = jnp.where((row_ids >= first) & (row_ids < last), part[:rows], 0.0)
        left = jnp.where(col_ids >= col_at, value, 0.0)
        sums = [sums[0] + left, sums[1] + (value - left)]
    return sums


def add_below_kernel(offs, *refs):
    parts, quarters, (below, probe_band) = refs[:8], refs[8:12], refs[12:]
    rows, cols = below.shape[1:]
    sums = add_parts(offs, parts, 2, rows, cols)
    col = here()[1]
    for side in range(2):
        below[jnp.bitwise_xor(col, side)] = sums[side]
    total = (quarters[0][...] + quarters[1][...]) + (quarters[2][...] + quarters[3][...])
    band = probe_band.shape[0]
    probe_band[:, :cols] = total[:band]
    probe_band[:, cols:] = total[band:]


def add_own_kernel(offs, *refs):
    parts, own = refs[:8], refs[8]
    rows, cols = own.shape[1:]
    for strip in range(2):
        own[2 * strip], own[2 * strip + 1] = add_parts(offs, parts, strip, rows, cols)


def top_kernel(own, above, *outs):
    half, col, unused = here()
    mine = 2 * half + col
    for turn, out in zip(FOUR, outs):
        extra = jnp.where(half == turn // 2, above[turn % 2], 0.0)
        out[...] = own[jnp.bitwise_xor(mine, turn)] + extra


def join_kernel(*refs):
    probe, out, probe_out, sems = refs[4:]
    half, col, unused = here()
    mine = 2 * half + col
    pairs = [(ref, out.at[jnp.bitwise_xor(mine, turn)]) for turn, ref in zip(FOUR, refs)]
    for copy in fetch([(probe, probe_out), *pairs], sems):
        copy.wait()


SMEM = pl.BlockSpec(memory_space=pltpu.SMEM)
VMEM = pl.BlockSpec(memory_space=pltpu.VMEM)
HBM = pl.BlockSpec(memory_space=pltpu.HBM)
ANY = pl.BlockSpec(memory_space=pl.ANY)


def call(kernel, outs, scalars, arrays, flops, scratch=(), copies=0):
    outs, arrays = ([x if isinstance(x, tuple) else (x, VMEM) for x in xs] for xs in (outs, arrays))
    moved = sum(math.prod(x.shape) * x.dtype.itemsize for x, unused in [*arrays, *outs])
    scratch = [pltpu.VMEM(dims, jnp.float32) if isinstance(dims, tuple) else dims for dims in scratch]
    return pl.pallas_call(
        kernel,
        out_shape=[x for x, unused in outs],
        in_specs=[SMEM] * len(scalars) + [spec for unused, spec in arrays],
        out_specs=[spec for unused, spec in outs],
        scratch_shapes=scratch + [pltpu.SemaphoreType.DMA((copies,))] * (copies > 0),
        compiler_params=pltpu.CompilerParams(vmem_limit_bytes=VMEM_LIMIT),
        cost_estimate=pl.CostEstimate(flops=flops, bytes_accessed=moved, transcendentals=0),
    )(*scalars, *(pltpu.with_memory_space_constraint(x, pltpu.HBM) if spec is HBM else x for x, spec in arrays))


def shape(*dims):
    return jax.ShapeDtypeStruct(dims, jnp.float32)


def deal(values, axes, order):
    return [
        lax.ppermute(value, axes, [(k, k ^ turn) for k in range(len(order))]) if turn else value
        for turn, value in zip(order, values)
    ]


def sum_over(value, axis, size):
    step = 2
    while step < size:
        value = value + lax.ppermute(value, axis, [(k, k ^ step) for k in range(size)])
        step *= 2
    return value


def local(object_field, probe, offsets, slot_range, measured):
    width = probe.shape[-1]
    planes, rows, cols = 4, object_field.shape[2], object_field.shape[3]
    band = width // 4
    pairs = lax.axis_size("pair")
    half, col, core = (lax.axis_index(name) for name in PLANE)

    block = object_field.reshape(planes, rows, cols)
    *dealt, given = call(
        deal_kernel,
        [shape(rows + 8, cols)] * 4 + [shape(width, width)],
        (),
        ((block, HBM), (measured, HBM), (offsets, HBM)),
        0,
        [pltpu.SMEM(offsets.shape, offsets.dtype)],
        copies=6,
    )
    own = deal(dealt, PLANE[:2], FOUR)
    (lowest,) = call(lowest_kernel, [shape(2, rows, cols)], (), own, 0)
    lowest, given = lax.optimization_barrier((lowest, given))
    below = lax.ppermute(lowest, "pair", [(k, k - 1) for k in range(1, pairs)])
    taken = lax.ppermute(given, "half", [(0, 1), (1, 0)])

    turned = dict(zip(FOUR, own))
    offs = jnp.stack([turned[turn][rows : rows + 4, 0] for turn in range(4)]).astype(jnp.int32)
    others = lax.ppermute(offs, "core", [(0, 1), (1, 0)])
    offs = jnp.concatenate([jnp.where(core == 0, offs, others), jnp.where(core == 0, others, offs)], axis=1)
    split_at = jnp.where(half == 0, slot_range[0, 1], slot_range[0, 0])
    offs = jnp.concatenate([offs, jnp.full((1, offs.shape[1]), split_at, jnp.int32)], axis=0)
    scalars = (offs,)
    parts = call(
        pick_kernel,
        [shape(rows, cols)] * 8,
        scalars,
        (*own, below),
        32 * rows * width,
        [(planes, rows, cols), (8, rows, cols)],
    )
    tabs, factors, order = (jnp.asarray(table) for table in tables(width))
    probe, target, tabs = call(
        ready_kernel,
        [shape(*probe.shape), shape(width, width), jax.ShapeDtypeStruct(tabs.shape, tabs.dtype)],
        scalars,
        (taken, (probe, HBM), (measured, HBM), (tabs, HBM), (order, HBM)),
        12 * width**3,
        [(width, width), pltpu.VMEM(order.shape, order.dtype)],
        copies=4,
    )
    *grad, keep = call(
        position_kernel,
        [shape(rows + 8 * band, cols)] + [shape(rows, cols)] * 7 + [shape(4, 2 * band, cols)],
        scalars,
        (*deal(parts, PLANE, EIGHT), probe, target, tabs, factors),
        8 * 12 * width**3,
        [(8, rows, cols)] * 2 + [(8, 2 * band, cols)],
    )
    got = deal(grad, PLANE, BACK)
    quarters = call(pair_kernel, [shape(2 * band, cols)] * 4, (), (keep, got[0]), 4 * band * width)
    lower_sums, probe_band = call(
        add_below_kernel,
        [shape(2, rows, cols), shape(band, width)],
        scalars,
        (*got, *deal(quarters, PLANE[:2], FOUR)),
        32 * rows * width,
    )
    above = lax.ppermute(lower_sums, "pair", [(k, k + 1) for k in range(pairs - 1)])
    doubling = pairs > 1 and pairs & (pairs - 1) == 0
    if doubling:
        near = lax.ppermute(probe_band, "pair", [(k, k ^ 1) for k in range(pairs)])
    (sums,) = call(add_own_kernel, [shape(planes, rows, cols)], scalars, got, 64 * rows * width)
    sums = call(top_kernel, [shape(rows, cols)] * 4, (), (sums, above), planes * rows * cols)
    if doubling:
        *sums, near = lax.optimization_barrier((*sums, near))
        probe_band = sum_over(probe_band + near, "pair", pairs)
    else:
        probe_band = lax.psum(probe_band, "pair")
    sums = deal(sums, PLANE[:2], FOUR)
    probe_grad = lax.all_gather(probe_band, PLANE, axis=0, tiled=True)
    object_grad, probe_grad = call(
        join_kernel,
        [(shape(planes, rows, cols), HBM), (shape(*probe_grad.shape), HBM)],
        (),
        [(x, ANY) for x in (*sums, probe_grad)],
        0,
        copies=5,
    )
    return (object_grad.reshape(object_field.shape), probe_grad.reshape(probe.shape))


def solution(mesh):
    tile, grp = mesh.shape["tile"], mesh.shape["grp"]
    devices = mesh.devices.reshape(tile // 2, 2, 2, grp // 2)
    inner = Mesh(devices, ("pair", "half", "col", "core"))
    strip, cols = ("pair", "half"), ("col", "core")
    in_specs = (
        P(None, None, strip, cols),
        P(),
        P(strip, cols, None),
        P(strip, None),
        P(strip, cols, None, None),
    )
    out_specs = (P(None, None, strip, cols), P())
    return jax.shard_map(local, mesh=inner, in_specs=in_specs, out_specs=out_specs, check_vma=False)
```

```python
import functools
import math

import jax
import jax.numpy as jnp
import ml_dtypes
import numpy as np
from jax import lax
from jax.experimental import pallas as pl
from jax.experimental.pallas import tpu as pltpu
from jax.sharding import Mesh, PartitionSpec as P

GRAD_WEIGHT = 0.0625
PLANE = ("half", "col", "core")
EIGHT, BACK, FOUR = (1, 2, 4, 3, 5, 6, 7, 0), (1, 4, 2, 5, 3, 6, 7, 0), (2, 1, 3, 0)
VMEM_LIMIT = 24 * 1024 * 1024


def tables(width):
    half = width // 2
    index = np.arange(half, dtype=np.int64)
    scale = 1.0 / math.sqrt(width)
    far = np.exp(-2j * math.pi / half * (index[:, None] * index[None, :] % half)) * scale
    near = []
    for offset in (0, half):
        shift = index[:, None] - index[None, :] + offset
        near.append(np.exp(1j * (math.pi / width * (shift * shift % (2 * width)) - math.pi / 4.0)) * scale)
    products = []
    for matrix in ((near[0] + near[1]) / 2.0, (near[0] - near[1]) / 2.0, far):
        for imag in (matrix.imag, -matrix.imag):
            table = np.block([[matrix.real, imag], [-imag, matrix.real]])
            high = table.astype(ml_dtypes.bfloat16)
            low = (table - high.astype(np.float64)).astype(ml_dtypes.bfloat16)
            products.append(np.concatenate([high, low], axis=0))
    angle = -2.0 * math.pi / width * index
    twiddles = []
    for part in (np.cos(angle), np.sin(angle)):
        rows = np.broadcast_to(part[:, None], (half, half))
        twiddles.append(np.concatenate([rows, np.broadcast_to(part[None, :], (8, half))], axis=0))
    order = np.zeros((width, width))
    order[np.arange(width), np.concatenate([2 * index, 2 * index + 1])] = 1.0
    order = np.stack([order, order.T]).astype(ml_dtypes.bfloat16)
    return np.stack(products), np.stack(twiddles).astype(np.float32), order


def split(value):
    high = value.astype(jnp.bfloat16)
    low = (value - high.astype(jnp.float32)).astype(jnp.bfloat16)
    return high, low


def dot(left, right):
    return jnp.dot(left, right, preferred_element_type=jnp.float32)


PLUS, MINUS, FAR = 0, 2, 4


def times_right(re, im, table):
    width = table.shape[1]
    high, low = split(jnp.concatenate([re, im], axis=1))
    twice = dot(jnp.concatenate([high, low], axis=0), table[:width])
    count = re.shape[0]
    out = twice[:count] + (twice[count:] + dot(high, table[width:]))
    return out[:, : width // 2], out[:, width // 2 :]


def times_left(re, im, table):
    width = table.shape[1]
    high, low = split(jnp.concatenate([re, im], axis=0))
    twice = dot(table[...], high)
    out = twice[:width] + (twice[width:] + dot(table[:width], low))
    return out[: width // 2], out[width // 2 :]


def butterfly(first, second):
    return first + second, first - second


def halves(value, axis):
    half = value.shape[axis] // 2
    return (value[:half], value[half:]) if axis == 0 else (value[:, :half], value[:, half:])


def turn_by(re, im, cos, sin):
    return re * cos - im * sin, re * sin + im * cos


def propagate(re, im, tabs, conj):
    for axis in (1, 0):
        (plus_re, minus_re), (plus_im, minus_im) = (butterfly(*halves(x, axis)) for x in (re, im))
        times = times_right if axis else times_left
        pick = int(conj) if axis else 1 - int(conj)
        plus_re, plus_im = times(plus_re, plus_im, tabs.at[PLUS + pick])
        minus_re, minus_im = times(minus_re, minus_im, tabs.at[MINUS + pick])
        re = jnp.concatenate(butterfly(plus_re, minus_re), axis=axis)
        im = jnp.concatenate(butterfly(plus_im, minus_im), axis=axis)
    return re, im


def twiddle(factors, axis, width):
    half = factors.shape[2]
    if axis:
        return factors[0, half : half + 1], factors[1, half : half + 1]
    return tuple(jnp.concatenate([factors[k, :half]] * (width // half), axis=1) for k in range(2))


def to_far(re, im, tabs, factors):
    for axis in (1, 0):
        (even_re, odd_re), (even_im, odd_im) = (butterfly(*halves(x, axis)) for x in (re, im))
        odd_re, odd_im = turn_by(odd_re, odd_im, *twiddle(factors, axis, re.shape[1]))
        times, table = (times_right, tabs.at[FAR]) if axis else (times_left, tabs.at[FAR + 1])
        (even_re, even_im), (odd_re, odd_im) = times(even_re, even_im, table), times(odd_re, odd_im, table)
        re, im = jnp.concatenate([even_re, odd_re], axis=axis), jnp.concatenate([even_im, odd_im], axis=axis)
    return re, im


def from_far(re, im, tabs, factors):
    for axis in (0, 1):
        (even_re, odd_re), (even_im, odd_im) = halves(re, axis), halves(im, axis)
        times, table = (times_right, tabs.at[FAR + 1]) if axis else (times_left, tabs.at[FAR])
        (even_re, even_im), (odd_re, odd_im) = times(even_re, even_im, table), times(odd_re, odd_im, table)
        cos, sin = twiddle(factors, axis, re.shape[1])
        odd_re, odd_im = turn_by(odd_re, odd_im, cos, -sin)
        re = jnp.concatenate(butterfly(even_re, odd_re), axis=axis)
        im = jnp.concatenate(butterfly(even_im, odd_im), axis=axis)
    return re, im


def slot_of(half, col, core):
    return 2 * (2 * col + core) + half


def receivers():
    return [slot_of(half, col, core) for half in range(2) for col in range(2) for core in range(2)]


def slot_place(offs, mine, slot):
    lower = jnp.where(slot >= offs[4, 0], 1, 0)
    holder, at = jnp.bitwise_xor(2 * lower + slot // 4, mine), 2 * (slot % 4)
    return lower, offs[holder, at], offs[holder, at + 1]


def here():
    return tuple(lax.axis_index(name) for name in PLANE)


def fetch(pairs, sems):
    copies = [pltpu.make_async_copy(source, into, sems.at[k]) for k, (source, into) in enumerate(pairs)]
    for copy in copies:
        copy.start()
    return copies


def deal_kernel(block, measured, offsets_from, *refs):
    outs, given, offsets, sems = refs[:4], refs[4], refs[5], refs[6]
    half, col, unused = here()
    mine = 2 * half + col
    rows, cols = block.shape[1:]
    pairs = [(block.at[jnp.bitwise_xor(mine, turn)], out.at[pl.ds(0, rows)]) for turn, out in zip(FOUR, outs)]
    copies = fetch([(offsets_from, offsets), *pairs, (measured.at[0, 1 - half], given)], sems)
    copies[0].wait()
    lines = [jnp.full((1, cols), offsets[0, slot, axis], jnp.int32) for slot in range(2) for axis in range(2)]
    lines = jnp.concatenate(lines * 2, axis=0).astype(jnp.float32)
    for out in outs:
        out[rows:] = lines
    for copy in copies[1:]:
        copy.wait()


def lowest_kernel(*refs):
    gotten, out = dict(zip(FOUR, refs)), refs[4]
    rows = out.shape[1]
    half = here()[0]
    for turn in range(2):
        out[turn] = jnp.where(half == 0, gotten[turn][:rows], gotten[2 + turn][:rows])


def pick_kernel(offs, *refs):
    gotten, below, outs, (own, parts) = dict(zip(FOUR, refs)), refs[4], refs[5:13], refs[13:]
    rows, cols = outs[0].shape
    half, col, core = here()
    mine = 2 * half + col
    for turn in range(4):
        own[jnp.bitwise_xor(mine, turn)] = gotten[turn][:rows]
    row_ids = lax.broadcasted_iota(jnp.int32, (rows, cols), 0)
    col_ids = lax.broadcasted_iota(jnp.int32, (rows, cols), 1) + core * cols
    for place, slot in enumerate(receivers()):
        lower, row_at, col_at = slot_place(offs, mine, slot)
        upper_rows = row_ids >= row_at
        left_cols = col_ids >= col_at

        def merged(side, lower=lower, upper_rows=upper_rows):
            second = own[2 + side]
            top = jnp.where(lower == 1, second, own[side])
            bottom = jnp.where(lower == 1, below[jnp.bitwise_xor(col, side)], second)
            return jnp.where(upper_rows, top, bottom)

        parts[place] = jnp.where(left_cols, merged(0), merged(1))
    for turn, out in zip(EIGHT, outs):
        out[...] = parts[jnp.bitwise_xor(2 * mine + core, turn)]


def roll(value, rows, cols):
    return pltpu.roll(pltpu.roll(value, rows, 0), cols, 1)


def ready_kernel(offs, taken, probe_from, measured, tabs_from, order_from, probe, target, tabs, kept, order, sems):
    half, col, core = here()
    probe_copy, kept_copy, order_copy, tabs_copy = fetch(
        [(probe_from, probe), (measured.at[0, half], kept), (order_from, order), (tabs_from, tabs)], sems
    )
    slot = slot_of(half, col, core)
    lower, row_at, col_at = slot_place(offs, 2 * half + col, slot)
    probe_copy.wait()
    for part in range(2):
        probe[part] = roll(probe[part], row_at, col_at)
    kept_copy.wait()
    order_copy.wait()
    rest = jnp.where(lower == half, kept[...], taken[...])
    total = jnp.zeros_like(rest)
    for unused in range(3):
        part = rest.astype(jnp.bfloat16)
        rest = rest - part.astype(jnp.float32)
        total += dot(order[0], dot(part, order[1]).astype(jnp.bfloat16))
    target[...] = total
    tabs_copy.wait()


def position_kernel(offs, *refs):
    gotten, (probe, target, tabs, factors) = dict(zip(EIGHT, refs)), refs[8:12]
    outs, keep, (patch, grad, bands) = refs[12:20], refs[20], refs[21:]
    half, col, core = here()
    mine = 2 * half + col
    flat = 2 * mine + core
    unused, row_at, col_at = slot_place(offs, mine, slot_of(half, col, core))
    width = probe.shape[-1]
    lanes, band = width // 2, width // 4
    for turn in range(8):
        patch[jnp.bitwise_xor(flat, turn)] = gotten[turn][...]

    def load(plane):
        return jnp.concatenate([patch[2 * plane], patch[2 * plane + 1]], axis=1)

    def store(plane, value):
        grad[2 * plane] = value[:, :lanes]
        grad[2 * plane + 1] = value[:, lanes:]

    wave_re, wave_im = probe[0], probe[1]
    o0_re, o0_im, o1_re, o1_im = load(0), load(2), load(1), load(3)
    exit_re = wave_re * o0_re - wave_im * o0_im
    exit_im = wave_re * o0_im + wave_im * o0_re
    mid_re, mid_im = propagate(exit_re, exit_im, tabs, False)
    exit_re = mid_re * o1_re - mid_im * o1_im
    exit_im = mid_re * o1_im + mid_im * o1_re
    far_re, far_im = to_far(exit_re, exit_im, tabs, factors)
    excess = 2.0 * GRAD_WEIGHT * (far_re * far_re + far_im * far_im - target[...])
    back_re, back_im = from_far(excess * far_re, excess * far_im, tabs, factors)
    store(1, mid_re * back_re + mid_im * back_im)
    store(3, mid_re * back_im - mid_im * back_re)
    up_re = o1_re * back_re + o1_im * back_im
    up_im = o1_re * back_im - o1_im * back_re
    back_re, back_im = propagate(up_re, up_im, tabs, True)
    wave_re, wave_im = probe[0], probe[1]
    o0_re, o0_im = load(0), load(2)
    store(0, wave_re * back_re + wave_im * back_im)
    store(2, wave_re * back_im - wave_im * back_re)
    up_re = o0_re * back_re + o0_im * back_im
    up_im = o0_re * back_im - o0_im * back_re
    back_row, back_col = lax.rem(width - row_at, width), lax.rem(2 * width - col_at, width)
    for part, value in enumerate((up_re, up_im)):
        value = roll(value, back_row, back_col)
        for step in range(4):
            rows = value[step * band : (step + 1) * band]
            bands[4 * part + step, :band] = rows[:, :lanes]
            bands[4 * part + step, band:] = rows[:, lanes:]
    for turn, out in zip(BACK, outs):
        out[:width] = grad[jnp.bitwise_xor(flat, turn)]
    for part in range(4):
        keep[part] = bands[2 * part + core]
        start = width + 2 * band * part
        outs[0][start : start + 2 * band] = bands[2 * part + 1 - core]


def pair_kernel(keep, got, *outs):
    band = keep.shape[1]
    half, col, unused = here()
    first = got.shape[0] - 4 * band
    for turn, out in zip(FOUR, outs):
        part = jnp.bitwise_xor(2 * half + col, turn)
        out[...] = keep[part] + got[pl.ds(pl.multiple_of(first + band * part, band), band)]


def add_parts(offs, parts, strip, rows, cols):
    half, col, core = here()
    mine = 2 * half + col
    row_ids = lax.broadcasted_iota(jnp.int32, (rows, cols), 0)
    col_ids = lax.broadcasted_iota(jnp.int32, (rows, cols), 1) + core * cols
    sums = [jnp.zeros((rows, cols), jnp.float32)] * 2
    for turn, part in zip(BACK, parts):
        flat = jnp.bitwise_xor(2 * mine + core, turn)
        slot = slot_of(flat // 4, (flat // 2) % 2, flat % 2)
        lower, row_at, col_at = slot_place(offs, mine, slot)
        first = jnp.where(strip == lower, row_at, jnp.where(strip == lower + 1, 0, rows))
        last = jnp.where(strip == lower, rows, jnp.where(strip == lower + 1, row_at, 0))
        value = jnp.where((row_ids >= first) & (row_ids < last), part[:rows], 0.0)
        left = jnp.where(col_ids >= col_at, value, 0.0)
        sums = [sums[0] + left, sums[1] + (value - left)]
    return sums


def add_below_kernel(offs, *refs):
    parts, quarters, (below, probe_band) = refs[:8], refs[8:12], refs[12:]
    rows, cols = below.shape[1:]
    sums = add_parts(offs, parts, 2, rows, cols)
    col = here()[1]
    for side in range(2):
        below[jnp.bitwise_xor(col, side)] = sums[side]
    total = (quarters[0][...] + quarters[1][...]) + (quarters[2][...] + quarters[3][...])
    band = probe_band.shape[0]
    probe_band[:, :cols] = total[:band]
    probe_band[:, cols:] = total[band:]


def add_own_kernel(offs, *refs):
    parts, own = refs[:8], refs[8]
    rows, cols = own.shape[1:]
    for strip in range(2):
        own[2 * strip], own[2 * strip + 1] = add_parts(offs, parts, strip, rows, cols)


def top_kernel(own, above, *outs):
    half, col, unused = here()
    mine = 2 * half + col
    for turn, out in zip(FOUR, outs):
        extra = jnp.where(half == turn // 2, above[turn % 2], 0.0)
        out[...] = own[jnp.bitwise_xor(mine, turn)] + extra


def join_kernel(*refs):
    probe, out, probe_out, sems = refs[4:]
    half, col, unused = here()
    mine = 2 * half + col
    pairs = [(ref, out.at[jnp.bitwise_xor(mine, turn)]) for turn, ref in zip(FOUR, refs)]
    for copy in fetch([(probe, probe_out), *pairs], sems):
        copy.wait()


SMEM = pl.BlockSpec(memory_space=pltpu.SMEM)
VMEM = pl.BlockSpec(memory_space=pltpu.VMEM)
HBM = pl.BlockSpec(memory_space=pltpu.HBM)
ANY = pl.BlockSpec(memory_space=pl.ANY)


def call(kernel, outs, scalars, arrays, flops, scratch=(), copies=0):
    outs, arrays = ([x if isinstance(x, tuple) else (x, VMEM) for x in xs] for xs in (outs, arrays))
    moved = sum(math.prod(x.shape) * x.dtype.itemsize for x, unused in [*arrays, *outs])
    scratch = [pltpu.VMEM(dims, jnp.float32) if isinstance(dims, tuple) else dims for dims in scratch]
    return pl.pallas_call(
        kernel,
        out_shape=[x for x, unused in outs],
        in_specs=[SMEM] * len(scalars) + [spec for unused, spec in arrays],
        out_specs=[spec for unused, spec in outs],
        scratch_shapes=scratch + [pltpu.SemaphoreType.DMA((copies,))] * (copies > 0),
        compiler_params=pltpu.CompilerParams(vmem_limit_bytes=VMEM_LIMIT),
        cost_estimate=pl.CostEstimate(flops=flops, bytes_accessed=moved, transcendentals=0),
    )(*scalars, *(pltpu.with_memory_space_constraint(x, pltpu.HBM) if spec is HBM else x for x, spec in arrays))


def shape(*dims):
    return jax.ShapeDtypeStruct(dims, jnp.float32)


def deal(values, axes, order):
    count = math.prod(lax.axis_size(axis) for axis in axes)
    return [
        lax.ppermute(value, axes, [(k, k ^ turn) for k in range(count)]) if turn else value
        for turn, value in zip(order, values)
    ]


def sum_over(value, axis, size):
    step = 2
    while step < size:
        value = value + lax.ppermute(value, axis, [(k, k ^ step) for k in range(size)])
        step *= 2
    return value


def local(object_field, probe, offsets, slot_range, measured):
    width = probe.shape[-1]
    planes, rows, cols = 4, object_field.shape[2], object_field.shape[3]
    band = width // 4
    pairs = lax.axis_size("pair")
    half, col, core = (lax.axis_index(name) for name in PLANE)

    block = object_field.reshape(planes, rows, cols)
    *dealt, given = call(
        deal_kernel,
        [shape(rows + 8, cols)] * 4 + [shape(width, width)],
        (),
        ((block, HBM), (measured, HBM), (offsets, HBM)),
        0,
        [pltpu.SMEM(offsets.shape, offsets.dtype)],
        copies=6,
    )
    own = deal(dealt, PLANE[:2], FOUR)
    (lowest,) = call(lowest_kernel, [shape(2, rows, cols)], (), own, 0)
    lowest, given = lax.optimization_barrier((lowest, given))
    below = lax.ppermute(lowest, "pair", [(k, k - 1) for k in range(1, pairs)])
    taken = lax.ppermute(given, "half", [(0, 1), (1, 0)])

    turned = dict(zip(FOUR, own))
    offs = jnp.stack([turned[turn][rows : rows + 4, 0] for turn in range(4)]).astype(jnp.int32)
    others = lax.ppermute(offs, "core", [(0, 1), (1, 0)])
    offs = jnp.concatenate([jnp.where(core == 0, offs, others), jnp.where(core == 0, others, offs)], axis=1)
    split_at = jnp.where(half == 0, slot_range[0, 1], slot_range[0, 0])
    offs = jnp.concatenate([offs, jnp.full((1, offs.shape[1]), split_at, jnp.int32)], axis=0)
    scalars = (offs,)
    parts = call(
        pick_kernel,
        [shape(rows, cols)] * 8,
        scalars,
        (*own, below),
        32 * rows * width,
        [(planes, rows, cols), (8, rows, cols)],
    )
    tabs, factors, order = (jnp.asarray(table) for table in tables(width))
    probe, target, tabs = call(
        ready_kernel,
        [shape(*probe.shape), shape(width, width), jax.ShapeDtypeStruct(tabs.shape, tabs.dtype)],
        scalars,
        (taken, (probe, HBM), (measured, HBM), (tabs, HBM), (order, HBM)),
        12 * width**3,
        [(width, width), pltpu.VMEM(order.shape, order.dtype)],
        copies=4,
    )
    *grad, keep = call(
        position_kernel,
        [shape(rows + 8 * band, cols)] + [shape(rows, cols)] * 7 + [shape(4, 2 * band, cols)],
        scalars,
        (*deal(parts, PLANE, EIGHT), probe, target, tabs, factors),
        8 * 12 * width**3,
        [(8, rows, cols)] * 2 + [(8, 2 * band, cols)],
    )
    first = deal(grad[:1], PLANE, BACK)
    quarters = list(call(pair_kernel, [shape(2 * band, cols)] * 4, (), (keep, first[0]), 4 * band * width))
    far = BACK.index(6)
    grad[far], quarters[0] = lax.optimization_barrier((grad[far], quarters[0]))
    got = first + deal(grad[1:], PLANE, BACK[1:])
    lower_sums, probe_band = call(
        add_below_kernel,
        [shape(2, rows, cols), shape(band, width)],
        scalars,
        (*got, *deal(quarters, PLANE[:2], FOUR)),
        32 * rows * width,
    )
    above = lax.ppermute(lower_sums, "pair", [(k, k + 1) for k in range(pairs - 1)])
    doubling = pairs > 1 and pairs & (pairs - 1) == 0
    if doubling:
        near = lax.ppermute(probe_band, "pair", [(k, k ^ 1) for k in range(pairs)])
    (sums,) = call(add_own_kernel, [shape(planes, rows, cols)], scalars, got, 64 * rows * width)
    sums = call(top_kernel, [shape(rows, cols)] * 4, (), (sums, above), planes * rows * cols)
    if doubling:
        *sums, near = lax.optimization_barrier((*sums, near))
        probe_band = sum_over(probe_band + near, "pair", pairs)
    else:
        probe_band = lax.psum(probe_band, "pair")
    sums = deal(sums, PLANE[:2], FOUR)
    probe_grad = lax.all_gather(probe_band, PLANE, axis=0, tiled=True)
    object_grad, probe_grad = call(
        join_kernel,
        [(shape(planes, rows, cols), HBM), (shape(*probe_grad.shape), HBM)],
        (),
        [(x, ANY) for x in (*sums, probe_grad)],
        0,
        copies=5,
    )
    return (object_grad.reshape(object_field.shape), probe_grad.reshape(probe.shape))


def solution(mesh):
    tile, grp = mesh.shape["tile"], mesh.shape["grp"]
    devices = mesh.devices.reshape(tile // 2, 2, 2, grp // 2)
    inner = Mesh(devices, ("pair", "half", "col", "core"))
    strip, cols = ("pair", "half"), ("col", "core")
    in_specs = (
        P(None, None, strip, cols),
        P(),
        P(strip, cols, None),
        P(strip, None),
        P(strip, cols, None, None),
    )
    out_specs = (P(None, None, strip, cols), P())
    return jax.shard_map(local, mesh=inner, in_specs=in_specs, out_specs=out_specs, check_vma=False)
```

```python
import functools
import math

import jax
import jax.numpy as jnp
import ml_dtypes
import numpy as np
from jax import lax
from jax.experimental import pallas as pl
from jax.experimental.pallas import tpu as pltpu
from jax.sharding import Mesh, PartitionSpec as P

GRAD_WEIGHT = 0.0625
PLANE = ("half", "col", "core")
EIGHT, BACK, FOUR = (2, 4, 3, 5, 6, 7, 1, 0), (1, 4, 2, 5, 3, 6, 7, 0), (2, 1, 3, 0)
VMEM_LIMIT = 24 * 1024 * 1024


def tables(width):
    half = width // 2
    index = np.arange(half, dtype=np.int64)
    scale = 1.0 / math.sqrt(width)
    far = np.exp(-2j * math.pi / half * (index[:, None] * index[None, :] % half)) * scale
    near = []
    for offset in (0, half):
        shift = index[:, None] - index[None, :] + offset
        near.append(np.exp(1j * (math.pi / width * (shift * shift % (2 * width)) - math.pi / 4.0)) * scale)
    products = []
    for matrix in ((near[0] + near[1]) / 2.0, (near[0] - near[1]) / 2.0, far):
        for imag in (matrix.imag, -matrix.imag):
            table = np.block([[matrix.real, imag], [-imag, matrix.real]])
            high = table.astype(ml_dtypes.bfloat16)
            low = (table - high.astype(np.float64)).astype(ml_dtypes.bfloat16)
            products.append(np.concatenate([high, low], axis=0))
    angle = -2.0 * math.pi / width * index
    twiddles = []
    for part in (np.cos(angle), np.sin(angle)):
        rows = np.broadcast_to(part[:, None], (half, half))
        twiddles.append(np.concatenate([rows, np.broadcast_to(part[None, :], (8, half))], axis=0))
    order = np.zeros((width, width))
    order[np.arange(width), np.concatenate([2 * index, 2 * index + 1])] = 1.0
    order = np.stack([order, order.T]).astype(ml_dtypes.bfloat16)
    return np.stack(products), np.stack(twiddles).astype(np.float32), order


def split(value):
    high = value.astype(jnp.bfloat16)
    low = (value - high.astype(jnp.float32)).astype(jnp.bfloat16)
    return high, low


def dot(left, right):
    return jnp.dot(left, right, preferred_element_type=jnp.float32)


PLUS, MINUS, FAR = 0, 2, 4


def times_right(re, im, table):
    width = table.shape[1]
    high, low = split(jnp.concatenate([re, im], axis=1))
    twice = dot(jnp.concatenate([high, low], axis=0), table[:width])
    count = re.shape[0]
    out = twice[:count] + (twice[count:] + dot(high, table[width:]))
    return out[:, : width // 2], out[:, width // 2 :]


def times_left(re, im, table):
    width = table.shape[1]
    high, low = split(jnp.concatenate([re, im], axis=0))
    twice = dot(table[...], high)
    out = twice[:width] + (twice[width:] + dot(table[:width], low))
    return out[: width // 2], out[width // 2 :]


def butterfly(first, second):
    return first + second, first - second


def halves(value, axis):
    half = value.shape[axis] // 2
    return (value[:half], value[half:]) if axis == 0 else (value[:, :half], value[:, half:])


def turn_by(re, im, cos, sin):
    return re * cos - im * sin, re * sin + im * cos


def propagate(re, im, tabs, conj):
    for axis in (1, 0):
        (plus_re, minus_re), (plus_im, minus_im) = (butterfly(*halves(x, axis)) for x in (re, im))
        times = times_right if axis else times_left
        pick = int(conj) if axis else 1 - int(conj)
        plus_re, plus_im = times(plus_re, plus_im, tabs.at[PLUS + pick])
        minus_re, minus_im = times(minus_re, minus_im, tabs.at[MINUS + pick])
        re = jnp.concatenate(butterfly(plus_re, minus_re), axis=axis)
        im = jnp.concatenate(butterfly(plus_im, minus_im), axis=axis)
    return re, im


def twiddle(factors, axis, width):
    half = factors.shape[2]
    if axis:
        return factors[0, half : half + 1], factors[1, half : half + 1]
    return tuple(jnp.concatenate([factors[k, :half]] * (width // half), axis=1) for k in range(2))


def to_far(re, im, tabs, factors):
    for axis in (1, 0):
        (even_re, odd_re), (even_im, odd_im) = (butterfly(*halves(x, axis)) for x in (re, im))
        odd_re, odd_im = turn_by(odd_re, odd_im, *twiddle(factors, axis, re.shape[1]))
        times, table = (times_right, tabs.at[FAR]) if axis else (times_left, tabs.at[FAR + 1])
        (even_re, even_im), (odd_re, odd_im) = times(even_re, even_im, table), times(odd_re, odd_im, table)
        re, im = jnp.concatenate([even_re, odd_re], axis=axis), jnp.concatenate([even_im, odd_im], axis=axis)
    return re, im


def from_far(re, im, tabs, factors):
    for axis in (0, 1):
        (even_re, odd_re), (even_im, odd_im) = halves(re, axis), halves(im, axis)
        times, table = (times_right, tabs.at[FAR + 1]) if axis else (times_left, tabs.at[FAR])
        (even_re, even_im), (odd_re, odd_im) = times(even_re, even_im, table), times(odd_re, odd_im, table)
        cos, sin = twiddle(factors, axis, re.shape[1])
        odd_re, odd_im = turn_by(odd_re, odd_im, cos, -sin)
        re = jnp.concatenate(butterfly(even_re, odd_re), axis=axis)
        im = jnp.concatenate(butterfly(even_im, odd_im), axis=axis)
    return re, im


def slot_of(half, col, core):
    return 2 * (2 * col + core) + half


def receivers():
    return [slot_of(half, col, core) for half in range(2) for col in range(2) for core in range(2)]


def slot_place(offs, mine, slot):
    lower = jnp.where(slot >= offs[4, 0], 1, 0)
    holder, at = jnp.bitwise_xor(2 * lower + slot // 4, mine), 2 * (slot % 4)
    return lower, offs[holder, at], offs[holder, at + 1]


def here():
    return tuple(lax.axis_index(name) for name in PLANE)


def fetch(pairs, sems):
    copies = [pltpu.make_async_copy(source, into, sems.at[k]) for k, (source, into) in enumerate(pairs)]
    for copy in copies:
        copy.start()
    return copies


def deal_kernel(block, measured, offsets_from, *refs):
    outs, given, offsets, sems = refs[:4], refs[4], refs[5], refs[6]
    half, col, unused = here()
    mine = 2 * half + col
    rows, cols = block.shape[1:]
    pairs = [(block.at[jnp.bitwise_xor(mine, turn)], out.at[pl.ds(0, rows)]) for turn, out in zip(FOUR, outs)]
    copies = fetch([(offsets_from, offsets), *pairs, (measured.at[0, 1 - half], given)], sems)
    copies[0].wait()
    lines = [jnp.full((1, cols), offsets[0, slot, axis], jnp.int32) for slot in range(2) for axis in range(2)]
    lines = jnp.concatenate(lines * 2, axis=0).astype(jnp.float32)
    for out in outs:
        out[rows:] = lines
    for copy in copies[1:]:
        copy.wait()


def lowest_kernel(*refs):
    gotten, out = dict(zip(FOUR, refs)), refs[4]
    rows = out.shape[1]
    half = here()[0]
    for turn in range(2):
        out[turn] = jnp.where(half == 0, gotten[turn][:rows], gotten[2 + turn][:rows])


def pick_kernel(offs, *refs):
    gotten, below, outs, (own, parts) = dict(zip(FOUR, refs)), refs[4], refs[5:13], refs[13:]
    rows, cols = outs[0].shape
    half, col, core = here()
    mine = 2 * half + col
    for turn in range(4):
        own[jnp.bitwise_xor(mine, turn)] = gotten[turn][:rows]
    row_ids = lax.broadcasted_iota(jnp.int32, (rows, cols), 0)
    col_ids = lax.broadcasted_iota(jnp.int32, (rows, cols), 1) + core * cols
    for place, slot in enumerate(receivers()):
        lower, row_at, col_at = slot_place(offs, mine, slot)
        upper_rows = row_ids >= row_at
        left_cols = col_ids >= col_at

        def merged(side, lower=lower, upper_rows=upper_rows):
            second = own[2 + side]
            top = jnp.where(lower == 1, second, own[side])
            bottom = jnp.where(lower == 1, below[jnp.bitwise_xor(col, side)], second)
            return jnp.where(upper_rows, top, bottom)

        parts[place] = jnp.where(left_cols, merged(0), merged(1))
    for turn, out in zip(EIGHT, outs):
        out[...] = parts[jnp.bitwise_xor(2 * mine + core, turn)]


def roll(value, rows, cols):
    return pltpu.roll(pltpu.roll(value, rows, 0), cols, 1)


def ready_kernel(offs, taken, probe_from, measured, tabs_from, order_from, probe, target, tabs, kept, order, sems):
    half, col, core = here()
    probe_copy, kept_copy, order_copy, tabs_copy = fetch(
        [(probe_from, probe), (measured.at[0, half], kept), (order_from, order), (tabs_from, tabs)], sems
    )
    slot = slot_of(half, col, core)
    lower, row_at, col_at = slot_place(offs, 2 * half + col, slot)
    probe_copy.wait()
    for part in range(2):
        probe[part] = roll(probe[part], row_at, col_at)
    kept_copy.wait()
    order_copy.wait()
    rest = jnp.where(lower == half, kept[...], taken[...])
    total = jnp.zeros_like(rest)
    for unused in range(3):
        part = rest.astype(jnp.bfloat16)
        rest = rest - part.astype(jnp.float32)
        total += dot(order[0], dot(part, order[1]).astype(jnp.bfloat16))
    target[...] = total
    tabs_copy.wait()


def position_kernel(offs, *refs):
    gotten, (probe, target, tabs, factors) = dict(zip(EIGHT, refs)), refs[8:12]
    outs, keep, (patch, grad, bands) = refs[12:20], refs[20], refs[21:]
    half, col, core = here()
    mine = 2 * half + col
    flat = 2 * mine + core
    unused, row_at, col_at = slot_place(offs, mine, slot_of(half, col, core))
    width = probe.shape[-1]
    lanes, band = width // 2, width // 4
    for turn in range(8):
        patch[jnp.bitwise_xor(flat, turn)] = gotten[turn][...]

    def load(plane):
        return jnp.concatenate([patch[2 * plane], patch[2 * plane + 1]], axis=1)

    def store(plane, value):
        grad[2 * plane] = value[:, :lanes]
        grad[2 * plane + 1] = value[:, lanes:]

    wave_re, wave_im = probe[0], probe[1]
    o0_re, o0_im, o1_re, o1_im = load(0), load(2), load(1), load(3)
    exit_re = wave_re * o0_re - wave_im * o0_im
    exit_im = wave_re * o0_im + wave_im * o0_re
    mid_re, mid_im = propagate(exit_re, exit_im, tabs, False)
    exit_re = mid_re * o1_re - mid_im * o1_im
    exit_im = mid_re * o1_im + mid_im * o1_re
    far_re, far_im = to_far(exit_re, exit_im, tabs, factors)
    excess = 2.0 * GRAD_WEIGHT * (far_re * far_re + far_im * far_im - target[...])
    back_re, back_im = from_far(excess * far_re, excess * far_im, tabs, factors)
    store(1, mid_re * back_re + mid_im * back_im)
    store(3, mid_re * back_im - mid_im * back_re)
    up_re = o1_re * back_re + o1_im * back_im
    up_im = o1_re * back_im - o1_im * back_re
    back_re, back_im = propagate(up_re, up_im, tabs, True)
    wave_re, wave_im = probe[0], probe[1]
    o0_re, o0_im = load(0), load(2)
    store(0, wave_re * back_re + wave_im * back_im)
    store(2, wave_re * back_im - wave_im * back_re)
    up_re = o0_re * back_re + o0_im * back_im
    up_im = o0_re * back_im - o0_im * back_re
    back_row, back_col = lax.rem(width - row_at, width), lax.rem(2 * width - col_at, width)
    for part, value in enumerate((up_re, up_im)):
        value = roll(value, back_row, back_col)
        for step in range(4):
            rows = value[step * band : (step + 1) * band]
            bands[4 * part + step, :band] = rows[:, :lanes]
            bands[4 * part + step, band:] = rows[:, lanes:]
    for turn, out in zip(BACK, outs):
        out[:width] = grad[jnp.bitwise_xor(flat, turn)]
    for part in range(4):
        keep[part] = bands[2 * part + core]
        start = width + 2 * band * part
        outs[0][start : start + 2 * band] = bands[2 * part + 1 - core]


def pair_kernel(keep, got, *outs):
    band = keep.shape[1]
    half, col, unused = here()
    first = got.shape[0] - 4 * band
    for turn, out in zip(FOUR, outs):
        part = jnp.bitwise_xor(2 * half + col, turn)
        out[...] = keep[part] + got[pl.ds(pl.multiple_of(first + band * part, band), band)]


def add_parts(offs, parts, strip, rows, cols):
    half, col, core = here()
    mine = 2 * half + col
    row_ids = lax.broadcasted_iota(jnp.int32, (rows, cols), 0)
    col_ids = lax.broadcasted_iota(jnp.int32, (rows, cols), 1) + core * cols
    sums = [jnp.zeros((rows, cols), jnp.float32)] * 2
    for turn, part in zip(BACK, parts):
        flat = jnp.bitwise_xor(2 * mine + core, turn)
        slot = slot_of(flat // 4, (flat // 2) % 2, flat % 2)
        lower, row_at, col_at = slot_place(offs, mine, slot)
        first = jnp.where(strip == lower, row_at, jnp.where(strip == lower + 1, 0, rows))
        last = jnp.where(strip == lower, rows, jnp.where(strip == lower + 1, row_at, 0))
        value = jnp.where((row_ids >= first) & (row_ids < last), part[:rows], 0.0)
        left = jnp.where(col_ids >= col_at, value, 0.0)
        sums = [sums[0] + left, sums[1] + (value - left)]
    return sums


def add_below_kernel(offs, *refs):
    parts, quarters, (below, probe_band) = refs[:8], refs[8:12], refs[12:]
    rows, cols = below.shape[1:]
    sums = add_parts(offs, parts, 2, rows, cols)
    col = here()[1]
    for side in range(2):
        below[jnp.bitwise_xor(col, side)] = sums[side]
    total = (quarters[0][...] + quarters[1][...]) + (quarters[2][...] + quarters[3][...])
    band = probe_band.shape[0]
    probe_band[:, :cols] = total[:band]
    probe_band[:, cols:] = total[band:]


def add_own_kernel(offs, *refs):
    parts, own = refs[:8], refs[8]
    rows, cols = own.shape[1:]
    for strip in range(2):
        own[2 * strip], own[2 * strip + 1] = add_parts(offs, parts, strip, rows, cols)


def top_kernel(own, above, *outs):
    half, col, unused = here()
    mine = 2 * half + col
    for turn, out in zip(FOUR, outs):
        extra = jnp.where(half == turn // 2, above[turn % 2], 0.0)
        out[...] = own[jnp.bitwise_xor(mine, turn)] + extra


def join_kernel(*refs):
    halves, (out, probe_out, sems) = refs[4:6], refs[6:]
    half, col, core = here()
    mine = 2 * half + col
    pairs = [(ref, out.at[jnp.bitwise_xor(mine, turn)]) for turn, ref in zip(FOUR, refs)]
    band = halves[0].shape[1]
    for side, bands in zip((core, 1 - core), halves):
        for part in range(4):
            start = pl.multiple_of(band * (2 * part + side), band)
            pairs.append((bands.at[part], probe_out.at[pl.ds(start, band)]))
    for copy in fetch(pairs, sems):
        copy.wait()


SMEM = pl.BlockSpec(memory_space=pltpu.SMEM)
VMEM = pl.BlockSpec(memory_space=pltpu.VMEM)
HBM = pl.BlockSpec(memory_space=pltpu.HBM)
ANY = pl.BlockSpec(memory_space=pl.ANY)


def call(kernel, outs, scalars, arrays, flops, scratch=(), copies=0):
    outs, arrays = ([x if isinstance(x, tuple) else (x, VMEM) for x in xs] for xs in (outs, arrays))
    moved = sum(math.prod(x.shape) * x.dtype.itemsize for x, unused in [*arrays, *outs])
    scratch = [pltpu.VMEM(dims, jnp.float32) if isinstance(dims, tuple) else dims for dims in scratch]
    return pl.pallas_call(
        kernel,
        out_shape=[x for x, unused in outs],
        in_specs=[SMEM] * len(scalars) + [spec for unused, spec in arrays],
        out_specs=[spec for unused, spec in outs],
        scratch_shapes=scratch + [pltpu.SemaphoreType.DMA((copies,))] * (copies > 0),
        compiler_params=pltpu.CompilerParams(vmem_limit_bytes=VMEM_LIMIT),
        cost_estimate=pl.CostEstimate(flops=flops, bytes_accessed=moved, transcendentals=0),
    )(*scalars, *(pltpu.with_memory_space_constraint(x, pltpu.HBM) if spec is HBM else x for x, spec in arrays))


def shape(*dims):
    return jax.ShapeDtypeStruct(dims, jnp.float32)


def deal(values, axes, order):
    return [
        lax.ppermute(value, axes, [(k, k ^ turn) for k in range(len(order))]) if turn else value
        for turn, value in zip(order, values)
    ]


def sum_over(value, axis, size):
    step = 2
    while step < size:
        value = value + lax.ppermute(value, axis, [(k, k ^ step) for k in range(size)])
        step *= 2
    return value


def local(object_field, probe, offsets, slot_range, measured):
    width = probe.shape[-1]
    planes, rows, cols = 4, object_field.shape[2], object_field.shape[3]
    band = width // 4
    pairs = lax.axis_size("pair")
    half, col, core = (lax.axis_index(name) for name in PLANE)

    block = object_field.reshape(planes, rows, cols)
    *dealt, given = call(
        deal_kernel,
        [shape(rows + 8, cols)] * 4 + [shape(width, width)],
        (),
        ((block, HBM), (measured, HBM), (offsets, HBM)),
        0,
        [pltpu.SMEM(offsets.shape, offsets.dtype)],
        copies=6,
    )
    own = deal(dealt, PLANE[:2], FOUR)
    (lowest,) = call(lowest_kernel, [shape(2, rows, cols)], (), own, 0)
    lowest, given = lax.optimization_barrier((lowest, given))
    below = lax.ppermute(lowest, "pair", [(k, k - 1) for k in range(1, pairs)])
    taken = lax.ppermute(given, "half", [(0, 1), (1, 0)])

    turned = dict(zip(FOUR, own))
    offs = jnp.stack([turned[turn][rows : rows + 4, 0] for turn in range(4)]).astype(jnp.int32)
    others = lax.ppermute(offs, "core", [(0, 1), (1, 0)])
    offs = jnp.concatenate([jnp.where(core == 0, offs, others), jnp.where(core == 0, others, offs)], axis=1)
    split_at = jnp.where(half == 0, slot_range[0, 1], slot_range[0, 0])
    offs = jnp.concatenate([offs, jnp.full((1, offs.shape[1]), split_at, jnp.int32)], axis=0)
    scalars = (offs,)
    parts = call(
        pick_kernel,
        [shape(rows, cols)] * 8,
        scalars,
        (*own, below),
        32 * rows * width,
        [(planes, rows, cols), (8, rows, cols)],
    )
    tabs, factors, order = (jnp.asarray(table) for table in tables(width))
    probe, target, tabs = call(
        ready_kernel,
        [shape(*probe.shape), shape(width, width), jax.ShapeDtypeStruct(tabs.shape, tabs.dtype)],
        scalars,
        (taken, (probe, HBM), (measured, HBM), (tabs, HBM), (order, HBM)),
        12 * width**3,
        [(width, width), pltpu.VMEM(order.shape, order.dtype)],
        copies=4,
    )
    *grad, keep = call(
        position_kernel,
        [shape(rows + 8 * band, cols)] + [shape(rows, cols)] * 7 + [shape(4, 2 * band, cols)],
        scalars,
        (*deal(parts, PLANE, EIGHT), probe, target, tabs, factors),
        8 * 12 * width**3,
        [(8, rows, cols)] * 2 + [(8, 2 * band, cols)],
    )
    got = deal(grad, PLANE, BACK)
    quarters = call(pair_kernel, [shape(2 * band, cols)] * 4, (), (keep, got[0]), 4 * band * width)
    lower_sums, probe_band = call(
        add_below_kernel,
        [shape(2, rows, cols), shape(band, width)],
        scalars,
        (*got, *deal(quarters, PLANE[:2], FOUR)),
        32 * rows * width,
    )
    above = lax.ppermute(lower_sums, "pair", [(k, k + 1) for k in range(pairs - 1)])
    doubling = pairs > 1 and pairs & (pairs - 1) == 0
    if doubling:
        near = lax.ppermute(probe_band, "pair", [(k, k ^ 1) for k in range(pairs)])
    (sums,) = call(add_own_kernel, [shape(planes, rows, cols)], scalars, got, 64 * rows * width)
    sums = call(top_kernel, [shape(rows, cols)] * 4, (), (sums, above), planes * rows * cols)
    if doubling:
        *sums, near = lax.optimization_barrier((*sums, near))
        probe_band = sum_over(probe_band + near, "pair", pairs)
    else:
        probe_band = lax.psum(probe_band, "pair")
    sums = deal(sums, PLANE[:2], FOUR)
    bands = lax.all_gather(probe_band, PLANE[:2], axis=0)
    others = lax.ppermute(bands, "core", [(0, 1), (1, 0)])
    object_grad, probe_grad = call(
        join_kernel,
        [(shape(planes, rows, cols), HBM), (shape(8 * band, width), HBM)],
        (),
        [(x, ANY) for x in (*sums, bands, others)],
        0,
        copies=12,
    )
    return (object_grad.reshape(object_field.shape), probe_grad.reshape(probe.shape))


def solution(mesh):
    tile, grp = mesh.shape["tile"], mesh.shape["grp"]
    devices = mesh.devices.reshape(tile // 2, 2, 2, grp // 2)
    inner = Mesh(devices, ("pair", "half", "col", "core"))
    strip, cols = ("pair", "half"), ("col", "core")
    in_specs = (
        P(None, None, strip, cols),
        P(),
        P(strip, cols, None),
        P(strip, None),
        P(strip, cols, None, None),
    )
    out_specs = (P(None, None, strip, cols), P())
    return jax.shard_map(local, mesh=inner, in_specs=in_specs, out_specs=out_specs, check_vma=False)
```

```python
import functools
import math

import jax
import jax.numpy as jnp
import ml_dtypes
import numpy as np
from jax import lax
from jax.experimental import pallas as pl
from jax.experimental.pallas import tpu as pltpu
from jax.sharding import Mesh, PartitionSpec as P

GRAD_WEIGHT = 0.0625
PLANE = ("half", "col", "core")
EIGHT, BACK, FOUR = (2, 4, 3, 5, 6, 7, 1, 0), (1, 4, 2, 5, 3, 6, 7, 0), (2, 1, 3, 0)
VMEM_LIMIT = 24 * 1024 * 1024


def tables(width):
    half = width // 2
    index = np.arange(half, dtype=np.int64)
    scale = 1.0 / math.sqrt(width)
    far = np.exp(-2j * math.pi / half * (index[:, None] * index[None, :] % half)) * scale
    near = []
    for offset in (0, half):
        shift = index[:, None] - index[None, :] + offset
        near.append(np.exp(1j * (math.pi / width * (shift * shift % (2 * width)) - math.pi / 4.0)) * scale)
    products = []
    for matrix in ((near[0] + near[1]) / 2.0, (near[0] - near[1]) / 2.0, far):
        for imag in (matrix.imag, -matrix.imag):
            table = np.block([[matrix.real, imag], [-imag, matrix.real]])
            high = table.astype(ml_dtypes.bfloat16)
            low = (table - high.astype(np.float64)).astype(ml_dtypes.bfloat16)
            products.append(np.concatenate([high, low], axis=0))
    angle = -2.0 * math.pi / width * index
    twiddles = []
    for part in (np.cos(angle), np.sin(angle)):
        rows = np.broadcast_to(part[:, None], (half, half))
        twiddles.append(np.concatenate([rows, np.broadcast_to(part[None, :], (8, half))], axis=0))
    order = np.zeros((width, width))
    order[np.arange(width), np.concatenate([2 * index, 2 * index + 1])] = 1.0
    order = np.stack([order, order.T]).astype(ml_dtypes.bfloat16)
    return np.stack(products), np.stack(twiddles).astype(np.float32), order


def split(value):
    high = value.astype(jnp.bfloat16)
    low = (value - high.astype(jnp.float32)).astype(jnp.bfloat16)
    return high, low


def dot(left, right):
    return jnp.dot(left, right, preferred_element_type=jnp.float32)


PLUS, MINUS, FAR = 0, 2, 4


def times_right(re, im, table):
    width = table.shape[1]
    high, low = split(jnp.concatenate([re, im], axis=1))
    twice = dot(jnp.concatenate([high, low], axis=0), table[:width])
    count = re.shape[0]
    out = twice[:count] + (twice[count:] + dot(high, table[width:]))
    return out[:, : width // 2], out[:, width // 2 :]


def times_left(re, im, table):
    width = table.shape[1]
    high, low = split(jnp.concatenate([re, im], axis=0))
    twice = dot(table[...], high)
    out = twice[:width] + (twice[width:] + dot(table[:width], low))
    return out[: width // 2], out[width // 2 :]


def butterfly(first, second):
    return first + second, first - second


def halves(value, axis):
    half = value.shape[axis] // 2
    return (value[:half], value[half:]) if axis == 0 else (value[:, :half], value[:, half:])


def turn_by(re, im, cos, sin):
    return re * cos - im * sin, re * sin + im * cos


def propagate(re, im, tabs, conj):
    for axis in (1, 0):
        (plus_re, minus_re), (plus_im, minus_im) = (butterfly(*halves(x, axis)) for x in (re, im))
        times = times_right if axis else times_left
        pick = int(conj) if axis else 1 - int(conj)
        plus_re, plus_im = times(plus_re, plus_im, tabs.at[PLUS + pick])
        minus_re, minus_im = times(minus_re, minus_im, tabs.at[MINUS + pick])
        re = jnp.concatenate(butterfly(plus_re, minus_re), axis=axis)
        im = jnp.concatenate(butterfly(plus_im, minus_im), axis=axis)
    return re, im


def twiddle(factors, axis, width):
    half = factors.shape[2]
    if axis:
        return factors[0, half : half + 1], factors[1, half : half + 1]
    return tuple(jnp.concatenate([factors[k, :half]] * (width // half), axis=1) for k in range(2))


def to_far(re, im, tabs, factors):
    for axis in (1, 0):
        (even_re, odd_re), (even_im, odd_im) = (butterfly(*halves(x, axis)) for x in (re, im))
        odd_re, odd_im = turn_by(odd_re, odd_im, *twiddle(factors, axis, re.shape[1]))
        times, table = (times_right, tabs.at[FAR]) if axis else (times_left, tabs.at[FAR + 1])
        (even_re, even_im), (odd_re, odd_im) = times(even_re, even_im, table), times(odd_re, odd_im, table)
        re, im = jnp.concatenate([even_re, odd_re], axis=axis), jnp.concatenate([even_im, odd_im], axis=axis)
    return re, im


def from_far(re, im, tabs, factors):
    for axis in (0, 1):
        (even_re, odd_re), (even_im, odd_im) = halves(re, axis), halves(im, axis)
        times, table = (times_right, tabs.at[FAR + 1]) if axis else (times_left, tabs.at[FAR])
        (even_re, even_im), (odd_re, odd_im) = times(even_re, even_im, table), times(odd_re, odd_im, table)
        cos, sin = twiddle(factors, axis, re.shape[1])
        odd_re, odd_im = turn_by(odd_re, odd_im, cos, -sin)
        re = jnp.concatenate(butterfly(even_re, odd_re), axis=axis)
        im = jnp.concatenate(butterfly(even_im, odd_im), axis=axis)
    return re, im


def slot_of(half, col, core):
    return 2 * (2 * col + core) + half


def receivers():
    return [slot_of(half, col, core) for half in range(2) for col in range(2) for core in range(2)]


def slot_place(offs, mine, slot):
    lower = jnp.where(slot >= offs[4, 0], 1, 0)
    holder, at = jnp.bitwise_xor(2 * lower + slot // 4, mine), 2 * (slot % 4)
    return lower, offs[holder, at], offs[holder, at + 1]


def here():
    return tuple(lax.axis_index(name) for name in PLANE)


def fetch(pairs, sems):
    copies = [pltpu.make_async_copy(source, into, sems.at[k]) for k, (source, into) in enumerate(pairs)]
    for copy in copies:
        copy.start()
    return copies


def deal_kernel(block, measured, offsets_from, *refs):
    outs, given, offsets, sems = refs[:4], refs[4], refs[5], refs[6]
    half, col, unused = here()
    mine = 2 * half + col
    rows, cols = block.shape[1:]
    pairs = [(block.at[jnp.bitwise_xor(mine, turn)], out.at[pl.ds(0, rows)]) for turn, out in zip(FOUR, outs)]
    copies = fetch([(offsets_from, offsets), *pairs, (measured.at[0, 1 - half], given)], sems)
    copies[0].wait()
    lines = [jnp.full((1, cols), offsets[0, slot, axis], jnp.int32) for slot in range(2) for axis in range(2)]
    lines = jnp.concatenate(lines * 2, axis=0).astype(jnp.float32)
    for out in outs:
        out[rows:] = lines
    for copy in copies[1:]:
        copy.wait()


def lowest_kernel(*refs):
    gotten, out = dict(zip(FOUR, refs)), refs[4]
    rows = out.shape[1]
    half = here()[0]
    for turn in range(2):
        out[turn] = jnp.where(half == 0, gotten[turn][:rows], gotten[2 + turn][:rows])


def pick_kernel(offs, *refs):
    gotten, below, outs, (own, parts) = dict(zip(FOUR, refs)), refs[4], refs[5:13], refs[13:]
    rows, cols = outs[0].shape
    half, col, core = here()
    mine = 2 * half + col
    for turn in range(4):
        own[jnp.bitwise_xor(mine, turn)] = gotten[turn][:rows]
    row_ids = lax.broadcasted_iota(jnp.int32, (rows, cols), 0)
    col_ids = lax.broadcasted_iota(jnp.int32, (rows, cols), 1) + core * cols
    for place, slot in enumerate(receivers()):
        lower, row_at, col_at = slot_place(offs, mine, slot)
        upper_rows = row_ids >= row_at
        left_cols = col_ids >= col_at

        def merged(side, lower=lower, upper_rows=upper_rows):
            second = own[2 + side]
            top = jnp.where(lower == 1, second, own[side])
            bottom = jnp.where(lower == 1, below[jnp.bitwise_xor(col, side)], second)
            return jnp.where(upper_rows, top, bottom)

        parts[place] = jnp.where(left_cols, merged(0), merged(1))
    for turn, out in zip(EIGHT, outs):
        out[...] = parts[jnp.bitwise_xor(2 * mine + core, turn)]


def roll(value, rows, cols):
    return pltpu.roll(pltpu.roll(value, rows, 0), cols, 1)


def ready_kernel(offs, taken, probe_from, measured, tabs_from, order_from, probe, target, tabs, kept, order, sems):
    half, col, core = here()
    probe_copy, kept_copy, order_copy, tabs_copy = fetch(
        [(probe_from, probe), (measured.at[0, half], kept), (order_from, order), (tabs_from, tabs)], sems
    )
    slot = slot_of(half, col, core)
    lower, row_at, col_at = slot_place(offs, 2 * half + col, slot)
    probe_copy.wait()
    for part in range(2):
        probe[part] = roll(probe[part], row_at, col_at)
    kept_copy.wait()
    order_copy.wait()
    rest = jnp.where(lower == half, kept[...], taken[...])
    total = jnp.zeros_like(rest)
    for unused in range(3):
        part = rest.astype(jnp.bfloat16)
        rest = rest - part.astype(jnp.float32)
        total += dot(order[0], dot(part, order[1]).astype(jnp.bfloat16))
    target[...] = total
    tabs_copy.wait()


def position_kernel(offs, *refs):
    gotten, (probe, target, tabs, factors) = dict(zip(EIGHT, refs)), refs[8:12]
    outs, keep, (patch, grad, bands) = refs[12:20], refs[20], refs[21:]
    half, col, core = here()
    mine = 2 * half + col
    flat = 2 * mine + core
    unused, row_at, col_at = slot_place(offs, mine, slot_of(half, col, core))
    width = probe.shape[-1]
    lanes, band = width // 2, width // 4
    for turn in range(8):
        patch[jnp.bitwise_xor(flat, turn)] = gotten[turn][...]

    def load(plane):
        return jnp.concatenate([patch[2 * plane], patch[2 * plane + 1]], axis=1)

    def store(plane, value):
        grad[2 * plane] = value[:, :lanes]
        grad[2 * plane + 1] = value[:, lanes:]

    wave_re, wave_im = probe[0], probe[1]
    o0_re, o0_im, o1_re, o1_im = load(0), load(2), load(1), load(3)
    exit_re = wave_re * o0_re - wave_im * o0_im
    exit_im = wave_re * o0_im + wave_im * o0_re
    mid_re, mid_im = propagate(exit_re, exit_im, tabs, False)
    exit_re = mid_re * o1_re - mid_im * o1_im
    exit_im = mid_re * o1_im + mid_im * o1_re
    far_re, far_im = to_far(exit_re, exit_im, tabs, factors)
    excess = 2.0 * GRAD_WEIGHT * (far_re * far_re + far_im * far_im - target[...])
    back_re, back_im = from_far(excess * far_re, excess * far_im, tabs, factors)
    store(1, mid_re * back_re + mid_im * back_im)
    store(3, mid_re * back_im - mid_im * back_re)
    up_re = o1_re * back_re + o1_im * back_im
    up_im = o1_re * back_im - o1_im * back_re
    back_re, back_im = propagate(up_re, up_im, tabs, True)
    wave_re, wave_im = probe[0], probe[1]
    o0_re, o0_im = load(0), load(2)
    store(0, wave_re * back_re + wave_im * back_im)
    store(2, wave_re * back_im - wave_im * back_re)
    up_re = o0_re * back_re + o0_im * back_im
    up_im = o0_re * back_im - o0_im * back_re
    back_row, back_col = lax.rem(width - row_at, width), lax.rem(2 * width - col_at, width)
    for part, value in enumerate((up_re, up_im)):
        value = roll(value, back_row, back_col)
        for step in range(4):
            rows = value[step * band : (step + 1) * band]
            bands[4 * part + step, :band] = rows[:, :lanes]
            bands[4 * part + step, band:] = rows[:, lanes:]
    for turn, out in zip(BACK, outs):
        out[:width] = grad[jnp.bitwise_xor(flat, turn)]
    for part in range(4):
        keep[part] = bands[2 * part + core]
        start = width + 2 * band * part
        outs[0][start : start + 2 * band] = bands[2 * part + 1 - core]


def pair_kernel(keep, got, *outs):
    band = keep.shape[1]
    half, col, unused = here()
    first = got.shape[0] - 4 * band
    for turn, out in zip(FOUR, outs):
        part = jnp.bitwise_xor(2 * half + col, turn)
        out[...] = keep[part] + got[pl.ds(pl.multiple_of(first + band * part, band), band)]


def add_parts(offs, parts, strip, rows, cols):
    half, col, core = here()
    mine = 2 * half + col
    row_ids = lax.broadcasted_iota(jnp.int32, (rows, cols), 0)
    col_ids = lax.broadcasted_iota(jnp.int32, (rows, cols), 1) + core * cols
    sums = [jnp.zeros((rows, cols), jnp.float32)] * 2
    for turn, part in zip(BACK, parts):
        flat = jnp.bitwise_xor(2 * mine + core, turn)
        slot = slot_of(flat // 4, (flat // 2) % 2, flat % 2)
        lower, row_at, col_at = slot_place(offs, mine, slot)
        first = jnp.where(strip == lower, row_at, jnp.where(strip == lower + 1, 0, rows))
        last = jnp.where(strip == lower, rows, jnp.where(strip == lower + 1, row_at, 0))
        value = jnp.where((row_ids >= first) & (row_ids < last), part[:rows], 0.0)
        left = jnp.where(col_ids >= col_at, value, 0.0)
        sums = [sums[0] + left, sums[1] + (value - left)]
    return sums


def add_below_kernel(offs, *refs):
    parts, below = refs[:8], refs[8]
    rows, cols = below.shape[1:]
    sums = add_parts(offs, parts, 2, rows, cols)
    col = here()[1]
    for side in range(2):
        below[jnp.bitwise_xor(col, side)] = sums[side]


def band_kernel(*refs):
    quarters, out = refs[:4], refs[4]
    total = (quarters[0][...] + quarters[1][...]) + (quarters[2][...] + quarters[3][...])
    band, cols = out.shape[0], total.shape[1]
    out[:, :cols] = total[:band]
    out[:, cols:] = total[band:]


def add_own_kernel(offs, *refs):
    parts, own = refs[:8], refs[8]
    rows, cols = own.shape[1:]
    for strip in range(2):
        own[2 * strip], own[2 * strip + 1] = add_parts(offs, parts, strip, rows, cols)


def top_kernel(own, above, *outs):
    half, col, unused = here()
    mine = 2 * half + col
    for turn, out in zip(FOUR, outs):
        extra = jnp.where(half == turn // 2, above[turn % 2], 0.0)
        out[...] = own[jnp.bitwise_xor(mine, turn)] + extra


def join_kernel(*refs):
    probe, out, probe_out, sems = refs[4:]
    half, col, unused = here()
    mine = 2 * half + col
    pairs = [(ref, out.at[jnp.bitwise_xor(mine, turn)]) for turn, ref in zip(FOUR, refs)]
    for copy in fetch([(probe, probe_out), *pairs], sems):
        copy.wait()


SMEM = pl.BlockSpec(memory_space=pltpu.SMEM)
VMEM = pl.BlockSpec(memory_space=pltpu.VMEM)
HBM = pl.BlockSpec(memory_space=pltpu.HBM)
ANY = pl.BlockSpec(memory_space=pl.ANY)


def call(kernel, outs, scalars, arrays, flops, scratch=(), copies=0):
    outs, arrays = ([x if isinstance(x, tuple) else (x, VMEM) for x in xs] for xs in (outs, arrays))
    moved = sum(math.prod(x.shape) * x.dtype.itemsize for x, unused in [*arrays, *outs])
    scratch = [pltpu.VMEM(dims, jnp.float32) if isinstance(dims, tuple) else dims for dims in scratch]
    return pl.pallas_call(
        kernel,
        out_shape=[x for x, unused in outs],
        in_specs=[SMEM] * len(scalars) + [spec for unused, spec in arrays],
        out_specs=[spec for unused, spec in outs],
        scratch_shapes=scratch + [pltpu.SemaphoreType.DMA((copies,))] * (copies > 0),
        compiler_params=pltpu.CompilerParams(vmem_limit_bytes=VMEM_LIMIT),
        cost_estimate=pl.CostEstimate(flops=flops, bytes_accessed=moved, transcendentals=0),
    )(*scalars, *(pltpu.with_memory_space_constraint(x, pltpu.HBM) if spec is HBM else x for x, spec in arrays))


def shape(*dims):
    return jax.ShapeDtypeStruct(dims, jnp.float32)


def deal(values, axes, order):
    return [
        lax.ppermute(value, axes, [(k, k ^ turn) for k in range(len(order))]) if turn else value
        for turn, value in zip(order, values)
    ]


def sum_over(value, axis, size):
    step = 2
    while step < size:
        value = value + lax.ppermute(value, axis, [(k, k ^ step) for k in range(size)])
        step *= 2
    return value


def local(object_field, probe, offsets, slot_range, measured):
    width = probe.shape[-1]
    planes, rows, cols = 4, object_field.shape[2], object_field.shape[3]
    band = width // 4
    pairs = lax.axis_size("pair")
    half, col, core = (lax.axis_index(name) for name in PLANE)

    block = object_field.reshape(planes, rows, cols)
    *dealt, given = call(
        deal_kernel,
        [shape(rows + 8, cols)] * 4 + [shape(width, width)],
        (),
        ((block, HBM), (measured, HBM), (offsets, HBM)),
        0,
        [pltpu.SMEM(offsets.shape, offsets.dtype)],
        copies=6,
    )
    own = deal(dealt, PLANE[:2], FOUR)
    (lowest,) = call(lowest_kernel, [shape(2, rows, cols)], (), own, 0)
    lowest, given = lax.optimization_barrier((lowest, given))
    below = lax.ppermute(lowest, "pair", [(k, k - 1) for k in range(1, pairs)])
    taken = lax.ppermute(given, "half", [(0, 1), (1, 0)])

    turned = dict(zip(FOUR, own))
    offs = jnp.stack([turned[turn][rows : rows + 4, 0] for turn in range(4)]).astype(jnp.int32)
    others = lax.ppermute(offs, "core", [(0, 1), (1, 0)])
    offs = jnp.concatenate([jnp.where(core == 0, offs, others), jnp.where(core == 0, others, offs)], axis=1)
    split_at = jnp.where(half == 0, slot_range[0, 1], slot_range[0, 0])
    offs = jnp.concatenate([offs, jnp.full((1, offs.shape[1]), split_at, jnp.int32)], axis=0)
    scalars = (offs,)
    parts = call(
        pick_kernel,
        [shape(rows, cols)] * 8,
        scalars,
        (*own, below),
        32 * rows * width,
        [(planes, rows, cols), (8, rows, cols)],
    )
    tabs, factors, order = (jnp.asarray(table) for table in tables(width))
    probe, target, tabs = call(
        ready_kernel,
        [shape(*probe.shape), shape(width, width), jax.ShapeDtypeStruct(tabs.shape, tabs.dtype)],
        scalars,
        (taken, (probe, HBM), (measured, HBM), (tabs, HBM), (order, HBM)),
        12 * width**3,
        [(width, width), pltpu.VMEM(order.shape, order.dtype)],
        copies=4,
    )
    *grad, keep = call(
        position_kernel,
        [shape(rows + 8 * band, cols)] + [shape(rows, cols)] * 7 + [shape(4, 2 * band, cols)],
        scalars,
        (*deal(parts, PLANE, EIGHT), probe, target, tabs, factors),
        8 * 12 * width**3,
        [(8, rows, cols)] * 2 + [(8, 2 * band, cols)],
    )
    got = deal(grad, PLANE, BACK)
    quarters = call(pair_kernel, [shape(2 * band, cols)] * 4, (), (keep, got[0]), 4 * band * width)
    quarters = deal(quarters, PLANE[:2], FOUR)
    *got, first, second = lax.optimization_barrier((*got, *quarters[:2]))
    (lower_sums,) = call(add_below_kernel, [shape(2, rows, cols)], scalars, got, 32 * rows * width)
    quarters = [first, second, *quarters[2:]]
    (probe_band,) = call(band_kernel, [shape(band, width)], (), quarters, 4 * band * width)
    above = lax.ppermute(lower_sums, "pair", [(k, k + 1) for k in range(pairs - 1)])
    doubling = pairs > 1 and pairs & (pairs - 1) == 0
    if doubling:
        near = lax.ppermute(probe_band, "pair", [(k, k ^ 1) for k in range(pairs)])
    (sums,) = call(add_own_kernel, [shape(planes, rows, cols)], scalars, got, 64 * rows * width)
    sums = call(top_kernel, [shape(rows, cols)] * 4, (), (sums, above), planes * rows * cols)
    if doubling:
        *sums, near = lax.optimization_barrier((*sums, near))
        probe_band = sum_over(probe_band + near, "pair", pairs)
    else:
        probe_band = lax.psum(probe_band, "pair")
    sums = deal(sums, PLANE[:2], FOUR)
    probe_grad = lax.all_gather(probe_band, PLANE, axis=0, tiled=True)
    object_grad, probe_grad = call(
        join_kernel,
        [(shape(planes, rows, cols), HBM), (shape(*probe_grad.shape), HBM)],
        (),
        [(x, ANY) for x in (*sums, probe_grad)],
        0,
        copies=5,
    )
    return (object_grad.reshape(object_field.shape), probe_grad.reshape(probe.shape))


def solution(mesh):
    tile, grp = mesh.shape["tile"], mesh.shape["grp"]
    devices = mesh.devices.reshape(tile // 2, 2, 2, grp // 2)
    inner = Mesh(devices, ("pair", "half", "col", "core"))
    strip, cols = ("pair", "half"), ("col", "core")
    in_specs = (
        P(None, None, strip, cols),
        P(),
        P(strip, cols, None),
        P(strip, None),
        P(strip, cols, None, None),
    )
    out_specs = (P(None, None, strip, cols), P())
    return jax.shard_map(local, mesh=inner, in_specs=in_specs, out_specs=out_specs, check_vma=False)
```

```python
import functools
import math

import jax
import jax.numpy as jnp
import ml_dtypes
import numpy as np
from jax import lax
from jax.experimental import pallas as pl
from jax.experimental.pallas import tpu as pltpu
from jax.sharding import Mesh, PartitionSpec as P

GRAD_WEIGHT = 0.0625
PLANE = ("half", "col", "core")
EIGHT, BACK, FOUR = (2, 4, 3, 5, 6, 7, 1, 0), (1, 4, 2, 5, 3, 6, 7, 0), (2, 1, 3, 0)
VMEM_LIMIT = 24 * 1024 * 1024


def tables(width):
    half = width // 2
    index = np.arange(half, dtype=np.int64)
    scale = 1.0 / math.sqrt(width)
    far = np.exp(-2j * math.pi / half * (index[:, None] * index[None, :] % half)) * scale
    near = []
    for offset in (0, half):
        shift = index[:, None] - index[None, :] + offset
        near.append(np.exp(1j * (math.pi / width * (shift * shift % (2 * width)) - math.pi / 4.0)) * scale)
    products = []
    for matrix in ((near[0] + near[1]) / 2.0, (near[0] - near[1]) / 2.0, far):
        for imag in (matrix.imag, -matrix.imag):
            table = np.block([[matrix.real, imag], [-imag, matrix.real]])
            high = table.astype(ml_dtypes.bfloat16)
            low = (table - high.astype(np.float64)).astype(ml_dtypes.bfloat16)
            products.append(np.concatenate([high, low], axis=0))
    angle = -2.0 * math.pi / width * index
    twiddles = []
    for part in (np.cos(angle), np.sin(angle)):
        rows = np.broadcast_to(part[:, None], (half, half))
        twiddles.append(np.concatenate([rows, np.broadcast_to(part[None, :], (8, half))], axis=0))
    order = np.zeros((width, width))
    order[np.arange(width), np.concatenate([2 * index, 2 * index + 1])] = 1.0
    order = np.stack([order, order.T]).astype(ml_dtypes.bfloat16)
    return np.stack(products), np.stack(twiddles).astype(np.float32), order


def split(value):
    high = value.astype(jnp.bfloat16)
    low = (value - high.astype(jnp.float32)).astype(jnp.bfloat16)
    return high, low


def dot(left, right):
    return jnp.dot(left, right, preferred_element_type=jnp.float32)


PLUS, MINUS, FAR = 0, 2, 4


def times_right(re, im, table):
    width = table.shape[1]
    high, low = split(jnp.concatenate([re, im], axis=1))
    twice = dot(jnp.concatenate([high, low], axis=0), table[:width])
    count = re.shape[0]
    out = twice[:count] + (twice[count:] + dot(high, table[width:]))
    return out[:, : width // 2], out[:, width // 2 :]


def times_left(re, im, table):
    width = table.shape[1]
    high, low = split(jnp.concatenate([re, im], axis=0))
    twice = dot(table[...], high)
    out = twice[:width] + (twice[width:] + dot(table[:width], low))
    return out[: width // 2], out[width // 2 :]


def butterfly(first, second):
    return first + second, first - second


def halves(value, axis):
    half = value.shape[axis] // 2
    return (value[:half], value[half:]) if axis == 0 else (value[:, :half], value[:, half:])


def turn_by(re, im, cos, sin):
    return re * cos - im * sin, re * sin + im * cos


def propagate(re, im, tabs, conj):
    for axis in (1, 0):
        (plus_re, minus_re), (plus_im, minus_im) = (butterfly(*halves(x, axis)) for x in (re, im))
        times = times_right if axis else times_left
        pick = int(conj) if axis else 1 - int(conj)
        plus_re, plus_im = times(plus_re, plus_im, tabs.at[PLUS + pick])
        minus_re, minus_im = times(minus_re, minus_im, tabs.at[MINUS + pick])
        re = jnp.concatenate(butterfly(plus_re, minus_re), axis=axis)
        im = jnp.concatenate(butterfly(plus_im, minus_im), axis=axis)
    return re, im


def twiddle(factors, axis, width):
    half = factors.shape[2]
    if axis:
        return factors[0, half : half + 1], factors[1, half : half + 1]
    return tuple(jnp.concatenate([factors[k, :half]] * (width // half), axis=1) for k in range(2))


def to_far(re, im, tabs, factors):
    for axis in (1, 0):
        (even_re, odd_re), (even_im, odd_im) = (butterfly(*halves(x, axis)) for x in (re, im))
        odd_re, odd_im = turn_by(odd_re, odd_im, *twiddle(factors, axis, re.shape[1]))
        times, table = (times_right, tabs.at[FAR]) if axis else (times_left, tabs.at[FAR + 1])
        (even_re, even_im), (odd_re, odd_im) = times(even_re, even_im, table), times(odd_re, odd_im, table)
        re, im = jnp.concatenate([even_re, odd_re], axis=axis), jnp.concatenate([even_im, odd_im], axis=axis)
    return re, im


def from_far(re, im, tabs, factors):
    for axis in (0, 1):
        (even_re, odd_re), (even_im, odd_im) = halves(re, axis), halves(im, axis)
        times, table = (times_right, tabs.at[FAR + 1]) if axis else (times_left, tabs.at[FAR])
        (even_re, even_im), (odd_re, odd_im) = times(even_re, even_im, table), times(odd_re, odd_im, table)
        cos, sin = twiddle(factors, axis, re.shape[1])
        odd_re, odd_im = turn_by(odd_re, odd_im, cos, -sin)
        re = jnp.concatenate(butterfly(even_re, odd_re), axis=axis)
        im = jnp.concatenate(butterfly(even_im, odd_im), axis=axis)
    return re, im


def slot_of(half, col, core):
    return 2 * (2 * col + core) + half


def receivers():
    return [slot_of(half, col, core) for half in range(2) for col in range(2) for core in range(2)]


def slot_place(offs, mine, slot):
    lower = jnp.where(slot >= offs[4, 0], 1, 0)
    holder, at = jnp.bitwise_xor(2 * lower + slot // 4, mine), 2 * (slot % 4)
    return lower, offs[holder, at], offs[holder, at + 1]


def here():
    return tuple(lax.axis_index(name) for name in PLANE)


def fetch(pairs, sems):
    copies = [pltpu.make_async_copy(source, into, sems.at[k]) for k, (source, into) in enumerate(pairs)]
    for copy in copies:
        copy.start()
    return copies


def deal_kernel(block, measured, offsets_from, *refs):
    outs, given, offsets, sems = refs[:4], refs[4], refs[5], refs[6]
    half, col, unused = here()
    mine = 2 * half + col
    rows, cols = block.shape[1:]
    pairs = [(block.at[jnp.bitwise_xor(mine, turn)], out.at[pl.ds(0, rows)]) for turn, out in zip(FOUR, outs)]
    copies = fetch([(offsets_from, offsets), *pairs, (measured.at[0, 1 - half], given)], sems)
    copies[0].wait()
    lines = [jnp.full((1, cols), offsets[0, slot, axis], jnp.int32) for slot in range(2) for axis in range(2)]
    lines = jnp.concatenate(lines * 2, axis=0).astype(jnp.float32)
    for out in outs:
        out[rows:] = lines
    for copy in copies[1:]:
        copy.wait()


def lowest_kernel(*refs):
    gotten, out = dict(zip(FOUR, refs)), refs[4]
    rows = out.shape[1]
    half = here()[0]
    for turn in range(2):
        out[turn] = jnp.where(half == 0, gotten[turn][:rows], gotten[2 + turn][:rows])


def pick_kernel(offs, *refs):
    gotten, below, outs, (own, parts) = dict(zip(FOUR, refs)), refs[4], refs[5:13], refs[13:]
    rows, cols = outs[0].shape
    half, col, core = here()
    mine = 2 * half + col
    for turn in range(4):
        own[jnp.bitwise_xor(mine, turn)] = gotten[turn][:rows]
    row_ids = lax.broadcasted_iota(jnp.int32, (rows, cols), 0)
    col_ids = lax.broadcasted_iota(jnp.int32, (rows, cols), 1) + core * cols
    for place, slot in enumerate(receivers()):
        lower, row_at, col_at = slot_place(offs, mine, slot)
        upper_rows = row_ids >= row_at
        left_cols = col_ids >= col_at

        def merged(side, lower=lower, upper_rows=upper_rows):
            second = own[2 + side]
            top = jnp.where(lower == 1, second, own[side])
            bottom = jnp.where(lower == 1, below[jnp.bitwise_xor(col, side)], second)
            return jnp.where(upper_rows, top, bottom)

        parts[place] = jnp.where(left_cols, merged(0), merged(1))
    for turn, out in zip(EIGHT, outs):
        out[...] = parts[jnp.bitwise_xor(2 * mine + core, turn)]


def roll(value, rows, cols):
    return pltpu.roll(pltpu.roll(value, rows, 0), cols, 1)


def ready_kernel(offs, taken, probe_from, measured, tabs_from, order_from, probe, target, tabs, kept, order, sems):
    half, col, core = here()
    probe_copy, kept_copy, order_copy, tabs_copy = fetch(
        [(probe_from, probe), (measured.at[0, half], kept), (order_from, order), (tabs_from, tabs)], sems
    )
    slot = slot_of(half, col, core)
    lower, row_at, col_at = slot_place(offs, 2 * half + col, slot)
    probe_copy.wait()
    for part in range(2):
        probe[part] = roll(probe[part], row_at, lax.rem(col_at, target.shape[1]))
    kept_copy.wait()
    order_copy.wait()
    rest = jnp.where(lower == half, kept[...], taken[...])
    total = jnp.zeros_like(rest)
    for unused in range(3):
        part = rest.astype(jnp.bfloat16)
        rest = rest - part.astype(jnp.float32)
        total += dot(order[0], dot(part, order[1]).astype(jnp.bfloat16))
    target[...] = total
    tabs_copy.wait()


def position_kernel(offs, *refs):
    gotten, (probe, target, tabs, factors) = dict(zip(EIGHT, refs)), refs[8:12]
    outs, keep, (patch, grad, bands) = refs[12:20], refs[20], refs[21:]
    half, col, core = here()
    mine = 2 * half + col
    flat = 2 * mine + core
    unused, row_at, col_at = slot_place(offs, mine, slot_of(half, col, core))
    width = probe.shape[-1]
    lanes, band = width // 2, width // 4
    for turn in range(8):
        patch[jnp.bitwise_xor(flat, turn)] = gotten[turn][...]

    def load(plane):
        return jnp.concatenate([patch[2 * plane], patch[2 * plane + 1]], axis=1)

    def store(plane, value):
        grad[2 * plane] = value[:, :lanes]
        grad[2 * plane + 1] = value[:, lanes:]

    wave_re, wave_im = probe[0], probe[1]
    o0_re, o0_im, o1_re, o1_im = load(0), load(2), load(1), load(3)
    exit_re = wave_re * o0_re - wave_im * o0_im
    exit_im = wave_re * o0_im + wave_im * o0_re
    mid_re, mid_im = propagate(exit_re, exit_im, tabs, False)
    exit_re = mid_re * o1_re - mid_im * o1_im
    exit_im = mid_re * o1_im + mid_im * o1_re
    far_re, far_im = to_far(exit_re, exit_im, tabs, factors)
    excess = 2.0 * GRAD_WEIGHT * (far_re * far_re + far_im * far_im - target[...])
    back_re, back_im = from_far(excess * far_re, excess * far_im, tabs, factors)
    store(1, mid_re * back_re + mid_im * back_im)
    store(3, mid_re * back_im - mid_im * back_re)
    up_re = o1_re * back_re + o1_im * back_im
    up_im = o1_re * back_im - o1_im * back_re
    back_re, back_im = propagate(up_re, up_im, tabs, True)
    wave_re, wave_im = probe[0], probe[1]
    o0_re, o0_im = load(0), load(2)
    store(0, wave_re * back_re + wave_im * back_im)
    store(2, wave_re * back_im - wave_im * back_re)
    up_re = o0_re * back_re + o0_im * back_im
    up_im = o0_re * back_im - o0_im * back_re
    back_row, back_col = lax.rem(width - row_at, width), lax.rem(2 * width - col_at, width)
    for part, value in enumerate((up_re, up_im)):
        value = roll(value, back_row, back_col)
        for step in range(4):
            rows = value[step * band : (step + 1) * band]
            bands[4 * part + step, :band] = rows[:, :lanes]
            bands[4 * part + step, band:] = rows[:, lanes:]
    for turn, out in zip(BACK, outs):
        out[:width] = grad[jnp.bitwise_xor(flat, turn)]
    for part in range(4):
        keep[part] = bands[2 * part + core]
        start = width + 2 * band * part
        outs[0][start : start + 2 * band] = bands[2 * part + 1 - core]


def pair_kernel(keep, got, *outs):
    band = keep.shape[1]
    half, col, unused = here()
    first = got.shape[0] - 4 * band
    for turn, out in zip(FOUR, outs):
        part = jnp.bitwise_xor(2 * half + col, turn)
        out[...] = keep[part] + got[pl.ds(pl.multiple_of(first + band * part, band), band)]


def add_parts(offs, parts, strip, rows, cols):
    half, col, core = here()
    mine = 2 * half + col
    row_ids = lax.broadcasted_iota(jnp.int32, (rows, cols), 0)
    col_ids = lax.broadcasted_iota(jnp.int32, (rows, cols), 1) + core * cols
    sums = [jnp.zeros((rows, cols), jnp.float32)] * 2
    for turn, part in zip(BACK, parts):
        flat = jnp.bitwise_xor(2 * mine + core, turn)
        slot = slot_of(flat // 4, (flat // 2) % 2, flat % 2)
        lower, row_at, col_at = slot_place(offs, mine, slot)
        first = jnp.where(strip == lower, row_at, jnp.where(strip == lower + 1, 0, rows))
        last = jnp.where(strip == lower, rows, jnp.where(strip == lower + 1, row_at, 0))
        value = jnp.where((row_ids >= first) & (row_ids < last), part[:rows], 0.0)
        left = jnp.where(col_ids >= col_at, value, 0.0)
        sums = [sums[0] + left, sums[1] + (value - left)]
    return sums


def add_below_kernel(offs, *refs):
    parts, quarters, (below, probe_band) = refs[:8], refs[8:12], refs[12:]
    rows, cols = below.shape[1:]
    sums = add_parts(offs, parts, 2, rows, cols)
    col = here()[1]
    for side in range(2):
        below[jnp.bitwise_xor(col, side)] = sums[side]
    total = (quarters[0][...] + quarters[1][...]) + (quarters[2][...] + quarters[3][...])
    band = probe_band.shape[0]
    probe_band[:, :cols] = total[:band]
    probe_band[:, cols:] = total[band:]


def add_own_kernel(offs, *refs):
    parts, own = refs[:8], refs[8]
    rows, cols = own.shape[1:]
    for strip in range(2):
        own[2 * strip], own[2 * strip + 1] = add_parts(offs, parts, strip, rows, cols)


def top_kernel(own, above, *outs):
    half, col, unused = here()
    mine = 2 * half + col
    for turn, out in zip(FOUR, outs):
        extra = jnp.where(half == turn // 2, above[turn % 2], 0.0)
        out[...] = own[jnp.bitwise_xor(mine, turn)] + extra


def join_kernel(*refs):
    probe, out, probe_out, sems = refs[4:]
    half, col, unused = here()
    mine = 2 * half + col
    pairs = [(ref, out.at[jnp.bitwise_xor(mine, turn)]) for turn, ref in zip(FOUR, refs)]
    for copy in fetch([(probe, probe_out), *pairs], sems):
        copy.wait()


SMEM = pl.BlockSpec(memory_space=pltpu.SMEM)
VMEM = pl.BlockSpec(memory_space=pltpu.VMEM)
HBM = pl.BlockSpec(memory_space=pltpu.HBM)
ANY = pl.BlockSpec(memory_space=pl.ANY)


def call(kernel, outs, scalars, arrays, flops, scratch=(), copies=0):
    outs, arrays = ([x if isinstance(x, tuple) else (x, VMEM) for x in xs] for xs in (outs, arrays))
    moved = sum(math.prod(x.shape) * x.dtype.itemsize for x, unused in [*arrays, *outs])
    scratch = [pltpu.VMEM(dims, jnp.float32) if isinstance(dims, tuple) else dims for dims in scratch]
    return pl.pallas_call(
        kernel,
        out_shape=[x for x, unused in outs],
        in_specs=[SMEM] * len(scalars) + [spec for unused, spec in arrays],
        out_specs=[spec for unused, spec in outs],
        scratch_shapes=scratch + [pltpu.SemaphoreType.DMA((copies,))] * (copies > 0),
        compiler_params=pltpu.CompilerParams(vmem_limit_bytes=VMEM_LIMIT),
        cost_estimate=pl.CostEstimate(flops=flops, bytes_accessed=moved, transcendentals=0),
    )(*scalars, *(pltpu.with_memory_space_constraint(x, pltpu.HBM) if spec is HBM else x for x, spec in arrays))


def shape(*dims):
    return jax.ShapeDtypeStruct(dims, jnp.float32)


def deal(values, axes, order):
    return [
        lax.ppermute(value, axes, [(k, k ^ turn) for k in range(len(order))]) if turn else value
        for turn, value in zip(order, values)
    ]


def sum_over(value, axis, size):
    step = 2
    while step < size:
        value = value + lax.ppermute(value, axis, [(k, k ^ step) for k in range(size)])
        step *= 2
    return value


def local(object_field, probe, offsets, slot_range, measured):
    width = probe.shape[-1]
    planes, rows, cols = 4, object_field.shape[2], object_field.shape[3]
    band = width // 4
    pairs = lax.axis_size("pair")
    half, col, core = (lax.axis_index(name) for name in PLANE)

    block = object_field.reshape(planes, rows, cols)
    *dealt, given = call(
        deal_kernel,
        [shape(rows + 8, cols)] * 4 + [shape(width, width)],
        (),
        ((block, HBM), (measured, HBM), (offsets, HBM)),
        0,
        [pltpu.SMEM(offsets.shape, offsets.dtype)],
        copies=6,
    )
    own = deal(dealt, PLANE[:2], FOUR)
    (lowest,) = call(lowest_kernel, [shape(2, rows, cols)], (), own, 0)
    lowest, given = lax.optimization_barrier((lowest, given))
    below = lax.ppermute(lowest, "pair", [(k, k - 1) for k in range(1, pairs)])
    taken = lax.ppermute(given, "half", [(0, 1), (1, 0)])

    turned = dict(zip(FOUR, own))
    offs = jnp.stack([turned[turn][rows : rows + 4, 0] for turn in range(4)]).astype(jnp.int32)
    others = lax.ppermute(offs, "core", [(0, 1), (1, 0)])
    offs = jnp.concatenate([jnp.where(core == 0, offs, others), jnp.where(core == 0, others, offs)], axis=1)
    split_at = jnp.where(half == 0, slot_range[0, 1], slot_range[0, 0])
    offs = jnp.concatenate([offs, jnp.full((1, offs.shape[1]), split_at, jnp.int32)], axis=0)
    scalars = (offs,)
    parts = call(
        pick_kernel,
        [shape(rows, cols)] * 8,
        scalars,
        (*own, below),
        32 * rows * width,
        [(planes, rows, cols), (8, rows, cols)],
    )
    tabs, factors, order = (jnp.asarray(table) for table in tables(width))
    probe, target, tabs = call(
        ready_kernel,
        [shape(*probe.shape), shape(width, width), jax.ShapeDtypeStruct(tabs.shape, tabs.dtype)],
        scalars,
        (taken, (probe, HBM), (measured, HBM), (tabs, HBM), (order, HBM)),
        12 * width**3,
        [(width, width), pltpu.VMEM(order.shape, order.dtype)],
        copies=4,
    )
    *grad, keep = call(
        position_kernel,
        [shape(rows + 8 * band, cols)] + [shape(rows, cols)] * 7 + [shape(4, 2 * band, cols)],
        scalars,
        (*deal(parts, PLANE, EIGHT), probe, target, tabs, factors),
        8 * 12 * width**3,
        [(8, rows, cols)] * 2 + [(8, 2 * band, cols)],
    )
    got = deal(grad, PLANE, BACK)
    quarters = call(pair_kernel, [shape(2 * band, cols)] * 4, (), (keep, got[0]), 4 * band * width)
    lower_sums, probe_band = call(
        add_below_kernel,
        [shape(2, rows, cols), shape(band, width)],
        scalars,
        (*got, *deal(quarters, PLANE[:2], FOUR)),
        32 * rows * width,
    )
    above = lax.ppermute(lower_sums, "pair", [(k, k + 1) for k in range(pairs - 1)])
    doubling = pairs > 1 and pairs & (pairs - 1) == 0
    if doubling:
        near = lax.ppermute(probe_band, "pair", [(k, k ^ 1) for k in range(pairs)])
    (sums,) = call(add_own_kernel, [shape(planes, rows, cols)], scalars, got, 64 * rows * width)
    sums = call(top_kernel, [shape(rows, cols)] * 4, (), (sums, above), planes * rows * cols)
    if doubling:
        *sums, near = lax.optimization_barrier((*sums, near))
        probe_band = sum_over(probe_band + near, "pair", pairs)
    else:
        probe_band = lax.psum(probe_band, "pair")
    sums = deal(sums, PLANE[:2], FOUR)
    probe_grad = lax.all_gather(probe_band, PLANE, axis=0, tiled=True)
    object_grad, probe_grad = call(
        join_kernel,
        [(shape(planes, rows, cols), HBM), (shape(*probe_grad.shape), HBM)],
        (),
        [(x, ANY) for x in (*sums, probe_grad)],
        0,
        copies=5,
    )
    return (object_grad.reshape(object_field.shape), probe_grad.reshape(probe.shape))


def solution(mesh):
    tile, grp = mesh.shape["tile"], mesh.shape["grp"]
    devices = mesh.devices.reshape(tile // 2, 2, 2, grp // 2)
    inner = Mesh(devices, ("pair", "half", "col", "core"))
    strip, cols = ("pair", "half"), ("col", "core")
    in_specs = (
        P(None, None, strip, cols),
        P(),
        P(strip, cols, None),
        P(strip, None),
        P(strip, cols, None, None),
    )
    out_specs = (P(None, None, strip, cols), P())
    return jax.shard_map(local, mesh=inner, in_specs=in_specs, out_specs=out_specs, check_vma=False)
```

```python
import functools
import math

import jax
import jax.numpy as jnp
import ml_dtypes
import numpy as np
from jax import lax
from jax.experimental import pallas as pl
from jax.experimental.pallas import tpu as pltpu
from jax.sharding import Mesh, PartitionSpec as P

GRAD_WEIGHT = 0.0625
PLANE = ("half", "col", "core")
EIGHT, BACK, FOUR = (2, 4, 3, 5, 6, 7, 1, 0), (1, 2, 4, 3, 5, 6, 7, 0), (2, 1, 3, 0)
VMEM_LIMIT = 24 * 1024 * 1024


def tables(width):
    half = width // 2
    index = np.arange(half, dtype=np.int64)
    scale = 1.0 / math.sqrt(width)
    far = np.exp(-2j * math.pi / half * (index[:, None] * index[None, :] % half)) * scale
    near = []
    for offset in (0, half):
        shift = index[:, None] - index[None, :] + offset
        near.append(np.exp(1j * (math.pi / width * (shift * shift % (2 * width)) - math.pi / 4.0)) * scale)
    products = []
    for matrix in ((near[0] + near[1]) / 2.0, (near[0] - near[1]) / 2.0, far):
        for imag in (matrix.imag, -matrix.imag):
            table = np.block([[matrix.real, imag], [-imag, matrix.real]])
            high = table.astype(ml_dtypes.bfloat16)
            low = (table - high.astype(np.float64)).astype(ml_dtypes.bfloat16)
            products.append(np.concatenate([high, low], axis=0))
    angle = -2.0 * math.pi / width * index
    twiddles = []
    for part in (np.cos(angle), np.sin(angle)):
        rows = np.broadcast_to(part[:, None], (half, half))
        twiddles.append(np.concatenate([rows, np.broadcast_to(part[None, :], (8, half))], axis=0))
    order = np.zeros((width, width))
    order[np.arange(width), np.concatenate([2 * index, 2 * index + 1])] = 1.0
    order = np.stack([order, order.T]).astype(ml_dtypes.bfloat16)
    return np.stack(products), np.stack(twiddles).astype(np.float32), order


def split(value):
    high = value.astype(jnp.bfloat16)
    low = (value - high.astype(jnp.float32)).astype(jnp.bfloat16)
    return high, low


def dot(left, right):
    return jnp.dot(left, right, preferred_element_type=jnp.float32)


PLUS, MINUS, FAR = 0, 2, 4


def times_right(re, im, table):
    width = table.shape[1]
    high, low = split(jnp.concatenate([re, im], axis=1))
    twice = dot(jnp.concatenate([high, low], axis=0), table[:width])
    count = re.shape[0]
    out = twice[:count] + (twice[count:] + dot(high, table[width:]))
    return out[:, : width // 2], out[:, width // 2 :]


def times_left(re, im, table):
    width = table.shape[1]
    high, low = split(jnp.concatenate([re, im], axis=0))
    twice = dot(table[...], high)
    out = twice[:width] + (twice[width:] + dot(table[:width], low))
    return out[: width // 2], out[width // 2 :]


def butterfly(first, second):
    return first + second, first - second


def halves(value, axis):
    half = value.shape[axis] // 2
    return (value[:half], value[half:]) if axis == 0 else (value[:, :half], value[:, half:])


def turn_by(re, im, cos, sin):
    return re * cos - im * sin, re * sin + im * cos


def propagate(re, im, tabs, conj):
    for axis in (1, 0):
        (plus_re, minus_re), (plus_im, minus_im) = (butterfly(*halves(x, axis)) for x in (re, im))
        times = times_right if axis else times_left
        pick = int(conj) if axis else 1 - int(conj)
        plus_re, plus_im = times(plus_re, plus_im, tabs.at[PLUS + pick])
        minus_re, minus_im = times(minus_re, minus_im, tabs.at[MINUS + pick])
        re = jnp.concatenate(butterfly(plus_re, minus_re), axis=axis)
        im = jnp.concatenate(butterfly(plus_im, minus_im), axis=axis)
    return re, im


def twiddle(factors, axis, width):
    half = factors.shape[2]
    if axis:
        return factors[0, half : half + 1], factors[1, half : half + 1]
    return tuple(jnp.concatenate([factors[k, :half]] * (width // half), axis=1) for k in range(2))


def to_far(re, im, tabs, factors):
    for axis in (1, 0):
        (even_re, odd_re), (even_im, odd_im) = (butterfly(*halves(x, axis)) for x in (re, im))
        odd_re, odd_im = turn_by(odd_re, odd_im, *twiddle(factors, axis, re.shape[1]))
        times, table = (times_right, tabs.at[FAR]) if axis else (times_left, tabs.at[FAR + 1])
        (even_re, even_im), (odd_re, odd_im) = times(even_re, even_im, table), times(odd_re, odd_im, table)
        re, im = jnp.concatenate([even_re, odd_re], axis=axis), jnp.concatenate([even_im, odd_im], axis=axis)
    return re, im


def from_far(re, im, tabs, factors):
    for axis in (0, 1):
        (even_re, odd_re), (even_im, odd_im) = halves(re, axis), halves(im, axis)
        times, table = (times_right, tabs.at[FAR + 1]) if axis else (times_left, tabs.at[FAR])
        (even_re, even_im), (odd_re, odd_im) = times(even_re, even_im, table), times(odd_re, odd_im, table)
        cos, sin = twiddle(factors, axis, re.shape[1])
        odd_re, odd_im = turn_by(odd_re, odd_im, cos, -sin)
        re = jnp.concatenate(butterfly(even_re, odd_re), axis=axis)
        im = jnp.concatenate(butterfly(even_im, odd_im), axis=axis)
    return re, im


def slot_of(half, col, core):
    return 2 * (2 * col + core) + half


def slot_place(offs, mine, slot):
    lower = jnp.where(slot >= offs[4, 0], 1, 0)
    holder, at = jnp.bitwise_xor(2 * lower + slot // 4, mine), 2 * (slot % 4)
    return lower, offs[holder, at], offs[holder, at + 1]


def here():
    return tuple(lax.axis_index(name) for name in PLANE)


def fetch(pairs, sems):
    copies = [pltpu.make_async_copy(source, into, sems.at[k]) for k, (source, into) in enumerate(pairs)]
    for copy in copies:
        copy.start()
    return copies


def deal_kernel(block, measured, offsets_from, *refs):
    outs, given, offsets, sems = refs[:4], refs[4], refs[5], refs[6]
    half, col, unused = here()
    mine = 2 * half + col
    rows, cols = block.shape[1:]
    pairs = [(block.at[jnp.bitwise_xor(mine, turn)], out.at[pl.ds(0, rows)]) for turn, out in zip(FOUR, outs)]
    copies = fetch([(offsets_from, offsets), *pairs, (measured.at[0, 1 - half], given)], sems)
    copies[0].wait()
    lines = [jnp.full((1, cols), offsets[0, slot, axis], jnp.int32) for slot in range(2) for axis in range(2)]
    lines = jnp.concatenate(lines * 2, axis=0).astype(jnp.float32)
    for out in outs:
        out[rows:] = lines
    for copy in copies[1:]:
        copy.wait()


def lowest_kernel(*refs):
    gotten, out = dict(zip(FOUR, refs)), refs[4]
    rows = out.shape[1]
    half = here()[0]
    for turn in range(2):
        out[turn] = jnp.where(half == 0, gotten[turn][:rows], gotten[2 + turn][:rows])


def pick_kernel(offs, *refs):
    gotten, below, outs, own = dict(zip(FOUR, refs)), refs[4], refs[5:13], refs[13]
    rows, cols = outs[0].shape
    half, col, core = here()
    mine = 2 * half + col
    for turn in range(4):
        own[jnp.bitwise_xor(mine, turn)] = gotten[turn][:rows]
    row_ids = lax.broadcasted_iota(jnp.int32, (rows, cols), 0)
    col_ids = lax.broadcasted_iota(jnp.int32, (rows, cols), 1) + core * cols
    for turn, out in zip(EIGHT, outs):
        flat = jnp.bitwise_xor(2 * mine + core, turn)
        slot = slot_of(flat // 4, (flat // 2) % 2, flat % 2)
        lower, row_at, col_at = slot_place(offs, mine, slot)
        upper_rows = row_ids >= row_at
        left_cols = col_ids >= col_at

        def merged(side, lower=lower, upper_rows=upper_rows):
            second = own[2 + side]
            top = jnp.where(lower == 1, second, own[side])
            bottom = jnp.where(lower == 1, below[jnp.bitwise_xor(col, side)], second)
            return jnp.where(upper_rows, top, bottom)

        out[...] = jnp.where(left_cols, merged(0), merged(1))


def roll(value, rows, cols):
    return pltpu.roll(pltpu.roll(value, rows, 0), cols, 1)


def ready_kernel(offs, taken, probe_from, measured, tabs_from, order_from, probe, target, tabs, kept, order, sems):
    half, col, core = here()
    probe_copy, kept_copy, order_copy, tabs_copy = fetch(
        [(probe_from, probe), (measured.at[0, half], kept), (order_from, order), (tabs_from, tabs)], sems
    )
    slot = slot_of(half, col, core)
    lower, row_at, col_at = slot_place(offs, 2 * half + col, slot)
    probe_copy.wait()
    for part in range(2):
        probe[part] = roll(probe[part], row_at, lax.rem(col_at, target.shape[1]))
    kept_copy.wait()
    order_copy.wait()
    rest = jnp.where(lower == half, kept[...], taken[...])
    total = jnp.zeros_like(rest)
    for unused in range(3):
        part = rest.astype(jnp.bfloat16)
        rest = rest - part.astype(jnp.float32)
        total += dot(order[0], dot(part, order[1]).astype(jnp.bfloat16))
    target[...] = total
    tabs_copy.wait()


def position_kernel(offs, *refs):
    gotten, (probe, target, tabs, factors) = dict(zip(EIGHT, refs)), refs[8:12]
    outs, keep, (patch, grad, bands) = refs[12:20], refs[20], refs[21:]
    half, col, core = here()
    mine = 2 * half + col
    flat = 2 * mine + core
    unused, row_at, col_at = slot_place(offs, mine, slot_of(half, col, core))
    width = probe.shape[-1]
    lanes, band = width // 2, width // 4
    for turn in range(8):
        patch[jnp.bitwise_xor(flat, turn)] = gotten[turn][...]

    def load(plane):
        return jnp.concatenate([patch[2 * plane], patch[2 * plane + 1]], axis=1)

    def store(plane, value):
        grad[2 * plane] = value[:, :lanes]
        grad[2 * plane + 1] = value[:, lanes:]

    wave_re, wave_im = probe[0], probe[1]
    o0_re, o0_im, o1_re, o1_im = load(0), load(2), load(1), load(3)
    exit_re = wave_re * o0_re - wave_im * o0_im
    exit_im = wave_re * o0_im + wave_im * o0_re
    mid_re, mid_im = propagate(exit_re, exit_im, tabs, False)
    exit_re = mid_re * o1_re - mid_im * o1_im
    exit_im = mid_re * o1_im + mid_im * o1_re
    far_re, far_im = to_far(exit_re, exit_im, tabs, factors)
    excess = 2.0 * GRAD_WEIGHT * (far_re * far_re + far_im * far_im - target[...])
    back_re, back_im = from_far(excess * far_re, excess * far_im, tabs, factors)
    store(1, mid_re * back_re + mid_im * back_im)
    store(3, mid_re * back_im - mid_im * back_re)
    up_re = o1_re * back_re + o1_im * back_im
    up_im = o1_re * back_im - o1_im * back_re
    back_re, back_im = propagate(up_re, up_im, tabs, True)
    wave_re, wave_im = probe[0], probe[1]
    o0_re, o0_im = load(0), load(2)
    store(0, wave_re * back_re + wave_im * back_im)
    store(2, wave_re * back_im - wave_im * back_re)
    up_re = o0_re * back_re + o0_im * back_im
    up_im = o0_re * back_im - o0_im * back_re
    back_row, back_col = lax.rem(width - row_at, width), lax.rem(2 * width - col_at, width)
    for part, value in enumerate((up_re, up_im)):
        value = roll(value, back_row, back_col)
        for step in range(4):
            rows = value[step * band : (step + 1) * band]
            bands[4 * part + step, :band] = rows[:, :lanes]
            bands[4 * part + step, band:] = rows[:, lanes:]
    for turn, out in zip(BACK, outs):
        out[:width] = grad[jnp.bitwise_xor(flat, turn)]
    for part in range(4):
        keep[part] = bands[2 * part + core]
        start = width + 2 * band * part
        outs[0][start : start + 2 * band] = bands[2 * part + 1 - core]


def pair_kernel(keep, got, *outs):
    band = keep.shape[1]
    half, col, unused = here()
    first = got.shape[0] - 4 * band
    for turn, out in zip(FOUR, outs):
        part = jnp.bitwise_xor(2 * half + col, turn)
        out[...] = keep[part] + got[pl.ds(pl.multiple_of(first + band * part, band), band)]


def add_parts(offs, parts, strip, rows, cols):
    half, col, core = here()
    mine = 2 * half + col
    row_ids = lax.broadcasted_iota(jnp.int32, (rows, cols), 0)
    col_ids = lax.broadcasted_iota(jnp.int32, (rows, cols), 1) + core * cols
    sums = [jnp.zeros((rows, cols), jnp.float32)] * 2
    for turn, part in zip(BACK, parts):
        flat = jnp.bitwise_xor(2 * mine + core, turn)
        slot = slot_of(flat // 4, (flat // 2) % 2, flat % 2)
        lower, row_at, col_at = slot_place(offs, mine, slot)
        first = jnp.where(strip == lower, row_at, jnp.where(strip == lower + 1, 0, rows))
        last = jnp.where(strip == lower, rows, jnp.where(strip == lower + 1, row_at, 0))
        value = jnp.where((row_ids >= first) & (row_ids < last), part[:rows], 0.0)
        left = jnp.where(col_ids >= col_at, value, 0.0)
        sums = [sums[0] + left, sums[1] + (value - left)]
    return sums


def add_below_kernel(offs, *refs):
    parts, quarters, (below, probe_band) = refs[:8], refs[8:12], refs[12:]
    rows, cols = below.shape[1:]
    sums = add_parts(offs, parts, 2, rows, cols)
    col = here()[1]
    for side in range(2):
        below[jnp.bitwise_xor(col, side)] = sums[side]
    total = (quarters[0][...] + quarters[1][...]) + (quarters[2][...] + quarters[3][...])
    band = probe_band.shape[0]
    probe_band[:, :cols] = total[:band]
    probe_band[:, cols:] = total[band:]


def add_own_kernel(offs, *refs):
    parts, own = refs[:8], refs[8]
    rows, cols = own.shape[1:]
    for strip in range(2):
        own[2 * strip], own[2 * strip + 1] = add_parts(offs, parts, strip, rows, cols)


def top_kernel(own, above, *outs):
    half, col, unused = here()
    mine = 2 * half + col
    for turn, out in zip(FOUR, outs):
        extra = jnp.where(half == turn // 2, above[turn % 2], 0.0)
        out[...] = own[jnp.bitwise_xor(mine, turn)] + extra


def join_kernel(*refs):
    probe, out, probe_out, sems = refs[4:]
    half, col, unused = here()
    mine = 2 * half + col
    pairs = [(ref, out.at[jnp.bitwise_xor(mine, turn)]) for turn, ref in zip(FOUR, refs)]
    for copy in fetch([(probe, probe_out), *pairs], sems):
        copy.wait()


SMEM = pl.BlockSpec(memory_space=pltpu.SMEM)
VMEM = pl.BlockSpec(memory_space=pltpu.VMEM)
HBM = pl.BlockSpec(memory_space=pltpu.HBM)
ANY = pl.BlockSpec(memory_space=pl.ANY)


def call(kernel, outs, scalars, arrays, flops, scratch=(), copies=0):
    outs, arrays = ([x if isinstance(x, tuple) else (x, VMEM) for x in xs] for xs in (outs, arrays))
    moved = sum(math.prod(x.shape) * x.dtype.itemsize for x, unused in [*arrays, *outs])
    scratch = [pltpu.VMEM(dims, jnp.float32) if isinstance(dims, tuple) else dims for dims in scratch]
    return pl.pallas_call(
        kernel,
        out_shape=[x for x, unused in outs],
        in_specs=[SMEM] * len(scalars) + [spec for unused, spec in arrays],
        out_specs=[spec for unused, spec in outs],
        scratch_shapes=scratch + [pltpu.SemaphoreType.DMA((copies,))] * (copies > 0),
        compiler_params=pltpu.CompilerParams(vmem_limit_bytes=VMEM_LIMIT),
        cost_estimate=pl.CostEstimate(flops=flops, bytes_accessed=moved, transcendentals=0),
    )(*scalars, *(pltpu.with_memory_space_constraint(x, pltpu.HBM) if spec is HBM else x for x, spec in arrays))


def shape(*dims):
    return jax.ShapeDtypeStruct(dims, jnp.float32)


def deal(values, axes, order):
    return [
        lax.ppermute(value, axes, [(k, k ^ turn) for k in range(len(order))]) if turn else value
        for turn, value in zip(order, values)
    ]


def sum_over(value, axis, size):
    step = 2
    while step < size:
        value = value + lax.ppermute(value, axis, [(k, k ^ step) for k in range(size)])
        step *= 2
    return value


def local(object_field, probe, offsets, slot_range, measured):
    width = probe.shape[-1]
    planes, rows, cols = 4, object_field.shape[2], object_field.shape[3]
    band = width // 4
    pairs = lax.axis_size("pair")
    half, col, core = (lax.axis_index(name) for name in PLANE)

    block = object_field.reshape(planes, rows, cols)
    *dealt, given = call(
        deal_kernel,
        [shape(rows + 8, cols)] * 4 + [shape(width, width)],
        (),
        ((block, HBM), (measured, HBM), (offsets, HBM)),
        0,
        [pltpu.SMEM(offsets.shape, offsets.dtype)],
        copies=6,
    )
    own = deal(dealt, PLANE[:2], FOUR)
    (lowest,) = call(lowest_kernel, [shape(2, rows, cols)], (), own, 0)
    lowest, given = lax.optimization_barrier((lowest, given))
    below = lax.ppermute(lowest, "pair", [(k, k - 1) for k in range(1, pairs)])
    taken = lax.ppermute(given, "half", [(0, 1), (1, 0)])

    turned = dict(zip(FOUR, own))
    offs = jnp.stack([turned[turn][rows : rows + 4, 0] for turn in range(4)]).astype(jnp.int32)
    others = lax.ppermute(offs, "core", [(0, 1), (1, 0)])
    offs = jnp.concatenate([jnp.where(core == 0, offs, others), jnp.where(core == 0, others, offs)], axis=1)
    split_at = jnp.where(half == 0, slot_range[0, 1], slot_range[0, 0])
    offs = jnp.concatenate([offs, jnp.full((1, offs.shape[1]), split_at, jnp.int32)], axis=0)
    scalars = (offs,)
    parts = call(
        pick_kernel,
        [shape(rows, cols)] * 8,
        scalars,
        (*own, below),
        32 * rows * width,
        [(planes, rows, cols)],
    )
    tabs, factors, order = (jnp.asarray(table) for table in tables(width))
    probe, target, tabs = call(
        ready_kernel,
        [shape(*probe.shape), shape(width, width), jax.ShapeDtypeStruct(tabs.shape, tabs.dtype)],
        scalars,
        (taken, (probe, HBM), (measured, HBM), (tabs, HBM), (order, HBM)),
        12 * width**3,
        [(width, width), pltpu.VMEM(order.shape, order.dtype)],
        copies=4,
    )
    *grad, keep = call(
        position_kernel,
        [shape(rows + 8 * band, cols)] + [shape(rows, cols)] * 7 + [shape(4, 2 * band, cols)],
        scalars,
        (*deal(parts, PLANE, EIGHT), probe, target, tabs, factors),
        8 * 12 * width**3,
        [(8, rows, cols)] * 2 + [(8, 2 * band, cols)],
    )
    got = deal(grad, PLANE, BACK)
    quarters = call(pair_kernel, [shape(2 * band, cols)] * 4, (), (keep, got[0]), 4 * band * width)
    lower_sums, probe_band = call(
        add_below_kernel,
        [shape(2, rows, cols), shape(band, width)],
        scalars,
        (*got, *deal(quarters, PLANE[:2], FOUR)),
        32 * rows * width,
    )
    above = lax.ppermute(lower_sums, "pair", [(k, k + 1) for k in range(pairs - 1)])
    doubling = pairs > 1 and pairs & (pairs - 1) == 0
    if doubling:
        near = lax.ppermute(probe_band, "pair", [(k, k ^ 1) for k in range(pairs)])
    (sums,) = call(add_own_kernel, [shape(planes, rows, cols)], scalars, got, 64 * rows * width)
    sums = call(top_kernel, [shape(rows, cols)] * 4, (), (sums, above), planes * rows * cols)
    if doubling:
        *sums, near = lax.optimization_barrier((*sums, near))
        probe_band = sum_over(probe_band + near, "pair", pairs)
    else:
        probe_band = lax.psum(probe_band, "pair")
    sums = deal(sums, PLANE[:2], FOUR)
    probe_grad = lax.all_gather(probe_band, PLANE, axis=0, tiled=True)
    object_grad, probe_grad = call(
        join_kernel,
        [(shape(planes, rows, cols), HBM), (shape(*probe_grad.shape), HBM)],
        (),
        [(x, ANY) for x in (*sums, probe_grad)],
        0,
        copies=5,
    )
    return (object_grad.reshape(object_field.shape), probe_grad.reshape(probe.shape))


def solution(mesh):
    tile, grp = mesh.shape["tile"], mesh.shape["grp"]
    devices = mesh.devices.reshape(tile // 2, 2, 2, grp // 2)
    inner = Mesh(devices, ("pair", "half", "col", "core"))
    strip, cols = ("pair", "half"), ("col", "core")
    in_specs = (
        P(None, None, strip, cols),
        P(),
        P(strip, cols, None),
        P(strip, None),
        P(strip, cols, None, None),
    )
    out_specs = (P(None, None, strip, cols), P())
    return jax.shard_map(local, mesh=inner, in_specs=in_specs, out_specs=out_specs, check_vma=False)
```

```python
import functools
import math

import jax
import jax.numpy as jnp
import ml_dtypes
import numpy as np
from jax import lax
from jax.experimental import pallas as pl
from jax.experimental.pallas import tpu as pltpu
from jax.sharding import Mesh, PartitionSpec as P

GRAD_WEIGHT = 0.0625
PLANE = ("half", "col", "core")
EIGHT, BACK, FOUR = (2, 4, 3, 5, 6, 7, 1, 0), (1, 4, 2, 5, 3, 6, 7, 0), (2, 1, 3, 0)
VMEM_LIMIT = 24 * 1024 * 1024


def tables(width):
    half = width // 2
    index = np.arange(half, dtype=np.int64)
    scale = 1.0 / math.sqrt(width)
    far = np.exp(-2j * math.pi / half * (index[:, None] * index[None, :] % half)) * scale
    near = []
    for offset in (0, half):
        shift = index[:, None] - index[None, :] + offset
        near.append(np.exp(1j * (math.pi / width * (shift * shift % (2 * width)) - math.pi / 4.0)) * scale)
    products = []
    for matrix in ((near[0] + near[1]) / 2.0, (near[0] - near[1]) / 2.0, far):
        for imag in (matrix.imag, -matrix.imag):
            table = np.block([[matrix.real, imag], [-imag, matrix.real]])
            high = table.astype(ml_dtypes.bfloat16)
            low = (table - high.astype(np.float64)).astype(ml_dtypes.bfloat16)
            products.append(np.concatenate([high, low], axis=0))
    angle = -2.0 * math.pi / width * index
    twiddles = []
    for part in (np.cos(angle), np.sin(angle)):
        rows = np.broadcast_to(part[:, None], (half, half))
        twiddles.append(np.concatenate([rows, np.broadcast_to(part[None, :], (8, half))], axis=0))
    order = np.zeros((width, width))
    order[np.arange(width), np.concatenate([2 * index, 2 * index + 1])] = 1.0
    order = np.stack([order, order.T]).astype(ml_dtypes.bfloat16)
    return np.stack(products), np.stack(twiddles).astype(np.float32), order


def split(value):
    high = value.astype(jnp.bfloat16)
    low = (value - high.astype(jnp.float32)).astype(jnp.bfloat16)
    return high, low


def dot(left, right):
    return jnp.dot(left, right, preferred_element_type=jnp.float32)


PLUS, MINUS, FAR = 0, 2, 4


def times_right(re, im, table):
    width = table.shape[1]
    high, low = split(jnp.concatenate([re, im], axis=1))
    twice = dot(jnp.concatenate([high, low], axis=0), table[:width])
    count = re.shape[0]
    out = twice[:count] + (twice[count:] + dot(high, table[width:]))
    return out[:, : width // 2], out[:, width // 2 :]


def times_left(re, im, table):
    width = table.shape[1]
    high, low = split(jnp.concatenate([re, im], axis=0))
    twice = dot(table[...], high)
    out = twice[:width] + (twice[width:] + dot(table[:width], low))
    return out[: width // 2], out[width // 2 :]


def butterfly(first, second):
    return first + second, first - second


def halves(value, axis):
    half = value.shape[axis] // 2
    return (value[:half], value[half:]) if axis == 0 else (value[:, :half], value[:, half:])


def turn_by(re, im, cos, sin):
    return re * cos - im * sin, re * sin + im * cos


def propagate(re, im, tabs, conj):
    for axis in (1, 0):
        (plus_re, minus_re), (plus_im, minus_im) = (butterfly(*halves(x, axis)) for x in (re, im))
        times = times_right if axis else times_left
        pick = int(conj) if axis else 1 - int(conj)
        plus_re, plus_im = times(plus_re, plus_im, tabs.at[PLUS + pick])
        minus_re, minus_im = times(minus_re, minus_im, tabs.at[MINUS + pick])
        re = jnp.concatenate(butterfly(plus_re, minus_re), axis=axis)
        im = jnp.concatenate(butterfly(plus_im, minus_im), axis=axis)
    return re, im


def twiddle(factors, axis, width):
    half = factors.shape[2]
    if axis:
        return factors[0, half : half + 1], factors[1, half : half + 1]
    return tuple(jnp.concatenate([factors[k, :half]] * (width // half), axis=1) for k in range(2))


def to_far(re, im, tabs, factors):
    for axis in (1, 0):
        (even_re, odd_re), (even_im, odd_im) = (butterfly(*halves(x, axis)) for x in (re, im))
        odd_re, odd_im = turn_by(odd_re, odd_im, *twiddle(factors, axis, re.shape[1]))
        times, table = (times_right, tabs.at[FAR]) if axis else (times_left, tabs.at[FAR + 1])
        (even_re, even_im), (odd_re, odd_im) = times(even_re, even_im, table), times(odd_re, odd_im, table)
        re, im = jnp.concatenate([even_re, odd_re], axis=axis), jnp.concatenate([even_im, odd_im], axis=axis)
    return re, im


def from_far(re, im, tabs, factors):
    for axis in (0, 1):
        (even_re, odd_re), (even_im, odd_im) = halves(re, axis), halves(im, axis)
        times, table = (times_right, tabs.at[FAR + 1]) if axis else (times_left, tabs.at[FAR])
        (even_re, even_im), (odd_re, odd_im) = times(even_re, even_im, table), times(odd_re, odd_im, table)
        cos, sin = twiddle(factors, axis, re.shape[1])
        odd_re, odd_im = turn_by(odd_re, odd_im, cos, -sin)
        re = jnp.concatenate(butterfly(even_re, odd_re), axis=axis)
        im = jnp.concatenate(butterfly(even_im, odd_im), axis=axis)
    return re, im


def slot_of(half, col, core):
    return 2 * (2 * col + core) + half


def slot_place(offs, mine, slot):
    lower = jnp.where(slot >= offs[4, 0], 1, 0)
    holder, at = jnp.bitwise_xor(2 * lower + slot // 4, mine), 2 * (slot % 4)
    return lower, offs[holder, at], offs[holder, at + 1]


def here():
    return tuple(lax.axis_index(name) for name in PLANE)


def fetch(pairs, sems):
    copies = [pltpu.make_async_copy(source, into, sems.at[k]) for k, (source, into) in enumerate(pairs)]
    for copy in copies:
        copy.start()
    return copies


def deal_kernel(block, measured, offsets_from, *refs):
    outs, given, offsets, sems = refs[:4], refs[4], refs[5], refs[6]
    half, col, unused = here()
    mine = 2 * half + col
    rows, cols = block.shape[1:]
    pairs = [(block.at[jnp.bitwise_xor(mine, turn)], out.at[pl.ds(0, rows)]) for turn, out in zip(FOUR, outs)]
    copies = fetch([(offsets_from, offsets), *pairs, (measured.at[0, 1 - half], given)], sems)
    copies[0].wait()
    lines = [jnp.full((1, cols), offsets[0, slot, axis], jnp.int32) for slot in range(2) for axis in range(2)]
    lines = jnp.concatenate(lines * 2, axis=0).astype(jnp.float32)
    for out in outs:
        out[rows:] = lines
    for copy in copies[1:]:
        copy.wait()


def lowest_kernel(*refs):
    gotten, out = dict(zip(FOUR, refs)), refs[4]
    rows = out.shape[1]
    half = here()[0]
    for turn in range(2):
        out[turn] = jnp.where(half == 0, gotten[turn][:rows], gotten[2 + turn][:rows])


def pick_kernel(offs, *refs):
    gotten, below, outs, own = dict(zip(FOUR, refs)), refs[4], refs[5:13], refs[13]
    rows, cols = outs[0].shape
    half, col, core = here()
    mine = 2 * half + col
    for turn in range(4):
        own[jnp.bitwise_xor(mine, turn)] = gotten[turn][:rows]
    row_ids = lax.broadcasted_iota(jnp.int32, (rows, cols), 0)
    col_ids = lax.broadcasted_iota(jnp.int32, (rows, cols), 1) + core * cols
    for turn, out in zip(EIGHT, outs):
        flat = jnp.bitwise_xor(2 * mine + core, turn)
        slot = slot_of(flat // 4, (flat // 2) % 2, flat % 2)
        lower, row_at, col_at = slot_place(offs, mine, slot)
        upper_rows = row_ids >= row_at
        left_cols = col_ids >= col_at

        def merged(side, lower=lower, upper_rows=upper_rows):
            second = own[2 + side]
            top = jnp.where(lower == 1, second, own[side])
            bottom = jnp.where(lower == 1, below[jnp.bitwise_xor(col, side)], second)
            return jnp.where(upper_rows, top, bottom)

        out[...] = jnp.where(left_cols, merged(0), merged(1))


def roll(value, rows, cols):
    return pltpu.roll(pltpu.roll(value, rows, 0), cols, 1)


def ready_kernel(offs, taken, probe_from, measured, tabs_from, order_from, probe, target, tabs, kept, order, sems):
    half, col, core = here()
    probe_copy, kept_copy, order_copy, tabs_copy = fetch(
        [(probe_from, probe), (measured.at[0, half], kept), (order_from, order), (tabs_from, tabs)], sems
    )
    slot = slot_of(half, col, core)
    lower, row_at, col_at = slot_place(offs, 2 * half + col, slot)
    probe_copy.wait()
    for part in range(2):
        probe[part] = roll(probe[part], row_at, lax.rem(col_at, target.shape[1]))
    kept_copy.wait()
    order_copy.wait()
    rest = jnp.where(lower == half, kept[...], taken[...])
    total = jnp.zeros_like(rest)
    for unused in range(3):
        part = rest.astype(jnp.bfloat16)
        rest = rest - part.astype(jnp.float32)
        total += dot(order[0], dot(part, order[1]).astype(jnp.bfloat16))
    target[...] = total
    tabs_copy.wait()


def position_kernel(offs, *refs):
    gotten, (probe, target, tabs, factors) = dict(zip(EIGHT, refs)), refs[8:12]
    outs, keep, (patch, grad, bands) = refs[12:20], refs[20], refs[21:]
    half, col, core = here()
    mine = 2 * half + col
    flat = 2 * mine + core
    unused, row_at, col_at = slot_place(offs, mine, slot_of(half, col, core))
    width = probe.shape[-1]
    lanes, band = width // 2, width // 4
    for turn in range(8):
        patch[jnp.bitwise_xor(flat, turn)] = gotten[turn][...]

    def load(plane):
        return jnp.concatenate([patch[2 * plane], patch[2 * plane + 1]], axis=1)

    def store(plane, value):
        grad[2 * plane] = value[:, :lanes]
        grad[2 * plane + 1] = value[:, lanes:]

    wave_re, wave_im = probe[0], probe[1]
    o0_re, o0_im, o1_re, o1_im = load(0), load(2), load(1), load(3)
    exit_re = wave_re * o0_re - wave_im * o0_im
    exit_im = wave_re * o0_im + wave_im * o0_re
    mid_re, mid_im = propagate(exit_re, exit_im, tabs, False)
    exit_re = mid_re * o1_re - mid_im * o1_im
    exit_im = mid_re * o1_im + mid_im * o1_re
    far_re, far_im = to_far(exit_re, exit_im, tabs, factors)
    excess = 2.0 * GRAD_WEIGHT * (far_re * far_re + far_im * far_im - target[...])
    back_re, back_im = from_far(excess * far_re, excess * far_im, tabs, factors)
    store(1, mid_re * back_re + mid_im * back_im)
    store(3, mid_re * back_im - mid_im * back_re)
    up_re = o1_re * back_re + o1_im * back_im
    up_im = o1_re * back_im - o1_im * back_re
    back_re, back_im = propagate(up_re, up_im, tabs, True)
    wave_re, wave_im = probe[0], probe[1]
    o0_re, o0_im = load(0), load(2)
    store(0, wave_re * back_re + wave_im * back_im)
    store(2, wave_re * back_im - wave_im * back_re)
    up_re = o0_re * back_re + o0_im * back_im
    up_im = o0_re * back_im - o0_im * back_re
    back_row, back_col = lax.rem(width - row_at, width), lax.rem(2 * width - col_at, width)
    for part, value in enumerate((up_re, up_im)):
        value = roll(value, back_row, back_col)
        for step in range(4):
            rows = value[step * band : (step + 1) * band]
            bands[4 * part + step, :band] = rows[:, :lanes]
            bands[4 * part + step, band:] = rows[:, lanes:]
    for turn, out in zip(BACK, outs):
        out[:width] = grad[jnp.bitwise_xor(flat, turn)]
    for part in range(4):
        keep[part] = bands[2 * part + core]
        start = width + 2 * band * part
        outs[0][start : start + 2 * band] = bands[2 * part + 1 - core]


def pair_kernel(keep, got, *outs):
    band = keep.shape[1]
    half, col, unused = here()
    first = got.shape[0] - 4 * band
    for turn, out in zip(FOUR, outs):
        part = jnp.bitwise_xor(2 * half + col, turn)
        out[...] = keep[part] + got[pl.ds(pl.multiple_of(first + band * part, band), band)]


def add_parts(offs, parts, strip, rows, cols):
    half, col, core = here()
    mine = 2 * half + col
    row_ids = lax.broadcasted_iota(jnp.int32, (rows, cols), 0)
    col_ids = lax.broadcasted_iota(jnp.int32, (rows, cols), 1) + core * cols
    sums = [jnp.zeros((rows, cols), jnp.float32)] * 2
    for turn, part in zip(BACK, parts):
        flat = jnp.bitwise_xor(2 * mine + core, turn)
        slot = slot_of(flat // 4, (flat // 2) % 2, flat % 2)
        lower, row_at, col_at = slot_place(offs, mine, slot)
        first = jnp.where(strip == lower, row_at, jnp.where(strip == lower + 1, 0, rows))
        last = jnp.where(strip == lower, rows, jnp.where(strip == lower + 1, row_at, 0))
        value = jnp.where((row_ids >= first) & (row_ids < last), part[:rows], 0.0)
        left = jnp.where(col_ids >= col_at, value, 0.0)
        sums = [sums[0] + left, sums[1] + (value - left)]
    return sums


def add_below_kernel(offs, *refs):
    parts, quarters, (below, probe_band) = refs[:8], refs[8:12], refs[12:]
    rows, cols = below.shape[1:]
    sums = add_parts(offs, parts, 2, rows, cols)
    col = here()[1]
    for side in range(2):
        below[jnp.bitwise_xor(col, side)] = sums[side]
    total = (quarters[0][...] + quarters[1][...]) + (quarters[2][...] + quarters[3][...])
    band = probe_band.shape[0]
    probe_band[:, :cols] = total[:band]
    probe_band[:, cols:] = total[band:]


def add_own_kernel(offs, *refs):
    parts, own = refs[:8], refs[8]
    rows, cols = own.shape[1:]
    for strip in range(2):
        own[2 * strip], own[2 * strip + 1] = add_parts(offs, parts, strip, rows, cols)


def top_kernel(own, above, *outs):
    half, col, unused = here()
    mine = 2 * half + col
    for turn, out in zip(FOUR, outs):
        extra = jnp.where(half == turn // 2, above[turn % 2], 0.0)
        out[...] = own[jnp.bitwise_xor(mine, turn)] + extra


def join_kernel(*refs):
    probe, out, probe_out, sems = refs[4:]
    half, col, unused = here()
    mine = 2 * half + col
    pairs = [(ref, out.at[jnp.bitwise_xor(mine, turn)]) for turn, ref in zip(FOUR, refs)]
    for copy in fetch([(probe, probe_out), *pairs], sems):
        copy.wait()


SMEM = pl.BlockSpec(memory_space=pltpu.SMEM)
VMEM = pl.BlockSpec(memory_space=pltpu.VMEM)
HBM = pl.BlockSpec(memory_space=pltpu.HBM)
ANY = pl.BlockSpec(memory_space=pl.ANY)


def call(kernel, outs, scalars, arrays, flops, scratch=(), copies=0):
    outs, arrays = ([x if isinstance(x, tuple) else (x, VMEM) for x in xs] for xs in (outs, arrays))
    moved = sum(math.prod(x.shape) * x.dtype.itemsize for x, unused in [*arrays, *outs])
    scratch = [pltpu.VMEM(dims, jnp.float32) if isinstance(dims, tuple) else dims for dims in scratch]
    return pl.pallas_call(
        kernel,
        out_shape=[x for x, unused in outs],
        in_specs=[SMEM] * len(scalars) + [spec for unused, spec in arrays],
        out_specs=[spec for unused, spec in outs],
        scratch_shapes=scratch + [pltpu.SemaphoreType.DMA((copies,))] * (copies > 0),
        compiler_params=pltpu.CompilerParams(vmem_limit_bytes=VMEM_LIMIT),
        cost_estimate=pl.CostEstimate(flops=flops, bytes_accessed=moved, transcendentals=0),
    )(*scalars, *(pltpu.with_memory_space_constraint(x, pltpu.HBM) if spec is HBM else x for x, spec in arrays))


def shape(*dims):
    return jax.ShapeDtypeStruct(dims, jnp.float32)


def deal(values, axes, order):
    return [
        lax.ppermute(value, axes, [(k, k ^ turn) for k in range(len(order))]) if turn else value
        for turn, value in zip(order, values)
    ]


def sum_over(value, axis, size):
    step = 2
    while step < size:
        value = value + lax.ppermute(value, axis, [(k, k ^ step) for k in range(size)])
        step *= 2
    return value


def local(object_field, probe, offsets, slot_range, measured):
    width = probe.shape[-1]
    planes, rows, cols = 4, object_field.shape[2], object_field.shape[3]
    band = width // 4
    pairs = lax.axis_size("pair")
    half, col, core = (lax.axis_index(name) for name in PLANE)

    block = object_field.reshape(planes, rows, cols)
    *dealt, given = call(
        deal_kernel,
        [shape(rows + 8, cols)] * 4 + [shape(width, width)],
        (),
        ((block, HBM), (measured, HBM), (offsets, HBM)),
        0,
        [pltpu.SMEM(offsets.shape, offsets.dtype)],
        copies=6,
    )
    own = deal(dealt, PLANE[:2], FOUR)
    (lowest,) = call(lowest_kernel, [shape(2, rows, cols)], (), own, 0)
    lowest, given = lax.optimization_barrier((lowest, given))
    below = lax.ppermute(lowest, "pair", [(k, k - 1) for k in range(1, pairs)])
    taken = lax.ppermute(given, "half", [(0, 1), (1, 0)])

    turned = dict(zip(FOUR, own))
    offs = jnp.stack([turned[turn][rows : rows + 4, 0] for turn in range(4)]).astype(jnp.int32)
    others = lax.ppermute(offs, "core", [(0, 1), (1, 0)])
    offs = jnp.concatenate([jnp.where(core == 0, offs, others), jnp.where(core == 0, others, offs)], axis=1)
    split_at = jnp.where(half == 0, slot_range[0, 1], slot_range[0, 0])
    offs = jnp.concatenate([offs, jnp.full((1, offs.shape[1]), split_at, jnp.int32)], axis=0)
    scalars = (offs,)
    parts = call(
        pick_kernel,
        [shape(rows, cols)] * 8,
        scalars,
        (*own, below),
        32 * rows * width,
        [(planes, rows, cols)],
    )
    tabs, factors, order = (jnp.asarray(table) for table in tables(width))
    probe, target, tabs = call(
        ready_kernel,
        [shape(*probe.shape), shape(width, width), jax.ShapeDtypeStruct(tabs.shape, tabs.dtype)],
        scalars,
        (taken, (probe, HBM), (measured, HBM), (tabs, HBM), (order, HBM)),
        12 * width**3,
        [(width, width), pltpu.VMEM(order.shape, order.dtype)],
        copies=4,
    )
    *grad, keep = call(
        position_kernel,
        [shape(rows + 8 * band, cols)] + [shape(rows, cols)] * 7 + [shape(4, 2 * band, cols)],
        scalars,
        (*deal(parts, PLANE, EIGHT), probe, target, tabs, factors),
        8 * 12 * width**3,
        [(8, rows, cols)] * 2 + [(8, 2 * band, cols)],
    )
    got = deal(grad, PLANE, BACK)
    quarters = call(pair_kernel, [shape(2 * band, cols)] * 4, (), (keep, got[0]), 4 * band * width)
    lower_sums, probe_band = call(
        add_below_kernel,
        [shape(2, rows, cols), shape(band, width)],
        scalars,
        (*got, *deal(quarters, PLANE[:2], FOUR)),
        32 * rows * width,
    )
    above = lax.ppermute(lower_sums, "pair", [(k, k + 1) for k in range(pairs - 1)])
    doubling = pairs > 1 and pairs & (pairs - 1) == 0
    if doubling:
        near = lax.ppermute(probe_band, "pair", [(k, k ^ 1) for k in range(pairs)])
    (sums,) = call(add_own_kernel, [shape(planes, rows, cols)], scalars, got, 64 * rows * width)
    sums = call(top_kernel, [shape(rows, cols)] * 4, (), (sums, above), planes * rows * cols)
    if doubling:
        *sums, near = lax.optimization_barrier((*sums, near))
        probe_band = sum_over(probe_band + near, "pair", pairs)
    else:
        probe_band = lax.psum(probe_band, "pair")
    sums = deal(sums, PLANE[:2], FOUR)
    probe_grad = lax.all_gather(probe_band, PLANE, axis=0, tiled=True)
    object_grad, probe_grad = call(
        join_kernel,
        [(shape(planes, rows, cols), HBM), (shape(*probe_grad.shape), HBM)],
        (),
        [(x, ANY) for x in (*sums, probe_grad)],
        0,
        copies=5,
    )
    return (object_grad.reshape(object_field.shape), probe_grad.reshape(probe.shape))


def solution(mesh):
    tile, grp = mesh.shape["tile"], mesh.shape["grp"]
    devices = mesh.devices.reshape(tile // 2, 2, 2, grp // 2)
    inner = Mesh(devices, ("pair", "half", "col", "core"))
    strip, cols = ("pair", "half"), ("col", "core")
    in_specs = (
        P(None, None, strip, cols),
        P(),
        P(strip, cols, None),
        P(strip, None),
        P(strip, cols, None, None),
    )
    out_specs = (P(None, None, strip, cols), P())
    return jax.shard_map(local, mesh=inner, in_specs=in_specs, out_specs=out_specs, check_vma=False)
```

```python
import functools
import math

import jax
import jax.numpy as jnp
import ml_dtypes
import numpy as np
from jax import lax
from jax.experimental import pallas as pl
from jax.experimental.pallas import tpu as pltpu
from jax.sharding import Mesh, PartitionSpec as P

GRAD_WEIGHT = 0.0625
PLANE = ("half", "col", "core")
EIGHT, BACK, FOUR = (4, 2, 5, 3, 6, 7, 1, 0), (1, 4, 2, 5, 3, 6, 7, 0), (2, 1, 3, 0)
VMEM_LIMIT = 24 * 1024 * 1024


def tables(width):
    half = width // 2
    index = np.arange(half, dtype=np.int64)
    scale = 1.0 / math.sqrt(width)
    far = np.exp(-2j * math.pi / half * (index[:, None] * index[None, :] % half)) * scale
    near = []
    for offset in (0, half):
        shift = index[:, None] - index[None, :] + offset
        near.append(np.exp(1j * (math.pi / width * (shift * shift % (2 * width)) - math.pi / 4.0)) * scale)
    products = []
    for matrix in ((near[0] + near[1]) / 2.0, (near[0] - near[1]) / 2.0, far):
        for imag in (matrix.imag, -matrix.imag):
            table = np.block([[matrix.real, imag], [-imag, matrix.real]])
            high = table.astype(ml_dtypes.bfloat16)
            low = (table - high.astype(np.float64)).astype(ml_dtypes.bfloat16)
            products.append(np.concatenate([high, low], axis=0))
    angle = -2.0 * math.pi / width * index
    twiddles = []
    for part in (np.cos(angle), np.sin(angle)):
        rows = np.broadcast_to(part[:, None], (half, half))
        twiddles.append(np.concatenate([rows, np.broadcast_to(part[None, :], (8, half))], axis=0))
    order = np.zeros((width, width))
    order[np.arange(width), np.concatenate([2 * index, 2 * index + 1])] = 1.0
    order = np.stack([order, order.T]).astype(ml_dtypes.bfloat16)
    return np.stack(products), np.stack(twiddles).astype(np.float32), order


def split(value):
    high = value.astype(jnp.bfloat16)
    low = (value - high.astype(jnp.float32)).astype(jnp.bfloat16)
    return high, low


def dot(left, right):
    return jnp.dot(left, right, preferred_element_type=jnp.float32)


PLUS, MINUS, FAR = 0, 2, 4


def times_right(re, im, table):
    width = table.shape[1]
    high, low = split(jnp.concatenate([re, im], axis=1))
    twice = dot(jnp.concatenate([high, low], axis=0), table[:width])
    count = re.shape[0]
    out = twice[:count] + (twice[count:] + dot(high, table[width:]))
    return out[:, : width // 2], out[:, width // 2 :]


def times_left(re, im, table):
    width = table.shape[1]
    high, low = split(jnp.concatenate([re, im], axis=0))
    twice = dot(table[...], high)
    out = twice[:width] + (twice[width:] + dot(table[:width], low))
    return out[: width // 2], out[width // 2 :]


def butterfly(first, second):
    return first + second, first - second


def halves(value, axis):
    half = value.shape[axis] // 2
    return (value[:half], value[half:]) if axis == 0 else (value[:, :half], value[:, half:])


def turn_by(re, im, cos, sin):
    return re * cos - im * sin, re * sin + im * cos


def propagate(re, im, tabs, conj):
    for axis in (1, 0):
        (plus_re, minus_re), (plus_im, minus_im) = (butterfly(*halves(x, axis)) for x in (re, im))
        times = times_right if axis else times_left
        pick = int(conj) if axis else 1 - int(conj)
        plus_re, plus_im = times(plus_re, plus_im, tabs.at[PLUS + pick])
        minus_re, minus_im = times(minus_re, minus_im, tabs.at[MINUS + pick])
        re = jnp.concatenate(butterfly(plus_re, minus_re), axis=axis)
        im = jnp.concatenate(butterfly(plus_im, minus_im), axis=axis)
    return re, im


def twiddle(factors, axis, width):
    half = factors.shape[2]
    if axis:
        return factors[0, half : half + 1], factors[1, half : half + 1]
    return tuple(jnp.concatenate([factors[k, :half]] * (width // half), axis=1) for k in range(2))


def to_far(re, im, tabs, factors):
    for axis in (1, 0):
        (even_re, odd_re), (even_im, odd_im) = (butterfly(*halves(x, axis)) for x in (re, im))
        odd_re, odd_im = turn_by(odd_re, odd_im, *twiddle(factors, axis, re.shape[1]))
        times, table = (times_right, tabs.at[FAR]) if axis else (times_left, tabs.at[FAR + 1])
        (even_re, even_im), (odd_re, odd_im) = times(even_re, even_im, table), times(odd_re, odd_im, table)
        re, im = jnp.concatenate([even_re, odd_re], axis=axis), jnp.concatenate([even_im, odd_im], axis=axis)
    return re, im


def from_far(re, im, tabs, factors):
    for axis in (0, 1):
        (even_re, odd_re), (even_im, odd_im) = halves(re, axis), halves(im, axis)
        times, table = (times_right, tabs.at[FAR + 1]) if axis else (times_left, tabs.at[FAR])
        (even_re, even_im), (odd_re, odd_im) = times(even_re, even_im, table), times(odd_re, odd_im, table)
        cos, sin = twiddle(factors, axis, re.shape[1])
        odd_re, odd_im = turn_by(odd_re, odd_im, cos, -sin)
        re = jnp.concatenate(butterfly(even_re, odd_re), axis=axis)
        im = jnp.concatenate(butterfly(even_im, odd_im), axis=axis)
    return re, im


def slot_of(half, col, core):
    return 2 * (2 * col + core) + half


def slot_place(offs, mine, slot):
    lower = jnp.where(slot >= offs[4, 0], 1, 0)
    holder, at = jnp.bitwise_xor(2 * lower + slot // 4, mine), 2 * (slot % 4)
    return lower, offs[holder, at], offs[holder, at + 1]


def here():
    return tuple(lax.axis_index(name) for name in PLANE)


def fetch(pairs, sems):
    copies = [pltpu.make_async_copy(source, into, sems.at[k]) for k, (source, into) in enumerate(pairs)]
    for copy in copies:
        copy.start()
    return copies


def deal_kernel(block, measured, offsets_from, *refs):
    outs, given, offsets, sems = refs[:4], refs[4], refs[5], refs[6]
    half, col, unused = here()
    mine = 2 * half + col
    rows, cols = block.shape[1:]
    pairs = [(block.at[jnp.bitwise_xor(mine, turn)], out.at[pl.ds(0, rows)]) for turn, out in zip(FOUR, outs)]
    copies = fetch([(offsets_from, offsets), *pairs, (measured.at[0, 1 - half], given)], sems)
    copies[0].wait()
    lines = [jnp.full((1, cols), offsets[0, slot, axis], jnp.int32) for slot in range(2) for axis in range(2)]
    lines = jnp.concatenate(lines * 2, axis=0).astype(jnp.float32)
    for out in outs:
        out[rows:] = lines
    for copy in copies[1:]:
        copy.wait()


def lowest_kernel(*refs):
    gotten, out = dict(zip(FOUR, refs)), refs[4]
    rows = out.shape[1]
    half = here()[0]
    for turn in range(2):
        out[turn] = jnp.where(half == 0, gotten[turn][:rows], gotten[2 + turn][:rows])


def pick_kernel(offs, *refs):
    gotten, below, outs, own = dict(zip(FOUR, refs)), refs[4], refs[5:13], refs[13]
    rows, cols = outs[0].shape
    half, col, core = here()
    mine = 2 * half + col
    for turn in range(4):
        own[jnp.bitwise_xor(mine, turn)] = gotten[turn][:rows]
    row_ids = lax.broadcasted_iota(jnp.int32, (rows, cols), 0)
    col_ids = lax.broadcasted_iota(jnp.int32, (rows, cols), 1) + core * cols
    for turn, out in zip(EIGHT, outs):
        flat = jnp.bitwise_xor(2 * mine + core, turn)
        slot = slot_of(flat // 4, (flat // 2) % 2, flat % 2)
        lower, row_at, col_at = slot_place(offs, mine, slot)
        upper_rows = row_ids >= row_at
        left_cols = col_ids >= col_at

        def merged(side, lower=lower, upper_rows=upper_rows):
            second = own[2 + side]
            top = jnp.where(lower == 1, second, own[side])
            bottom = jnp.where(lower == 1, below[jnp.bitwise_xor(col, side)], second)
            return jnp.where(upper_rows, top, bottom)

        out[...] = jnp.where(left_cols, merged(0), merged(1))


def roll(value, rows, cols):
    return pltpu.roll(pltpu.roll(value, rows, 0), cols, 1)


def ready_kernel(offs, taken, probe_from, measured, tabs_from, order_from, probe, target, tabs, kept, order, sems):
    half, col, core = here()
    probe_copy, kept_copy, order_copy, tabs_copy = fetch(
        [(probe_from, probe), (measured.at[0, half], kept), (order_from, order), (tabs_from, tabs)], sems
    )
    slot = slot_of(half, col, core)
    lower, row_at, col_at = slot_place(offs, 2 * half + col, slot)
    probe_copy.wait()
    for part in range(2):
        probe[part] = roll(probe[part], row_at, lax.rem(col_at, target.shape[1]))
    kept_copy.wait()
    order_copy.wait()
    rest = jnp.where(lower == half, kept[...], taken[...])
    total = jnp.zeros_like(rest)
    for unused in range(3):
        part = rest.astype(jnp.bfloat16)
        rest = rest - part.astype(jnp.float32)
        total += dot(order[0], dot(part, order[1]).astype(jnp.bfloat16))
    target[...] = total
    tabs_copy.wait()


def position_kernel(offs, *refs):
    gotten, (probe, target, tabs, factors) = dict(zip(EIGHT, refs)), refs[8:12]
    outs, keep, (patch, grad, bands) = refs[12:20], refs[20], refs[21:]
    half, col, core = here()
    mine = 2 * half + col
    flat = 2 * mine + core
    unused, row_at, col_at = slot_place(offs, mine, slot_of(half, col, core))
    width = probe.shape[-1]
    lanes, band = width // 2, width // 4
    for turn in range(8):
        patch[jnp.bitwise_xor(flat, turn)] = gotten[turn][...]

    def load(plane):
        return jnp.concatenate([patch[2 * plane], patch[2 * plane + 1]], axis=1)

    def store(plane, value):
        grad[2 * plane] = value[:, :lanes]
        grad[2 * plane + 1] = value[:, lanes:]

    wave_re, wave_im = probe[0], probe[1]
    o0_re, o0_im, o1_re, o1_im = load(0), load(2), load(1), load(3)
    exit_re = wave_re * o0_re - wave_im * o0_im
    exit_im = wave_re * o0_im + wave_im * o0_re
    mid_re, mid_im = propagate(exit_re, exit_im, tabs, False)
    exit_re = mid_re * o1_re - mid_im * o1_im
    exit_im = mid_re * o1_im + mid_im * o1_re
    far_re, far_im = to_far(exit_re, exit_im, tabs, factors)
    excess = 2.0 * GRAD_WEIGHT * (far_re * far_re + far_im * far_im - target[...])
    back_re, back_im = from_far(excess * far_re, excess * far_im, tabs, factors)
    store(1, mid_re * back_re + mid_im * back_im)
    store(3, mid_re * back_im - mid_im * back_re)
    up_re = o1_re * back_re + o1_im * back_im
    up_im = o1_re * back_im - o1_im * back_re
    back_re, back_im = propagate(up_re, up_im, tabs, True)
    wave_re, wave_im = probe[0], probe[1]
    o0_re, o0_im = load(0), load(2)
    store(0, wave_re * back_re + wave_im * back_im)
    store(2, wave_re * back_im - wave_im * back_re)
    up_re = o0_re * back_re + o0_im * back_im
    up_im = o0_re * back_im - o0_im * back_re
    back_row, back_col = lax.rem(width - row_at, width), lax.rem(2 * width - col_at, width)
    for part, value in enumerate((up_re, up_im)):
        value = roll(value, back_row, back_col)
        for step in range(4):
            rows = value[step * band : (step + 1) * band]
            bands[4 * part + step, :band] = rows[:, :lanes]
            bands[4 * part + step, band:] = rows[:, lanes:]
    for turn, out in zip(BACK, outs):
        out[:width] = grad[jnp.bitwise_xor(flat, turn)]
    for part in range(4):
        keep[part] = bands[2 * part + core]
        start = width + 2 * band * part
        outs[0][start : start + 2 * band] = bands[2 * part + 1 - core]


def pair_kernel(keep, got, *outs):
    band = keep.shape[1]
    half, col, unused = here()
    first = got.shape[0] - 4 * band
    for turn, out in zip(FOUR, outs):
        part = jnp.bitwise_xor(2 * half + col, turn)
        out[...] = keep[part] + got[pl.ds(pl.multiple_of(first + band * part, band), band)]


def add_parts(offs, parts, strip, rows, cols):
    half, col, core = here()
    mine = 2 * half + col
    row_ids = lax.broadcasted_iota(jnp.int32, (rows, cols), 0)
    col_ids = lax.broadcasted_iota(jnp.int32, (rows, cols), 1) + core * cols
    sums = [jnp.zeros((rows, cols), jnp.float32)] * 2
    for turn, part in zip(BACK, parts):
        flat = jnp.bitwise_xor(2 * mine + core, turn)
        slot = slot_of(flat // 4, (flat // 2) % 2, flat % 2)
        lower, row_at, col_at = slot_place(offs, mine, slot)
        first = jnp.where(strip == lower, row_at, jnp.where(strip == lower + 1, 0, rows))
        last = jnp.where(strip == lower, rows, jnp.where(strip == lower + 1, row_at, 0))
        value = jnp.where((row_ids >= first) & (row_ids < last), part[:rows], 0.0)
        left = jnp.where(col_ids >= col_at, value, 0.0)
        sums = [sums[0] + left, sums[1] + (value - left)]
    return sums


def add_below_kernel(offs, *refs):
    parts, quarters, (below, probe_band) = refs[:8], refs[8:12], refs[12:]
    rows, cols = below.shape[1:]
    sums = add_parts(offs, parts, 2, rows, cols)
    col = here()[1]
    for side in range(2):
        below[jnp.bitwise_xor(col, side)] = sums[side]
    total = (quarters[0][...] + quarters[1][...]) + (quarters[2][...] + quarters[3][...])
    band = probe_band.shape[0]
    probe_band[:, :cols] = total[:band]
    probe_band[:, cols:] = total[band:]


def add_own_kernel(offs, *refs):
    parts, own = refs[:8], refs[8]
    rows, cols = own.shape[1:]
    for strip in range(2):
        own[2 * strip], own[2 * strip + 1] = add_parts(offs, parts, strip, rows, cols)


def top_kernel(own, above, *outs):
    half, col, unused = here()
    mine = 2 * half + col
    for turn, out in zip(FOUR, outs):
        extra = jnp.where(half == turn // 2, above[turn % 2], 0.0)
        out[...] = own[jnp.bitwise_xor(mine, turn)] + extra


def join_kernel(*refs):
    probe, out, probe_out, sems = refs[4:]
    half, col, unused = here()
    mine = 2 * half + col
    pairs = [(ref, out.at[jnp.bitwise_xor(mine, turn)]) for turn, ref in zip(FOUR, refs)]
    for copy in fetch([(probe, probe_out), *pairs], sems):
        copy.wait()


SMEM = pl.BlockSpec(memory_space=pltpu.SMEM)
VMEM = pl.BlockSpec(memory_space=pltpu.VMEM)
HBM = pl.BlockSpec(memory_space=pltpu.HBM)
ANY = pl.BlockSpec(memory_space=pl.ANY)


def call(kernel, outs, scalars, arrays, flops, scratch=(), copies=0):
    outs, arrays = ([x if isinstance(x, tuple) else (x, VMEM) for x in xs] for xs in (outs, arrays))
    moved = sum(math.prod(x.shape) * x.dtype.itemsize for x, unused in [*arrays, *outs])
    scratch = [pltpu.VMEM(dims, jnp.float32) if isinstance(dims, tuple) else dims for dims in scratch]
    return pl.pallas_call(
        kernel,
        out_shape=[x for x, unused in outs],
        in_specs=[SMEM] * len(scalars) + [spec for unused, spec in arrays],
        out_specs=[spec for unused, spec in outs],
        scratch_shapes=scratch + [pltpu.SemaphoreType.DMA((copies,))] * (copies > 0),
        compiler_params=pltpu.CompilerParams(vmem_limit_bytes=VMEM_LIMIT),
        cost_estimate=pl.CostEstimate(flops=flops, bytes_accessed=moved, transcendentals=0),
    )(*scalars, *(pltpu.with_memory_space_constraint(x, pltpu.HBM) if spec is HBM else x for x, spec in arrays))


def shape(*dims):
    return jax.ShapeDtypeStruct(dims, jnp.float32)


def deal(values, axes, order):
    return [
        lax.ppermute(value, axes, [(k, k ^ turn) for k in range(len(order))]) if turn else value
        for turn, value in zip(order, values)
    ]


def sum_over(value, axis, size):
    step = 2
    while step < size:
        value = value + lax.ppermute(value, axis, [(k, k ^ step) for k in range(size)])
        step *= 2
    return value


def local(object_field, probe, offsets, slot_range, measured):
    width = probe.shape[-1]
    planes, rows, cols = 4, object_field.shape[2], object_field.shape[3]
    band = width // 4
    pairs = lax.axis_size("pair")
    half, col, core = (lax.axis_index(name) for name in PLANE)

    block = object_field.reshape(planes, rows, cols)
    *dealt, given = call(
        deal_kernel,
        [shape(rows + 8, cols)] * 4 + [shape(width, width)],
        (),
        ((block, HBM), (measured, HBM), (offsets, HBM)),
        0,
        [pltpu.SMEM(offsets.shape, offsets.dtype)],
        copies=6,
    )
    own = deal(dealt, PLANE[:2], FOUR)
    (lowest,) = call(lowest_kernel, [shape(2, rows, cols)], (), own, 0)
    lowest, given = lax.optimization_barrier((lowest, given))
    below = lax.ppermute(lowest, "pair", [(k, k - 1) for k in range(1, pairs)])
    taken = lax.ppermute(given, "half", [(0, 1), (1, 0)])

    turned = dict(zip(FOUR, own))
    offs = jnp.stack([turned[turn][rows : rows + 4, 0] for turn in range(4)]).astype(jnp.int32)
    others = lax.ppermute(offs, "core", [(0, 1), (1, 0)])
    offs = jnp.concatenate([jnp.where(core == 0, offs, others), jnp.where(core == 0, others, offs)], axis=1)
    split_at = jnp.where(half == 0, slot_range[0, 1], slot_range[0, 0])
    offs = jnp.concatenate([offs, jnp.full((1, offs.shape[1]), split_at, jnp.int32)], axis=0)
    scalars = (offs,)
    parts = call(
        pick_kernel,
        [shape(rows, cols)] * 8,
        scalars,
        (*own, below),
        32 * rows * width,
        [(planes, rows, cols)],
    )
    tabs, factors, order = (jnp.asarray(table) for table in tables(width))
    probe, target, tabs = call(
        ready_kernel,
        [shape(*probe.shape), shape(width, width), jax.ShapeDtypeStruct(tabs.shape, tabs.dtype)],
        scalars,
        (taken, (probe, HBM), (measured, HBM), (tabs, HBM), (order, HBM)),
        12 * width**3,
        [(width, width), pltpu.VMEM(order.shape, order.dtype)],
        copies=4,
    )
    *grad, keep = call(
        position_kernel,
        [shape(rows + 8 * band, cols)] + [shape(rows, cols)] * 7 + [shape(4, 2 * band, cols)],
        scalars,
        (*deal(parts, PLANE, EIGHT), probe, target, tabs, factors),
        8 * 12 * width**3,
        [(8, rows, cols)] * 2 + [(8, 2 * band, cols)],
    )
    got = deal(grad, PLANE, BACK)
    quarters = call(pair_kernel, [shape(2 * band, cols)] * 4, (), (keep, got[0]), 4 * band * width)
    lower_sums, probe_band = call(
        add_below_kernel,
        [shape(2, rows, cols), shape(band, width)],
        scalars,
        (*got, *deal(quarters, PLANE[:2], FOUR)),
        32 * rows * width,
    )
    above = lax.ppermute(lower_sums, "pair", [(k, k + 1) for k in range(pairs - 1)])
    doubling = pairs > 1 and pairs & (pairs - 1) == 0
    if doubling:
        near = lax.ppermute(probe_band, "pair", [(k, k ^ 1) for k in range(pairs)])
    (sums,) = call(add_own_kernel, [shape(planes, rows, cols)], scalars, got, 64 * rows * width)
    sums = call(top_kernel, [shape(rows, cols)] * 4, (), (sums, above), planes * rows * cols)
    if doubling:
        *sums, near = lax.optimization_barrier((*sums, near))
        probe_band = sum_over(probe_band + near, "pair", pairs)
    else:
        probe_band = lax.psum(probe_band, "pair")
    sums = deal(sums, PLANE[:2], FOUR)
    probe_grad = lax.all_gather(probe_band, PLANE, axis=0, tiled=True)
    object_grad, probe_grad = call(
        join_kernel,
        [(shape(planes, rows, cols), HBM), (shape(*probe_grad.shape), HBM)],
        (),
        [(x, ANY) for x in (*sums, probe_grad)],
        0,
        copies=5,
    )
    return (object_grad.reshape(object_field.shape), probe_grad.reshape(probe.shape))


def solution(mesh):
    tile, grp = mesh.shape["tile"], mesh.shape["grp"]
    devices = mesh.devices.reshape(tile // 2, 2, 2, grp // 2)
    inner = Mesh(devices, ("pair", "half", "col", "core"))
    strip, cols = ("pair", "half"), ("col", "core")
    in_specs = (
        P(None, None, strip, cols),
        P(),
        P(strip, cols, None),
        P(strip, None),
        P(strip, cols, None, None),
    )
    out_specs = (P(None, None, strip, cols), P())
    return jax.shard_map(local, mesh=inner, in_specs=in_specs, out_specs=out_specs, check_vma=False)
```
